32 devices in a mesh: grp: 2 (over y), dp: 8 (over z, x), head: 2 (over core).
Axes of the slice: x: 2, y: 2, z: 4, core: 2. Of those that a mesh axis runs over, the one named last changes fastest.
Arguments:
- tokens: bfloat16 [2, 896, 4096], P(None, ('grp', 'dp'), 'head'), parts along dimension 1, may hold values from -6 to 6
- inner_weight: bfloat16 [4096, 256], P(None, 'head'), may hold values from -0.09375 to 0.09375
- gate_weight: bfloat16 [4096, 256], P(None, 'head'), may hold values from -0.09375 to 0.09375
- group_weight: bfloat16 [4096, 128], P(None, 'head'), may hold values from -0.09375 to 0.09375
- delta_weight: bfloat16 [4096, 2], P(None, 'head'), may hold values from -0.09375 to 0.09375
- inner_taps: float32 [4, 256], P(None, 'head'), may hold values from -1 to 1
- inner_offset: float32 [256], P('head'), may hold values from -0.5 to 0.5
- group_taps: float32 [4, 128], P(None, 'head'), may hold values from -1 to 1
- group_offset: float32 [128], P('head'), may hold values from -0.5 to 0.5
- decay_log: float32 [2], P('head'), may hold values from -2.3 to 0.5
- delta_bias: float32 [2], P('head'), may hold values from -1 to 1
- skip_gain: float32 [2], P('head'), may hold values from 0.5 to 2
- inner_window: bfloat16 [896, 3, 256], P(('grp', 'dp'), None, 'head'), parts along dimension 0, may hold values from -6 to 6
- group_window: bfloat16 [896, 3, 128], P(('grp', 'dp'), None, 'head'), parts along dimension 0, may hold values from -6 to 6
- scan_state: bfloat16 [896, 256, 64], P(('grp', 'dp'), 'head'), parts along dimension 0, may hold values from -6 to 6
- send_list: int32 [16, 56], P(('grp', 'dp')), parts along dimension 0, may hold values from -1 to 55, as said below
- receive_list: int32 [16, 56], P(('grp', 'dp')), parts along dimension 0, may hold values from -1 to 55, as said below
- live_count: int32 [16], P(('grp', 'dp')), parts along dimension 0, may hold values from 1 to 56, as said below
Outputs:
- gated_output: bfloat16 [2, 896, 256], P(None, ('grp', 'dp'), 'head'), parts along dimension 1
- inner_next: bfloat16 [896, 3, 256], P(('grp', 'dp'), None, 'head'), parts along dimension 0
- group_next: bfloat16 [896, 3, 128], P(('grp', 'dp'), None, 'head'), parts along dimension 0
- scan_next: bfloat16 [896, 256, 64], P(('grp', 'dp'), 'head'), parts along dimension 0
The draws below stay inside these ranges and needn't reach their ends.
There are 2 independent parts, one for each index of `grp`. The reference program is written for one: setup_inputs(seed, part) draws one part's arguments, and reference() takes and returns one part's arrays. A program takes and returns all parts, laid end to end along the dimension named above; an argument that names none is the same for every part. Nothing has to cross between parts.
Inputs may be any that keep to these rules, and one draw needn't show every extreme that they name: `send_list`: row s lists, at position d * 7 + c, the local slot of old replica s whose states become the c-th arrival at replica d, or -1; each replica sends exactly 28 distinct slots, exactly 7 to each of 4 other replicas and none to itself. `receive_list`: entry d, k is -1 when new slot k of replica d keeps the state of old slot k of the same replica, else s * 7 * 7 + c (7 = 1) where the c-th state that replica s sends to replica d is the one it takes; a slot takes an arrival exactly when replica d sends its own old slot k away; it agrees with send_list. `live_count`: some replica is full and some holds a single live request.
All inputs are finite; a program needn't handle non-finite values.
Results may differ from the reference program's by a relative error of at most 0.008.
Values may be sent and summed in bfloat16 or wider, within the bound.
No kernel may reach another device: no remote copies, remote signals or barrier semaphores. Data moves between devices by JAX's collectives and lax.ppermute only.
A program may use at most 64 MiB of HBM per device.

```python
import jax
import jax.numpy as jnp
from jax import lax

D = 4096
P_SIZE = 128
N = 64
CONV_K = 4
STEPS = 2
REQ_DEV = 56
HEADS = 2
SLOTS = 448
CAP = 7
N_DP = 8


def plan(key):
    replicas = SLOTS // REQ_DEV
    moving = REQ_DEV // 2
    capacity = max(1, moving // (replicas // 2))
    groups = moving // capacity
    key_shift, key_order = jax.random.split(key)
    shifts = 1 + jax.random.permutation(key_shift, replicas - 1)[:groups]
    orders = jax.vmap(lambda single: jax.random.permutation(single, REQ_DEV))(jax.random.split(key_order, replicas))
    sender = jnp.arange(replicas, dtype=jnp.int32)[:, None]
    lift = jnp.where(sender == 0, orders[:, :1] + 1, 0)
    leaving = (orders[:, :moving] - lift) % REQ_DEV
    position = jnp.arange(moving, dtype=jnp.int32)[None, :]
    group = position // capacity
    ranking = position % capacity
    target = (sender + shifts[group]) % replicas
    source = (sender - shifts[group]) % replicas
    rows = jnp.broadcast_to(sender, leaving.shape)
    outgoing = jnp.full((replicas, replicas * capacity), -1, jnp.int32)
    outgoing = outgoing.at[rows, target * capacity + ranking].set(leaving.astype(jnp.int32))
    incoming = jnp.full((replicas, REQ_DEV), -1, jnp.int32)
    incoming = incoming.at[rows, leaving].set((source * capacity + ranking).astype(jnp.int32))
    return (outgoing.astype(jnp.int32), incoming.astype(jnp.int32))


def draw_send_list(key, part):
    tables = plan(key)
    return tables[0]


def draw_receive_list(key, part):
    tables = plan(key)
    return tables[1]


def draw_live_count(key, part):
    key = jax.random.fold_in(key, 5)
    replicas = SLOTS // REQ_DEV
    key_count, key_pick = jax.random.split(key)
    counts = jax.random.randint(key_count, (replicas,), 1, REQ_DEV + 1)
    chosen = jax.random.permutation(key_pick, replicas)
    counts = counts.at[chosen[0]].set(REQ_DEV)
    counts = counts.at[chosen[1]].set(1)
    return counts.astype(jnp.int32)


def steps_of(stream_key, dims, cuts, smallest, high):
    factor_of, own = 1.0, jax.random.fold_in(stream_key, 6)
    for dim, parts in cuts:
        heights = jnp.exp(jax.random.uniform(jax.random.fold_in(own, dim), (parts,), jnp.float32, smallest / len(cuts), high / len(cuts)))
        factor_of = factor_of * jnp.repeat(heights, dims[dim] // parts).reshape([-1 if axis == dim else 1 for axis in range(len(dims))])
    return factor_of


def noise(stream_key, shape, width, limit, cuts=(), kind=jnp.bfloat16):
    drawn = width * jax.random.normal(stream_key, shape, jnp.float32)
    if cuts:
        drawn = drawn * steps_of(stream_key, shape, cuts, -0.22, 0.18)
    return jnp.clip(drawn, -limit, limit).astype(kind)


def setup_inputs(seed: int = 0, part: int = 0) -> dict:
    keys = jax.random.split(jax.random.key(seed), 19)
    own_keys = jax.random.split(jax.random.fold_in(keys[18], part), 19)
    return {
        "tokens": noise(own_keys[0], (STEPS, SLOTS, D), 1.0, 6.0, ((1, 8), (2, 2))),
        "inner_weight": noise(keys[1], (D, HEADS * P_SIZE), D ** -0.5, 0.09375, ((1, 2),)),
        "gate_weight": noise(keys[2], (D, HEADS * P_SIZE), D ** -0.5, 0.09375, ((1, 2),)),
        "group_weight": noise(keys[3], (D, 2 * N), D ** -0.5, 0.09375, ((1, 2),)),
        "delta_weight": noise(keys[4], (D, HEADS), D ** -0.5, 0.09375, ((1, 2),)),
        "inner_taps": jnp.clip(jax.random.uniform(keys[5], (CONV_K, HEADS * P_SIZE), jnp.float32, -1.0, 1.0) * steps_of(keys[5], (CONV_K, HEADS * P_SIZE), ((1, 2),), -0.4, 0.0), -1.0, 1.0),
        "inner_offset": jnp.clip(jax.random.uniform(keys[6], (HEADS * P_SIZE,), jnp.float32, -0.5, 0.5) * steps_of(keys[6], (HEADS * P_SIZE,), ((0, 2),), -0.4, 0.0), -0.5, 0.5),
        "group_taps": jnp.clip(jax.random.uniform(keys[7], (CONV_K, 2 * N), jnp.float32, -1.0, 1.0) * steps_of(keys[7], (CONV_K, 2 * N), ((1, 2),), -0.4, 0.0), -1.0, 1.0),
        "group_offset": jnp.clip(jax.random.uniform(keys[8], (2 * N,), jnp.float32, -0.5, 0.5) * steps_of(keys[8], (2 * N,), ((0, 2),), -0.4, 0.0), -0.5, 0.5),
        "decay_log": jnp.clip(-2.3 + 2.8 * jax.random.uniform(keys[9], (HEADS,), jnp.float32) ** steps_of(keys[9], (HEADS,), ((0, 2),), -0.2, 0.2), -2.3, 0.5),
        "delta_bias": jnp.clip(jax.random.uniform(keys[10], (HEADS,), jnp.float32, -1.0, 1.0) * steps_of(keys[10], (HEADS,), ((0, 2),), -0.4, 0.0), -1.0, 1.0),
        "skip_gain": jnp.clip(0.5 + 1.5 * jax.random.uniform(keys[11], (HEADS,), jnp.float32) ** steps_of(keys[11], (HEADS,), ((0, 2),), -0.2, 0.2), 0.5, 2.0),
        "inner_window": noise(own_keys[12], (SLOTS, CONV_K - 1, HEADS * P_SIZE), 1.0, 6.0, ((0, 8), (2, 2))),
        "group_window": noise(own_keys[13], (SLOTS, CONV_K - 1, 2 * N), 1.0, 6.0, ((0, 8), (2, 2))),
        "scan_state": noise(own_keys[14], (SLOTS, HEADS * P_SIZE, N), 1.0, 6.0, ((0, 8), (1, 2))),
        "send_list": draw_send_list(jax.random.fold_in(jax.random.fold_in(keys[18], part), 71), part),
        "receive_list": draw_receive_list(jax.random.fold_in(jax.random.fold_in(keys[18], part), 71), part),
        "live_count": draw_live_count(jax.random.fold_in(jax.random.fold_in(keys[18], part), 71), part),
    }


def convolve(carried, incoming, taps, offset):
    tap_count = taps.shape[0]
    step_count = incoming.shape[0]
    joined = jnp.concatenate([carried, jnp.transpose(incoming, (1, 0, 2))], axis=1)
    widened = joined.astype(jnp.float32)
    outputs = []
    for position in range(step_count):
        window = widened[:, position:position + tap_count]
        summed = jnp.sum(window * taps[None], axis=1) + offset[None]
        outputs.append(jax.nn.silu(summed).astype(jnp.bfloat16))
    return jnp.stack(outputs), joined[:, step_count:]


def recurrence(inner_conv, gate_raw, group_conv, delta_rate, decay_rate, carried, skip_value):
    state_width = group_conv.shape[2] // 2
    hidden = carried.astype(jnp.float32)
    rounded = carried
    outputs = []
    for position in range(inner_conv.shape[0]):
        inner_now = inner_conv[position].astype(jnp.float32)
        input_map = group_conv[position, :, :state_width].astype(jnp.float32)
        output_map = group_conv[position, :, state_width:].astype(jnp.float32)
        hidden = decay_rate[position][:, :, None] * hidden + (delta_rate[position] * inner_now)[:, :, None] * input_map[:, None, :]
        output = jnp.sum(hidden * output_map[:, None, :], axis=2) + skip_value[None, :] * inner_now
        outputs.append((output * jax.nn.silu(gate_raw[position].astype(jnp.float32))).astype(jnp.bfloat16))
        rounded = hidden.astype(jnp.bfloat16)
        hidden = lax.optimization_barrier(rounded).astype(jnp.float32)
    return jnp.stack(outputs), rounded


def reference(tokens, inner_weight, gate_weight, group_weight, delta_weight, inner_taps, inner_offset, group_taps, group_offset, decay_log, delta_bias, skip_gain, inner_window, group_window, scan_state, send_list, receive_list, live_count):
    token_rows = tokens.reshape(STEPS * SLOTS, D)

    def project(weight):
        return jnp.dot(token_rows, weight, preferred_element_type=jnp.float32).astype(jnp.bfloat16).reshape(STEPS, SLOTS, -1)

    inner_raw = project(inner_weight)
    gate_raw = project(gate_weight)
    group_raw = project(group_weight)
    delta_raw = project(delta_weight)
    slot_ids = jnp.arange(SLOTS, dtype=jnp.int32)
    replica = slot_ids // REQ_DEV
    arrival = receive_list.reshape(SLOTS)
    moved = arrival >= 0
    safe = jnp.where(moved, arrival, 0)
    sender = safe // CAP
    column = replica * CAP + safe % CAP
    anchor = jnp.where(moved, sender * REQ_DEV + send_list[sender, column], slot_ids).astype(jnp.int32)
    inner_here = inner_window[anchor]
    group_here = group_window[anchor]
    scan_here = scan_state[anchor]
    inner_conv, inner_carry = convolve(inner_here, inner_raw, inner_taps, inner_offset)
    group_conv, group_carry = convolve(group_here, group_raw, group_taps, group_offset)
    delta_head = jax.nn.softplus(delta_raw.astype(jnp.float32) + delta_bias)
    decay_head = jnp.exp(-delta_head * jnp.exp(decay_log))
    delta_rate = jnp.repeat(delta_head, P_SIZE, axis=-1)
    decay_rate = jnp.repeat(decay_head, P_SIZE, axis=-1)
    skip_value = jnp.repeat(skip_gain, P_SIZE)

    def blocked(array):
        return jnp.swapaxes(array.reshape((STEPS, N_DP, REQ_DEV) + array.shape[2:]), 0, 1)

    def per_replica(pieces):
        return recurrence(pieces[0], pieces[1], pieces[2], pieces[3], pieces[4], pieces[5], skip_value)

    gated_blocks, scan_blocks = lax.map(per_replica, (blocked(inner_conv), blocked(gate_raw), blocked(group_conv), blocked(delta_rate), blocked(decay_rate), scan_here.reshape(N_DP, REQ_DEV, HEADS * P_SIZE, N)))
    gated_all = jnp.swapaxes(gated_blocks, 0, 1).reshape(STEPS, SLOTS, HEADS * P_SIZE)
    scan_all = scan_blocks.reshape(SLOTS, HEADS * P_SIZE, N)
    living = (slot_ids % REQ_DEV) < live_count[replica]
    zero = jnp.zeros((), jnp.bfloat16)
    gated_output = jnp.where(living[None, :, None], gated_all, zero)
    inner_next = jnp.where(living[:, None, None], inner_carry, zero)
    group_next = jnp.where(living[:, None, None], group_carry, zero)
    scan_next = jnp.where(living[:, None, None], scan_all, zero)
    return gated_output, inner_next, group_next, scan_next
```

```python
import functools

import jax
import jax.numpy as jnp
from jax import lax
from jax.experimental import pallas as pl
from jax.experimental.pallas import tpu as pltpu
from jax.sharding import PartitionSpec as P

F32 = jnp.float32
BF16 = jnp.bfloat16
VMEM_LIMIT = 32 * 1024 * 1024
MAX_SHIFTS = 16
LANES = 128


def round_up(value, step):
    return -(-value // step) * step


def silu(value):
    return value * jax.nn.sigmoid(value)


def block_rows_of(replicas):
    return 1 if replicas <= MAX_SHIFTS else replicas


def pack_kernel(replicas, cap, cap_rows, send, scan, inner, group, *refs):
    per_block = block_rows_of(replicas)
    count = replicas - 1 if per_block == 1 else 1
    state_out, window_out = refs[:count], refs[count : 2 * count]
    table, picked, sem = refs[2 * count :]
    me = lax.axis_index("dp")
    plan = []
    for block in range(count):
        for inside in range(per_block):
            target = lax.rem(me + block + 1, replicas) if per_block == 1 else inside
            for c in range(cap):
                plan.append((block, inside * cap + c, inside * cap_rows + c, target * cap + c))

    def copy(position, block, row, index):
        return pltpu.make_async_copy(scan.at[index], state_out[block].at[row], sem.at[position])

    indices = []
    for position, (block, row, _, place) in enumerate(plan):
        index = send[0, place]
        indices.append(index)

        @pl.when(index >= 0)
        def _():
            copy(position, block, row, index).start()

    taps = inner.shape[0]
    width = group.shape[2]
    for tap in range(taps):
        table[:, tap * LANES : (tap + 1) * LANES] = inner[tap].astype(F32)
        table[:, (taps + tap) * LANES : (taps + tap) * LANES + width] = group[tap].astype(F32)
        table[:, (taps + tap) * LANES + width : (taps + tap + 1) * LANES] = jnp.zeros(
            (table.shape[0], LANES - width), F32
        )
    picked[...] = jnp.zeros_like(picked)
    rows = per_block * cap_rows
    for (block, _, row, _), index in zip(plan, indices):
        picked[pl.ds(block * rows + row, 1), :] = table[pl.ds(jnp.maximum(index, 0), 1), :]
    for block in range(count):
        window_out[block][...] = picked[block * rows : (block + 1) * rows, :].astype(BF16)
    for (position, (block, row, _, _)), index in zip(enumerate(plan), indices):

        @pl.when(index >= 0)
        def _():
            copy(position, block, row, index).wait()


def pack(replicas, cap, send_list, scan, inner, group):
    per_block = block_rows_of(replicas)
    count = replicas - 1 if per_block == 1 else 1
    cap_rows = round_up(cap, 8)
    taps, slots, _ = inner.shape
    lanes = 2 * taps * LANES
    rows = per_block * cap_rows
    state_shape = jax.ShapeDtypeStruct((per_block * cap,) + scan.shape[1:], BF16)
    window_shape = jax.ShapeDtypeStruct((rows, lanes), BF16)
    vmem = pl.BlockSpec(memory_space=pltpu.VMEM)
    smem = pl.BlockSpec(memory_space=pltpu.SMEM)
    hbm = pl.BlockSpec(memory_space=pl.ANY)
    outs = pl.pallas_call(
        functools.partial(pack_kernel, replicas, cap, cap_rows),
        out_shape=[state_shape] * count + [window_shape] * count,
        in_specs=[smem, hbm, vmem, vmem],
        out_specs=[hbm] * count + [vmem] * count,
        scratch_shapes=[
            pltpu.VMEM((slots, lanes), F32),
            pltpu.VMEM((count * rows, lanes), F32),
            pltpu.SemaphoreType.DMA((replicas * cap,)),
        ],
        compiler_params=pltpu.CompilerParams(vmem_limit_bytes=VMEM_LIMIT),
        cost_estimate=pl.CostEstimate(flops=0, bytes_accessed=2_000_000, transcendentals=0),
        name="pack_leaving",
    )(send_list, scan, inner, group)
    return outs[:count], outs[count:]


def arrival_row(replicas, cap, cap_rows, me, entry):
    source = entry // cap
    inside = entry - source * cap
    if block_rows_of(replicas) == 1:
        source = lax.rem(me - source + replicas, replicas) - 1
    return source * cap_rows + inside


def split_order(receive, slots, order):
    def step(slot, counts):
        kept, moved = counts
        stays = receive[0, slot] < 0
        order[jnp.where(stays, kept, slots // 2 + moved)] = slot
        return (kept + jnp.where(stays, 1, 0), moved + jnp.where(stays, 0, 1))

    lax.fori_loop(0, slots, step, (jnp.int32(0), jnp.int32(0)))


def project_kernel(
    replicas,
    cap,
    cap_rows,
    receive,
    live,
    decay_log,
    delta_bias,
    skip_gain,
    own,
    other,
    inner_weight,
    gate_weight,
    group_weight,
    delta_weight,
    inner_taps,
    inner_offset,
    group_taps,
    group_offset,
    inner,
    group,
    *refs,
):
    arrived = refs[:-12]
    (
        inner_next,
        group_next,
        driven,
        decay,
        skipped,
        gate,
        maps,
        table,
        landed,
        small,
        ordered,
        order,
    ) = refs[-12:]
    me = lax.axis_index("dp")
    head = lax.axis_index("head")
    taps, slots, _ = inner.shape
    half = own.shape[1]
    width = group.shape[2]
    steps = own.shape[0] // slots

    split_order(receive, slots, order)
    for tap in range(taps):
        table[:, tap * LANES : (tap + 1) * LANES] = inner[tap].astype(F32)
        table[:, (taps + tap) * LANES : (taps + tap) * LANES + width] = group[tap].astype(F32)
    rows = arrived[0].shape[0]
    for block, ref in enumerate(arrived):
        landed[block * rows : (block + 1) * rows, :] = ref[...].astype(F32)
    for position in range(slots // 2):
        slot = order[slots // 2 + position]
        row = arrival_row(replicas, cap, cap_rows, me, receive[0, slot])
        table[pl.ds(slot, 1), :] = landed[pl.ds(row, 1), :]

    mine = pl.ds(pl.multiple_of(head * half, half), half)
    theirs = pl.ds(pl.multiple_of((1 - head) * half, half), half)

    def columns(weight):
        return jnp.dot(own[...], weight[mine, :], preferred_element_type=F32) + jnp.dot(
            other[...], weight[theirs, :], preferred_element_type=F32
        )

    def rows_of(weight, count):
        def one(tokens, part):
            piece = weight[:, part]
            if count > 1:
                piece = jnp.broadcast_to(piece, (count, half))
            return lax.dot_general(
                tokens, piece, (((1,), (1,)), ((), ())), preferred_element_type=F32
            )

        return one(own[...], mine) + one(other[...], theirs)

    def rounded(value):
        return value.astype(BF16).astype(F32)

    inner_raw = rounded(columns(inner_weight))
    gate_raw = rounded(columns(gate_weight))
    group_raw = rounded(rows_of(group_weight, 1))
    delta_raw = rounded(rows_of(delta_weight, LANES))

    living = lax.broadcasted_iota(jnp.int32, (slots, LANES), 0) < live[0]
    gate[...] = silu(gate_raw)
    shifted = delta_raw + delta_bias[0]
    delta = jnp.maximum(shifted, 0.0) + jnp.log1p(jnp.exp(-jnp.abs(shifted)))
    slope = jnp.exp(jnp.full((1, LANES), decay_log[0], F32))
    decay[...] = jnp.exp(-delta * slope)

    def convolve(carried, raw, weights, offset):
        joined = carried + [raw[step * slots : (step + 1) * slots] for step in range(steps)]
        results = []
        for step in range(steps):
            summed = offset[...]
            for tap in range(taps + 1):
                summed = summed + joined[step + tap] * weights[tap : tap + 1, :]
            results.append(rounded(silu(summed)))
        return results, joined[steps:]

    inner_conv, inner_carry = convolve(
        [table[:, tap * LANES : (tap + 1) * LANES] for tap in range(taps)],
        inner_raw,
        inner_taps,
        inner_offset,
    )
    group_conv, group_carry = convolve(
        [
            table[:, (taps + tap) * LANES : (taps + tap) * LANES + width]
            for tap in range(taps)
        ],
        group_raw,
        group_taps,
        group_offset,
    )
    for tap in range(taps):
        inner_next[tap] = jnp.where(living, inner_carry[tap], 0.0).astype(BF16)
        group_next[tap] = jnp.where(living[:, :width], group_carry[tap], 0.0).astype(BF16)
    for step in range(steps):
        part = slice(step * slots, (step + 1) * slots)
        driven[part, :] = delta[part] * inner_conv[step]
        skipped[part, :] = inner_conv[step] * skip_gain[0]
        small[part, :width] = group_conv[step]
        small[part, width:] = jnp.zeros((slots, LANES - width), F32)
    stride = LANES // steps
    ordered[...] = jnp.zeros_like(ordered)
    for position in range(slots):
        slot = order[position]
        for step in range(steps):
            ordered[pl.ds(step * stride + position, 1), :] = small[
                pl.ds(step * slots + slot, 1), :
            ]
    maps[...] = ordered[...].T[:width].astype(BF16)


def project(replicas, cap, scalars, operands, arrived):
    cap_rows = round_up(cap, 8)
    own, inner, group = operands[0], operands[-2], operands[-1]
    taps, slots, _ = inner.shape
    width = group.shape[2]
    rows = own.shape[0]
    lanes = 2 * taps * LANES
    vmem = pl.BlockSpec(memory_space=pltpu.VMEM)
    smem = pl.BlockSpec(memory_space=pltpu.SMEM)
    full = jax.ShapeDtypeStruct((rows, LANES), F32)
    return pl.pallas_call(
        functools.partial(project_kernel, replicas, cap, cap_rows),
        out_shape=[
            jax.ShapeDtypeStruct(inner.shape, BF16),
            jax.ShapeDtypeStruct(group.shape, BF16),
            full,
            full,
            full,
            full,
            jax.ShapeDtypeStruct((width, LANES), BF16),
        ],
        in_specs=[smem] * len(scalars) + [vmem] * (len(operands) + len(arrived)),
        out_specs=[vmem] * 7,
        scratch_shapes=[
            pltpu.VMEM((slots, lanes), F32),
            pltpu.VMEM((sum(block.shape[0] for block in arrived), lanes), F32),
            pltpu.VMEM((rows, LANES), F32),
            pltpu.VMEM((LANES, LANES), F32),
            pltpu.SMEM((slots,), jnp.int32),
        ],
        compiler_params=pltpu.CompilerParams(vmem_limit_bytes=VMEM_LIMIT),
        cost_estimate=pl.CostEstimate(
            flops=300_000_000, bytes_accessed=5_000_000, transcendentals=100_000
        ),
        name="project_convolve",
    )(*scalars, *operands, *arrived)


def advance_slot(state, driven, decay, sums, maps, position, slot, slots, steps):
    input_map, output_map = maps
    stride = LANES // steps
    hidden = state.astype(F32)
    for step in range(steps):
        lane = step * stride + position
        row = pl.ds(step * slots + slot, 1)
        hidden = decay[row, :] * hidden + driven[row, :] * input_map[:, lane : lane + 1]
        sums[row, :] = jnp.sum(hidden * output_map[:, lane : lane + 1], axis=0, keepdims=True)
        result = hidden.astype(BF16)
        hidden = result.astype(F32)
    return result


def pair_maps(own_maps, other_maps):
    first = lax.axis_index("head") == 0
    mine, theirs = own_maps[...].astype(F32), other_maps[...].astype(F32)
    return jnp.where(first, mine, theirs), jnp.where(first, theirs, mine)


def stay_kernel(
    steps, receive, live, driven, decay, own_maps, other_maps, scan, sums, scan_next, done, order, sem
):
    slots = scan.shape[0]
    split_order(receive, slots, order)
    maps = pair_maps(own_maps, other_maps)
    copies = []
    for position in range(slots // 2):
        slot = order[position]
        result = advance_slot(
            scan[slot], driven, decay, sums, maps, position, slot, slots, steps
        )
        done[position] = jnp.where(slot < live[0], result, jnp.zeros_like(result))
        copies.append(
            pltpu.make_async_copy(done.at[position], scan_next.at[slot], sem.at[position])
        )
        copies[-1].start()
    for copy in copies:
        copy.wait()


def arrive_kernel(
    replicas,
    cap,
    steps,
    receive,
    live,
    driven,
    decay,
    skipped,
    gate,
    own_maps,
    other_maps,
    sums_in,
    scan_in,
    *refs,
):
    del scan_in
    arrived = refs[:-7]
    gated, scan_next, sums, held, done, order, sem = refs[-7:]
    slots = scan_next.shape[0]
    rows = arrived[0].shape[0]
    loads = []
    for block, ref in enumerate(arrived):
        loads.append(
            pltpu.make_async_copy(
                ref, held.at[pl.ds(block * rows, rows)], sem.at[slots // 2 + block]
            )
        )
        loads[-1].start()
    me = lax.axis_index("dp")
    split_order(receive, slots, order)
    maps = pair_maps(own_maps, other_maps)
    sums[...] = sums_in[...]
    for load in loads:
        load.wait()
    copies = []
    for position in range(slots // 2):
        slot = order[slots // 2 + position]
        row = arrival_row(replicas, cap, cap, me, receive[0, slot])
        result = advance_slot(
            held[row], driven, decay, sums, maps, slots // 2 + position, slot, slots, steps
        )
        done[position] = jnp.where(slot < live[0], result, jnp.zeros_like(result))
        copies.append(
            pltpu.make_async_copy(done.at[position], scan_next.at[slot], sem.at[position])
        )
        copies[-1].start()
    living = lax.broadcasted_iota(jnp.int32, (slots, LANES), 0) < live[0]
    for step in range(steps):
        part = slice(step * slots, (step + 1) * slots)
        value = (sums[part, :] + skipped[part, :]) * gate[part, :]
        gated[step] = jnp.where(living, value, 0.0).astype(BF16)
    for copy in copies:
        copy.wait()


def stay(steps, receive, live, driven, decay, own_maps, other_maps, scan):
    slots = scan.shape[0]
    vmem = pl.BlockSpec(memory_space=pltpu.VMEM)
    smem = pl.BlockSpec(memory_space=pltpu.SMEM)
    hbm = pl.BlockSpec(memory_space=pl.ANY)
    return pl.pallas_call(
        functools.partial(stay_kernel, steps),
        out_shape=[
            jax.ShapeDtypeStruct(driven.shape, F32),
            jax.ShapeDtypeStruct(scan.shape, BF16),
        ],
        in_specs=[smem] * 2 + [vmem] * 5,
        out_specs=[vmem, hbm],
        scratch_shapes=[
            pltpu.VMEM((slots // 2,) + scan.shape[1:], BF16),
            pltpu.SMEM((slots,), jnp.int32),
            pltpu.SemaphoreType.DMA((slots // 2,)),
        ],
        compiler_params=pltpu.CompilerParams(vmem_limit_bytes=VMEM_LIMIT),
        cost_estimate=pl.CostEstimate(
            flops=10_000_000, bytes_accessed=2_000_000, transcendentals=0
        ),
        name="advance_staying",
    )(receive, live, driven, decay, own_maps, other_maps, scan)


def arrive(replicas, cap, steps, receive, live, operands, sums, scan_next, arrived):
    slots = scan_next.shape[0]
    vmem = pl.BlockSpec(memory_space=pltpu.VMEM)
    smem = pl.BlockSpec(memory_space=pltpu.SMEM)
    hbm = pl.BlockSpec(memory_space=pl.ANY)
    held = sum(block.shape[0] for block in arrived)
    return pl.pallas_call(
        functools.partial(arrive_kernel, replicas, cap, steps),
        out_shape=[
            jax.ShapeDtypeStruct((steps, slots, LANES), BF16),
            jax.ShapeDtypeStruct(scan_next.shape, BF16),
        ],
        in_specs=[smem] * 2 + [vmem] * (len(operands) + 1) + [hbm] * (1 + len(arrived)),
        out_specs=[vmem, hbm],
        scratch_shapes=[
            pltpu.VMEM(sums.shape, F32),
            pltpu.VMEM((held,) + scan_next.shape[1:], BF16),
            pltpu.VMEM((slots // 2,) + scan_next.shape[1:], BF16),
            pltpu.SMEM((slots,), jnp.int32),
            pltpu.SemaphoreType.DMA((slots // 2 + len(arrived),)),
        ],
        input_output_aliases={3 + len(operands): 1},
        compiler_params=pltpu.CompilerParams(vmem_limit_bytes=VMEM_LIMIT),
        cost_estimate=pl.CostEstimate(
            flops=10_000_000, bytes_accessed=2_000_000, transcendentals=0
        ),
        name="advance_arrived",
    )(receive, live, *operands, sums, scan_next, *arrived)


def swap_heads(value):
    return lax.ppermute(value, "head", [(0, 1), (1, 0)])


def move(replicas, blocks):
    if block_rows_of(replicas) > 1:
        return [lax.all_to_all(block, "dp", 0, 0, tiled=True) for block in blocks]
    return [
        lax.ppermute(
            block, "dp", [(source, (source + shift) % replicas) for source in range(replicas)]
        )
        for shift, block in enumerate(blocks, 1)
    ]


def per_device(
    replicas,
    tokens,
    inner_weight,
    gate_weight,
    group_weight,
    delta_weight,
    inner_taps,
    inner_offset,
    group_taps,
    group_offset,
    decay_log,
    delta_bias,
    skip_gain,
    inner_window,
    group_window,
    scan_state,
    send_list,
    receive_list,
    live_count,
):
    steps, slots, half = tokens.shape
    cap = send_list.shape[1] // replicas
    scan = jnp.transpose(scan_state, (0, 2, 1))
    inner = jnp.transpose(inner_window, (1, 0, 2))
    group = jnp.transpose(group_window, (1, 0, 2))
    own = tokens.reshape(steps * slots, half)

    states, windows = pack(replicas, cap, send_list, scan, inner, group)
    windows = move(replicas, windows)
    states = move(replicas, states)
    other = swap_heads(own)
    scalars = (receive_list, live_count, decay_log, delta_bias, skip_gain)
    operands = (
        own,
        other,
        inner_weight,
        gate_weight,
        group_weight.T,
        delta_weight.T,
        inner_taps,
        inner_offset[None],
        group_taps,
        group_offset[None],
        inner,
        group,
    )
    inner_next, group_next, driven, decay, skipped, gate, maps = project(
        replicas, cap, scalars, operands, windows
    )
    other_maps = swap_heads(maps)
    sums, scan_next = stay(
        steps, receive_list, live_count, driven, decay, maps, other_maps, scan
    )
    gated, scan_next = arrive(
        replicas,
        cap,
        steps,
        receive_list,
        live_count,
        (driven, decay, skipped, gate, maps, other_maps),
        sums,
        scan_next,
        states,
    )
    return (
        gated,
        jnp.transpose(inner_next, (1, 0, 2)),
        jnp.transpose(group_next, (1, 0, 2)),
        jnp.transpose(scan_next, (0, 2, 1)),
    )


def solution(mesh):
    in_specs = (
        P(None, ("grp", "dp"), "head"),
        P(None, "head"),
        P(None, "head"),
        P(None, "head"),
        P(None, "head"),
        P(None, "head"),
        P("head"),
        P(None, "head"),
        P("head"),
        P("head"),
        P("head"),
        P("head"),
        P(("grp", "dp"), None, "head"),
        P(("grp", "dp"), None, "head"),
        P(("grp", "dp"), "head", None),
        P(("grp", "dp"), None),
        P(("grp", "dp"), None),
        P(("grp", "dp")),
    )
    out_specs = (
        P(None, ("grp", "dp"), "head"),
        P(("grp", "dp"), None, "head"),
        P(("grp", "dp"), None, "head"),
        P(("grp", "dp"), "head", None),
    )
    return jax.shard_map(
        functools.partial(per_device, mesh.shape["dp"]),
        mesh=mesh,
        in_specs=in_specs,
        out_specs=out_specs,
        check_vma=False,
    )
```

```python
import functools

import jax
import jax.numpy as jnp
from jax import lax
from jax.experimental import pallas as pl
from jax.experimental.pallas import tpu as pltpu
from jax.sharding import PartitionSpec as P

F32 = jnp.float32
BF16 = jnp.bfloat16
VMEM_LIMIT = 32 * 1024 * 1024
SMALL_LIMIT = 8 * 1024 * 1024
LARGE_LIMIT = 60 * 1024 * 1024
PLAN = 128
LANES = 128


def round_up(value, step):
    return -(-value // step) * step


def silu(value):
    return value * jax.nn.sigmoid(value)


def pack_kernel(scan, send, out, table, sem, list_sem):
    load = pltpu.make_async_copy(send, table, list_sem)
    load.start()
    load.wait()

    def each(act):
        for place in range(out.shape[0]):
            index = table[0, place]

            @pl.when(index >= 0)
            def _():
                act(pltpu.make_async_copy(scan.at[index], out.at[place], sem.at[place]))

    each(lambda copy: copy.start())
    each(lambda copy: copy.wait())


def pack(send_list, scan):
    places = send_list.shape[1]
    hbm = pl.BlockSpec(memory_space=pl.ANY)
    return pl.pallas_call(
        pack_kernel,
        out_shape=jax.ShapeDtypeStruct((places,) + scan.shape[1:], BF16),
        in_specs=[hbm, hbm],
        out_specs=hbm,
        scratch_shapes=[
            pltpu.SMEM(send_list.shape, jnp.int32),
            pltpu.SemaphoreType.DMA((places,)),
            pltpu.SemaphoreType.DMA,
        ],
        compiler_params=pltpu.CompilerParams(vmem_limit_bytes=LARGE_LIMIT),
        cost_estimate=pl.CostEstimate(flops=0, bytes_accessed=1_000_000, transcendentals=0),
        name="pack_states",
    )(scan, send_list)


def lane_table(inner, group, table, key):
    taps, _, channels = inner.shape
    width = group.shape[2]
    for tap in range(taps):
        table[:, tap * channels : (tap + 1) * channels] = inner[tap].astype(F32)
    first = taps * channels
    for tap in range(taps):
        table[:, first + tap * width : first + (tap + 1) * width] = group[tap].astype(F32)
    first += taps * width
    table[:, first:] = jnp.full((table.shape[0], table.shape[1] - first), key, F32)


def window_lanes(inner, group):
    taps = inner.shape[0]
    return round_up(taps * (inner.shape[2] + group.shape[2]) + 1, LANES)


def windows_kernel(send, inner, group, out, table, picked):
    lane_table(inner, group, table, -1.0)
    picked[...] = jnp.full(picked.shape, -1.0, F32)
    key_lane = inner.shape[0] * (inner.shape[2] + group.shape[2])
    is_key = lax.broadcasted_iota(jnp.int32, (1, table.shape[1]), 1) >= key_lane
    count = 0
    for place in range(send.shape[1]):
        index = send[0, place]
        key = jnp.where(index >= 0, place, -1).astype(F32)
        row = table[pl.ds(jnp.maximum(index, 0), 1), :]
        picked[pl.ds(count, 1), :] = jnp.where(is_key, key, row)
        count = count + jnp.where(index >= 0, 1, 0)
    out[...] = picked[: out.shape[0]].astype(BF16)


def pack_windows(send_list, inner, group):
    _, slots, _ = inner.shape
    lanes = window_lanes(inner, group)
    rows = round_up(slots // 2, 16)
    vmem = pl.BlockSpec(memory_space=pltpu.VMEM)
    smem = pl.BlockSpec(memory_space=pltpu.SMEM)
    return pl.pallas_call(
        windows_kernel,
        out_shape=jax.ShapeDtypeStruct((rows, lanes), BF16),
        in_specs=[smem, vmem, vmem],
        out_specs=vmem,
        scratch_shapes=[
            pltpu.VMEM((slots, lanes), F32),
            pltpu.VMEM((round_up(send_list.shape[1] + 1, 8), lanes), F32),
        ],
        compiler_params=pltpu.CompilerParams(vmem_limit_bytes=SMALL_LIMIT),
        cost_estimate=pl.CostEstimate(flops=0, bytes_accessed=200_000, transcendentals=0),
        name="pack_windows",
    )(send_list, inner, group)


def split_order(receive, slots, plan):
    def step(slot, counts):
        kept, moved = counts
        entry = receive[0, slot]
        stays = entry < 0
        plan[0, jnp.where(stays, kept, slots // 2 + moved)] = slot
        plan[0, jnp.where(stays, PLAN - 1, slots + moved)] = entry
        return (kept + jnp.where(stays, 1, 0), moved + jnp.where(stays, 0, 1))

    lax.fori_loop(0, slots, step, (jnp.int32(0), jnp.int32(0)))


def project_kernel(
    replicas,
    cap,
    receive,
    live,
    decay_log,
    delta_bias,
    skip_gain,
    own,
    other,
    inner_weight,
    gate_weight,
    group_weight,
    delta_weight,
    inner_taps,
    inner_offset,
    group_taps,
    group_offset,
    inner,
    group,
    receive_lanes,
    arrived,
    inner_next,
    group_next,
    driven,
    decay,
    skipped,
    gate,
    maps,
    plan,
    table,
    small,
    ordered,
):
    me = lax.axis_index("dp")
    head = lax.axis_index("head")
    taps, slots, channels = inner.shape
    half = own.shape[1]
    width = group.shape[2]
    steps = own.shape[0] // slots

    split_order(receive, slots, plan)
    lane_table(inner, group, table, 0.0)
    rows = arrived.shape[0] // replicas
    places = replicas * cap
    entry = receive_lanes[...].astype(F32)
    source = jnp.floor((entry + 0.5) * (1.0 / cap))
    wanted = entry + source * float(places - cap) + (me * cap).astype(F32)
    wanted = jnp.where(entry >= 0.0, wanted, -2.0)
    key_lane = taps * (channels + width)
    key = arrived[:, key_lane : key_lane + 1].astype(F32)
    owner = (lax.broadcasted_iota(jnp.int32, (arrived.shape[0], 1), 0) // rows).astype(F32)
    key = jnp.where(key >= 0.0, key + owner * float(places), -1.0)
    hits = (key == wanted).astype(F32).astype(BF16)

    def pick(value):
        return lax.dot_general(
            hits, value, (((0,), (0,)), ((), ())), preferred_element_type=F32
        )

    taken = pick(jnp.ones((arrived.shape[0], LANES), BF16)) > 0.5
    for first in range(0, table.shape[1], LANES):
        lanes = slice(first, first + LANES)
        table[:, lanes] = jnp.where(taken, pick(arrived[:, lanes]), table[:, lanes])

    mine = pl.ds(pl.multiple_of(head * half, half), half)
    theirs = pl.ds(pl.multiple_of((1 - head) * half, half), half)

    def columns(weight):
        return jnp.dot(own[...], weight[mine, :], preferred_element_type=F32) + jnp.dot(
            other[...], weight[theirs, :], preferred_element_type=F32
        )

    def rows_of(weight, count):
        def one(tokens, part):
            piece = weight[:, part]
            if count > 1:
                piece = jnp.broadcast_to(piece, (count, half))
            return lax.dot_general(
                tokens, piece, (((1,), (1,)), ((), ())), preferred_element_type=F32
            )

        return one(own[...], mine) + one(other[...], theirs)

    def rounded(value):
        return value.astype(BF16).astype(F32)

    inner_raw = rounded(columns(inner_weight))
    gate_raw = rounded(columns(gate_weight))
    group_raw = rounded(rows_of(group_weight, 1))
    delta_raw = rounded(rows_of(delta_weight, LANES))

    living = lax.broadcasted_iota(jnp.int32, (slots, LANES), 0) < live[0]
    gate[...] = silu(gate_raw)
    shifted = delta_raw + delta_bias[0]
    delta = jnp.maximum(shifted, 0.0) + jnp.log1p(jnp.exp(-jnp.abs(shifted)))
    slope = jnp.exp(jnp.full((1, LANES), decay_log[0], F32))
    decay[...] = jnp.exp(-delta * slope)

    def convolve(carried, raw, weights, offset):
        joined = carried + [raw[step * slots : (step + 1) * slots] for step in range(steps)]
        results = []
        for step in range(steps):
            summed = offset[...]
            for tap in range(taps + 1):
                summed = summed + joined[step + tap] * weights[tap : tap + 1, :]
            results.append(rounded(silu(summed)))
        return results, joined[steps:]

    inner_conv, inner_carry = convolve(
        [table[:, tap * channels : (tap + 1) * channels] for tap in range(taps)],
        inner_raw,
        inner_taps,
        inner_offset,
    )
    first = taps * channels
    group_conv, group_carry = convolve(
        [table[:, first + tap * width : first + (tap + 1) * width] for tap in range(taps)],
        group_raw,
        group_taps,
        group_offset,
    )
    for tap in range(taps):
        inner_next[tap] = jnp.where(living, inner_carry[tap], 0.0).astype(BF16)
        group_next[tap] = jnp.where(living[:, :width], group_carry[tap], 0.0).astype(BF16)
    for step in range(steps):
        part = slice(step * slots, (step + 1) * slots)
        driven[part, :] = delta[part] * inner_conv[step]
        skipped[part, :] = inner_conv[step] * skip_gain[0]
        small[part, :width] = group_conv[step]
        small[part, width:] = jnp.zeros((slots, LANES - width), F32)
    stride = LANES // steps
    ordered[...] = jnp.zeros_like(ordered)
    for position in range(slots):
        slot = plan[0, position]
        for step in range(steps):
            ordered[pl.ds(step * stride + position, 1), :] = small[
                pl.ds(step * slots + slot, 1), :
            ]
    maps[...] = ordered[...].T[:width].astype(BF16)


def project(replicas, cap, scalars, operands):
    own, inner, group = operands[0], operands[-4], operands[-3]
    _, slots, _ = inner.shape
    width = group.shape[2]
    rows = own.shape[0]
    vmem = pl.BlockSpec(memory_space=pltpu.VMEM)
    smem = pl.BlockSpec(memory_space=pltpu.SMEM)
    full = jax.ShapeDtypeStruct((rows, LANES), F32)
    return pl.pallas_call(
        functools.partial(project_kernel, replicas, cap),
        out_shape=[
            jax.ShapeDtypeStruct(inner.shape, BF16),
            jax.ShapeDtypeStruct(group.shape, BF16),
            full,
            full,
            full,
            full,
            jax.ShapeDtypeStruct((width, LANES), BF16),
            jax.ShapeDtypeStruct((1, PLAN), jnp.int32),
        ],
        in_specs=[smem] * len(scalars) + [vmem] * len(operands),
        out_specs=[vmem] * 7 + [smem],
        scratch_shapes=[
            pltpu.VMEM((slots, window_lanes(inner, group)), F32),
            pltpu.VMEM((rows, LANES), F32),
            pltpu.VMEM((LANES, LANES), F32),
        ],
        compiler_params=pltpu.CompilerParams(vmem_limit_bytes=VMEM_LIMIT),
        cost_estimate=pl.CostEstimate(
            flops=300_000_000, bytes_accessed=5_000_000, transcendentals=100_000
        ),
        name="project_convolve",
    )(*scalars, *operands)


def advance_slot(state, driven, decay, sums, maps, position, slot, slots, steps):
    input_map, output_map = maps
    stride = LANES // steps
    hidden = state.astype(F32)
    for step in range(steps):
        lane = step * stride + position
        row = pl.ds(step * slots + slot, 1)
        hidden = decay[row, :] * hidden + driven[row, :] * input_map[:, lane : lane + 1]
        sums[row, :] = jnp.sum(hidden * output_map[:, lane : lane + 1], axis=0, keepdims=True)
        result = hidden.astype(BF16)
        hidden = result.astype(F32)
    return result


def pair_maps(own_maps, other_maps):
    first = lax.axis_index("head") == 0
    mine, theirs = own_maps[...].astype(F32), other_maps[...].astype(F32)
    return jnp.where(first, mine, theirs), jnp.where(first, theirs, mine)


def stay_kernel(
    steps, plan, live, driven, decay, own_maps, other_maps, scan, sums, scan_next, done, sem
):
    slots = scan.shape[0]
    maps = pair_maps(own_maps, other_maps)
    copies = []
    for position in range(slots // 2):
        slot = plan[0, position]
        result = advance_slot(
            scan[slot], driven, decay, sums, maps, position, slot, slots, steps
        )
        done[position] = jnp.where(slot < live[0], result, jnp.zeros_like(result))
        copies.append(
            pltpu.make_async_copy(done.at[position], scan_next.at[slot], sem.at[position])
        )
        copies[-1].start()
    for copy in copies:
        copy.wait()


def arrive_kernel(
    steps,
    plan,
    live,
    driven,
    decay,
    skipped,
    gate,
    own_maps,
    other_maps,
    sums_in,
    scan_in,
    arrived,
    gated_out,
    scan_next,
    sums,
    done,
    gated,
    sem,
):
    del scan_in
    slots = scan_next.shape[0]
    moving = slots // 2
    maps = pair_maps(own_maps, other_maps)
    sums[...] = sums_in[...]
    copies = []
    for position in range(moving, slots):
        slot = plan[0, position]
        result = advance_slot(
            arrived[plan[0, moving + position]],
            driven,
            decay,
            sums,
            maps,
            position,
            slot,
            slots,
            steps,
        )
        place = position - moving
        done[place] = jnp.where(slot < live[0], result, jnp.zeros_like(result))
        copies.append(pltpu.make_async_copy(done.at[place], scan_next.at[slot], sem.at[place]))
        copies[-1].start()
    living = lax.broadcasted_iota(jnp.int32, (slots, LANES), 0) < live[0]
    for step in range(steps):
        part = slice(step * slots, (step + 1) * slots)
        value = (sums[part, :] + skipped[part, :]) * gate[part, :]
        gated[step] = jnp.where(living, value, 0.0).astype(BF16)
    copies.append(pltpu.make_async_copy(gated, gated_out, sem.at[moving]))
    copies[-1].start()
    for copy in copies:
        copy.wait()


def stay(steps, plan, live, driven, decay, own_maps, other_maps, scan):
    slots = scan.shape[0]
    vmem = pl.BlockSpec(memory_space=pltpu.VMEM)
    smem = pl.BlockSpec(memory_space=pltpu.SMEM)
    hbm = pl.BlockSpec(memory_space=pl.ANY)
    return pl.pallas_call(
        functools.partial(stay_kernel, steps),
        out_shape=[
            jax.ShapeDtypeStruct(driven.shape, F32),
            jax.ShapeDtypeStruct(scan.shape, BF16),
        ],
        in_specs=[smem] * 2 + [vmem] * 5,
        out_specs=[vmem, hbm],
        scratch_shapes=[
            pltpu.VMEM((slots // 2,) + scan.shape[1:], BF16),
            pltpu.SemaphoreType.DMA((slots // 2,)),
        ],
        compiler_params=pltpu.CompilerParams(vmem_limit_bytes=SMALL_LIMIT),
        cost_estimate=pl.CostEstimate(
            flops=10_000_000, bytes_accessed=2_000_000, transcendentals=0
        ),
        name="advance_staying",
    )(plan, live, driven, decay, own_maps, other_maps, scan)


def arrive(steps, plan, live, operands, sums, scan_next, arrived):
    slots = scan_next.shape[0]
    vmem = pl.BlockSpec(memory_space=pltpu.VMEM)
    smem = pl.BlockSpec(memory_space=pltpu.SMEM)
    hbm = pl.BlockSpec(memory_space=pl.ANY)
    gated = jax.ShapeDtypeStruct((steps, slots, LANES), BF16)
    return pl.pallas_call(
        functools.partial(arrive_kernel, steps),
        out_shape=[gated, jax.ShapeDtypeStruct(scan_next.shape, BF16)],
        in_specs=[smem] * 2 + [vmem] * (len(operands) + 1) + [hbm, vmem],
        out_specs=[hbm, hbm],
        scratch_shapes=[
            pltpu.VMEM(sums.shape, F32),
            pltpu.VMEM((slots // 2,) + scan_next.shape[1:], BF16),
            pltpu.VMEM(gated.shape, BF16),
            pltpu.SemaphoreType.DMA((slots // 2 + 1,)),
        ],
        input_output_aliases={3 + len(operands): 1},
        compiler_params=pltpu.CompilerParams(vmem_limit_bytes=SMALL_LIMIT),
        cost_estimate=pl.CostEstimate(
            flops=10_000_000, bytes_accessed=2_000_000, transcendentals=0
        ),
        name="advance_arrived",
    )(plan, live, *operands, sums, scan_next, arrived)


def swap_heads(value):
    return lax.ppermute(value, "head", [(0, 1), (1, 0)])


def per_device(
    replicas,
    tokens,
    inner_weight,
    gate_weight,
    group_weight,
    delta_weight,
    inner_taps,
    inner_offset,
    group_taps,
    group_offset,
    decay_log,
    delta_bias,
    skip_gain,
    inner_window,
    group_window,
    scan_state,
    send_list,
    receive_list,
    live_count,
):
    steps, slots, half = tokens.shape
    cap = send_list.shape[1] // replicas
    scan = jnp.transpose(scan_state, (0, 2, 1))
    inner = jnp.transpose(inner_window, (1, 0, 2))
    group = jnp.transpose(group_window, (1, 0, 2))
    own = tokens.reshape(steps * slots, half)

    states = lax.all_to_all(pack(send_list, scan), "dp", 0, 0, tiled=True)
    windows = lax.all_gather(pack_windows(send_list, inner, group), "dp", axis=0, tiled=True)
    scalars = (receive_list, live_count, decay_log, delta_bias, skip_gain)
    operands = (
        own,
        swap_heads(own),
        inner_weight,
        gate_weight,
        group_weight.T,
        delta_weight.T,
        inner_taps,
        inner_offset[None],
        group_taps,
        group_offset[None],
        inner,
        group,
        receive_list,
        windows,
    )
    inner_next, group_next, driven, decay, skipped, gate, maps, plan = project(
        replicas, cap, scalars, operands
    )
    other_maps = swap_heads(maps)
    sums, scan_next = stay(steps, plan, live_count, driven, decay, maps, other_maps, scan)
    gated, scan_next = arrive(
        steps,
        plan,
        live_count,
        (driven, decay, skipped, gate, maps, other_maps),
        sums,
        scan_next,
        states,
    )
    return (
        gated,
        jnp.transpose(inner_next, (1, 0, 2)),
        jnp.transpose(group_next, (1, 0, 2)),
        jnp.transpose(scan_next, (0, 2, 1)),
    )


def solution(mesh):
    in_specs = (
        P(None, ("grp", "dp"), "head"),
        P(None, "head"),
        P(None, "head"),
        P(None, "head"),
        P(None, "head"),
        P(None, "head"),
        P("head"),
        P(None, "head"),
        P("head"),
        P("head"),
        P("head"),
        P("head"),
        P(("grp", "dp"), None, "head"),
        P(("grp", "dp"), None, "head"),
        P(("grp", "dp"), "head", None),
        P(("grp", "dp"), None),
        P(("grp", "dp"), None),
        P(("grp", "dp")),
    )
    out_specs = (
        P(None, ("grp", "dp"), "head"),
        P(("grp", "dp"), None, "head"),
        P(("grp", "dp"), None, "head"),
        P(("grp", "dp"), "head", None),
    )
    return jax.shard_map(
        functools.partial(per_device, mesh.shape["dp"]),
        mesh=mesh,
        in_specs=in_specs,
        out_specs=out_specs,
        check_vma=False,
    )
```

```python
import functools

import jax
import jax.numpy as jnp
from jax import lax
from jax.experimental import pallas as pl
from jax.experimental.pallas import tpu as pltpu
from jax.sharding import PartitionSpec as P

F32 = jnp.float32
BF16 = jnp.bfloat16
SMALL_LIMIT = 8 * 1024 * 1024
MEDIUM_LIMIT = 32 * 1024 * 1024
LARGE_LIMIT = 60 * 1024 * 1024
MAX_SHIFTS = 16
LANES = 128
ROWS = 8

VMEM = pl.BlockSpec(memory_space=pltpu.VMEM)
SMEM = pl.BlockSpec(memory_space=pltpu.SMEM)
HBM = pl.BlockSpec(memory_space=pl.ANY)


def round_up(value, step):
    return -(-value // step) * step


def silu(value):
    return value * jax.nn.sigmoid(value)


def rounded(value):
    return value.astype(BF16).astype(F32)


def shifts_of(replicas):
    if replicas > MAX_SHIFTS:
        return []
    return sorted(range(1, replicas), key=lambda shift: abs(2 * shift - replicas))


def both_halves(mine, theirs):
    first = lax.axis_index("head") == 0
    return jnp.concatenate(
        [jnp.where(first, mine, theirs), jnp.where(first, theirs, mine)], axis=-1
    )


def pack_kernel(replicas, cap, scan, send, inner, group, group_other, *refs):
    shifts = shifts_of(replicas)
    count = max(1, len(shifts))
    outs = refs[:count]
    (indices, inner_in, mine_in, theirs_in, held, table, picked, cast) = refs[count : count + 8]
    load_sem, in_sem, out_sem, window_sem = refs[count + 8 :]
    loads = [
        pltpu.make_async_copy(source, target, load_sem.at[place])
        for place, (source, target) in enumerate(
            [(send, indices), (inner, inner_in), (group, mine_in), (group_other, theirs_in)]
        )
    ]
    for load in loads:
        load.start()
    me = lax.axis_index("dp")
    taps, _, channels = inner_in.shape
    state_rows = scan.shape[1]
    blocks = []
    if shifts:
        for ref, shift in zip(outs, shifts):
            blocks.append((ref.at[0], lax.rem(me + shift, replicas)))
    else:
        blocks = [(outs[0].at[target], target) for target in range(replicas)]
    loads[0].wait()

    plan = []
    for block, (ref, target) in enumerate(blocks):
        for c in range(cap):
            plan.append((block, ref, c, indices[0, target * cap + c]))

    def fetch(place, index):
        return pltpu.make_async_copy(scan.at[index], held.at[place], in_sem.at[place])

    def store(place, ref, c):
        return pltpu.make_async_copy(
            held.at[place], ref.at[pl.ds(c * state_rows, state_rows)], out_sem.at[place]
        )

    for place, (_, _, _, index) in enumerate(plan):

        @pl.when(index >= 0)
        def _():
            fetch(place, index).start()

    for load in loads[1:]:
        load.wait()
    for tap in range(taps):
        table[:, tap * LANES : (tap + 1) * LANES] = inner_in[tap].astype(F32)
        table[:, (taps + tap) * LANES : (taps + tap + 1) * LANES] = both_halves(
            mine_in[tap].astype(F32), theirs_in[tap].astype(F32)
        )
    picked[...] = jnp.zeros_like(picked)
    for place, (block, _, c, index) in enumerate(plan):
        row = table[pl.ds(jnp.maximum(index, 0), 1), :]
        for kind in range(2 * taps):
            picked[block, kind * ROWS + c : kind * ROWS + c + 1, :] = row[
                :, kind * LANES : (kind + 1) * LANES
            ]
    windows = []
    for block, (ref, _) in enumerate(blocks):
        cast[block] = picked[block].astype(BF16)
        windows.append(
            pltpu.make_async_copy(
                cast.at[block],
                ref.at[pl.ds(cap * state_rows, cast.shape[1])],
                window_sem.at[block],
            )
        )
        windows[-1].start()

    for place, (_, ref, c, index) in enumerate(plan):

        @pl.when(index >= 0)
        def _():
            fetch(place, index).wait()
            store(place, ref, c).start()

    for place, (_, ref, c, index) in enumerate(plan):

        @pl.when(index >= 0)
        def _():
            store(place, ref, c).wait()

    for window in windows:
        window.wait()


def pack(replicas, cap, send_list, scan, inner, group, group_other):
    shifts = shifts_of(replicas)
    count = max(1, len(shifts))
    per_block = 1 if shifts else replicas
    taps, slots, _ = inner.shape
    window_rows = 2 * taps * ROWS
    rows = cap * scan.shape[1] + window_rows
    blocks = count * per_block
    places = blocks * cap
    return pl.pallas_call(
        functools.partial(pack_kernel, replicas, cap),
        out_shape=[jax.ShapeDtypeStruct((per_block, rows, LANES), BF16)] * count,
        in_specs=[HBM] * 5,
        out_specs=[HBM] * count,
        scratch_shapes=[
            pltpu.SMEM(send_list.shape, jnp.int32),
            pltpu.VMEM(inner.shape, BF16),
            pltpu.VMEM(group.shape, BF16),
            pltpu.VMEM(group.shape, BF16),
            pltpu.VMEM((places,) + scan.shape[1:], BF16),
            pltpu.VMEM((slots, 2 * taps * LANES), F32),
            pltpu.VMEM((blocks, window_rows, LANES), F32),
            pltpu.VMEM((blocks, window_rows, LANES), BF16),
            pltpu.SemaphoreType.DMA((4,)),
            pltpu.SemaphoreType.DMA((places,)),
            pltpu.SemaphoreType.DMA((places,)),
            pltpu.SemaphoreType.DMA((blocks,)),
        ],
        compiler_params=pltpu.CompilerParams(vmem_limit_bytes=LARGE_LIMIT),
        cost_estimate=pl.CostEstimate(flops=0, bytes_accessed=2_000_000, transcendentals=0),
        name="pack_leaving",
    )(scan, send_list, inner, group, group_other)


def make_plan(replicas, cap, receive, slots, plan, inverse):
    moving = slots // 2
    for entry in range(replicas * cap):
        inverse[entry] = -1

    def kept_step(slot, kept):
        entry = receive[0, slot]
        stays = entry < 0
        plan[0, jnp.where(stays, kept, slots - 1)] = slot
        inverse[jnp.where(stays, replicas * cap, entry)] = slot
        return kept + jnp.where(stays, 1, 0)

    lax.fori_loop(0, slots, kept_step, 0)

    def source_step(source, units):
        present = inverse[source * cap] >= 0
        unit = jnp.minimum(units, moving // cap - 1)

        @pl.when(present)
        def _():
            for c in range(cap):
                plan[0, moving + unit * cap + c] = inverse[source * cap + c]

        plan[0, slots + source] = jnp.where(present, unit, -1)
        return units + jnp.where(present, 1, 0)

    lax.fori_loop(0, replicas, source_step, 0)


def project_kernel(
    replicas,
    cap,
    receive,
    decay_log,
    delta_bias,
    own,
    other,
    inner_weight,
    gate_weight,
    group_weight,
    delta_weight,
    group_taps,
    group_offset,
    inner_raw,
    gate,
    delta_out,
    decay,
    shared,
    plan,
    inverse,
):
    head = lax.axis_index("head")
    half = own.shape[1]
    rows = own.shape[0]
    taps = group_taps.shape[0]
    slots = receive.shape[1]
    make_plan(replicas, cap, receive, slots, plan, inverse)
    mine = pl.ds(pl.multiple_of(head * half, half), half)
    theirs = pl.ds(pl.multiple_of((1 - head) * half, half), half)

    def columns(weight):
        return jnp.dot(own[...], weight[mine, :], preferred_element_type=F32) + jnp.dot(
            other[...], weight[theirs, :], preferred_element_type=F32
        )

    def rows_of(weight, count):
        def one(tokens, part):
            piece = weight[:, part]
            if count > 1:
                piece = jnp.broadcast_to(piece, (count, half))
            return lax.dot_general(
                tokens, piece, (((1,), (1,)), ((), ())), preferred_element_type=F32
            )

        return one(own[...], mine) + one(other[...], theirs)

    shared[:rows, :] = rounded(rows_of(group_weight, 1))
    shared[rows : rows + taps, :] = group_taps[...]
    shared[rows + taps : rows + taps + 1, :] = group_offset[...]
    shared[rows + taps + 1 :, :] = jnp.zeros_like(shared[rows + taps + 1 :, :])
    inner_raw[...] = rounded(columns(inner_weight))
    gate[...] = silu(rounded(columns(gate_weight)))
    shifted = rounded(rows_of(delta_weight, LANES)) + delta_bias[0]
    delta = jnp.maximum(shifted, 0.0) + jnp.log1p(jnp.exp(-jnp.abs(shifted)))
    slope = jnp.exp(jnp.full((1, LANES), decay_log[0], F32))
    delta_out[...] = delta
    decay[...] = jnp.exp(-delta * slope)


def project(replicas, cap, scalars, operands):
    receive = scalars[0]
    own, group_taps = operands[0], operands[-2]
    rows = own.shape[0]
    slots = receive.shape[1]
    full = jax.ShapeDtypeStruct((rows, LANES), F32)
    shared_rows = round_up(rows + group_taps.shape[0] + 1, ROWS)
    return pl.pallas_call(
        functools.partial(project_kernel, replicas, cap),
        out_shape=[full] * 4
        + [
            jax.ShapeDtypeStruct((shared_rows, group_taps.shape[1]), F32),
            jax.ShapeDtypeStruct((1, round_up(slots + replicas, LANES)), jnp.int32),
        ],
        in_specs=[SMEM] * len(scalars) + [VMEM] * len(operands),
        out_specs=[VMEM] * 5 + [SMEM],
        scratch_shapes=[pltpu.SMEM((replicas * cap + 1,), jnp.int32)],
        compiler_params=pltpu.CompilerParams(vmem_limit_bytes=MEDIUM_LIMIT),
        cost_estimate=pl.CostEstimate(
            flops=300_000_000, bytes_accessed=5_000_000, transcendentals=100_000
        ),
        name="project_tokens",
    )(*scalars, *operands)


def convolve(carried, raw, weights, offset):
    joined = carried + raw
    results = []
    for step in range(len(raw)):
        summed = offset
        for tap in range(len(carried) + 1):
            summed = summed + joined[step + tap] * weights[tap : tap + 1, :]
        results.append(rounded(silu(summed)))
    return results


def transposed(rows, scratch, stride):
    scratch[...] = jnp.zeros_like(scratch)
    for step, value in enumerate(rows):
        scratch[step * stride : step * stride + value.shape[0], :] = value
    return [scratch[first : first + LANES].T for first in range(0, scratch.shape[0], LANES)]


def advance_slot(state, rows, driven, decay, sums, maps, lanes):
    hidden = state.astype(F32)
    width = state.shape[0]
    for row, lane in zip(rows, lanes):
        piece = maps[lane // LANES]
        column = piece[:, lane % LANES : lane % LANES + 1]
        hidden = decay[row, :] * hidden + driven[row, :] * column[:width]
        sums[row, :] = jnp.sum(hidden * column[width:], axis=0, keepdims=True)
        result = hidden.astype(BF16)
        hidden = result.astype(F32)
    return result


def stay_kernel(
    replicas,
    cap,
    plan,
    live,
    skip_gain,
    inner_raw,
    gate,
    delta,
    decay,
    shared,
    shared_other,
    inner_taps,
    inner_offset,
    inner,
    group,
    group_other,
    scan,
    gated,
    group_weights,
    inner_moved,
    group_moved,
    gate_moved,
    delta_moved,
    decay_moved,
    scan_next,
    both,
    driven,
    skipped,
    sums,
    maps_in,
    ordered,
    done,
    sem,
):
    taps, slots, _ = inner.shape
    rows = inner_raw.shape[0]
    steps = rows // slots
    moving = slots // 2
    moved_rows = inner_moved.shape[0] // steps
    both[...] = both_halves(shared[...], shared_other[...])
    group_weights[...] = both[rows : rows + group_weights.shape[0], :]

    def parts(ref):
        return [ref[step * slots : (step + 1) * slots, :] for step in range(steps)]

    inner_conv = convolve(
        [inner[tap].astype(F32) for tap in range(taps)],
        parts(inner_raw),
        inner_taps[...],
        inner_offset[...],
    )
    group_conv = convolve(
        [both_halves(group[tap].astype(F32), group_other[tap].astype(F32)) for tap in range(taps)],
        parts(both),
        group_weights[: taps + 1, :],
        group_weights[taps + 1 : taps + 2, :],
    )
    for step in range(steps):
        part = slice(step * slots, (step + 1) * slots)
        driven[part, :] = delta[part, :] * inner_conv[step]
        skipped[part, :] = inner_conv[step] * skip_gain[0]
        maps_in[part, :] = group_conv[step]
    sums[...] = jnp.zeros_like(sums)
    stride = ordered.shape[0] // steps
    ordered[...] = jnp.zeros_like(ordered)
    for position in range(moving):
        slot = plan[0, position]
        for step in range(steps):
            ordered[step * stride + position : step * stride + position + 1, :] = maps_in[
                pl.ds(step * slots + slot, 1), :
            ]
    maps = [ordered[first : first + LANES].T for first in range(0, ordered.shape[0], LANES)]
    copies = []
    for position in range(moving):
        slot = plan[0, position]
        result = advance_slot(
            scan[slot],
            [pl.ds(step * slots + slot, 1) for step in range(steps)],
            driven,
            decay,
            sums,
            maps,
            [step * stride + position for step in range(steps)],
        )
        done[position] = jnp.where(slot < live[0], result, jnp.zeros_like(result))
        copies.append(
            pltpu.make_async_copy(done.at[position], scan_next.at[slot], sem.at[position])
        )
        copies[-1].start()
    gated[...] = (sums[...] + skipped[...]) * gate[...]
    pairs = (
        (inner_raw, inner_moved),
        (both, group_moved),
        (gate, gate_moved),
        (delta, delta_moved),
        (decay, decay_moved),
    )
    for _, target in pairs:
        target[...] = jnp.zeros_like(target)
    for position in range(moving):
        slot = plan[0, moving + position]
        place = position // cap * ROWS + position % cap
        for step in range(steps):
            row = step * moved_rows + place
            for source, target in pairs:
                target[row : row + 1, :] = source[pl.ds(step * slots + slot, 1), :]
    for copy in copies:
        copy.wait()


def stay(replicas, cap, scalars, operands):
    inner_raw, inner, scan = operands[0], operands[-4], operands[-1]
    _, slots, _ = inner.shape
    rows = inner_raw.shape[0]
    steps = rows // slots
    taps = operands[6].shape[0]
    moving = slots // 2
    moved_rows = moving // cap * ROWS
    full = jax.ShapeDtypeStruct((rows, LANES), F32)
    moved = jax.ShapeDtypeStruct((steps * moved_rows, LANES), F32)
    return pl.pallas_call(
        functools.partial(stay_kernel, replicas, cap),
        out_shape=[full, jax.ShapeDtypeStruct((round_up(taps + 1, ROWS), LANES), F32)]
        + [moved] * 5
        + [jax.ShapeDtypeStruct(scan.shape, BF16)],
        in_specs=[SMEM] * len(scalars) + [VMEM] * len(operands),
        out_specs=[VMEM] * 7 + [HBM],
        scratch_shapes=[
            pltpu.VMEM(operands[4].shape[:1] + (LANES,), F32),
            pltpu.VMEM((rows, LANES), F32),
            pltpu.VMEM((rows, LANES), F32),
            pltpu.VMEM((rows, LANES), F32),
            pltpu.VMEM((rows, LANES), F32),
            pltpu.VMEM((round_up(rows, LANES), LANES), F32),
            pltpu.VMEM((moving,) + scan.shape[1:], BF16),
            pltpu.SemaphoreType.DMA((moving,)),
        ],
        compiler_params=pltpu.CompilerParams(vmem_limit_bytes=SMALL_LIMIT),
        cost_estimate=pl.CostEstimate(
            flops=10_000_000, bytes_accessed=2_000_000, transcendentals=0
        ),
        name="advance_staying",
    )(*scalars, *operands)


def arrive_kernel(
    replicas,
    cap,
    plan,
    live,
    skip_gain,
    gated_in,
    group_weights,
    inner_moved,
    group_moved,
    gate_moved,
    delta_moved,
    decay_moved,
    inner_raw,
    shared,
    inner_taps,
    inner_offset,
    inner,
    group,
    scan_in,
    *refs,
):
    del scan_in
    arrived = refs[:-16]
    gated_out, inner_next, group_next, scan_next = refs[-16:-12]
    (held, driven, sums, ordered, table, gated, inner_out, group_out) = refs[-12:-4]
    done, load_sem, sem, out_sem = refs[-4:]
    shifts = shifts_of(replicas)
    taps, slots, _ = inner.shape
    moving = slots // 2
    units = moving // cap
    state_rows = scan_next.shape[1]
    moved_rows = units * ROWS
    steps = inner_raw.shape[0] // slots
    width = group.shape[2]
    me = lax.axis_index("dp")
    head = lax.axis_index("head")

    if shifts:
        sources = [
            (ref.at[0], lax.rem(me - shift + replicas, replicas))
            for ref, shift in zip(arrived, shifts)
        ]
    else:
        sources = [(arrived[0].at[source], source) for source in range(replicas)]

    def each(act):
        for ref, source in sources:
            unit = plan[0, slots + source]

            @pl.when(unit >= 0)
            def _():
                act(pltpu.make_async_copy(ref, held.at[unit], load_sem.at[unit]))

    each(lambda copy: copy.start())

    living = lax.broadcasted_iota(jnp.int32, (slots, LANES), 0) < live[0]
    for step in range(steps):
        part = slice(step * slots, (step + 1) * slots)
        tap = taps - steps + step
        inner_out[tap] = jnp.where(living, inner_raw[part, :], 0.0).astype(BF16)
        group_out[tap] = jnp.where(living[:, :width], shared[part, :], 0.0).astype(BF16)
    table[:, :LANES] = inner[steps].astype(F32)
    group_own = group[steps].astype(F32)
    table[:, LANES:] = jnp.concatenate([group_own, group_own], axis=1)
    gated[...] = gated_in[...]
    each(lambda copy: copy.wait())

    kinds = [[] for _ in range(2 * taps)]
    for unit in range(units):
        block = held[unit, cap * state_rows :, :].astype(F32)
        for kind in range(2 * taps):
            kinds[kind].append(block[kind * ROWS : (kind + 1) * ROWS])
    windows = [jnp.concatenate(kind, axis=0) for kind in kinds]

    def parts(ref):
        return [ref[step * moved_rows : (step + 1) * moved_rows, :] for step in range(steps)]

    inner_conv = convolve(
        windows[:taps], parts(inner_moved), inner_taps[...], inner_offset[...]
    )
    group_conv = convolve(
        windows[taps:],
        parts(group_moved),
        group_weights[: taps + 1, :],
        group_weights[taps + 1 : taps + 2, :],
    )
    for step, delta in enumerate(parts(delta_moved)):
        driven[step * moved_rows : (step + 1) * moved_rows, :] = delta * inner_conv[step]
    stride = ordered.shape[0] // steps
    maps = transposed(group_conv, ordered, stride)
    sums[...] = jnp.zeros_like(sums)
    copies = []
    for position in range(moving):
        unit, c = position // cap, position % cap
        place = unit * ROWS + c
        slot = plan[0, moving + position]
        result = advance_slot(
            held[unit, c * state_rows : (c + 1) * state_rows, :],
            [slice(step * moved_rows + place, step * moved_rows + place + 1) for step in range(steps)],
            driven,
            decay_moved,
            sums,
            maps,
            [step * stride + place for step in range(steps)],
        )
        done[position] = jnp.where(slot < live[0], result, jnp.zeros_like(result))
        copies.append(
            pltpu.make_async_copy(done.at[position], scan_next.at[slot], sem.at[position])
        )
        copies[-1].start()

    for step in range(steps):
        part = slice(step * moved_rows, (step + 1) * moved_rows)
        skipped = inner_conv[step] * skip_gain[0]
        sums[part, :] = (sums[part, :] + skipped) * gate_moved[part, :]
    driven[:moved_rows, :] = windows[steps]
    driven[moved_rows : 2 * moved_rows, :] = windows[taps + steps]
    for position in range(moving):
        place = position // cap * ROWS + position % cap
        slot = plan[0, moving + position]
        for step in range(steps):
            row = step * moved_rows + place
            gated[pl.ds(step * slots + slot, 1), :] = sums[row : row + 1, :]
        table[pl.ds(slot, 1), :] = jnp.concatenate(
            [driven[place : place + 1, :], driven[moved_rows + place : moved_rows + place + 1, :]],
            axis=1,
        )
    for step in range(steps):
        part = slice(step * slots, (step + 1) * slots)
        done_gated = jnp.where(living, gated[part, :], 0.0).astype(BF16)
        inner_out[taps + step] = done_gated
    inner_out[0] = jnp.where(living, table[:, :LANES], 0.0).astype(BF16)
    carried = jnp.where(head == 0, table[:, LANES : LANES + width], table[:, LANES + width :])
    group_out[0] = jnp.where(living[:, :width], carried, 0.0).astype(BF16)
    for place, (source, target) in enumerate(
        [
            (inner_out.at[pl.ds(0, taps)], inner_next),
            (inner_out.at[pl.ds(taps, steps)], gated_out),
            (group_out, group_next),
        ]
    ):
        copies.append(pltpu.make_async_copy(source, target, out_sem.at[place]))
        copies[-1].start()
    for copy in copies:
        copy.wait()


def arrive(replicas, cap, scalars, operands, scan_next, arrived):
    inner_moved, inner_raw, inner, group = operands[2], operands[7], operands[-2], operands[-1]
    taps, slots, _ = inner.shape
    rows = inner_raw.shape[0]
    steps = rows // slots
    moving = slots // 2
    units = moving // cap
    gated = jax.ShapeDtypeStruct((steps, slots, LANES), BF16)
    return pl.pallas_call(
        functools.partial(arrive_kernel, replicas, cap),
        out_shape=[
            gated,
            jax.ShapeDtypeStruct(inner.shape, BF16),
            jax.ShapeDtypeStruct(group.shape, BF16),
            jax.ShapeDtypeStruct(scan_next.shape, BF16),
        ],
        in_specs=[SMEM] * len(scalars) + [VMEM] * len(operands) + [HBM] * (1 + len(arrived)),
        out_specs=[HBM] * 4,
        scratch_shapes=[
            pltpu.VMEM((units,) + arrived[0].shape[1:], BF16),
            pltpu.VMEM(inner_moved.shape, F32),
            pltpu.VMEM(inner_moved.shape, F32),
            pltpu.VMEM((round_up(inner_moved.shape[0], LANES), LANES), F32),
            pltpu.VMEM((slots, 2 * LANES), F32),
            pltpu.VMEM((rows, LANES), F32),
            pltpu.VMEM((taps + steps, slots, LANES), BF16),
            pltpu.VMEM(group.shape, BF16),
            pltpu.VMEM((moving,) + scan_next.shape[1:], BF16),
            pltpu.SemaphoreType.DMA((units,)),
            pltpu.SemaphoreType.DMA((moving,)),
            pltpu.SemaphoreType.DMA((3,)),
        ],
        input_output_aliases={len(scalars) + len(operands): 3},
        compiler_params=pltpu.CompilerParams(vmem_limit_bytes=SMALL_LIMIT),
        cost_estimate=pl.CostEstimate(
            flops=10_000_000, bytes_accessed=2_000_000, transcendentals=0
        ),
        name="advance_arrived",
    )(*scalars, *operands, scan_next, *arrived)


def swap_heads(value):
    return lax.ppermute(value, "head", [(0, 1), (1, 0)])


def move(replicas, blocks):
    shifts = shifts_of(replicas)
    if not shifts:
        return [lax.all_to_all(blocks[0], "dp", 0, 0, tiled=True)]
    return [
        lax.ppermute(
            block, "dp", [(source, (source + shift) % replicas) for source in range(replicas)]
        )
        for shift, block in zip(shifts, blocks)
    ]


def per_device(
    replicas,
    tokens,
    inner_weight,
    gate_weight,
    group_weight,
    delta_weight,
    inner_taps,
    inner_offset,
    group_taps,
    group_offset,
    decay_log,
    delta_bias,
    skip_gain,
    inner_window,
    group_window,
    scan_state,
    send_list,
    receive_list,
    live_count,
):
    steps, slots, half = tokens.shape
    cap = send_list.shape[1] // replicas
    scan = jnp.transpose(scan_state, (0, 2, 1))
    inner = jnp.transpose(inner_window, (1, 0, 2))
    group = jnp.transpose(group_window, (1, 0, 2))
    own = tokens.reshape(steps * slots, half)

    group_other = swap_heads(group)
    arrived = move(replicas, pack(replicas, cap, send_list, scan, inner, group, group_other))
    inner_raw, gate, delta, decay, shared, plan = project(
        replicas,
        cap,
        (receive_list, decay_log, delta_bias),
        (
            own,
            swap_heads(own),
            inner_weight,
            gate_weight,
            group_weight.T,
            delta_weight.T,
            group_taps,
            group_offset[None],
        ),
    )
    scalars = (plan, live_count, skip_gain)
    *prepared, scan_next = stay(
        replicas,
        cap,
        scalars,
        (
            inner_raw,
            gate,
            delta,
            decay,
            shared,
            swap_heads(shared),
            inner_taps,
            inner_offset[None],
            inner,
            group,
            group_other,
            scan,
        ),
    )
    gated, inner_next, group_next, scan_next = arrive(
        replicas,
        cap,
        scalars,
        (*prepared, inner_raw, shared, inner_taps, inner_offset[None], inner, group),
        scan_next,
        arrived,
    )
    return (
        gated,
        jnp.transpose(inner_next, (1, 0, 2)),
        jnp.transpose(group_next, (1, 0, 2)),
        jnp.transpose(scan_next, (0, 2, 1)),
    )


def solution(mesh):
    in_specs = (
        P(None, ("grp", "dp"), "head"),
        P(None, "head"),
        P(None, "head"),
        P(None, "head"),
        P(None, "head"),
        P(None, "head"),
        P("head"),
        P(None, "head"),
        P("head"),
        P("head"),
        P("head"),
        P("head"),
        P(("grp", "dp"), None, "head"),
        P(("grp", "dp"), None, "head"),
        P(("grp", "dp"), "head", None),
        P(("grp", "dp"), None),
        P(("grp", "dp"), None),
        P(("grp", "dp")),
    )
    out_specs = (
        P(None, ("grp", "dp"), "head"),
        P(("grp", "dp"), None, "head"),
        P(("grp", "dp"), None, "head"),
        P(("grp", "dp"), "head", None),
    )
    return jax.shard_map(
        functools.partial(per_device, mesh.shape["dp"]),
        mesh=mesh,
        in_specs=in_specs,
        out_specs=out_specs,
        check_vma=False,
    )
```

```python
import functools

import jax
import jax.numpy as jnp
from jax import lax
from jax.experimental import pallas as pl
from jax.experimental.pallas import tpu as pltpu
from jax.sharding import PartitionSpec as P

F32 = jnp.float32
BF16 = jnp.bfloat16
SMALL_LIMIT = 8 * 1024 * 1024
MEDIUM_LIMIT = 32 * 1024 * 1024
LARGE_LIMIT = 60 * 1024 * 1024
MAX_SHIFTS = 16
WINDOWS_LIMIT = 8 * 1024 * 1024
LANES = 128
ROWS = 8
EARLIER = 2

VMEM = pl.BlockSpec(memory_space=pltpu.VMEM)
SMEM = pl.BlockSpec(memory_space=pltpu.SMEM)
HBM = pl.BlockSpec(memory_space=pl.ANY)


def round_up(value, step):
    return -(-value // step) * step


def silu(value):
    return value * jax.nn.sigmoid(value)


def rounded(value):
    return value.astype(BF16).astype(F32)


def shifts_of(replicas):
    if replicas > MAX_SHIFTS:
        return []
    return sorted(range(1, replicas), key=lambda shift: abs(2 * shift - replicas))


def both_halves(mine, theirs):
    first = lax.axis_index("head") == 0
    return jnp.concatenate(
        [jnp.where(first, mine, theirs), jnp.where(first, theirs, mine)], axis=-1
    )


def destinations(replicas, outs):
    shifts = shifts_of(replicas)
    me = lax.axis_index("dp")
    if shifts:
        return [
            (ref.at[0], lax.rem(me + shift, replicas)) for ref, shift in zip(outs, shifts)
        ]
    return [(outs[0].at[target], target) for target in range(replicas)]


def states_kernel(replicas, cap, scan, send, *refs):
    count = max(1, len(shifts_of(replicas)))
    outs = refs[:count]
    indices, held, load_sem, in_sem, out_sem = refs[count:]
    load = pltpu.make_async_copy(send, indices, load_sem)
    load.start()
    blocks = destinations(replicas, outs)
    state_rows = scan.shape[1]
    load.wait()
    plan = []
    for ref, target in blocks:
        for c in range(cap):
            plan.append((ref, c, indices[0, target * cap + c]))

    def fetch(place, index):
        return pltpu.make_async_copy(scan.at[index], held.at[place], in_sem.at[place])

    def store(place, ref, c):
        return pltpu.make_async_copy(
            held.at[place], ref.at[pl.ds(c * state_rows, state_rows)], out_sem.at[place]
        )

    for place, (_, _, index) in enumerate(plan):

        @pl.when(index >= 0)
        def _():
            fetch(place, index).start()

    for place, (ref, c, index) in enumerate(plan):

        @pl.when(index >= 0)
        def _():
            fetch(place, index).wait()
            store(place, ref, c).start()

    for place, (ref, c, index) in enumerate(plan):

        @pl.when(index >= 0)
        def _():
            store(place, ref, c).wait()


def windows_kernel(replicas, cap, state_rows, send, inner, group, group_other, *refs):
    count = max(1, len(shifts_of(replicas)))
    outs = refs[-9 - count : -9]
    indices, inner_in, mine_in, theirs_in, table, picked, cast = refs[-9:-2]
    load_sem, window_sem = refs[-2:]
    loads = [
        pltpu.make_async_copy(source, target, load_sem.at[place])
        for place, (source, target) in enumerate(
            [(send, indices), (inner, inner_in), (group, mine_in), (group_other, theirs_in)]
        )
    ]
    for load in loads:
        load.start()
    for load in loads:
        load.wait()
    taps = inner_in.shape[0]
    for tap in range(taps):
        table[:, tap * LANES : (tap + 1) * LANES] = inner_in[tap].astype(F32)
        table[:, (taps + tap) * LANES : (taps + tap + 1) * LANES] = both_halves(
            mine_in[tap].astype(F32), theirs_in[tap].astype(F32)
        )
    windows = []
    for block, (ref, target) in enumerate(destinations(replicas, outs)):
        picked[block] = jnp.zeros(picked.shape[1:], F32)
        for c in range(cap):
            index = indices[0, target * cap + c]
            row = table[pl.ds(jnp.maximum(index, 0), 1), :]
            for kind in range(2 * taps):
                picked[block, kind * ROWS + c : kind * ROWS + c + 1, :] = row[
                    :, kind * LANES : (kind + 1) * LANES
                ]
        cast[block] = picked[block].astype(BF16)
        windows.append(
            pltpu.make_async_copy(
                cast.at[block],
                ref.at[pl.ds(cap * state_rows, cast.shape[1])],
                window_sem.at[block],
            )
        )
        windows[-1].start()
    for window in windows:
        window.wait()


def pack(replicas, cap, send_list, scan, inner, group, group_other, swapped):
    shifts = shifts_of(replicas)
    count = max(1, len(shifts))
    per_block = 1 if shifts else replicas
    taps, slots, _ = inner.shape
    window_rows = 2 * taps * ROWS
    rows = cap * scan.shape[1] + window_rows
    blocks = count * per_block
    places = blocks * cap
    shapes = [jax.ShapeDtypeStruct((per_block, rows, LANES), BF16)] * count
    states = pl.pallas_call(
        functools.partial(states_kernel, replicas, cap),
        out_shape=shapes,
        in_specs=[HBM] * 2,
        out_specs=[HBM] * count,
        scratch_shapes=[
            pltpu.SMEM(send_list.shape, jnp.int32),
            pltpu.VMEM((places,) + scan.shape[1:], BF16),
            pltpu.SemaphoreType.DMA,
            pltpu.SemaphoreType.DMA((places,)),
            pltpu.SemaphoreType.DMA((places,)),
        ],
        compiler_params=pltpu.CompilerParams(vmem_limit_bytes=LARGE_LIMIT),
        cost_estimate=pl.CostEstimate(flops=0, bytes_accessed=2_000_000, transcendentals=0),
        name="pack_states",
    )(scan, send_list)
    return pl.pallas_call(
        functools.partial(windows_kernel, replicas, cap, scan.shape[1]),
        out_shape=shapes,
        in_specs=[HBM] * (4 + count + len(swapped)),
        out_specs=[HBM] * count,
        scratch_shapes=[
            pltpu.SMEM(send_list.shape, jnp.int32),
            pltpu.VMEM(inner.shape, BF16),
            pltpu.VMEM(group.shape, BF16),
            pltpu.VMEM(group.shape, BF16),
            pltpu.VMEM((slots, 2 * taps * LANES), F32),
            pltpu.VMEM((blocks, window_rows, LANES), F32),
            pltpu.VMEM((blocks, window_rows, LANES), BF16),
            pltpu.SemaphoreType.DMA((4,)),
            pltpu.SemaphoreType.DMA((blocks,)),
        ],
        input_output_aliases={4 + block: block for block in range(count)},
        compiler_params=pltpu.CompilerParams(vmem_limit_bytes=WINDOWS_LIMIT),
        cost_estimate=pl.CostEstimate(flops=0, bytes_accessed=500_000, transcendentals=0),
        name="pack_windows",
    )(send_list, inner, group, group_other, *states, *swapped)


def make_plan(replicas, cap, receive, slots, plan, inverse):
    moving = slots // 2
    for entry in range(replicas * cap):
        inverse[entry] = -1

    def kept_step(slot, kept):
        entry = receive[0, slot]
        stays = entry < 0
        plan[0, jnp.where(stays, kept, slots - 1)] = slot
        inverse[jnp.where(stays, replicas * cap, entry)] = slot
        return kept + jnp.where(stays, 1, 0)

    lax.fori_loop(0, slots, kept_step, 0)

    def source_step(source, units):
        present = inverse[source * cap] >= 0
        unit = jnp.minimum(units, moving // cap - 1)

        @pl.when(present)
        def _():
            for c in range(cap):
                plan[0, moving + unit * cap + c] = inverse[source * cap + c]

        plan[0, slots + source] = jnp.where(present, unit, -1)
        return units + jnp.where(present, 1, 0)

    lax.fori_loop(0, replicas, source_step, 0)


def convolve(carried, raw, weights, offset):
    joined = carried + raw
    results = []
    for step in range(len(raw)):
        summed = offset
        for tap in range(len(carried) + 1):
            summed = summed + joined[step + tap] * weights[tap : tap + 1, :]
        results.append(rounded(silu(summed)))
    return results


def transposed(rows, scratch, stride):
    scratch[...] = jnp.zeros_like(scratch)
    for step, value in enumerate(rows):
        scratch[step * stride : step * stride + value.shape[0], :] = value
    return [scratch[first : first + LANES].T for first in range(0, scratch.shape[0], LANES)]


def advance_slot(state, rows, driven, decay, sums, maps, lanes):
    hidden = state.astype(F32)
    width = state.shape[0]
    for row, lane in zip(rows, lanes):
        piece = maps[lane // LANES]
        column = piece[:, lane % LANES : lane % LANES + 1]
        hidden = decay[row, :] * hidden + driven[row, :] * column[:width]
        sums[row, :] = jnp.sum(hidden * column[width:], axis=0, keepdims=True)
        result = hidden.astype(BF16)
        hidden = result.astype(F32)
    return result


def stay_kernel(
    replicas,
    cap,
    receive,
    live,
    decay_log,
    delta_bias,
    skip_gain,
    own,
    other,
    inner_weight,
    gate_weight,
    group_weight,
    group_weight_other,
    delta_weight,
    inner_taps,
    inner_offset,
    group_taps,
    group_taps_other,
    inner,
    group,
    group_other,
    scan,
    *refs,
):
    (
        plan,
        gated,
        group_weights,
        inner_raw,
        both,
        inner_moved,
        group_moved,
        gate_moved,
        delta_moved,
        decay_moved,
        scan_next,
        inverse,
        gate,
        delta,
        decay,
        driven,
        skipped,
        sums,
        maps_in,
        ordered,
        done,
        sem,
    ) = refs[-22:]
    taps, slots, _ = inner.shape
    rows, half = own.shape
    steps = rows // slots
    moving = slots // 2
    moved_rows = inner_moved.shape[0] // steps
    head = lax.axis_index("head")
    make_plan(replicas, cap, receive, slots, plan, inverse)
    mine = pl.ds(pl.multiple_of(head * half, half), half)
    theirs = pl.ds(pl.multiple_of((1 - head) * half, half), half)

    def columns(weight):
        return jnp.dot(own[...], weight[mine, :], preferred_element_type=F32) + jnp.dot(
            other[...], weight[theirs, :], preferred_element_type=F32
        )

    def rows_of(weight, count):
        def one(tokens, part):
            piece = weight[:, part]
            if count > 1:
                piece = jnp.broadcast_to(piece, (count, half))
            return lax.dot_general(
                tokens, piece, (((1,), (1,)), ((), ())), preferred_element_type=F32
            )

        return one(own[...], mine) + one(other[...], theirs)

    both[...] = rounded(both_halves(rows_of(group_weight, 1), rows_of(group_weight_other, 1)))
    inner_raw[...] = rounded(columns(inner_weight))
    gate[...] = silu(rounded(columns(gate_weight)))
    shifted = rounded(rows_of(delta_weight, LANES)) + delta_bias[0]
    rate = jnp.maximum(shifted, 0.0) + jnp.log1p(jnp.exp(-jnp.abs(shifted)))
    delta[...] = rate
    decay[...] = jnp.exp(-rate * jnp.exp(jnp.full((1, LANES), decay_log[0], F32)))
    group_weights[: taps + 2, :] = both_halves(group_taps[...], group_taps_other[...])

    def parts(ref):
        return [ref[step * slots : (step + 1) * slots, :] for step in range(steps)]

    inner_conv = convolve(
        [inner[tap].astype(F32) for tap in range(taps)],
        parts(inner_raw),
        inner_taps[...],
        inner_offset[...],
    )
    group_conv = convolve(
        [both_halves(group[tap].astype(F32), group_other[tap].astype(F32)) for tap in range(taps)],
        parts(both),
        group_weights[: taps + 1, :],
        group_weights[taps + 1 : taps + 2, :],
    )
    for step in range(steps):
        part = slice(step * slots, (step + 1) * slots)
        driven[part, :] = delta[part, :] * inner_conv[step]
        skipped[part, :] = inner_conv[step] * skip_gain[0]
        maps_in[part, :] = group_conv[step]
    sums[...] = jnp.zeros_like(sums)
    stride = ordered.shape[0] // steps
    ordered[...] = jnp.zeros_like(ordered)
    for position in range(moving):
        slot = plan[0, position]
        for step in range(steps):
            ordered[step * stride + position : step * stride + position + 1, :] = maps_in[
                pl.ds(step * slots + slot, 1), :
            ]
    maps = [ordered[first : first + LANES].T for first in range(0, ordered.shape[0], LANES)]
    copies = []
    for position in range(moving):
        slot = plan[0, position]
        result = advance_slot(
            scan[slot],
            [pl.ds(step * slots + slot, 1) for step in range(steps)],
            driven,
            decay,
            sums,
            maps,
            [step * stride + position for step in range(steps)],
        )
        done[position] = jnp.where(slot < live[0], result, jnp.zeros_like(result))
        copies.append(
            pltpu.make_async_copy(done.at[position], scan_next.at[slot], sem.at[position])
        )
        copies[-1].start()
    gated[...] = (sums[...] + skipped[...]) * gate[...]
    pairs = (
        (inner_raw, inner_moved),
        (both, group_moved),
        (gate, gate_moved),
        (delta, delta_moved),
        (decay, decay_moved),
    )
    for _, target in pairs:
        target[...] = jnp.zeros_like(target)
    for position in range(moving):
        slot = plan[0, moving + position]
        place = position // cap * ROWS + position % cap
        for step in range(steps):
            row = step * moved_rows + place
            for source, target in pairs:
                target[row : row + 1, :] = source[pl.ds(step * slots + slot, 1), :]
    for copy in copies:
        copy.wait()


def stay(replicas, cap, scalars, operands, earlier):
    own, inner, scan = operands[0], operands[-4], operands[-1]
    taps, slots, _ = inner.shape
    rows = own.shape[0]
    steps = rows // slots
    moving = slots // 2
    moved_rows = moving // cap * ROWS
    full = jax.ShapeDtypeStruct((rows, LANES), F32)
    moved = jax.ShapeDtypeStruct((steps * moved_rows, LANES), F32)
    return pl.pallas_call(
        functools.partial(stay_kernel, replicas, cap),
        out_shape=[
            jax.ShapeDtypeStruct((1, round_up(slots + replicas, LANES)), jnp.int32),
            full,
            jax.ShapeDtypeStruct((round_up(taps + 2, ROWS), LANES), F32),
            full,
            full,
        ]
        + [moved] * 5
        + [jax.ShapeDtypeStruct(scan.shape, BF16)],
        in_specs=[SMEM] * len(scalars) + [VMEM] * len(operands) + [HBM] * len(earlier),
        out_specs=[SMEM] + [VMEM] * 9 + [HBM],
        scratch_shapes=[pltpu.SMEM((replicas * cap + 1,), jnp.int32)]
        + [pltpu.VMEM((rows, LANES), F32)] * 7
        + [
            pltpu.VMEM((round_up(rows, LANES), LANES), F32),
            pltpu.VMEM((moving,) + scan.shape[1:], BF16),
            pltpu.SemaphoreType.DMA((moving,)),
        ],
        compiler_params=pltpu.CompilerParams(vmem_limit_bytes=MEDIUM_LIMIT),
        cost_estimate=pl.CostEstimate(
            flops=300_000_000, bytes_accessed=6_000_000, transcendentals=100_000
        ),
        name="advance_staying",
    )(*scalars, *operands, *earlier)


def arrive_kernel(
    replicas,
    cap,
    plan,
    live,
    skip_gain,
    gated_in,
    group_weights,
    inner_moved,
    group_moved,
    gate_moved,
    delta_moved,
    decay_moved,
    inner_raw,
    both,
    inner_taps,
    inner_offset,
    inner,
    group,
    scan_in,
    *refs,
):
    del scan_in
    arrived = refs[:-16]
    gated_out, inner_next, group_next, scan_next = refs[-16:-12]
    (held, driven, sums, ordered, table, gated, inner_out, group_out) = refs[-12:-4]
    done, load_sem, sem, out_sem = refs[-4:]
    shifts = shifts_of(replicas)
    taps, slots, _ = inner.shape
    moving = slots // 2
    units = moving // cap
    state_rows = scan_next.shape[1]
    moved_rows = units * ROWS
    steps = inner_raw.shape[0] // slots
    width = group.shape[2]
    me = lax.axis_index("dp")
    head = lax.axis_index("head")

    if shifts:
        sources = [
            (ref.at[0], lax.rem(me - shift + replicas, replicas))
            for ref, shift in zip(arrived, shifts)
        ]
    else:
        sources = [(arrived[0].at[source], source) for source in range(replicas)]

    def each(act):
        for ref, source in sources:
            unit = plan[0, slots + source]

            @pl.when(unit >= 0)
            def _():
                act(pltpu.make_async_copy(ref, held.at[unit], load_sem.at[unit]))

    each(lambda copy: copy.start())

    living = lax.broadcasted_iota(jnp.int32, (slots, LANES), 0) < live[0]
    for step in range(steps):
        part = slice(step * slots, (step + 1) * slots)
        tap = taps - steps + step
        inner_out[tap] = jnp.where(living, inner_raw[part, :], 0.0).astype(BF16)
        raw = jnp.where(head == 0, both[part, :width], both[part, width:])
        group_out[tap] = jnp.where(living[:, :width], raw, 0.0).astype(BF16)
    table[:, :LANES] = inner[steps].astype(F32)
    group_own = group[steps].astype(F32)
    table[:, LANES:] = jnp.concatenate([group_own, group_own], axis=1)
    gated[...] = gated_in[...]
    each(lambda copy: copy.wait())

    kinds = [[] for _ in range(2 * taps)]
    for unit in range(units):
        block = held[unit, cap * state_rows :, :].astype(F32)
        for kind in range(2 * taps):
            kinds[kind].append(block[kind * ROWS : (kind + 1) * ROWS])
    windows = [jnp.concatenate(kind, axis=0) for kind in kinds]

    def parts(ref):
        return [ref[step * moved_rows : (step + 1) * moved_rows, :] for step in range(steps)]

    inner_conv = convolve(
        windows[:taps], parts(inner_moved), inner_taps[...], inner_offset[...]
    )
    group_conv = convolve(
        windows[taps:],
        parts(group_moved),
        group_weights[: taps + 1, :],
        group_weights[taps + 1 : taps + 2, :],
    )
    for step, delta in enumerate(parts(delta_moved)):
        driven[step * moved_rows : (step + 1) * moved_rows, :] = delta * inner_conv[step]
    stride = ordered.shape[0] // steps
    maps = transposed(group_conv, ordered, stride)
    sums[...] = jnp.zeros_like(sums)
    copies = []
    for position in range(moving):
        unit, c = position // cap, position % cap
        place = unit * ROWS + c
        slot = plan[0, moving + position]
        result = advance_slot(
            held[unit, c * state_rows : (c + 1) * state_rows, :],
            [slice(step * moved_rows + place, step * moved_rows + place + 1) for step in range(steps)],
            driven,
            decay_moved,
            sums,
            maps,
            [step * stride + place for step in range(steps)],
        )
        done[position] = jnp.where(slot < live[0], result, jnp.zeros_like(result))
        copies.append(
            pltpu.make_async_copy(done.at[position], scan_next.at[slot], sem.at[position])
        )
        copies[-1].start()

    for step in range(steps):
        part = slice(step * moved_rows, (step + 1) * moved_rows)
        skipped = inner_conv[step] * skip_gain[0]
        sums[part, :] = (sums[part, :] + skipped) * gate_moved[part, :]
    driven[:moved_rows, :] = windows[steps]
    driven[moved_rows : 2 * moved_rows, :] = windows[taps + steps]
    for position in range(moving):
        place = position // cap * ROWS + position % cap
        slot = plan[0, moving + position]
        for step in range(steps):
            row = step * moved_rows + place
            gated[pl.ds(step * slots + slot, 1), :] = sums[row : row + 1, :]
        table[pl.ds(slot, 1), :] = jnp.concatenate(
            [driven[place : place + 1, :], driven[moved_rows + place : moved_rows + place + 1, :]],
            axis=1,
        )
    for step in range(steps):
        part = slice(step * slots, (step + 1) * slots)
        done_gated = jnp.where(living, gated[part, :], 0.0).astype(BF16)
        inner_out[taps + step] = done_gated
    inner_out[0] = jnp.where(living, table[:, :LANES], 0.0).astype(BF16)
    carried = jnp.where(head == 0, table[:, LANES : LANES + width], table[:, LANES + width :])
    group_out[0] = jnp.where(living[:, :width], carried, 0.0).astype(BF16)
    for place, (source, target) in enumerate(
        [
            (inner_out.at[pl.ds(0, taps)], inner_next),
            (inner_out.at[pl.ds(taps, steps)], gated_out),
            (group_out, group_next),
        ]
    ):
        copies.append(pltpu.make_async_copy(source, target, out_sem.at[place]))
        copies[-1].start()
    for copy in copies:
        copy.wait()


def arrive(replicas, cap, scalars, operands, scan_next, arrived):
    inner_moved, inner_raw, inner, group = operands[2], operands[7], operands[-2], operands[-1]
    taps, slots, _ = inner.shape
    rows = inner_raw.shape[0]
    steps = rows // slots
    moving = slots // 2
    units = moving // cap
    gated = jax.ShapeDtypeStruct((steps, slots, LANES), BF16)
    return pl.pallas_call(
        functools.partial(arrive_kernel, replicas, cap),
        out_shape=[
            gated,
            jax.ShapeDtypeStruct(inner.shape, BF16),
            jax.ShapeDtypeStruct(group.shape, BF16),
            jax.ShapeDtypeStruct(scan_next.shape, BF16),
        ],
        in_specs=[SMEM] * len(scalars) + [VMEM] * len(operands) + [HBM] * (1 + len(arrived)),
        out_specs=[HBM] * 4,
        scratch_shapes=[
            pltpu.VMEM((units,) + arrived[0].shape[1:], BF16),
            pltpu.VMEM(inner_moved.shape, F32),
            pltpu.VMEM(inner_moved.shape, F32),
            pltpu.VMEM((round_up(inner_moved.shape[0], LANES), LANES), F32),
            pltpu.VMEM((slots, 2 * LANES), F32),
            pltpu.VMEM((rows, LANES), F32),
            pltpu.VMEM((taps + steps, slots, LANES), BF16),
            pltpu.VMEM(group.shape, BF16),
            pltpu.VMEM((moving,) + scan_next.shape[1:], BF16),
            pltpu.SemaphoreType.DMA((units,)),
            pltpu.SemaphoreType.DMA((moving,)),
            pltpu.SemaphoreType.DMA((3,)),
        ],
        input_output_aliases={len(scalars) + len(operands): 3},
        compiler_params=pltpu.CompilerParams(vmem_limit_bytes=SMALL_LIMIT),
        cost_estimate=pl.CostEstimate(
            flops=10_000_000, bytes_accessed=2_000_000, transcendentals=0
        ),
        name="advance_arrived",
    )(*scalars, *operands, scan_next, *arrived)


def swap_heads(value):
    return lax.ppermute(value, "head", [(0, 1), (1, 0)])


def move(replicas, blocks):
    shifts = shifts_of(replicas)
    if not shifts:
        return [lax.all_to_all(blocks[0], "dp", 0, 0, tiled=True)]
    return [
        lax.ppermute(
            block, "dp", [(source, (source + shift) % replicas) for source in range(replicas)]
        )
        for shift, block in zip(shifts, blocks)
    ]


def per_device(
    replicas,
    tokens,
    inner_weight,
    gate_weight,
    group_weight,
    delta_weight,
    inner_taps,
    inner_offset,
    group_taps,
    group_offset,
    decay_log,
    delta_bias,
    skip_gain,
    inner_window,
    group_window,
    scan_state,
    send_list,
    receive_list,
    live_count,
):
    steps, slots, half = tokens.shape
    cap = send_list.shape[1] // replicas
    scan = jnp.transpose(scan_state, (0, 2, 1))
    inner = jnp.transpose(inner_window, (1, 0, 2))
    group = jnp.transpose(group_window, (1, 0, 2))
    own = tokens.reshape(steps * slots, half)

    group_weight = group_weight.T
    inner_offset = inner_offset[None]
    group_taps = jnp.concatenate([group_taps, group_offset[None]], axis=0)
    group_other = swap_heads(group)
    swapped = [swap_heads(value) for value in (own, group_weight, group_taps)]
    blocks = pack(replicas, cap, send_list, scan, inner, group, group_other, swapped)
    arrived = move(replicas, blocks)
    plan, gated, group_weights, inner_raw, both, *moved, scan_next = stay(
        replicas,
        cap,
        (receive_list, live_count, decay_log, delta_bias, skip_gain),
        (
            own,
            swapped[0],
            inner_weight,
            gate_weight,
            group_weight,
            swapped[1],
            delta_weight.T,
            inner_taps,
            inner_offset,
            group_taps,
            swapped[2],
            inner,
            group,
            group_other,
            scan,
        ),
        arrived[:EARLIER],
    )
    gated, inner_next, group_next, scan_next = arrive(
        replicas,
        cap,
        (plan, live_count, skip_gain),
        (gated, group_weights, *moved, inner_raw, both, inner_taps, inner_offset, inner, group),
        scan_next,
        arrived,
    )
    return (
        gated,
        jnp.transpose(inner_next, (1, 0, 2)),
        jnp.transpose(group_next, (1, 0, 2)),
        jnp.transpose(scan_next, (0, 2, 1)),
    )


def solution(mesh):
    in_specs = (
        P(None, ("grp", "dp"), "head"),
        P(None, "head"),
        P(None, "head"),
        P(None, "head"),
        P(None, "head"),
        P(None, "head"),
        P("head"),
        P(None, "head"),
        P("head"),
        P("head"),
        P("head"),
        P("head"),
        P(("grp", "dp"), None, "head"),
        P(("grp", "dp"), None, "head"),
        P(("grp", "dp"), "head", None),
        P(("grp", "dp"), None),
        P(("grp", "dp"), None),
        P(("grp", "dp")),
    )
    out_specs = (
        P(None, ("grp", "dp"), "head"),
        P(("grp", "dp"), None, "head"),
        P(("grp", "dp"), None, "head"),
        P(("grp", "dp"), "head", None),
    )
    return jax.shard_map(
        functools.partial(per_device, mesh.shape["dp"]),
        mesh=mesh,
        in_specs=in_specs,
        out_specs=out_specs,
        check_vma=False,
    )
```

```python
import functools
import itertools

import jax
import jax.numpy as jnp
from jax import lax
from jax.experimental import pallas as pl
from jax.experimental.pallas import tpu as pltpu
from jax.sharding import PartitionSpec as P

F32 = jnp.float32
BF16 = jnp.bfloat16
SMALL_LIMIT = 8 * 1024 * 1024
LARGE_LIMIT = 60 * 1024 * 1024
MAX_SHIFTS = 16
LANES = 128
ROWS = 8
MAX_SETS = 64

VMEM = pl.BlockSpec(memory_space=pltpu.VMEM)
SMEM = pl.BlockSpec(memory_space=pltpu.SMEM)
HBM = pl.BlockSpec(memory_space=pl.ANY)


def round_up(value, step):
    return -(-value // step) * step


def silu(value):
    return value * jax.nn.sigmoid(value)


def rounded(value):
    return value.astype(BF16).astype(F32)


def shifts_of(replicas):
    return list(range(1, replicas)) if replicas <= MAX_SHIFTS else []


def both_halves(mine, theirs):
    first = lax.axis_index("head") == 0
    return jnp.concatenate(
        [jnp.where(first, mine, theirs), jnp.where(first, theirs, mine)], axis=-1
    )


def pack_kernel(replicas, cap, scan, send, inner, group, group_other, *refs):
    shifts = shifts_of(replicas)
    count = max(1, len(shifts))
    outs = refs[:count]
    (indices, inner_in, mine_in, theirs_in, held, table, picked, cast) = refs[count : count + 8]
    load_sem, in_sem, out_sem, window_sem = refs[count + 8 :]
    loads = [
        pltpu.make_async_copy(source, target, load_sem.at[place])
        for place, (source, target) in enumerate(
            [(send, indices), (inner, inner_in), (group, mine_in), (group_other, theirs_in)]
        )
    ]
    for load in loads:
        load.start()
    me = lax.axis_index("dp")
    taps, _, channels = inner_in.shape
    state_rows = scan.shape[1]
    blocks = []
    if shifts:
        for ref, shift in zip(outs, shifts):
            blocks.append((ref.at[0], lax.rem(me + shift, replicas)))
    else:
        blocks = [(outs[0].at[target], target) for target in range(replicas)]
    loads[0].wait()

    plan = []
    for block, (ref, target) in enumerate(blocks):
        for c in range(cap):
            plan.append((block, ref, c, indices[0, target * cap + c]))

    def fetch(place, index):
        return pltpu.make_async_copy(scan.at[index], held.at[place], in_sem.at[place])

    def store(place, ref, c):
        return pltpu.make_async_copy(
            held.at[place], ref.at[pl.ds(c * state_rows, state_rows)], out_sem.at[place]
        )

    for place, (_, _, _, index) in enumerate(plan):

        @pl.when(index >= 0)
        def _():
            fetch(place, index).start()

    for load in loads[1:]:
        load.wait()
    for tap in range(taps):
        table[:, tap * LANES : (tap + 1) * LANES] = inner_in[tap].astype(F32)
        table[:, (taps + tap) * LANES : (taps + tap + 1) * LANES] = both_halves(
            mine_in[tap].astype(F32), theirs_in[tap].astype(F32)
        )
    picked[...] = jnp.zeros_like(picked)
    for place, (block, _, c, index) in enumerate(plan):
        row = table[pl.ds(jnp.maximum(index, 0), 1), :]
        for kind in range(2 * taps):
            picked[block, kind * ROWS + c : kind * ROWS + c + 1, :] = row[
                :, kind * LANES : (kind + 1) * LANES
            ]
    windows = []
    for block, (ref, _) in enumerate(blocks):
        cast[block] = picked[block].astype(BF16)
        windows.append(
            pltpu.make_async_copy(
                cast.at[block],
                ref.at[pl.ds(cap * state_rows, cast.shape[1])],
                window_sem.at[block],
            )
        )
        windows[-1].start()

    for place, (_, ref, c, index) in enumerate(plan):

        @pl.when(index >= 0)
        def _():
            fetch(place, index).wait()
            store(place, ref, c).start()

    for place, (_, ref, c, index) in enumerate(plan):

        @pl.when(index >= 0)
        def _():
            store(place, ref, c).wait()

    for window in windows:
        window.wait()


def pack(replicas, cap, send_list, scan, inner, group, group_other):
    shifts = shifts_of(replicas)
    count = max(1, len(shifts))
    per_block = 1 if shifts else replicas
    taps, slots, _ = inner.shape
    window_rows = 2 * taps * ROWS
    rows = cap * scan.shape[1] + window_rows
    blocks = count * per_block
    places = blocks * cap
    return pl.pallas_call(
        functools.partial(pack_kernel, replicas, cap),
        out_shape=[jax.ShapeDtypeStruct((per_block, rows, LANES), BF16)] * count,
        in_specs=[HBM] * 5,
        out_specs=[HBM] * count,
        scratch_shapes=[
            pltpu.SMEM(send_list.shape, jnp.int32),
            pltpu.VMEM(inner.shape, BF16),
            pltpu.VMEM(group.shape, BF16),
            pltpu.VMEM(group.shape, BF16),
            pltpu.VMEM((places,) + scan.shape[1:], BF16),
            pltpu.VMEM((slots, 2 * taps * LANES), F32),
            pltpu.VMEM((blocks, window_rows, LANES), F32),
            pltpu.VMEM((blocks, window_rows, LANES), BF16),
            pltpu.SemaphoreType.DMA((4,)),
            pltpu.SemaphoreType.DMA((places,)),
            pltpu.SemaphoreType.DMA((places,)),
            pltpu.SemaphoreType.DMA((blocks,)),
        ],
        compiler_params=pltpu.CompilerParams(vmem_limit_bytes=LARGE_LIMIT),
        cost_estimate=pl.CostEstimate(flops=0, bytes_accessed=2_000_000, transcendentals=0),
        name="pack_leaving",
    )(scan, send_list, inner, group, group_other)


def make_plan(replicas, cap, receive, slots, plan, inverse):
    moving = slots // 2
    me = lax.axis_index("dp")
    by_shift = bool(shifts_of(replicas))
    kept = 0
    for entry in range(replicas * cap):
        inverse[entry] = -1
    for slot in range(slots):
        entry = receive[0, slot]
        stays = entry < 0
        plan[0, jnp.where(stays, kept, slots - 1)] = slot
        inverse[jnp.where(stays, replicas * cap, entry)] = slot
        kept = kept + jnp.where(stays, 1, 0)

    units = 0
    for place in range(replicas):
        source = lax.rem(me - place + replicas, replicas) if by_shift else place
        present = inverse[source * cap] >= 0
        unit = jnp.minimum(units, moving // cap - 1)

        @pl.when(present)
        def _():
            for c in range(cap):
                plan[0, moving + unit * cap + c] = inverse[source * cap + c]

        plan[0, slots + source] = jnp.where(present, unit, -1)
        units = units + jnp.where(present, 1, 0)


def convolve(carried, raw, weights, offset):
    joined = carried + raw
    results = []
    for step in range(len(raw)):
        summed = offset
        for tap in range(len(carried) + 1):
            summed = summed + joined[step + tap] * weights[tap : tap + 1, :]
        results.append(rounded(silu(summed)))
    return results


def transposed(rows, scratch, stride):
    scratch[...] = jnp.zeros_like(scratch)
    for step, value in enumerate(rows):
        scratch[step * stride : step * stride + value.shape[0], :] = value
    return [scratch[first : first + LANES].T for first in range(0, scratch.shape[0], LANES)]


def advance_slot(state, rows, driven, decay, sums, maps, lanes):
    hidden = state.astype(F32)
    width = state.shape[0]
    for row, lane in zip(rows, lanes):
        piece = maps[lane // LANES]
        column = piece[:, lane % LANES : lane % LANES + 1]
        hidden = decay[row, :] * hidden + driven[row, :] * column[:width]
        sums[row, :] = jnp.sum(hidden * column[width:], axis=0, keepdims=True)
        result = hidden.astype(BF16)
        hidden = result.astype(F32)
    return result


def stay_kernel(
    replicas,
    cap,
    receive_hbm,
    live_hbm,
    decay_log_hbm,
    delta_bias_hbm,
    skip_gain_hbm,
    own_hbm,
    other_hbm,
    inner_weight,
    gate_weight,
    group_weight,
    group_weight_other,
    delta_weight,
    inner_taps_hbm,
    inner_offset_hbm,
    group_taps_hbm,
    group_taps_other_hbm,
    inner_hbm,
    group_hbm,
    group_other_hbm,
    scan_hbm,
    plan,
    gated,
    group_weights,
    inner_raw,
    both,
    inner_moved,
    group_moved,
    gate_moved,
    delta_moved,
    decay_moved,
    scan_next,
    receive,
    live,
    decay_log,
    delta_bias,
    skip_gain,
    own,
    other,
    wide,
    tall,
    delta_row,
    inner_taps,
    inner_offset,
    group_taps,
    group_taps_other,
    inner,
    group,
    group_other,
    scan,
    inverse,
    gate,
    delta,
    decay,
    driven,
    skipped,
    sums,
    maps_in,
    ordered,
    done,
    sem,
    load_sem,
):
    taps, slots, _ = inner.shape
    rows, half = own.shape
    steps = rows // slots
    moving = slots // 2
    moved_rows = inner_moved.shape[0] // steps
    width = group.shape[2]
    head = lax.axis_index("head")

    def band(place):
        return tall.at[pl.ds(pl.multiple_of(place * width, width), width)]

    pairs = [
        (receive_hbm, receive),
        (delta_weight, delta_row),
        (own_hbm, own),
        (inner_weight, wide.at[:, pl.ds(0, LANES)]),
        (gate_weight, wide.at[:, pl.ds(LANES, LANES)]),
        (other_hbm, other),
        (group_weight, band(head)),
        (group_weight_other, band(1 - head)),
        (live_hbm, live),
        (decay_log_hbm, decay_log),
        (delta_bias_hbm, delta_bias),
        (skip_gain_hbm, skip_gain),
        (inner_taps_hbm, inner_taps),
        (inner_offset_hbm, inner_offset),
        (group_taps_hbm, group_taps),
        (group_taps_other_hbm, group_taps_other),
        (inner_hbm, inner),
        (group_hbm, group),
        (group_other_hbm, group_other),
        (scan_hbm, scan),
    ]
    loads = [
        pltpu.make_async_copy(source, target, load_sem.at[place])
        for place, (source, target) in enumerate(pairs)
    ]
    for load in loads:
        load.start()
    loads[0].wait()
    make_plan(replicas, cap, receive, slots, plan, inverse)
    loads[1].wait()
    first = 2 * width
    tall[first:, :] = jnp.broadcast_to(delta_row[...], (tall.shape[0] - first, 2 * half))
    for load in loads[2:]:
        load.wait()
    mine = pl.ds(pl.multiple_of(head * half, half), half)
    theirs = pl.ds(pl.multiple_of((1 - head) * half, half), half)
    flat = jnp.dot(own[...], wide[mine, :], preferred_element_type=F32) + jnp.dot(
        other[...], wide[theirs, :], preferred_element_type=F32
    )

    def across(tokens, part):
        return lax.dot_general(
            tokens, tall[:, part], (((1,), (1,)), ((), ())), preferred_element_type=F32
        )

    deep = across(own[...], mine) + across(other[...], theirs)
    inner_raw[...] = rounded(flat[:, :LANES])
    gate[...] = silu(rounded(flat[:, LANES:]))
    both[...] = rounded(deep[:, :first])
    shifted = rounded(jnp.broadcast_to(deep[:, first : first + 1], (rows, LANES))) + delta_bias[0]
    rate = jnp.maximum(shifted, 0.0) + jnp.log1p(jnp.exp(-jnp.abs(shifted)))
    delta[...] = rate
    decay[...] = jnp.exp(-rate * jnp.exp(jnp.full((1, LANES), decay_log[0], F32)))
    group_weights[: taps + 2, :] = both_halves(group_taps[...], group_taps_other[...])

    def parts(ref):
        return [ref[step * slots : (step + 1) * slots, :] for step in range(steps)]

    inner_conv = convolve(
        [inner[tap].astype(F32) for tap in range(taps)],
        parts(inner_raw),
        inner_taps[...],
        inner_offset[...],
    )
    group_conv = convolve(
        [both_halves(group[tap].astype(F32), group_other[tap].astype(F32)) for tap in range(taps)],
        parts(both),
        group_weights[: taps + 1, :],
        group_weights[taps + 1 : taps + 2, :],
    )
    for step in range(steps):
        part = slice(step * slots, (step + 1) * slots)
        driven[part, :] = delta[part, :] * inner_conv[step]
        skipped[part, :] = inner_conv[step] * skip_gain[0]
        maps_in[part, :] = group_conv[step]
    sums[...] = jnp.zeros_like(sums)
    stride = ordered.shape[0] // steps
    ordered[...] = jnp.zeros_like(ordered)
    for position in range(moving):
        slot = plan[0, position]
        for step in range(steps):
            ordered[step * stride + position : step * stride + position + 1, :] = maps_in[
                pl.ds(step * slots + slot, 1), :
            ]
    maps = [ordered[first : first + LANES].T for first in range(0, ordered.shape[0], LANES)]
    copies = []
    for position in range(moving):
        slot = plan[0, position]
        result = advance_slot(
            scan[slot],
            [pl.ds(step * slots + slot, 1) for step in range(steps)],
            driven,
            decay,
            sums,
            maps,
            [step * stride + position for step in range(steps)],
        )
        done[position] = jnp.where(slot < live[0], result, jnp.zeros_like(result))
        copies.append(
            pltpu.make_async_copy(done.at[position], scan_next.at[slot], sem.at[position])
        )
        copies[-1].start()
    gated[...] = (sums[...] + skipped[...]) * gate[...]
    pairs = (
        (inner_raw, inner_moved),
        (both, group_moved),
        (gate, gate_moved),
        (delta, delta_moved),
        (decay, decay_moved),
    )
    for _, target in pairs:
        target[...] = jnp.zeros_like(target)
    for position in range(moving):
        slot = plan[0, moving + position]
        place = position // cap * ROWS + position % cap
        for step in range(steps):
            row = step * moved_rows + place
            for source, target in pairs:
                target[row : row + 1, :] = source[pl.ds(step * slots + slot, 1), :]
    for copy in copies:
        copy.wait()


def stay(replicas, cap, operands):
    scalars, arrays = operands[:5], operands[5:]
    own, inner_weight, group_weight, delta_weight = arrays[0], arrays[2], arrays[4], arrays[6]
    inner, scan = arrays[-4], arrays[-1]
    taps, slots, _ = inner.shape
    rows = own.shape[0]
    steps = rows // slots
    moving = slots // 2
    moved_rows = moving // cap * ROWS
    width, features = group_weight.shape
    full = jax.ShapeDtypeStruct((rows, LANES), F32)
    moved = jax.ShapeDtypeStruct((steps * moved_rows, LANES), F32)

    def like(value):
        return pltpu.VMEM(value.shape, value.dtype)

    return pl.pallas_call(
        functools.partial(stay_kernel, replicas, cap),
        out_shape=[
            jax.ShapeDtypeStruct((1, round_up(slots + replicas, LANES)), jnp.int32),
            full,
            jax.ShapeDtypeStruct((round_up(taps + 2, ROWS), LANES), F32),
            full,
            full,
        ]
        + [moved] * 5
        + [jax.ShapeDtypeStruct(scan.shape, BF16)],
        in_specs=[HBM] * len(operands),
        out_specs=[SMEM] + [VMEM] * 9 + [HBM],
        scratch_shapes=[pltpu.SMEM(value.shape, value.dtype) for value in scalars]
        + [
            like(own),
            like(own),
            pltpu.VMEM((features, 2 * LANES), BF16),
            pltpu.VMEM((2 * width + 2 * ROWS, features), BF16),
            like(delta_weight),
        ]
        + [like(value) for value in arrays[7:]]
        + [pltpu.SMEM((replicas * cap + 1,), jnp.int32)]
        + [pltpu.VMEM((rows, LANES), F32)] * 7
        + [
            pltpu.VMEM((round_up(rows, LANES), LANES), F32),
            pltpu.VMEM((moving,) + scan.shape[1:], BF16),
            pltpu.SemaphoreType.DMA((moving,)),
            pltpu.SemaphoreType.DMA((20,)),
        ],
        compiler_params=pltpu.CompilerParams(vmem_limit_bytes=LARGE_LIMIT),
        cost_estimate=pl.CostEstimate(
            flops=300_000_000, bytes_accessed=6_000_000, transcendentals=100_000
        ),
        name="advance_staying",
    )(*operands)


def arrive_kernel(
    replicas,
    cap,
    plan,
    live,
    skip_gain,
    gated_in,
    group_weights,
    inner_moved,
    group_moved,
    gate_moved,
    delta_moved,
    decay_moved,
    inner_raw,
    both,
    inner_taps,
    inner_offset,
    inner,
    group,
    scan_in,
    *refs,
):
    del scan_in
    arrived = refs[:-16]
    gated_out, inner_next, group_next, scan_next = refs[-16:-12]
    (held, driven, sums, ordered, table, gated, inner_out, group_out) = refs[-12:-4]
    done, load_sem, sem, out_sem = refs[-4:]
    shifts = shifts_of(replicas)
    taps, slots, _ = inner.shape
    moving = slots // 2
    units = moving // cap
    state_rows = scan_next.shape[1]
    moved_rows = units * ROWS
    steps = inner_raw.shape[0] // slots
    width = group.shape[2]
    head = lax.axis_index("head")

    def each(act):
        if shifts:
            for unit, ref in enumerate(arrived):
                act(pltpu.make_async_copy(ref.at[0], held.at[unit], load_sem.at[unit]))
            return
        for source in range(replicas):
            unit = plan[0, slots + source]

            @pl.when(unit >= 0)
            def _():
                act(pltpu.make_async_copy(arrived[0].at[source], held.at[unit], load_sem.at[unit]))

    each(lambda copy: copy.start())

    living = lax.broadcasted_iota(jnp.int32, (slots, LANES), 0) < live[0]
    for step in range(steps):
        part = slice(step * slots, (step + 1) * slots)
        tap = taps - steps + step
        inner_out[tap] = jnp.where(living, inner_raw[part, :], 0.0).astype(BF16)
        raw = jnp.where(head == 0, both[part, :width], both[part, width:])
        group_out[tap] = jnp.where(living[:, :width], raw, 0.0).astype(BF16)
    table[:, :LANES] = inner[steps].astype(F32)
    group_own = group[steps].astype(F32)
    table[:, LANES:] = jnp.concatenate([group_own, group_own], axis=1)
    gated[...] = gated_in[...]
    each(lambda copy: copy.wait())

    kinds = [[] for _ in range(2 * taps)]
    for unit in range(units):
        block = held[unit, cap * state_rows :, :].astype(F32)
        for kind in range(2 * taps):
            kinds[kind].append(block[kind * ROWS : (kind + 1) * ROWS])
    windows = [jnp.concatenate(kind, axis=0) for kind in kinds]

    def parts(ref):
        return [ref[step * moved_rows : (step + 1) * moved_rows, :] for step in range(steps)]

    inner_conv = convolve(
        windows[:taps], parts(inner_moved), inner_taps[...], inner_offset[...]
    )
    group_conv = convolve(
        windows[taps:],
        parts(group_moved),
        group_weights[: taps + 1, :],
        group_weights[taps + 1 : taps + 2, :],
    )
    for step, delta in enumerate(parts(delta_moved)):
        driven[step * moved_rows : (step + 1) * moved_rows, :] = delta * inner_conv[step]
    stride = ordered.shape[0] // steps
    maps = transposed(group_conv, ordered, stride)
    sums[...] = jnp.zeros_like(sums)
    copies = []
    for position in range(moving):
        unit, c = position // cap, position % cap
        place = unit * ROWS + c
        slot = plan[0, moving + position]
        result = advance_slot(
            held[unit, c * state_rows : (c + 1) * state_rows, :],
            [slice(step * moved_rows + place, step * moved_rows + place + 1) for step in range(steps)],
            driven,
            decay_moved,
            sums,
            maps,
            [step * stride + place for step in range(steps)],
        )
        done[position] = jnp.where(slot < live[0], result, jnp.zeros_like(result))
        copies.append(
            pltpu.make_async_copy(done.at[position], scan_next.at[slot], sem.at[position])
        )
        copies[-1].start()

    for step in range(steps):
        part = slice(step * moved_rows, (step + 1) * moved_rows)
        skipped = inner_conv[step] * skip_gain[0]
        sums[part, :] = (sums[part, :] + skipped) * gate_moved[part, :]
    driven[:moved_rows, :] = windows[steps]
    driven[moved_rows : 2 * moved_rows, :] = windows[taps + steps]
    for position in range(moving):
        place = position // cap * ROWS + position % cap
        slot = plan[0, moving + position]
        for step in range(steps):
            row = step * moved_rows + place
            gated[pl.ds(step * slots + slot, 1), :] = sums[row : row + 1, :]
        table[pl.ds(slot, 1), :] = jnp.concatenate(
            [driven[place : place + 1, :], driven[moved_rows + place : moved_rows + place + 1, :]],
            axis=1,
        )
    for step in range(steps):
        part = slice(step * slots, (step + 1) * slots)
        done_gated = jnp.where(living, gated[part, :], 0.0).astype(BF16)
        inner_out[taps + step] = done_gated
    inner_out[0] = jnp.where(living, table[:, :LANES], 0.0).astype(BF16)
    carried = jnp.where(head == 0, table[:, LANES : LANES + width], table[:, LANES + width :])
    group_out[0] = jnp.where(living[:, :width], carried, 0.0).astype(BF16)
    for place, (source, target) in enumerate(
        [
            (inner_out.at[pl.ds(0, taps)], inner_next),
            (inner_out.at[pl.ds(taps, steps)], gated_out),
            (group_out, group_next),
        ]
    ):
        copies.append(pltpu.make_async_copy(source, target, out_sem.at[place]))
        copies[-1].start()
    for copy in copies:
        copy.wait()


def arrive(replicas, cap, scalars, operands, scan_next, arrived):
    inner_moved, inner_raw, inner, group = operands[2], operands[7], operands[-2], operands[-1]
    taps, slots, _ = inner.shape
    rows = inner_raw.shape[0]
    steps = rows // slots
    moving = slots // 2
    units = moving // cap
    gated = jax.ShapeDtypeStruct((steps, slots, LANES), BF16)
    return pl.pallas_call(
        functools.partial(arrive_kernel, replicas, cap),
        out_shape=[
            gated,
            jax.ShapeDtypeStruct(inner.shape, BF16),
            jax.ShapeDtypeStruct(group.shape, BF16),
            jax.ShapeDtypeStruct(scan_next.shape, BF16),
        ],
        in_specs=[SMEM] * len(scalars) + [VMEM] * len(operands) + [HBM] * (1 + len(arrived)),
        out_specs=[HBM] * 4,
        scratch_shapes=[
            pltpu.VMEM((units,) + arrived[0].shape[1:], BF16),
            pltpu.VMEM(inner_moved.shape, F32),
            pltpu.VMEM(inner_moved.shape, F32),
            pltpu.VMEM((round_up(inner_moved.shape[0], LANES), LANES), F32),
            pltpu.VMEM((slots, 2 * LANES), F32),
            pltpu.VMEM((rows, LANES), F32),
            pltpu.VMEM((taps + steps, slots, LANES), BF16),
            pltpu.VMEM(group.shape, BF16),
            pltpu.VMEM((moving,) + scan_next.shape[1:], BF16),
            pltpu.SemaphoreType.DMA((units,)),
            pltpu.SemaphoreType.DMA((moving,)),
            pltpu.SemaphoreType.DMA((3,)),
        ],
        input_output_aliases={len(scalars) + len(operands): 3},
        compiler_params=pltpu.CompilerParams(vmem_limit_bytes=SMALL_LIMIT),
        cost_estimate=pl.CostEstimate(
            flops=10_000_000, bytes_accessed=2_000_000, transcendentals=0
        ),
        name="advance_arrived",
    )(*scalars, *operands, scan_next, *arrived)


def swap_heads(value):
    return lax.ppermute(value, "head", [(0, 1), (1, 0)])


def compact_kernel(replicas, cap, receive_hbm, *refs):
    count = replicas - 1
    blocks, outs, (receive, load_sem, sem) = refs[:count], refs[count:-3], refs[-3:]
    load = pltpu.make_async_copy(receive_hbm, receive, load_sem)
    load.start()
    load.wait()
    me = lax.axis_index("dp")
    sources = [lax.rem(me - shift + replicas, replicas) for shift in range(1, replicas)]
    counts = [0] * count
    for slot in range(receive.shape[1]):
        entry = receive[0, slot]
        for place, source in enumerate(sources):
            inside = (entry >= source * cap) & (entry < (source + 1) * cap)
            counts[place] = counts[place] + jnp.where(inside, 1, 0)

    def each(act):
        units = 0
        for place, block in enumerate(blocks):
            present = counts[place] > 0
            for unit, out in enumerate(outs):

                @pl.when(present & (units == unit))
                def _():
                    act(pltpu.make_async_copy(block, out, sem.at[unit]))

            units = units + jnp.where(present, 1, 0)

    each(lambda copy: copy.start())
    each(lambda copy: copy.wait())


def compact(replicas, cap, units, receive_list, blocks):
    return pl.pallas_call(
        functools.partial(compact_kernel, replicas, cap),
        out_shape=[jax.ShapeDtypeStruct(blocks[0].shape, BF16)] * units,
        in_specs=[HBM] * (1 + len(blocks)),
        out_specs=[HBM] * units,
        scratch_shapes=[
            pltpu.SMEM(receive_list.shape, jnp.int32),
            pltpu.SemaphoreType.DMA,
            pltpu.SemaphoreType.DMA((units,)),
        ],
        compiler_params=pltpu.CompilerParams(vmem_limit_bytes=LARGE_LIMIT),
        name="compact_arrivals",
    )(receive_list, *blocks)


def rotate(replicas, shift, block):
    return lax.ppermute(
        block, "dp", [(source, (source + shift) % replicas) for source in range(replicas)]
    )


def used_shifts(replicas, send_list):
    cap = send_list.shape[1] // replicas
    base = replicas + 1
    target = lax.broadcasted_iota(jnp.int32, send_list.shape, 1) // cap
    shift = (target - lax.axis_index("dp") + replicas) % replicas
    inside = lax.broadcasted_iota(jnp.int32, send_list.shape, 1) % cap
    digits = jnp.zeros(send_list.shape, jnp.int32)
    for number in range(1, replicas):
        digits = jnp.where(shift == number, base ** (number - 1), digits)
    mine = jnp.sum(jnp.where((send_list >= 0) & (inside == 0), digits, 0))
    return lax.psum(mine, "dp")


def exchange(replicas, cap, units, send_list, receive_list, blocks, beside):
    shifts = shifts_of(replicas)
    if not shifts:
        return [lax.all_to_all(blocks[0], "dp", 0, 0, tiled=True)], beside()

    def every(blocks):
        moved = [rotate(replicas, shift, block) for shift, block in zip(shifts, blocks)]
        return list(compact(replicas, cap, units, receive_list, moved)), beside()

    sets = list(itertools.combinations(shifts, units))
    if len(sets) > MAX_SETS or (replicas + 1) ** len(shifts) >= 2**31:
        return every(blocks)

    def only(chosen):
        def run(blocks):
            return [rotate(replicas, shift, blocks[shift - 1]) for shift in chosen], beside()

        return run

    total = used_shifts(replicas, send_list)
    codes = [replicas * sum((replicas + 1) ** (shift - 1) for shift in chosen) for chosen in sets]
    index = len(sets)
    for place, code in enumerate(codes):
        index = jnp.where(total == code, place, index)
    return lax.switch(index, [only(chosen) for chosen in sets] + [every], blocks)


def per_device(
    replicas,
    tokens,
    inner_weight,
    gate_weight,
    group_weight,
    delta_weight,
    inner_taps,
    inner_offset,
    group_taps,
    group_offset,
    decay_log,
    delta_bias,
    skip_gain,
    inner_window,
    group_window,
    scan_state,
    send_list,
    receive_list,
    live_count,
):
    steps, slots, half = tokens.shape
    cap = send_list.shape[1] // replicas
    scan = jnp.transpose(scan_state, (0, 2, 1))
    inner = jnp.transpose(inner_window, (1, 0, 2))
    group = jnp.transpose(group_window, (1, 0, 2))
    own = tokens.reshape(steps * slots, half)

    group_weight = group_weight.T
    inner_offset = inner_offset[None]
    group_taps = jnp.concatenate([group_taps, group_offset[None]], axis=0)
    group_other = swap_heads(group)
    operands = (
        receive_list,
        live_count,
        decay_log,
        delta_bias,
        skip_gain,
        own,
        swap_heads(own),
        inner_weight,
        gate_weight,
        group_weight,
        swap_heads(group_weight),
        delta_weight.T,
        inner_taps,
        inner_offset,
        group_taps,
        swap_heads(group_taps),
        inner,
        group,
        group_other,
        scan,
    )
    blocks = pack(replicas, cap, send_list, scan, inner, group, group_other)
    arrived, prepared = exchange(
        replicas,
        cap,
        slots // 2 // cap,
        send_list,
        receive_list,
        blocks,
        lambda: stay(replicas, cap, operands),
    )
    plan, gated, group_weights, inner_raw, both, *moved, scan_next = prepared
    gated, inner_next, group_next, scan_next = arrive(
        replicas,
        cap,
        (plan, live_count, skip_gain),
        (gated, group_weights, *moved, inner_raw, both, inner_taps, inner_offset, inner, group),
        scan_next,
        arrived,
    )
    return (
        gated,
        jnp.transpose(inner_next, (1, 0, 2)),
        jnp.transpose(group_next, (1, 0, 2)),
        jnp.transpose(scan_next, (0, 2, 1)),
    )


def solution(mesh):
    in_specs = (
        P(None, ("grp", "dp"), "head"),
        P(None, "head"),
        P(None, "head"),
        P(None, "head"),
        P(None, "head"),
        P(None, "head"),
        P("head"),
        P(None, "head"),
        P("head"),
        P("head"),
        P("head"),
        P("head"),
        P(("grp", "dp"), None, "head"),
        P(("grp", "dp"), None, "head"),
        P(("grp", "dp"), "head", None),
        P(("grp", "dp"), None),
        P(("grp", "dp"), None),
        P(("grp", "dp")),
    )
    out_specs = (
        P(None, ("grp", "dp"), "head"),
        P(("grp", "dp"), None, "head"),
        P(("grp", "dp"), None, "head"),
        P(("grp", "dp"), "head", None),
    )
    return jax.shard_map(
        functools.partial(per_device, mesh.shape["dp"]),
        mesh=mesh,
        in_specs=in_specs,
        out_specs=out_specs,
        check_vma=False,
    )
```

```python
import functools

import jax
import jax.numpy as jnp
from jax import lax
from jax.experimental import pallas as pl
from jax.experimental.pallas import tpu as pltpu
from jax.sharding import PartitionSpec as P

F32 = jnp.float32
BF16 = jnp.bfloat16
SMALL_LIMIT = 8 * 1024 * 1024
LARGE_LIMIT = 60 * 1024 * 1024
MAX_ROUNDS = 16
EARLIER = 2
LANES = 128
ROWS = 8
MAX_SETS = 64

VMEM = pl.BlockSpec(memory_space=pltpu.VMEM)
SMEM = pl.BlockSpec(memory_space=pltpu.SMEM)
HBM = pl.BlockSpec(memory_space=pl.ANY)


def round_up(value, step):
    return -(-value // step) * step


def silu(value):
    return value * jax.nn.sigmoid(value)


def rounded(value):
    return value.astype(BF16).astype(F32)


def rounds_of(replicas):
    if replicas > MAX_ROUNDS or replicas & (replicas - 1):
        return []
    light = list(range(1, replicas // 2))
    heavy = list(range(replicas // 2, replicas))
    order = []
    while light or heavy:
        order += light[:1] + heavy[:1] if len(order) < 4 else heavy[:1] or light[:1]
        light = [mask for mask in light if mask not in order]
        heavy = [mask for mask in heavy if mask not in order]
    return order


def partner(replicas, mask):
    return jnp.bitwise_xor(lax.axis_index("dp"), mask)


def both_halves(mine, theirs):
    first = lax.axis_index("head") == 0
    return jnp.concatenate(
        [jnp.where(first, mine, theirs), jnp.where(first, theirs, mine)], axis=-1
    )


def pack_kernel(replicas, cap, scan, send, inner, group, group_other, *refs):
    rounds = rounds_of(replicas)
    count = max(1, len(rounds))
    outs = refs[:count]
    (indices, inner_in, mine_in, theirs_in, held, table, picked, cast) = refs[count : count + 8]
    load_sem, in_sem, out_sem, window_sem = refs[count + 8 :]
    loads = [
        pltpu.make_async_copy(source, target, load_sem.at[place])
        for place, (source, target) in enumerate(
            [(send, indices), (inner, inner_in), (group, mine_in), (group_other, theirs_in)]
        )
    ]
    for load in loads:
        load.start()
    taps = inner_in.shape[0]
    state_rows = scan.shape[1]
    blocks = []
    if rounds:
        for ref, mask in zip(outs, rounds):
            blocks.append((ref.at[0], partner(replicas, mask)))
    else:
        blocks = [(outs[0].at[target], target) for target in range(replicas)]
    loads[0].wait()

    plan = []
    for block, (ref, target) in enumerate(blocks):
        for c in range(cap):
            plan.append((block, ref, c, indices[0, target * cap + c]))

    def fetch(place, index):
        return pltpu.make_async_copy(scan.at[index], held.at[place], in_sem.at[place])

    def store(place, ref, c):
        return pltpu.make_async_copy(
            held.at[place], ref.at[pl.ds(c * state_rows, state_rows)], out_sem.at[place]
        )

    for place, (_, _, _, index) in enumerate(plan):

        @pl.when(index >= 0)
        def _():
            fetch(place, index).start()

    for load in loads[1:]:
        load.wait()
    for tap in range(taps):
        table[:, tap * LANES : (tap + 1) * LANES] = inner_in[tap].astype(F32)
        table[:, (taps + tap) * LANES : (taps + tap + 1) * LANES] = both_halves(
            mine_in[tap].astype(F32), theirs_in[tap].astype(F32)
        )
    picked[...] = jnp.zeros_like(picked)
    for place, (block, _, c, index) in enumerate(plan):
        row = table[pl.ds(jnp.maximum(index, 0), 1), :]
        for kind in range(2 * taps):
            picked[block, kind * ROWS + c : kind * ROWS + c + 1, :] = row[
                :, kind * LANES : (kind + 1) * LANES
            ]
    windows = []
    for block, (ref, _) in enumerate(blocks):
        cast[block] = picked[block].astype(BF16)
        windows.append(
            pltpu.make_async_copy(
                cast.at[block],
                ref.at[pl.ds(cap * state_rows, cast.shape[1])],
                window_sem.at[block],
            )
        )
        windows[-1].start()

    for place, (_, ref, c, index) in enumerate(plan):

        @pl.when(index >= 0)
        def _():
            fetch(place, index).wait()
            store(place, ref, c).start()

    for place, (_, ref, c, index) in enumerate(plan):

        @pl.when(index >= 0)
        def _():
            store(place, ref, c).wait()

    for window in windows:
        window.wait()


def pack(replicas, cap, send_list, scan, inner, group, group_other):
    rounds = rounds_of(replicas)
    count = max(1, len(rounds))
    per_block = 1 if rounds else replicas
    taps, slots, _ = inner.shape
    window_rows = 2 * taps * ROWS
    rows = cap * scan.shape[1] + window_rows
    blocks = count * per_block
    places = blocks * cap
    return pl.pallas_call(
        functools.partial(pack_kernel, replicas, cap),
        out_shape=[jax.ShapeDtypeStruct((per_block, rows, LANES), BF16)] * count,
        in_specs=[HBM] * 5,
        out_specs=[HBM] * count,
        scratch_shapes=[
            pltpu.SMEM(send_list.shape, jnp.int32),
            pltpu.VMEM(inner.shape, BF16),
            pltpu.VMEM(group.shape, BF16),
            pltpu.VMEM(group.shape, BF16),
            pltpu.VMEM((places,) + scan.shape[1:], BF16),
            pltpu.VMEM((slots, 2 * taps * LANES), F32),
            pltpu.VMEM((blocks, window_rows, LANES), F32),
            pltpu.VMEM((blocks, window_rows, LANES), BF16),
            pltpu.SemaphoreType.DMA((4,)),
            pltpu.SemaphoreType.DMA((places,)),
            pltpu.SemaphoreType.DMA((places,)),
            pltpu.SemaphoreType.DMA((blocks,)),
        ],
        compiler_params=pltpu.CompilerParams(vmem_limit_bytes=LARGE_LIMIT),
        cost_estimate=pl.CostEstimate(flops=0, bytes_accessed=2_000_000, transcendentals=0),
        name="pack_leaving",
    )(scan, send_list, inner, group, group_other)


def sources_of(replicas):
    rounds = rounds_of(replicas)
    if rounds:
        return [partner(replicas, mask) for mask in rounds]
    return list(range(replicas))


def make_plan(replicas, cap, receive, slots, plan, inverse):
    moving = slots // 2
    kept = 0
    for entry in range(replicas * cap):
        inverse[entry] = -1
    for slot in range(slots):
        entry = receive[0, slot]
        stays = entry < 0
        plan[0, jnp.where(stays, kept, moving)] = slot
        inverse[jnp.where(stays, replicas * cap, entry)] = slot
        kept = kept + jnp.where(stays, 1, 0)
    for block, source in enumerate(sources_of(replicas)):
        for c in range(cap):
            plan[0, moving + block * cap + c] = inverse[source * cap + c]


def convolve(carried, raw, weights, offset):
    joined = carried + raw
    results = []
    for step in range(len(raw)):
        summed = offset
        for tap in range(len(carried) + 1):
            summed = summed + joined[step + tap] * weights[tap : tap + 1, :]
        results.append(rounded(silu(summed)))
    return results


def transposed(rows, scratch, stride):
    scratch[...] = jnp.zeros_like(scratch)
    for step, value in enumerate(rows):
        scratch[step * stride : step * stride + value.shape[0], :] = value
    return [scratch[first : first + LANES].T for first in range(0, scratch.shape[0], LANES)]


def advance_slot(state, rows, driven, decay, sums, maps, lanes):
    hidden = state.astype(F32)
    width = state.shape[0]
    for row, lane in zip(rows, lanes):
        piece = maps[lane // LANES]
        column = piece[:, lane % LANES : lane % LANES + 1]
        hidden = decay[row, :] * hidden + driven[row, :] * column[:width]
        sums[row, :] = jnp.sum(hidden * column[width:], axis=0, keepdims=True)
        result = hidden.astype(BF16)
        hidden = result.astype(F32)
    return result


def stay_kernel(
    replicas,
    cap,
    receive_hbm,
    live_hbm,
    decay_log_hbm,
    delta_bias_hbm,
    skip_gain_hbm,
    own_hbm,
    other_hbm,
    inner_weight,
    gate_weight,
    group_weight,
    group_weight_other,
    delta_weight,
    inner_taps_hbm,
    inner_offset_hbm,
    group_taps_hbm,
    group_taps_other_hbm,
    inner_hbm,
    group_hbm,
    group_other_hbm,
    scan_hbm,
    *refs,
):
    (
        plan,
        gated,
        group_weights,
        inner_raw,
        both,
        inner_moved,
        group_moved,
        gate_moved,
        delta_moved,
        decay_moved,
        scan_next,
        receive,
        live,
        decay_log,
        delta_bias,
        skip_gain,
        own,
        other,
        wide,
        tall,
        delta_row,
        inner_taps,
        inner_offset,
        group_taps,
        group_taps_other,
        inner,
        group,
        group_other,
        scan,
        inverse,
        gate,
        delta,
        decay,
        driven,
        skipped,
        sums,
        maps_in,
        ordered,
        done,
        sem,
        load_sem,
    ) = refs[-41:]
    taps, slots, _ = inner.shape
    rows, half = own.shape
    steps = rows // slots
    moving = slots // 2
    moved_rows = inner_moved.shape[0] // steps
    width = group.shape[2]
    head = lax.axis_index("head")

    def band(place):
        return tall.at[pl.ds(pl.multiple_of(place * width, width), width)]

    pairs = [
        (receive_hbm, receive),
        (delta_weight, delta_row),
        (own_hbm, own),
        (inner_weight, wide.at[:, pl.ds(0, LANES)]),
        (gate_weight, wide.at[:, pl.ds(LANES, LANES)]),
        (other_hbm, other),
        (group_weight, band(head)),
        (group_weight_other, band(1 - head)),
        (live_hbm, live),
        (decay_log_hbm, decay_log),
        (delta_bias_hbm, delta_bias),
        (skip_gain_hbm, skip_gain),
        (inner_taps_hbm, inner_taps),
        (inner_offset_hbm, inner_offset),
        (group_taps_hbm, group_taps),
        (group_taps_other_hbm, group_taps_other),
        (inner_hbm, inner),
        (group_hbm, group),
        (group_other_hbm, group_other),
        (scan_hbm, scan),
    ]
    loads = [
        pltpu.make_async_copy(source, target, load_sem.at[place])
        for place, (source, target) in enumerate(pairs)
    ]
    for load in loads:
        load.start()
    loads[0].wait()
    make_plan(replicas, cap, receive, slots, plan, inverse)
    loads[1].wait()
    first = 2 * width
    tall[first:, :] = jnp.broadcast_to(delta_row[...], (tall.shape[0] - first, 2 * half))
    for load in loads[2:]:
        load.wait()
    mine = pl.ds(pl.multiple_of(head * half, half), half)
    theirs = pl.ds(pl.multiple_of((1 - head) * half, half), half)
    flat = jnp.dot(own[...], wide[mine, :], preferred_element_type=F32) + jnp.dot(
        other[...], wide[theirs, :], preferred_element_type=F32
    )

    def across(tokens, part):
        return lax.dot_general(
            tokens, tall[:, part], (((1,), (1,)), ((), ())), preferred_element_type=F32
        )

    deep = across(own[...], mine) + across(other[...], theirs)
    inner_raw[...] = rounded(flat[:, :LANES])
    gate[...] = silu(rounded(flat[:, LANES:]))
    both[...] = rounded(deep[:, :first])
    shifted = rounded(jnp.broadcast_to(deep[:, first : first + 1], (rows, LANES))) + delta_bias[0]
    rate = jnp.maximum(shifted, 0.0) + jnp.log1p(jnp.exp(-jnp.abs(shifted)))
    delta[...] = rate
    decay[...] = jnp.exp(-rate * jnp.exp(jnp.full((1, LANES), decay_log[0], F32)))
    group_weights[: taps + 2, :] = both_halves(group_taps[...], group_taps_other[...])

    def parts(ref):
        return [ref[step * slots : (step + 1) * slots, :] for step in range(steps)]

    inner_conv = convolve(
        [inner[tap].astype(F32) for tap in range(taps)],
        parts(inner_raw),
        inner_taps[...],
        inner_offset[...],
    )
    group_conv = convolve(
        [both_halves(group[tap].astype(F32), group_other[tap].astype(F32)) for tap in range(taps)],
        parts(both),
        group_weights[: taps + 1, :],
        group_weights[taps + 1 : taps + 2, :],
    )
    for step in range(steps):
        part = slice(step * slots, (step + 1) * slots)
        driven[part, :] = delta[part, :] * inner_conv[step]
        skipped[part, :] = inner_conv[step] * skip_gain[0]
        maps_in[part, :] = group_conv[step]
    sums[...] = jnp.zeros_like(sums)
    stride = ordered.shape[0] // steps
    ordered[...] = jnp.zeros_like(ordered)
    for position in range(moving):
        slot = plan[0, position]
        for step in range(steps):
            ordered[step * stride + position : step * stride + position + 1, :] = maps_in[
                pl.ds(step * slots + slot, 1), :
            ]
    maps = [ordered[first : first + LANES].T for first in range(0, ordered.shape[0], LANES)]
    copies = []
    for position in range(moving):
        slot = plan[0, position]
        result = advance_slot(
            scan[slot],
            [pl.ds(step * slots + slot, 1) for step in range(steps)],
            driven,
            decay,
            sums,
            maps,
            [step * stride + position for step in range(steps)],
        )
        done[position] = jnp.where(slot < live[0], result, jnp.zeros_like(result))
        copies.append(
            pltpu.make_async_copy(done.at[position], scan_next.at[slot], sem.at[position])
        )
        copies[-1].start()
    gated[...] = (sums[...] + skipped[...]) * gate[...]
    pairs = (
        (inner_raw, inner_moved),
        (both, group_moved),
        (gate, gate_moved),
        (delta, delta_moved),
        (decay, decay_moved),
    )
    for _, target in pairs:
        target[...] = jnp.zeros_like(target)
    for block in range(moved_rows // ROWS):

        @pl.when(plan[0, moving + block * cap] >= 0)
        def _():
            for c in range(cap):
                slot = plan[0, moving + block * cap + c]
                for step in range(steps):
                    row = step * moved_rows + block * ROWS + c
                    for source, target in pairs:
                        target[row : row + 1, :] = source[pl.ds(step * slots + slot, 1), :]

    for copy in copies:
        copy.wait()


def stay(replicas, cap, operands, earlier):
    scalars, arrays = operands[:5], operands[5:]
    own, inner_weight, group_weight, delta_weight = arrays[0], arrays[2], arrays[4], arrays[6]
    inner, scan = arrays[-4], arrays[-1]
    taps, slots, _ = inner.shape
    rows = own.shape[0]
    steps = rows // slots
    moving = slots // 2
    blocks = len(sources_of(replicas))
    moved_rows = blocks * ROWS
    width, features = group_weight.shape
    full = jax.ShapeDtypeStruct((rows, LANES), F32)
    moved = jax.ShapeDtypeStruct((steps * moved_rows, LANES), F32)

    def like(value):
        return pltpu.VMEM(value.shape, value.dtype)

    return pl.pallas_call(
        functools.partial(stay_kernel, replicas, cap),
        out_shape=[
            jax.ShapeDtypeStruct((1, round_up(moving + blocks * cap, LANES)), jnp.int32),
            full,
            jax.ShapeDtypeStruct((round_up(taps + 2, ROWS), LANES), F32),
            full,
            full,
        ]
        + [moved] * 5
        + [jax.ShapeDtypeStruct(scan.shape, BF16)],
        in_specs=[HBM] * (len(operands) + len(earlier)),
        out_specs=[SMEM] + [VMEM] * 9 + [HBM],
        scratch_shapes=[pltpu.SMEM(value.shape, value.dtype) for value in scalars]
        + [
            like(own),
            like(own),
            pltpu.VMEM((features, 2 * LANES), BF16),
            pltpu.VMEM((2 * width + 2 * ROWS, features), BF16),
            like(delta_weight),
        ]
        + [like(value) for value in arrays[7:]]
        + [pltpu.SMEM((replicas * cap + 1,), jnp.int32)]
        + [pltpu.VMEM((rows, LANES), F32)] * 7
        + [
            pltpu.VMEM((round_up(rows, LANES), LANES), F32),
            pltpu.VMEM((moving,) + scan.shape[1:], BF16),
            pltpu.SemaphoreType.DMA((moving,)),
            pltpu.SemaphoreType.DMA((20,)),
        ],
        compiler_params=pltpu.CompilerParams(vmem_limit_bytes=LARGE_LIMIT),
        cost_estimate=pl.CostEstimate(
            flops=300_000_000, bytes_accessed=6_000_000, transcendentals=100_000
        ),
        name="advance_staying",
    )(*operands, *earlier)


def arrive_kernel(
    replicas,
    cap,
    plan_hbm,
    live_hbm,
    skip_gain_hbm,
    gated_in,
    group_weights,
    inner_moved,
    group_moved,
    gate_moved,
    delta_moved,
    decay_moved,
    inner_raw,
    both,
    inner_taps,
    inner_offset,
    inner,
    group,
    scan_in,
    *refs,
):
    del scan_in
    arrived = refs[:-18]
    gated_out, inner_next, group_next, scan_next = refs[-18:-14]
    plan, live, skip_gain = refs[-14:-11]
    (driven, sums, ordered, table, gated, gated_cast, inner_out, group_out) = refs[-11:-3]
    done, sem, out_sem = refs[-3:]
    taps, slots, _ = inner.shape
    moving = slots // 2
    state_rows = scan_next.shape[1]
    steps = inner_raw.shape[0] // slots
    width = group.shape[2]
    head = lax.axis_index("head")
    loads = [
        pltpu.make_async_copy(source, target, out_sem.at[place])
        for place, (source, target) in enumerate(
            [(plan_hbm, plan), (live_hbm, live), (skip_gain_hbm, skip_gain)]
        )
    ]
    for load in loads:
        load.start()
    if rounds_of(replicas):
        blocks = [ref.at[0] for ref in arrived]
    else:
        blocks = [arrived[0].at[source] for source in range(replicas)]
    moved_rows = len(blocks) * ROWS

    kinds = [[] for _ in range(2 * taps)]
    for ref in blocks:
        block = ref[cap * state_rows :, :].astype(F32)
        for kind in range(2 * taps):
            kinds[kind].append(block[kind * ROWS : (kind + 1) * ROWS])
    windows = [jnp.concatenate(kind, axis=0) for kind in kinds]

    def parts(ref):
        return [ref[step * moved_rows : (step + 1) * moved_rows, :] for step in range(steps)]

    inner_conv = convolve(
        windows[:taps], parts(inner_moved), inner_taps[...], inner_offset[...]
    )
    group_conv = convolve(
        windows[taps:],
        parts(group_moved),
        group_weights[: taps + 1, :],
        group_weights[taps + 1 : taps + 2, :],
    )
    for step, delta in enumerate(parts(delta_moved)):
        driven[step * moved_rows : (step + 1) * moved_rows, :] = delta * inner_conv[step]
    stride = ordered.shape[0] // steps
    maps = transposed(group_conv, ordered, stride)
    sums[...] = jnp.zeros_like(sums)
    for load in loads:
        load.wait()

    def each(act):
        for block in range(len(blocks)):

            @pl.when(plan[0, moving + block * cap] >= 0)
            def _():
                for c in range(cap):
                    act(block, c, plan[0, moving + block * cap + c])

    def store(block, c, slot):
        place = block * cap + c
        return pltpu.make_async_copy(done.at[place], scan_next.at[slot], sem.at[place])

    def advance(block, c, slot):
        place = block * ROWS + c
        result = advance_slot(
            blocks[block][c * state_rows : (c + 1) * state_rows, :],
            [
                slice(step * moved_rows + place, step * moved_rows + place + 1)
                for step in range(steps)
            ],
            driven,
            decay_moved,
            sums,
            maps,
            [step * stride + place for step in range(steps)],
        )
        done[block * cap + c] = jnp.where(slot < live[0], result, jnp.zeros_like(result))
        store(block, c, slot).start()

    each(advance)
    living = lax.broadcasted_iota(jnp.int32, (slots, LANES), 0) < live[0]
    for step in range(steps):
        part = slice(step * slots, (step + 1) * slots)
        tap = taps - steps + step
        inner_out[tap] = jnp.where(living, inner_raw[part, :], 0.0).astype(BF16)
        raw = jnp.where(head == 0, both[part, :width], both[part, width:])
        group_out[tap] = jnp.where(living[:, :width], raw, 0.0).astype(BF16)
    table[:, :LANES] = inner[steps].astype(F32)
    group_own = group[steps].astype(F32)
    table[:, LANES:] = jnp.concatenate([group_own, group_own], axis=1)
    gated[...] = gated_in[...]
    for step in range(steps):
        part = slice(step * moved_rows, (step + 1) * moved_rows)
        skipped = inner_conv[step] * skip_gain[0]
        sums[part, :] = (sums[part, :] + skipped) * gate_moved[part, :]
    driven[:moved_rows, :] = windows[steps]
    driven[moved_rows : 2 * moved_rows, :] = windows[taps + steps]

    def scatter(block, c, slot):
        place = block * ROWS + c
        for step in range(steps):
            row = step * moved_rows + place
            gated[pl.ds(step * slots + slot, 1), :] = sums[row : row + 1, :]
        table[pl.ds(slot, 1), :] = jnp.concatenate(
            [driven[place : place + 1, :], driven[moved_rows + place : moved_rows + place + 1, :]],
            axis=1,
        )

    each(scatter)
    for step in range(steps):
        part = slice(step * slots, (step + 1) * slots)
        gated_cast[step] = jnp.where(living, gated[part, :], 0.0).astype(BF16)
    inner_out[0] = jnp.where(living, table[:, :LANES], 0.0).astype(BF16)
    carried = jnp.where(head == 0, table[:, LANES : LANES + width], table[:, LANES + width :])
    group_out[0] = jnp.where(living[:, :width], carried, 0.0).astype(BF16)
    copies = [
        pltpu.make_async_copy(source, target, out_sem.at[place])
        for place, (source, target) in enumerate(
            [(inner_out, inner_next), (gated_cast, gated_out), (group_out, group_next)]
        )
    ]
    for copy in copies:
        copy.start()
    each(lambda block, c, slot: store(block, c, slot).wait())
    for copy in copies:
        copy.wait()


def arrive(replicas, cap, scalars, operands, scan_next, arrived):
    inner_moved, inner_raw, inner, group = operands[2], operands[7], operands[-2], operands[-1]
    taps, slots, _ = inner.shape
    rows = inner_raw.shape[0]
    steps = rows // slots
    places = len(sources_of(replicas)) * cap
    gated = jax.ShapeDtypeStruct((steps, slots, LANES), BF16)
    limit = SMALL_LIMIT if rounds_of(replicas) else LARGE_LIMIT
    return pl.pallas_call(
        functools.partial(arrive_kernel, replicas, cap),
        out_shape=[
            gated,
            jax.ShapeDtypeStruct(inner.shape, BF16),
            jax.ShapeDtypeStruct(group.shape, BF16),
            jax.ShapeDtypeStruct(scan_next.shape, BF16),
        ],
        in_specs=[HBM] * len(scalars) + [VMEM] * len(operands) + [HBM] + [VMEM] * len(arrived),
        out_specs=[HBM] * 4,
        scratch_shapes=[pltpu.SMEM(value.shape, value.dtype) for value in scalars]
        + [
            pltpu.VMEM(inner_moved.shape, F32),
            pltpu.VMEM(inner_moved.shape, F32),
            pltpu.VMEM((round_up(inner_moved.shape[0], LANES), LANES), F32),
            pltpu.VMEM((slots, 2 * LANES), F32),
            pltpu.VMEM((rows, LANES), F32),
            pltpu.VMEM(gated.shape, BF16),
            pltpu.VMEM(inner.shape, BF16),
            pltpu.VMEM(group.shape, BF16),
            pltpu.VMEM((places,) + scan_next.shape[1:], BF16),
            pltpu.SemaphoreType.DMA((places,)),
            pltpu.SemaphoreType.DMA((3,)),
        ],
        input_output_aliases={len(scalars) + len(operands): 3},
        compiler_params=pltpu.CompilerParams(vmem_limit_bytes=limit),
        cost_estimate=pl.CostEstimate(
            flops=10_000_000, bytes_accessed=2_000_000, transcendentals=0
        ),
        name="advance_arrived",
    )(*scalars, *operands, scan_next, *arrived)


def swap_heads(value):
    return lax.ppermute(value, "head", [(0, 1), (1, 0)])


def exchange(replicas, blocks):
    rounds = rounds_of(replicas)
    if not rounds:
        return [lax.all_to_all(blocks[0], "dp", 0, 0, tiled=True)]
    return [
        lax.ppermute(block, "dp", [(source, source ^ mask) for source in range(replicas)])
        for mask, block in zip(rounds, blocks)
    ]


def per_device(
    replicas,
    tokens,
    inner_weight,
    gate_weight,
    group_weight,
    delta_weight,
    inner_taps,
    inner_offset,
    group_taps,
    group_offset,
    decay_log,
    delta_bias,
    skip_gain,
    inner_window,
    group_window,
    scan_state,
    send_list,
    receive_list,
    live_count,
):
    steps, slots, half = tokens.shape
    cap = send_list.shape[1] // replicas
    scan = jnp.transpose(scan_state, (0, 2, 1))
    inner = jnp.transpose(inner_window, (1, 0, 2))
    group = jnp.transpose(group_window, (1, 0, 2))
    own = tokens.reshape(steps * slots, half)

    group_weight = group_weight.T
    inner_offset = inner_offset[None]
    group_taps = jnp.concatenate([group_taps, group_offset[None]], axis=0)
    group_other = swap_heads(group)
    operands = (
        receive_list,
        live_count,
        decay_log,
        delta_bias,
        skip_gain,
        own,
        swap_heads(own),
        inner_weight,
        gate_weight,
        group_weight,
        swap_heads(group_weight),
        delta_weight.T,
        inner_taps,
        inner_offset,
        group_taps,
        swap_heads(group_taps),
        inner,
        group,
        group_other,
        scan,
    )
    blocks = pack(replicas, cap, send_list, scan, inner, group, group_other)
    arrived = exchange(replicas, blocks)
    light = [
        block for mask, block in zip(rounds_of(replicas), arrived) if mask < replicas // 2
    ]
    prepared = stay(replicas, cap, operands, light[:EARLIER])
    plan, gated, group_weights, inner_raw, both, *moved, scan_next = prepared
    gated, inner_next, group_next, scan_next = arrive(
        replicas,
        cap,
        (plan, live_count, skip_gain),
        (gated, group_weights, *moved, inner_raw, both, inner_taps, inner_offset, inner, group),
        scan_next,
        arrived,
    )
    return (
        gated,
        jnp.transpose(inner_next, (1, 0, 2)),
        jnp.transpose(group_next, (1, 0, 2)),
        jnp.transpose(scan_next, (0, 2, 1)),
    )


def solution(mesh):
    in_specs = (
        P(None, ("grp", "dp"), "head"),
        P(None, "head"),
        P(None, "head"),
        P(None, "head"),
        P(None, "head"),
        P(None, "head"),
        P("head"),
        P(None, "head"),
        P("head"),
        P("head"),
        P("head"),
        P("head"),
        P(("grp", "dp"), None, "head"),
        P(("grp", "dp"), None, "head"),
        P(("grp", "dp"), "head", None),
        P(("grp", "dp"), None),
        P(("grp", "dp"), None),
        P(("grp", "dp")),
    )
    out_specs = (
        P(None, ("grp", "dp"), "head"),
        P(("grp", "dp"), None, "head"),
        P(("grp", "dp"), None, "head"),
        P(("grp", "dp"), "head", None),
    )
    return jax.shard_map(
        functools.partial(per_device, mesh.shape["dp"]),
        mesh=mesh,
        in_specs=in_specs,
        out_specs=out_specs,
        check_vma=False,
    )
```

```python
import functools

import jax
import jax.numpy as jnp
from jax import lax
from jax.experimental import pallas as pl
from jax.experimental.pallas import tpu as pltpu
from jax.sharding import PartitionSpec as P

F32 = jnp.float32
BF16 = jnp.bfloat16
SMALL_LIMIT = 8 * 1024 * 1024
MEDIUM_LIMIT = 32 * 1024 * 1024
LARGE_LIMIT = 60 * 1024 * 1024
MAX_ROUNDS = 16
LANES = 128
ROWS = 8
MAX_SETS = 64

VMEM = pl.BlockSpec(memory_space=pltpu.VMEM)
SMEM = pl.BlockSpec(memory_space=pltpu.SMEM)
HBM = pl.BlockSpec(memory_space=pl.ANY)


def round_up(value, step):
    return -(-value // step) * step


def silu(value):
    return value * jax.nn.sigmoid(value)


def rounded(value):
    return value.astype(BF16).astype(F32)


def rounds_of(replicas):
    if replicas > MAX_ROUNDS or replicas & (replicas - 1):
        return []
    light = list(range(1, replicas // 2))
    heavy = list(range(replicas // 2, replicas))
    order = []
    while light or heavy:
        order += light[:1] + heavy[:2] if len(order) < 2 else light[:1] + heavy[:1]
        light = [mask for mask in light if mask not in order]
        heavy = [mask for mask in heavy if mask not in order]
    return order


def partner(replicas, mask):
    return jnp.bitwise_xor(lax.axis_index("dp"), mask)


def both_halves(mine, theirs):
    first = lax.axis_index("head") == 0
    return jnp.concatenate(
        [jnp.where(first, mine, theirs), jnp.where(first, theirs, mine)], axis=-1
    )


def pack_kernel(replicas, cap, scan, send, inner, group, group_other, *refs):
    rounds = rounds_of(replicas)
    count = max(1, len(rounds))
    outs = refs[-12 - count : -12]
    (indices, inner_in, mine_in, theirs_in, held, table, picked, cast) = refs[-12:-4]
    load_sem, in_sem, out_sem, window_sem = refs[-4:]
    loads = [
        pltpu.make_async_copy(source, target, load_sem.at[place])
        for place, (source, target) in enumerate(
            [(send, indices), (inner, inner_in), (group, mine_in), (group_other, theirs_in)]
        )
    ]
    for load in loads:
        load.start()
    taps = inner_in.shape[0]
    state_rows = scan.shape[1]
    blocks = []
    if rounds:
        for ref, mask in zip(outs, rounds):
            blocks.append((ref.at[0], partner(replicas, mask)))
    else:
        blocks = [(outs[0].at[target], target) for target in range(replicas)]
    loads[0].wait()

    plan = []
    for block, (ref, target) in enumerate(blocks):
        for c in range(cap):
            plan.append((block, ref, c, indices[0, target * cap + c]))

    def fetch(place, index):
        return pltpu.make_async_copy(scan.at[index], held.at[place], in_sem.at[place])

    def store(place, ref, c):
        return pltpu.make_async_copy(
            held.at[place], ref.at[pl.ds(c * state_rows, state_rows)], out_sem.at[place]
        )

    for place, (_, _, _, index) in enumerate(plan):

        @pl.when(index >= 0)
        def _():
            fetch(place, index).start()

    for load in loads[1:]:
        load.wait()
    for tap in range(taps):
        table[:, tap * LANES : (tap + 1) * LANES] = inner_in[tap].astype(F32)
        table[:, (taps + tap) * LANES : (taps + tap + 1) * LANES] = both_halves(
            mine_in[tap].astype(F32), theirs_in[tap].astype(F32)
        )
    picked[...] = jnp.zeros_like(picked)
    for place, (block, _, c, index) in enumerate(plan):
        row = table[pl.ds(jnp.maximum(index, 0), 1), :]
        for kind in range(2 * taps):
            picked[block, kind * ROWS + c : kind * ROWS + c + 1, :] = row[
                :, kind * LANES : (kind + 1) * LANES
            ]
    windows = []
    for block, (ref, _) in enumerate(blocks):
        cast[block] = picked[block].astype(BF16)
        windows.append(
            pltpu.make_async_copy(
                cast.at[block],
                ref.at[pl.ds(cap * state_rows, cast.shape[1])],
                window_sem.at[block],
            )
        )
        windows[-1].start()

    for place, (_, ref, c, index) in enumerate(plan):

        @pl.when(index >= 0)
        def _():
            fetch(place, index).wait()
            store(place, ref, c).start()

    for place, (_, ref, c, index) in enumerate(plan):

        @pl.when(index >= 0)
        def _():
            store(place, ref, c).wait()

    for window in windows:
        window.wait()


def pack(replicas, cap, send_list, scan, inner, group, group_other, swapped):
    rounds = rounds_of(replicas)
    count = max(1, len(rounds))
    per_block = 1 if rounds else replicas
    taps, slots, _ = inner.shape
    window_rows = 2 * taps * ROWS
    rows = cap * scan.shape[1] + window_rows
    blocks = count * per_block
    places = blocks * cap
    return pl.pallas_call(
        functools.partial(pack_kernel, replicas, cap),
        out_shape=[jax.ShapeDtypeStruct((per_block, rows, LANES), BF16)] * count,
        in_specs=[HBM] * (5 + len(swapped)),
        out_specs=[HBM] * count,
        scratch_shapes=[
            pltpu.SMEM(send_list.shape, jnp.int32),
            pltpu.VMEM(inner.shape, BF16),
            pltpu.VMEM(group.shape, BF16),
            pltpu.VMEM(group.shape, BF16),
            pltpu.VMEM((places,) + scan.shape[1:], BF16),
            pltpu.VMEM((slots, 2 * taps * LANES), F32),
            pltpu.VMEM((blocks, window_rows, LANES), F32),
            pltpu.VMEM((blocks, window_rows, LANES), BF16),
            pltpu.SemaphoreType.DMA((4,)),
            pltpu.SemaphoreType.DMA((places,)),
            pltpu.SemaphoreType.DMA((places,)),
            pltpu.SemaphoreType.DMA((blocks,)),
        ],
        compiler_params=pltpu.CompilerParams(vmem_limit_bytes=LARGE_LIMIT),
        cost_estimate=pl.CostEstimate(flops=0, bytes_accessed=2_000_000, transcendentals=0),
        name="pack_leaving",
    )(scan, send_list, inner, group, group_other, *swapped)


def sources_of(replicas):
    rounds = rounds_of(replicas)
    if rounds:
        return [partner(replicas, mask) for mask in rounds]
    return list(range(replicas))


def make_plan(replicas, cap, receive, slots, plan, inverse):
    moving = slots // 2
    kept = 0
    for entry in range(replicas * cap):
        inverse[entry] = -1
    for slot in range(slots):
        entry = receive[0, slot]
        stays = entry < 0
        plan[0, jnp.where(stays, kept, moving)] = slot
        inverse[jnp.where(stays, replicas * cap, entry)] = slot
        kept = kept + jnp.where(stays, 1, 0)
    for block, source in enumerate(sources_of(replicas)):
        for c in range(cap):
            plan[0, moving + block * cap + c] = inverse[source * cap + c]


def convolve(carried, raw, weights, offset):
    joined = carried + raw
    results = []
    for step in range(len(raw)):
        summed = offset
        for tap in range(len(carried) + 1):
            summed = summed + joined[step + tap] * weights[tap : tap + 1, :]
        results.append(rounded(silu(summed)))
    return results


def transposed(rows, scratch, stride):
    scratch[...] = jnp.zeros_like(scratch)
    for step, value in enumerate(rows):
        scratch[step * stride : step * stride + value.shape[0], :] = value
    return [scratch[first : first + LANES].T for first in range(0, scratch.shape[0], LANES)]


def advance_slot(state, rows, driven, decay, sums, maps, lanes):
    hidden = state.astype(F32)
    width = state.shape[0]
    for row, lane in zip(rows, lanes):
        piece = maps[lane // LANES]
        column = piece[:, lane % LANES : lane % LANES + 1]
        hidden = decay[row, :] * hidden + driven[row, :] * column[:width]
        sums[row, :] = jnp.sum(hidden * column[width:], axis=0, keepdims=True)
        result = hidden.astype(BF16)
        hidden = result.astype(F32)
    return result


def stay_kernel(
    replicas,
    cap,
    receive_hbm,
    own_hbm,
    other_hbm,
    inner_weight,
    gate_weight,
    group_weight,
    group_weight_other,
    delta_weight,
    inner_taps_hbm,
    inner_offset_hbm,
    small_hbm,
    small_other_hbm,
    inner_hbm,
    group_hbm,
    group_other_hbm,
    scan_hbm,
    *refs,
):
    (
        plan,
        gated,
        group_weights,
        inner_raw,
        both,
        inner_moved,
        group_moved,
        gate_moved,
        delta_moved,
        decay_moved,
        scan_next,
        receive,
        own,
        other,
        wide,
        tall,
        delta_row,
        inner_taps,
        inner_offset,
        small,
        small_other,
        inner,
        group,
        group_other,
        scan,
        inverse,
        gate,
        delta,
        decay,
        driven,
        skipped,
        sums,
        maps_in,
        ordered,
        done,
        sem,
        load_sem,
    ) = refs[-37:]
    taps, slots, _ = inner.shape
    rows, half = own.shape
    steps = rows // slots
    moving = slots // 2
    moved_rows = inner_moved.shape[0] // steps
    width = group.shape[2]
    head = lax.axis_index("head")

    def band(place):
        return tall.at[pl.ds(pl.multiple_of(place * width, width), width)]

    pairs = [
        (receive_hbm, receive),
        (delta_weight, delta_row),
        (own_hbm, own),
        (inner_weight, wide.at[:, pl.ds(0, LANES)]),
        (gate_weight, wide.at[:, pl.ds(LANES, LANES)]),
        (other_hbm, other),
        (group_weight, band(head)),
        (group_weight_other, band(1 - head)),
        (inner_taps_hbm, inner_taps),
        (inner_offset_hbm, inner_offset),
        (small_hbm, small),
        (small_other_hbm, small_other),
        (inner_hbm, inner),
        (group_hbm, group),
        (group_other_hbm, group_other),
        (scan_hbm, scan),
    ]
    loads = [
        pltpu.make_async_copy(source, target, load_sem.at[place])
        for place, (source, target) in enumerate(pairs)
    ]
    for load in loads:
        load.start()
    loads[0].wait()
    make_plan(replicas, cap, receive, slots, plan, inverse)
    loads[1].wait()
    first = 2 * width
    tall[first:, :] = jnp.broadcast_to(delta_row[...], (tall.shape[0] - first, 2 * half))
    for load in loads[2:]:
        load.wait()
    mine = pl.ds(pl.multiple_of(head * half, half), half)
    theirs = pl.ds(pl.multiple_of((1 - head) * half, half), half)
    flat = jnp.dot(own[...], wide[mine, :], preferred_element_type=F32) + jnp.dot(
        other[...], wide[theirs, :], preferred_element_type=F32
    )

    def across(tokens, part):
        return lax.dot_general(
            tokens, tall[:, part], (((1,), (1,)), ((), ())), preferred_element_type=F32
        )

    deep = across(own[...], mine) + across(other[...], theirs)
    inner_raw[...] = rounded(flat[:, :LANES])
    gate[...] = silu(rounded(flat[:, LANES:]))
    both[...] = rounded(deep[:, :first])
    count = taps + 2

    def full_row(number):
        value = small[count + number : count + number + 1, :]
        return jnp.concatenate([value, value], axis=1)

    decay_log, delta_bias, skip_gain = (full_row(number) for number in range(3))
    shifted = rounded(jnp.broadcast_to(deep[:, first : first + 1], (rows, LANES))) + delta_bias
    rate = jnp.maximum(shifted, 0.0) + jnp.log1p(jnp.exp(-jnp.abs(shifted)))
    delta[...] = rate
    decay[...] = jnp.exp(-rate * jnp.exp(decay_log))
    group_weights[:count, :] = both_halves(small[:count, :], small_other[:count, :])
    group_weights[count : count + 1, :] = skip_gain
    live = small[count + 3, 0].astype(jnp.int32)
    plan[0, plan.shape[1] - 1] = live

    def parts(ref):
        return [ref[step * slots : (step + 1) * slots, :] for step in range(steps)]

    inner_conv = convolve(
        [inner[tap].astype(F32) for tap in range(taps)],
        parts(inner_raw),
        inner_taps[...],
        inner_offset[...],
    )
    group_conv = convolve(
        [both_halves(group[tap].astype(F32), group_other[tap].astype(F32)) for tap in range(taps)],
        parts(both),
        group_weights[: taps + 1, :],
        group_weights[taps + 1 : taps + 2, :],
    )
    for step in range(steps):
        part = slice(step * slots, (step + 1) * slots)
        driven[part, :] = delta[part, :] * inner_conv[step]
        skipped[part, :] = inner_conv[step] * skip_gain
        maps_in[part, :] = group_conv[step]
    sums[...] = jnp.zeros_like(sums)
    stride = ordered.shape[0] // steps
    ordered[...] = jnp.zeros_like(ordered)
    for position in range(moving):
        slot = plan[0, position]
        for step in range(steps):
            ordered[step * stride + position : step * stride + position + 1, :] = maps_in[
                pl.ds(step * slots + slot, 1), :
            ]
    maps = [ordered[first : first + LANES].T for first in range(0, ordered.shape[0], LANES)]
    copies = []
    for position in range(moving):
        slot = plan[0, position]
        result = advance_slot(
            scan[slot],
            [pl.ds(step * slots + slot, 1) for step in range(steps)],
            driven,
            decay,
            sums,
            maps,
            [step * stride + position for step in range(steps)],
        )
        done[position] = jnp.where(slot < live, result, jnp.zeros_like(result))
        copies.append(
            pltpu.make_async_copy(done.at[position], scan_next.at[slot], sem.at[position])
        )
        copies[-1].start()
    gated[...] = (sums[...] + skipped[...]) * gate[...]
    pairs = (
        (inner_raw, inner_moved),
        (both, group_moved),
        (gate, gate_moved),
        (delta, delta_moved),
        (decay, decay_moved),
    )
    for _, target in pairs:
        target[...] = jnp.zeros_like(target)
    for block in range(moved_rows // ROWS):

        @pl.when(plan[0, moving + block * cap] >= 0)
        def _():
            for c in range(cap):
                slot = plan[0, moving + block * cap + c]
                for step in range(steps):
                    row = step * moved_rows + block * ROWS + c
                    for source, target in pairs:
                        target[row : row + 1, :] = source[pl.ds(step * slots + slot, 1), :]

    for copy in copies:
        copy.wait()


def stay(replicas, cap, operands):
    scalars, arrays = operands[:1], operands[1:]
    own, inner_weight, group_weight, delta_weight = arrays[0], arrays[2], arrays[4], arrays[6]
    inner, scan = arrays[-4], arrays[-1]
    taps, slots, _ = inner.shape
    rows = own.shape[0]
    steps = rows // slots
    moving = slots // 2
    blocks = len(sources_of(replicas))
    moved_rows = blocks * ROWS
    width, features = group_weight.shape
    full = jax.ShapeDtypeStruct((rows, LANES), F32)
    moved = jax.ShapeDtypeStruct((steps * moved_rows, LANES), F32)

    def like(value):
        return pltpu.VMEM(value.shape, value.dtype)

    return pl.pallas_call(
        functools.partial(stay_kernel, replicas, cap),
        out_shape=[
            jax.ShapeDtypeStruct((1, round_up(moving + blocks * cap + 1, LANES)), jnp.int32),
            full,
            jax.ShapeDtypeStruct((round_up(taps + 3, ROWS), LANES), F32),
            full,
            full,
        ]
        + [moved] * 5
        + [jax.ShapeDtypeStruct(scan.shape, BF16)],
        in_specs=[HBM] * len(operands),
        out_specs=[SMEM] + [VMEM] * 9 + [HBM],
        scratch_shapes=[pltpu.SMEM(value.shape, value.dtype) for value in scalars]
        + [
            like(own),
            like(own),
            pltpu.VMEM((features, 2 * LANES), BF16),
            pltpu.VMEM((2 * width + 2 * ROWS, features), BF16),
            like(delta_weight),
        ]
        + [like(value) for value in arrays[7:]]
        + [pltpu.SMEM((replicas * cap + 1,), jnp.int32)]
        + [pltpu.VMEM((rows, LANES), F32)] * 7
        + [
            pltpu.VMEM((round_up(rows, LANES), LANES), F32),
            pltpu.VMEM((moving,) + scan.shape[1:], BF16),
            pltpu.SemaphoreType.DMA((moving,)),
            pltpu.SemaphoreType.DMA((16,)),
        ],
        compiler_params=pltpu.CompilerParams(vmem_limit_bytes=MEDIUM_LIMIT),
        cost_estimate=pl.CostEstimate(
            flops=300_000_000, bytes_accessed=6_000_000, transcendentals=100_000
        ),
        name="advance_staying",
    )(*operands)


def arrive_kernel(
    replicas,
    cap,
    plan_hbm,
    gated_in,
    group_weights,
    inner_moved,
    group_moved,
    gate_moved,
    delta_moved,
    decay_moved,
    inner_raw,
    both,
    inner_taps,
    inner_offset,
    inner,
    group,
    scan_in,
    *refs,
):
    del scan_in
    arrived = refs[:-16]
    gated_out, inner_next, group_next, scan_next, plan = refs[-16:-11]
    (driven, sums, ordered, table, gated, gated_cast, inner_out, group_out) = refs[-11:-3]
    done, sem, out_sem = refs[-3:]
    taps, slots, _ = inner.shape
    moving = slots // 2
    state_rows = scan_next.shape[1]
    steps = inner_raw.shape[0] // slots
    width = group.shape[2]
    head = lax.axis_index("head")
    load = pltpu.make_async_copy(plan_hbm, plan, out_sem.at[0])
    load.start()
    if rounds_of(replicas):
        blocks = [ref.at[0] for ref in arrived]
    else:
        blocks = [arrived[0].at[source] for source in range(replicas)]
    moved_rows = len(blocks) * ROWS

    kinds = [[] for _ in range(2 * taps)]
    for ref in blocks:
        block = ref[cap * state_rows :, :].astype(F32)
        for kind in range(2 * taps):
            kinds[kind].append(block[kind * ROWS : (kind + 1) * ROWS])
    windows = [jnp.concatenate(kind, axis=0) for kind in kinds]

    def parts(ref):
        return [ref[step * moved_rows : (step + 1) * moved_rows, :] for step in range(steps)]

    inner_conv = convolve(
        windows[:taps], parts(inner_moved), inner_taps[...], inner_offset[...]
    )
    group_conv = convolve(
        windows[taps:],
        parts(group_moved),
        group_weights[: taps + 1, :],
        group_weights[taps + 1 : taps + 2, :],
    )
    for step, delta in enumerate(parts(delta_moved)):
        driven[step * moved_rows : (step + 1) * moved_rows, :] = delta * inner_conv[step]
    stride = ordered.shape[0] // steps
    maps = transposed(group_conv, ordered, stride)
    sums[...] = jnp.zeros_like(sums)
    load.wait()
    live = plan[0, plan.shape[1] - 1]

    def each(act):
        for block in range(len(blocks)):

            @pl.when(plan[0, moving + block * cap] >= 0)
            def _():
                for c in range(cap):
                    act(block, c, plan[0, moving + block * cap + c])

    def store(block, c, slot):
        place = block * cap + c
        return pltpu.make_async_copy(done.at[place], scan_next.at[slot], sem.at[place])

    def advance(block, c, slot):
        place = block * ROWS + c
        result = advance_slot(
            blocks[block][c * state_rows : (c + 1) * state_rows, :],
            [
                slice(step * moved_rows + place, step * moved_rows + place + 1)
                for step in range(steps)
            ],
            driven,
            decay_moved,
            sums,
            maps,
            [step * stride + place for step in range(steps)],
        )
        done[block * cap + c] = jnp.where(slot < live, result, jnp.zeros_like(result))
        store(block, c, slot).start()

    each(advance)
    living = lax.broadcasted_iota(jnp.int32, (slots, LANES), 0) < live
    for step in range(steps):
        part = slice(step * slots, (step + 1) * slots)
        tap = taps - steps + step
        inner_out[tap] = jnp.where(living, inner_raw[part, :], 0.0).astype(BF16)
        raw = jnp.where(head == 0, both[part, :width], both[part, width:])
        group_out[tap] = jnp.where(living[:, :width], raw, 0.0).astype(BF16)
    table[:, :LANES] = inner[steps].astype(F32)
    group_own = group[steps].astype(F32)
    table[:, LANES:] = jnp.concatenate([group_own, group_own], axis=1)
    gated[...] = gated_in[...]
    for step in range(steps):
        part = slice(step * moved_rows, (step + 1) * moved_rows)
        skipped = inner_conv[step] * group_weights[taps + 2 : taps + 3, :]
        sums[part, :] = (sums[part, :] + skipped) * gate_moved[part, :]
    driven[:moved_rows, :] = windows[steps]
    driven[moved_rows : 2 * moved_rows, :] = windows[taps + steps]

    def scatter(block, c, slot):
        place = block * ROWS + c
        for step in range(steps):
            row = step * moved_rows + place
            gated[pl.ds(step * slots + slot, 1), :] = sums[row : row + 1, :]
        table[pl.ds(slot, 1), :] = jnp.concatenate(
            [driven[place : place + 1, :], driven[moved_rows + place : moved_rows + place + 1, :]],
            axis=1,
        )

    each(scatter)
    for step in range(steps):
        part = slice(step * slots, (step + 1) * slots)
        gated_cast[step] = jnp.where(living, gated[part, :], 0.0).astype(BF16)
    inner_out[0] = jnp.where(living, table[:, :LANES], 0.0).astype(BF16)
    carried = jnp.where(head == 0, table[:, LANES : LANES + width], table[:, LANES + width :])
    group_out[0] = jnp.where(living[:, :width], carried, 0.0).astype(BF16)
    copies = [
        pltpu.make_async_copy(source, target, out_sem.at[place])
        for place, (source, target) in enumerate(
            [(inner_out, inner_next), (gated_cast, gated_out), (group_out, group_next)]
        )
    ]
    for copy in copies:
        copy.start()
    each(lambda block, c, slot: store(block, c, slot).wait())
    for copy in copies:
        copy.wait()


def arrive(replicas, cap, plan, operands, scan_next, arrived):
    inner_moved, inner_raw, inner, group = operands[2], operands[7], operands[-2], operands[-1]
    taps, slots, _ = inner.shape
    rows = inner_raw.shape[0]
    steps = rows // slots
    places = len(sources_of(replicas)) * cap
    gated = jax.ShapeDtypeStruct((steps, slots, LANES), BF16)
    limit = SMALL_LIMIT if rounds_of(replicas) else LARGE_LIMIT
    return pl.pallas_call(
        functools.partial(arrive_kernel, replicas, cap),
        out_shape=[
            gated,
            jax.ShapeDtypeStruct(inner.shape, BF16),
            jax.ShapeDtypeStruct(group.shape, BF16),
            jax.ShapeDtypeStruct(scan_next.shape, BF16),
        ],
        in_specs=[HBM] + [VMEM] * len(operands) + [HBM] + [VMEM] * len(arrived),
        out_specs=[HBM] * 4,
        scratch_shapes=[
            pltpu.SMEM(plan.shape, plan.dtype),
            pltpu.VMEM(inner_moved.shape, F32),
            pltpu.VMEM(inner_moved.shape, F32),
            pltpu.VMEM((round_up(inner_moved.shape[0], LANES), LANES), F32),
            pltpu.VMEM((slots, 2 * LANES), F32),
            pltpu.VMEM((rows, LANES), F32),
            pltpu.VMEM(gated.shape, BF16),
            pltpu.VMEM(inner.shape, BF16),
            pltpu.VMEM(group.shape, BF16),
            pltpu.VMEM((places,) + scan_next.shape[1:], BF16),
            pltpu.SemaphoreType.DMA((places,)),
            pltpu.SemaphoreType.DMA((3,)),
        ],
        input_output_aliases={1 + len(operands): 3},
        compiler_params=pltpu.CompilerParams(vmem_limit_bytes=limit),
        cost_estimate=pl.CostEstimate(
            flops=10_000_000, bytes_accessed=2_000_000, transcendentals=0
        ),
        name="advance_arrived",
    )(plan, *operands, scan_next, *arrived)


def swap_heads(value):
    return lax.ppermute(value, "head", [(0, 1), (1, 0)])


def exchange(replicas, blocks):
    rounds = rounds_of(replicas)
    if not rounds:
        return [lax.all_to_all(blocks[0], "dp", 0, 0, tiled=True)]
    return [
        lax.ppermute(block, "dp", [(source, source ^ mask) for source in range(replicas)])
        for mask, block in zip(rounds, blocks)
    ]


def per_device(
    replicas,
    tokens,
    inner_weight,
    gate_weight,
    group_weight,
    delta_weight,
    inner_taps,
    inner_offset,
    group_taps,
    group_offset,
    decay_log,
    delta_bias,
    skip_gain,
    inner_window,
    group_window,
    scan_state,
    send_list,
    receive_list,
    live_count,
):
    steps, slots, half = tokens.shape
    cap = send_list.shape[1] // replicas
    scan = jnp.transpose(scan_state, (0, 2, 1))
    inner = jnp.transpose(inner_window, (1, 0, 2))
    group = jnp.transpose(group_window, (1, 0, 2))
    own = tokens.reshape(steps * slots, half)

    group_weight = group_weight.T
    inner_offset = inner_offset[None]
    numbers = jnp.concatenate([decay_log, delta_bias, skip_gain, live_count.astype(F32)])
    numbers = jnp.broadcast_to(numbers[:, None], (numbers.shape[0], group_taps.shape[1]))
    small = jnp.concatenate([group_taps, group_offset[None], numbers], axis=0)
    group_other = swap_heads(group)
    swapped = [swap_heads(value) for value in (own, group_weight, small)]
    blocks = pack(replicas, cap, send_list, scan, inner, group, group_other, swapped)
    arrived = exchange(replicas, blocks)
    plan, gated, group_weights, inner_raw, both, *moved, scan_next = stay(
        replicas,
        cap,
        (
            receive_list,
            own,
            swapped[0],
            inner_weight,
            gate_weight,
            group_weight,
            swapped[1],
            delta_weight.T,
            inner_taps,
            inner_offset,
            small,
            swapped[2],
            inner,
            group,
            group_other,
            scan,
        ),
    )
    gated, inner_next, group_next, scan_next = arrive(
        replicas,
        cap,
        plan,
        (gated, group_weights, *moved, inner_raw, both, inner_taps, inner_offset, inner, group),
        scan_next,
        arrived,
    )
    return (
        gated,
        jnp.transpose(inner_next, (1, 0, 2)),
        jnp.transpose(group_next, (1, 0, 2)),
        jnp.transpose(scan_next, (0, 2, 1)),
    )


def solution(mesh):
    in_specs = (
        P(None, ("grp", "dp"), "head"),
        P(None, "head"),
        P(None, "head"),
        P(None, "head"),
        P(None, "head"),
        P(None, "head"),
        P("head"),
        P(None, "head"),
        P("head"),
        P("head"),
        P("head"),
        P("head"),
        P(("grp", "dp"), None, "head"),
        P(("grp", "dp"), None, "head"),
        P(("grp", "dp"), "head", None),
        P(("grp", "dp"), None),
        P(("grp", "dp"), None),
        P(("grp", "dp")),
    )
    out_specs = (
        P(None, ("grp", "dp"), "head"),
        P(("grp", "dp"), None, "head"),
        P(("grp", "dp"), None, "head"),
        P(("grp", "dp"), "head", None),
    )
    return jax.shard_map(
        functools.partial(per_device, mesh.shape["dp"]),
        mesh=mesh,
        in_specs=in_specs,
        out_specs=out_specs,
        check_vma=False,
    )
```

```python
import functools

import jax
import jax.numpy as jnp
from jax import lax
from jax.experimental import pallas as pl
from jax.experimental.pallas import tpu as pltpu
from jax.sharding import PartitionSpec as P

F32 = jnp.float32
BF16 = jnp.bfloat16
SMALL_LIMIT = 8 * 1024 * 1024
MEDIUM_LIMIT = 16 * 1024 * 1024
LARGE_LIMIT = 48 * 1024 * 1024
MAX_ROUNDS = 16
EARLIER = 3
LANES = 128
ROWS = 8
MAX_SETS = 64

VMEM = pl.BlockSpec(memory_space=pltpu.VMEM)
SMEM = pl.BlockSpec(memory_space=pltpu.SMEM)
HBM = pl.BlockSpec(memory_space=pl.ANY)


def in_hbm(value):
    return pltpu.with_memory_space_constraint(value, pltpu.HBM)


def round_up(value, step):
    return -(-value // step) * step


def silu(value):
    return value * jax.nn.sigmoid(value)


def rounded(value):
    return value.astype(BF16).astype(F32)


def rounds_of(replicas):
    if replicas > MAX_ROUNDS or replicas & (replicas - 1):
        return []
    light = list(range(1, replicas // 2))
    heavy = list(range(replicas // 2, replicas))
    return heavy[:1] + light[:2] + heavy[1:] + light[2:]


def partner(replicas, mask):
    return jnp.bitwise_xor(lax.axis_index("dp"), mask)


def both_halves(mine, theirs):
    first = lax.axis_index("head") == 0
    return jnp.concatenate(
        [jnp.where(first, mine, theirs), jnp.where(first, theirs, mine)], axis=-1
    )


def pack_kernel(replicas, cap, scan, send, inner, group, group_other, *refs):
    rounds = rounds_of(replicas)
    count = max(1, len(rounds))
    outs = refs[-8 - count : -8]
    indices, inner_in, group_in, table, picked, load_sem, list_sem, sem = refs[-8:]
    load_list = pltpu.make_async_copy(send, indices, list_sem)
    load_list.start()
    loads = [
        pltpu.make_async_copy(source, target, load_sem.at[place])
        for place, (source, target) in enumerate([(inner, inner_in), (group, group_in)])
    ]
    for load in loads:
        load.start()
    state_rows = scan.shape[1]
    if rounds:
        blocks = [(ref.at[0], partner(replicas, mask)) for ref, mask in zip(outs, rounds)]
    else:
        blocks = [(outs[0].at[target], target) for target in range(replicas)]
    load_list.wait()

    plan = []
    for block, (ref, target) in enumerate(blocks):
        for c in range(cap):
            plan.append((block, ref, c, indices[0, target * cap + c]))

    def each(act):
        for place, (_, ref, c, index) in enumerate(plan):

            @pl.when(index >= 0)
            def _():
                act(
                    pltpu.make_async_copy(
                        scan.at[index],
                        ref.at[pl.ds(c * state_rows, state_rows)],
                        sem.at[place],
                    )
                )

    each(lambda copy: copy.start())
    for load in loads:
        load.wait()
    taps = inner_in.shape[0]
    for tap in range(taps):
        table[:, tap * LANES : (tap + 1) * LANES] = inner_in[tap].astype(F32)
        table[:, (taps + tap) * LANES : (taps + tap + 1) * LANES] = both_halves(
            group_in[tap].astype(F32), group_other[tap].astype(F32)
        )
    picked[...] = jnp.zeros_like(picked)
    for block, _, c, index in plan:
        row = table[pl.ds(jnp.maximum(index, 0), 1), :]
        for kind in range(2 * taps):
            picked[block, kind * ROWS + c : kind * ROWS + c + 1, :] = row[
                :, kind * LANES : (kind + 1) * LANES
            ]
    for block, (ref, _) in enumerate(blocks):
        ref[cap * state_rows :, :] = picked[block].astype(BF16)
    each(lambda copy: copy.wait())


def pack(replicas, cap, send_list, scan, inner, group, group_other, swapped):
    rounds = rounds_of(replicas)
    count = max(1, len(rounds))
    per_block = 1 if rounds else replicas
    taps, slots, _ = inner.shape
    window_rows = 2 * taps * ROWS
    rows = cap * scan.shape[1] + window_rows
    blocks = count * per_block
    return pl.pallas_call(
        functools.partial(pack_kernel, replicas, cap),
        out_shape=[pltpu.VMEM((per_block, rows, LANES), BF16)] * count,
        in_specs=[HBM] * 4 + [VMEM] + [HBM] * len(swapped),
        out_specs=[VMEM] * count,
        scratch_shapes=[
            pltpu.SMEM(send_list.shape, jnp.int32),
            pltpu.VMEM(inner.shape, BF16),
            pltpu.VMEM(group.shape, BF16),
            pltpu.VMEM((slots, 2 * taps * LANES), F32),
            pltpu.VMEM((blocks, window_rows, LANES), F32),
            pltpu.SemaphoreType.DMA((2,)),
            pltpu.SemaphoreType.DMA,
            pltpu.SemaphoreType.DMA((blocks * cap,)),
        ],
        compiler_params=pltpu.CompilerParams(vmem_limit_bytes=SMALL_LIMIT),
        cost_estimate=pl.CostEstimate(flops=0, bytes_accessed=2_000_000, transcendentals=0),
        name="pack_leaving",
    )(in_hbm(scan), in_hbm(send_list), in_hbm(inner), in_hbm(group), group_other, *swapped)


def sources_of(replicas):
    rounds = rounds_of(replicas)
    if rounds:
        return [partner(replicas, mask) for mask in rounds]
    return list(range(replicas))


def make_plan(replicas, cap, receive, slots, plan, inverse):
    moving = slots // 2
    kept = 0
    for entry in range(replicas * cap):
        inverse[entry] = -1
    for slot in range(slots):
        entry = receive[0, slot]
        stays = entry < 0
        plan[0, jnp.where(stays, kept, moving)] = slot
        inverse[jnp.where(stays, replicas * cap, entry)] = slot
        kept = kept + jnp.where(stays, 1, 0)
    for block, source in enumerate(sources_of(replicas)):
        for c in range(cap):
            plan[0, moving + block * cap + c] = inverse[source * cap + c]


def convolve(carried, raw, weights, offset):
    joined = carried + raw
    results = []
    for step in range(len(raw)):
        summed = offset
        for tap in range(len(carried) + 1):
            summed = summed + joined[step + tap] * weights[tap : tap + 1, :]
        results.append(rounded(silu(summed)))
    return results


def transposed(rows, scratch, stride):
    scratch[...] = jnp.zeros_like(scratch)
    for step, value in enumerate(rows):
        scratch[step * stride : step * stride + value.shape[0], :] = value
    return [scratch[first : first + LANES].T for first in range(0, scratch.shape[0], LANES)]


def advance_slot(state, rows, driven, decay, sums, maps, lanes):
    hidden = state.astype(F32)
    width = state.shape[0]
    for row, lane in zip(rows, lanes):
        piece = maps[lane // LANES]
        column = piece[:, lane % LANES : lane % LANES + 1]
        hidden = decay[row, :] * hidden + driven[row, :] * column[:width]
        sums[row, :] = jnp.sum(hidden * column[width:], axis=0, keepdims=True)
        result = hidden.astype(BF16)
        hidden = result.astype(F32)
    return result


def stay_kernel(
    replicas,
    cap,
    decay_log,
    delta_bias,
    skip_gain,
    live,
    receive_hbm,
    own_hbm,
    inner_weight,
    gate_weight,
    group_weight,
    delta_weight,
    inner_taps_hbm,
    inner_offset_hbm,
    inner_hbm,
    group_hbm,
    scan_hbm,
    other,
    group_weight_other,
    small,
    small_other,
    group_other,
    *refs,
):
    (
        plan_out,
        gated,
        group_weights,
        inner_raw,
        both,
        inner_moved,
        group_moved,
        gate_moved,
        delta_moved,
        decay_moved,
        scan_next,
        plan,
        receive,
        own,
        wide,
        tall,
        delta_row,
        inner_taps,
        inner_offset,
        inner,
        group,
        scan,
        inverse,
        gate,
        delta,
        decay,
        driven,
        skipped,
        sums,
        maps_in,
        ordered,
        done,
        sem,
        load_sem,
    ) = refs[-34:]
    taps, slots, _ = inner.shape
    rows, half = own.shape
    steps = rows // slots
    moving = slots // 2
    moved_rows = inner_moved.shape[0] // steps
    width = group.shape[2]
    head = lax.axis_index("head")

    def band(place):
        return tall.at[pl.ds(pl.multiple_of(place * width, width), width)]

    pairs = [
        (receive_hbm, receive),
        (delta_weight, delta_row),
        (own_hbm, own),
        (inner_weight, wide.at[:, pl.ds(0, LANES)]),
        (gate_weight, wide.at[:, pl.ds(LANES, LANES)]),
        (group_weight, band(head)),
        (group_weight_other, band(1 - head)),
        (inner_taps_hbm, inner_taps),
        (inner_offset_hbm, inner_offset),
        (inner_hbm, inner),
        (group_hbm, group),
        (scan_hbm, scan),
    ]
    loads = [
        pltpu.make_async_copy(source, target, load_sem.at[place])
        for place, (source, target) in enumerate(pairs)
    ]
    for load in loads:
        load.start()
    loads[0].wait()
    make_plan(replicas, cap, receive, slots, plan, inverse)
    loads[1].wait()
    first = 2 * width
    tall[first:, :] = jnp.broadcast_to(delta_row[...], (tall.shape[0] - first, 2 * half))
    for load in loads[2:]:
        load.wait()
    mine = pl.ds(pl.multiple_of(head * half, half), half)
    theirs = pl.ds(pl.multiple_of((1 - head) * half, half), half)
    flat = jnp.dot(own[...], wide[mine, :], preferred_element_type=F32) + jnp.dot(
        other[...], wide[theirs, :], preferred_element_type=F32
    )

    def across(tokens, part):
        return lax.dot_general(
            tokens, tall[:, part], (((1,), (1,)), ((), ())), preferred_element_type=F32
        )

    deep = across(own[...], mine) + across(other[...], theirs)
    inner_raw[...] = rounded(flat[:, :LANES])
    gate[...] = silu(rounded(flat[:, LANES:]))
    both[...] = rounded(deep[:, :first])
    shifted = rounded(jnp.broadcast_to(deep[:, first : first + 1], (rows, LANES)))
    shifted = shifted + delta_bias[0]
    rate = jnp.maximum(shifted, 0.0) + jnp.log1p(jnp.exp(-jnp.abs(shifted)))
    delta[...] = rate
    decay[...] = jnp.exp(-rate * jnp.exp(jnp.full((1, LANES), decay_log[0], F32)))
    count = taps + 2
    group_weights[:count, :] = both_halves(small[...], small_other[...])
    group_weights[count : count + 1, :] = jnp.full((1, LANES), skip_gain[0], F32)
    plan[0, plan.shape[1] - 1] = live[0]
    save_plan = pltpu.make_async_copy(plan, plan_out, load_sem.at[0])
    save_plan.start()

    def parts(ref):
        return [ref[step * slots : (step + 1) * slots, :] for step in range(steps)]

    inner_conv = convolve(
        [inner[tap].astype(F32) for tap in range(taps)],
        parts(inner_raw),
        inner_taps[...],
        inner_offset[...],
    )
    group_conv = convolve(
        [both_halves(group[tap].astype(F32), group_other[tap].astype(F32)) for tap in range(taps)],
        parts(both),
        group_weights[: taps + 1, :],
        group_weights[taps + 1 : taps + 2, :],
    )
    for step in range(steps):
        part = slice(step * slots, (step + 1) * slots)
        driven[part, :] = delta[part, :] * inner_conv[step]
        skipped[part, :] = inner_conv[step] * skip_gain[0]
        maps_in[part, :] = group_conv[step]
    sums[...] = jnp.zeros_like(sums)
    stride = ordered.shape[0] // steps
    ordered[...] = jnp.zeros_like(ordered)
    for position in range(moving):
        slot = plan[0, position]
        for step in range(steps):
            ordered[step * stride + position : step * stride + position + 1, :] = maps_in[
                pl.ds(step * slots + slot, 1), :
            ]
    maps = [ordered[first : first + LANES].T for first in range(0, ordered.shape[0], LANES)]
    copies = []
    for position in range(moving):
        slot = plan[0, position]
        result = advance_slot(
            scan[slot],
            [pl.ds(step * slots + slot, 1) for step in range(steps)],
            driven,
            decay,
            sums,
            maps,
            [step * stride + position for step in range(steps)],
        )
        done[position] = jnp.where(slot < live[0], result, jnp.zeros_like(result))
        copies.append(
            pltpu.make_async_copy(done.at[position], scan_next.at[slot], sem.at[position])
        )
        copies[-1].start()
    gated[...] = (sums[...] + skipped[...]) * gate[...]
    pairs = (
        (inner_raw, inner_moved),
        (both, group_moved),
        (gate, gate_moved),
        (delta, delta_moved),
        (decay, decay_moved),
    )
    for _, target in pairs:
        target[...] = jnp.zeros_like(target)
    for block in range(moved_rows // ROWS):

        @pl.when(plan[0, moving + block * cap] >= 0)
        def _():
            for c in range(cap):
                slot = plan[0, moving + block * cap + c]
                for step in range(steps):
                    row = step * moved_rows + block * ROWS + c
                    for source, target in pairs:
                        target[row : row + 1, :] = source[pl.ds(step * slots + slot, 1), :]

    for copy in copies:
        copy.wait()
    save_plan.wait()


def stay(replicas, cap, scalars, arrays, near, earlier):
    receive, own, group_weight, delta_weight = arrays[0], arrays[1], arrays[4], arrays[5]
    inner, scan = arrays[-3], arrays[-1]
    taps, slots, _ = inner.shape
    rows = own.shape[0]
    steps = rows // slots
    moving = slots // 2
    blocks = len(sources_of(replicas))
    moved_rows = blocks * ROWS
    width, features = group_weight.shape
    full = pltpu.VMEM((rows, LANES), F32)
    moved = pltpu.VMEM((steps * moved_rows, LANES), F32)
    plan_shape = (1, round_up(moving + blocks * cap + 1, LANES))

    def like(value):
        return pltpu.VMEM(value.shape, value.dtype)

    far = [in_hbm(value) for value in arrays]
    return pl.pallas_call(
        functools.partial(stay_kernel, replicas, cap),
        out_shape=[
            pltpu.VMEM(plan_shape, jnp.int32),
            full,
            pltpu.VMEM((round_up(taps + 3, ROWS), LANES), F32),
            full,
            full,
        ]
        + [moved] * 5
        + [jax.ShapeDtypeStruct(scan.shape, BF16)],
        in_specs=[SMEM] * len(scalars)
        + [HBM] * len(far)
        + [VMEM] * len(near)
        + [HBM] * len(earlier),
        out_specs=[VMEM] * 10 + [HBM],
        scratch_shapes=[
            pltpu.SMEM(plan_shape, jnp.int32),
            pltpu.SMEM(receive.shape, jnp.int32),
            like(own),
            pltpu.VMEM((features, 2 * LANES), BF16),
            pltpu.VMEM((2 * width + 2 * ROWS, features), BF16),
            like(delta_weight),
        ]
        + [like(value) for value in arrays[6:]]
        + [pltpu.SMEM((replicas * cap + 1,), jnp.int32)]
        + [pltpu.VMEM((rows, LANES), F32)] * 7
        + [
            pltpu.VMEM((round_up(rows, LANES), LANES), F32),
            pltpu.VMEM((moving,) + scan.shape[1:], BF16),
            pltpu.SemaphoreType.DMA((moving,)),
            pltpu.SemaphoreType.DMA((16,)),
        ],
        compiler_params=pltpu.CompilerParams(vmem_limit_bytes=MEDIUM_LIMIT),
        cost_estimate=pl.CostEstimate(
            flops=300_000_000, bytes_accessed=6_000_000, transcendentals=100_000
        ),
        name="advance_staying",
    )(*scalars, *far, *near, *earlier)


def arrive_kernel(
    replicas,
    cap,
    plan_hbm,
    gated_in,
    group_weights,
    inner_moved,
    group_moved,
    gate_moved,
    delta_moved,
    decay_moved,
    inner_raw,
    both,
    inner_taps,
    inner_offset,
    inner,
    group,
    scan_in,
    *refs,
):
    del scan_in
    arrived = refs[:-16]
    gated_out, inner_next, group_next, scan_next, plan = refs[-16:-11]
    (driven, sums, ordered, table, gated, gated_cast, inner_out, group_out) = refs[-11:-3]
    done, sem, out_sem = refs[-3:]
    taps, slots, _ = inner.shape
    moving = slots // 2
    state_rows = scan_next.shape[1]
    steps = inner_raw.shape[0] // slots
    width = group.shape[2]
    head = lax.axis_index("head")
    load = pltpu.make_async_copy(plan_hbm, plan, out_sem.at[0])
    load.start()
    if rounds_of(replicas):
        blocks = [ref.at[0] for ref in arrived]
    else:
        blocks = [arrived[0].at[source] for source in range(replicas)]
    moved_rows = len(blocks) * ROWS

    kinds = [[] for _ in range(2 * taps)]
    for ref in blocks:
        block = ref[cap * state_rows :, :].astype(F32)
        for kind in range(2 * taps):
            kinds[kind].append(block[kind * ROWS : (kind + 1) * ROWS])
    windows = [jnp.concatenate(kind, axis=0) for kind in kinds]

    def parts(ref):
        return [ref[step * moved_rows : (step + 1) * moved_rows, :] for step in range(steps)]

    inner_conv = convolve(
        windows[:taps], parts(inner_moved), inner_taps[...], inner_offset[...]
    )
    group_conv = convolve(
        windows[taps:],
        parts(group_moved),
        group_weights[: taps + 1, :],
        group_weights[taps + 1 : taps + 2, :],
    )
    for step, delta in enumerate(parts(delta_moved)):
        driven[step * moved_rows : (step + 1) * moved_rows, :] = delta * inner_conv[step]
    stride = ordered.shape[0] // steps
    maps = transposed(group_conv, ordered, stride)
    sums[...] = jnp.zeros_like(sums)
    load.wait()
    live = plan[0, plan.shape[1] - 1]

    def each(act):
        for block in range(len(blocks)):

            @pl.when(plan[0, moving + block * cap] >= 0)
            def _():
                for c in range(cap):
                    act(block, c, plan[0, moving + block * cap + c])

    def store(block, c, slot):
        place = block * cap + c
        return pltpu.make_async_copy(done.at[place], scan_next.at[slot], sem.at[place])

    def advance(block, c, slot):
        place = block * ROWS + c
        result = advance_slot(
            blocks[block][c * state_rows : (c + 1) * state_rows, :],
            [
                slice(step * moved_rows + place, step * moved_rows + place + 1)
                for step in range(steps)
            ],
            driven,
            decay_moved,
            sums,
            maps,
            [step * stride + place for step in range(steps)],
        )
        done[block * cap + c] = jnp.where(slot < live, result, jnp.zeros_like(result))
        store(block, c, slot).start()

    each(advance)
    living = lax.broadcasted_iota(jnp.int32, (slots, LANES), 0) < live
    for step in range(steps):
        part = slice(step * slots, (step + 1) * slots)
        tap = taps - steps + step
        inner_out[tap] = jnp.where(living, inner_raw[part, :], 0.0).astype(BF16)
        raw = jnp.where(head == 0, both[part, :width], both[part, width:])
        group_out[tap] = jnp.where(living[:, :width], raw, 0.0).astype(BF16)
    table[:, :LANES] = inner[steps].astype(F32)
    group_own = group[steps].astype(F32)
    table[:, LANES:] = jnp.concatenate([group_own, group_own], axis=1)
    gated[...] = gated_in[...]
    for step in range(steps):
        part = slice(step * moved_rows, (step + 1) * moved_rows)
        skipped = inner_conv[step] * group_weights[taps + 2 : taps + 3, :]
        sums[part, :] = (sums[part, :] + skipped) * gate_moved[part, :]
    driven[:moved_rows, :] = windows[steps]
    driven[moved_rows : 2 * moved_rows, :] = windows[taps + steps]

    def scatter(block, c, slot):
        place = block * ROWS + c
        for step in range(steps):
            row = step * moved_rows + place
            gated[pl.ds(step * slots + slot, 1), :] = sums[row : row + 1, :]
        table[pl.ds(slot, 1), :] = jnp.concatenate(
            [driven[place : place + 1, :], driven[moved_rows + place : moved_rows + place + 1, :]],
            axis=1,
        )

    each(scatter)
    for step in range(steps):
        part = slice(step * slots, (step + 1) * slots)
        gated_cast[step] = jnp.where(living, gated[part, :], 0.0).astype(BF16)
    inner_out[0] = jnp.where(living, table[:, :LANES], 0.0).astype(BF16)
    carried = jnp.where(head == 0, table[:, LANES : LANES + width], table[:, LANES + width :])
    group_out[0] = jnp.where(living[:, :width], carried, 0.0).astype(BF16)
    copies = [
        pltpu.make_async_copy(source, target, out_sem.at[place])
        for place, (source, target) in enumerate(
            [(inner_out, inner_next), (gated_cast, gated_out), (group_out, group_next)]
        )
    ]
    for copy in copies:
        copy.start()
    each(lambda block, c, slot: store(block, c, slot).wait())
    for copy in copies:
        copy.wait()


def arrive(replicas, cap, plan, operands, scan_next, arrived):
    inner_moved, inner_raw, inner, group = operands[2], operands[7], operands[-2], operands[-1]
    taps, slots, _ = inner.shape
    rows = inner_raw.shape[0]
    steps = rows // slots
    places = len(sources_of(replicas)) * cap
    gated = jax.ShapeDtypeStruct((steps, slots, LANES), BF16)
    limit = SMALL_LIMIT if rounds_of(replicas) else LARGE_LIMIT
    return pl.pallas_call(
        functools.partial(arrive_kernel, replicas, cap),
        out_shape=[
            gated,
            jax.ShapeDtypeStruct(inner.shape, BF16),
            jax.ShapeDtypeStruct(group.shape, BF16),
            jax.ShapeDtypeStruct(scan_next.shape, BF16),
        ],
        in_specs=[HBM] + [VMEM] * len(operands) + [HBM] + [VMEM] * len(arrived),
        out_specs=[HBM] * 4,
        scratch_shapes=[
            pltpu.SMEM(plan.shape, plan.dtype),
            pltpu.VMEM(inner_moved.shape, F32),
            pltpu.VMEM(inner_moved.shape, F32),
            pltpu.VMEM((round_up(inner_moved.shape[0], LANES), LANES), F32),
            pltpu.VMEM((slots, 2 * LANES), F32),
            pltpu.VMEM((rows, LANES), F32),
            pltpu.VMEM(gated.shape, BF16),
            pltpu.VMEM(inner.shape, BF16),
            pltpu.VMEM(group.shape, BF16),
            pltpu.VMEM((places,) + scan_next.shape[1:], BF16),
            pltpu.SemaphoreType.DMA((places,)),
            pltpu.SemaphoreType.DMA((3,)),
        ],
        input_output_aliases={1 + len(operands): 3},
        compiler_params=pltpu.CompilerParams(vmem_limit_bytes=limit),
        cost_estimate=pl.CostEstimate(
            flops=10_000_000, bytes_accessed=2_000_000, transcendentals=0
        ),
        name="advance_arrived",
    )(plan, *operands, scan_next, *arrived)


def swap_heads(value):
    return lax.ppermute(value, "head", [(0, 1), (1, 0)])


def exchange(replicas, blocks):
    rounds = rounds_of(replicas)
    if not rounds:
        return [lax.all_to_all(blocks[0], "dp", 0, 0, tiled=True)]
    return [
        lax.ppermute(block, "dp", [(source, source ^ mask) for source in range(replicas)])
        for mask, block in zip(rounds, blocks)
    ]


def per_device(
    replicas,
    tokens,
    inner_weight,
    gate_weight,
    group_weight,
    delta_weight,
    inner_taps,
    inner_offset,
    group_taps,
    group_offset,
    decay_log,
    delta_bias,
    skip_gain,
    inner_window,
    group_window,
    scan_state,
    send_list,
    receive_list,
    live_count,
):
    steps, slots, half = tokens.shape
    cap = send_list.shape[1] // replicas
    scan = jnp.transpose(scan_state, (0, 2, 1))
    inner = jnp.transpose(inner_window, (1, 0, 2))
    group = jnp.transpose(group_window, (1, 0, 2))
    own = tokens.reshape(steps * slots, half)

    group_weight = group_weight.T
    inner_offset = inner_offset[None]
    small = jnp.concatenate([group_taps, group_offset[None]], axis=0)
    group_other = swap_heads(group)
    swapped = [swap_heads(value) for value in (own, group_weight, small)]
    blocks = pack(replicas, cap, send_list, scan, inner, group, group_other, swapped)
    arrived = exchange(replicas, blocks)
    plan, gated, group_weights, inner_raw, both, *moved, scan_next = stay(
        replicas,
        cap,
        (decay_log, delta_bias, skip_gain, live_count),
        (
            receive_list,
            own,
            inner_weight,
            gate_weight,
            group_weight,
            delta_weight.T,
            inner_taps,
            inner_offset,
            inner,
            group,
            scan,
        ),
        (swapped[0], swapped[1], small, swapped[2], group_other),
        arrived[:EARLIER] if rounds_of(replicas) else [],
    )
    gated, inner_next, group_next, scan_next = arrive(
        replicas,
        cap,
        plan,
        (gated, group_weights, *moved, inner_raw, both, inner_taps, inner_offset, inner, group),
        scan_next,
        arrived,
    )
    return (
        gated,
        jnp.transpose(inner_next, (1, 0, 2)),
        jnp.transpose(group_next, (1, 0, 2)),
        jnp.transpose(scan_next, (0, 2, 1)),
    )


def solution(mesh):
    in_specs = (
        P(None, ("grp", "dp"), "head"),
        P(None, "head"),
        P(None, "head"),
        P(None, "head"),
        P(None, "head"),
        P(None, "head"),
        P("head"),
        P(None, "head"),
        P("head"),
        P("head"),
        P("head"),
        P("head"),
        P(("grp", "dp"), None, "head"),
        P(("grp", "dp"), None, "head"),
        P(("grp", "dp"), "head", None),
        P(("grp", "dp"), None),
        P(("grp", "dp"), None),
        P(("grp", "dp")),
    )
    out_specs = (
        P(None, ("grp", "dp"), "head"),
        P(("grp", "dp"), None, "head"),
        P(("grp", "dp"), None, "head"),
        P(("grp", "dp"), "head", None),
    )
    return jax.shard_map(
        functools.partial(per_device, mesh.shape["dp"]),
        mesh=mesh,
        in_specs=in_specs,
        out_specs=out_specs,
        check_vma=False,
    )
```

```python
import functools

import jax
import jax.numpy as jnp
from jax import lax
from jax.experimental import pallas as pl
from jax.experimental.pallas import tpu as pltpu
from jax.sharding import PartitionSpec as P

F32 = jnp.float32
BF16 = jnp.bfloat16
SMALL_LIMIT = 8 * 1024 * 1024
MEDIUM_LIMIT = 16 * 1024 * 1024
LARGE_LIMIT = 48 * 1024 * 1024
MAX_ROUNDS = 16
EARLIER = 3
LAST = 2
LANES = 128
ROWS = 8
MAX_SETS = 64

VMEM = pl.BlockSpec(memory_space=pltpu.VMEM)
SMEM = pl.BlockSpec(memory_space=pltpu.SMEM)
HBM = pl.BlockSpec(memory_space=pl.ANY)


def in_hbm(value):
    return pltpu.with_memory_space_constraint(value, pltpu.HBM)


def in_vmem(value):
    return pltpu.with_memory_space_constraint(value, pltpu.VMEM)


def round_up(value, step):
    return -(-value // step) * step


def silu(value):
    return value * jax.nn.sigmoid(value)


def rounded(value):
    return value.astype(BF16).astype(F32)


def rounds_of(replicas):
    if replicas > MAX_ROUNDS or replicas & (replicas - 1):
        return []
    light = list(range(1, replicas // 2))
    heavy = list(range(replicas // 2, replicas))
    return heavy[:1] + light[:2] + heavy[1:2] + light[2:] + heavy[2:]


def partner(replicas, mask):
    return jnp.bitwise_xor(lax.axis_index("dp"), mask)


def both_halves(mine, theirs):
    first = lax.axis_index("head") == 0
    return jnp.concatenate(
        [jnp.where(first, mine, theirs), jnp.where(first, theirs, mine)], axis=-1
    )


def destinations(replicas, outs):
    rounds = rounds_of(replicas)
    if rounds:
        return [(ref.at[0], partner(replicas, mask)) for ref, mask in zip(outs, rounds)]
    return [(outs[0].at[target], target) for target in range(replicas)]


def states_kernel(replicas, cap, scan, send, inner, group, *refs):
    outs, (picked, group_out, indices_out) = refs[:-11], refs[-11:-8]
    indices, inner_in, table, load_sem, group_sem, list_sem, save_sem, sem = refs[-8:]
    load_list = pltpu.make_async_copy(send, indices, list_sem)
    load_list.start()
    load = pltpu.make_async_copy(inner, inner_in, load_sem)
    load.start()
    load_group = pltpu.make_async_copy(group, group_out, group_sem)
    load_group.start()
    state_rows = scan.shape[1]
    blocks = destinations(replicas, outs)
    load_list.wait()
    save = pltpu.make_async_copy(indices, indices_out, save_sem)
    save.start()
    plan = []
    for block, (ref, target) in enumerate(blocks):
        for c in range(cap):
            plan.append((block, ref, c, indices[0, target * cap + c]))

    def each(act):
        for place, (_, ref, c, index) in enumerate(plan):

            @pl.when(index >= 0)
            def _():
                act(
                    pltpu.make_async_copy(
                        scan.at[index],
                        ref.at[pl.ds(c * state_rows, state_rows)],
                        sem.at[place],
                    )
                )

    each(lambda copy: copy.start())
    load.wait()
    taps = inner_in.shape[0]
    for tap in range(taps):
        table[:, tap * LANES : (tap + 1) * LANES] = inner_in[tap].astype(F32)
    picked[...] = jnp.zeros_like(picked)
    for block, _, c, index in plan:
        row = table[pl.ds(jnp.maximum(index, 0), 1), :]
        for tap in range(taps):
            picked[block, tap * ROWS + c : tap * ROWS + c + 1, :] = row[
                :, tap * LANES : (tap + 1) * LANES
            ]
    load_group.wait()
    save.wait()
    each(lambda copy: copy.wait())


def windows_kernel(replicas, cap, state_rows, indices_in, group, group_other, picked_in, *refs):
    count = max(1, len(rounds_of(replicas)))
    outs = refs[-4 - count : -4]
    indices, table, picked, sem = refs[-4:]
    load = pltpu.make_async_copy(indices_in, indices, sem)
    load.start()
    taps = group.shape[0]
    for tap in range(taps):
        table[:, tap * LANES : (tap + 1) * LANES] = both_halves(
            group[tap].astype(F32), group_other[tap].astype(F32)
        )
    picked[...] = jnp.zeros_like(picked)
    load.wait()
    for block, (ref, target) in enumerate(destinations(replicas, outs)):
        for c in range(cap):
            index = jnp.maximum(indices[0, target * cap + c], 0)
            row = table[pl.ds(index, 1), :]
            for tap in range(taps):
                picked[block, tap * ROWS + c : tap * ROWS + c + 1, :] = row[
                    :, tap * LANES : (tap + 1) * LANES
                ]
        ref[cap * state_rows :, :] = jnp.concatenate(
            [picked_in[block], picked[block]], axis=0
        ).astype(BF16)


def pack(replicas, cap, send_list, scan, inner, group, group_other, swapped):
    rounds = rounds_of(replicas)
    count = max(1, len(rounds))
    per_block = 1 if rounds else replicas
    taps, slots, _ = inner.shape
    rows = cap * scan.shape[1] + 2 * taps * ROWS
    blocks = count * per_block
    shapes = [pltpu.VMEM((per_block, rows, LANES), BF16)] * count
    half = (blocks, taps * ROWS, LANES)
    limit = SMALL_LIMIT if rounds else MEDIUM_LIMIT
    *states, picked, group_near, indices = pl.pallas_call(
        functools.partial(states_kernel, replicas, cap),
        out_shape=shapes
        + [
            pltpu.VMEM(half, F32),
            pltpu.VMEM(group.shape, BF16),
            pltpu.VMEM(send_list.shape, jnp.int32),
        ],
        in_specs=[HBM] * 4,
        out_specs=[VMEM] * (count + 3),
        scratch_shapes=[
            pltpu.SMEM(send_list.shape, jnp.int32),
            pltpu.VMEM(inner.shape, BF16),
            pltpu.VMEM((slots, taps * LANES), F32),
            pltpu.SemaphoreType.DMA,
            pltpu.SemaphoreType.DMA,
            pltpu.SemaphoreType.DMA,
            pltpu.SemaphoreType.DMA,
            pltpu.SemaphoreType.DMA((blocks * cap,)),
        ],
        compiler_params=pltpu.CompilerParams(vmem_limit_bytes=limit),
        cost_estimate=pl.CostEstimate(flops=0, bytes_accessed=2_000_000, transcendentals=0),
        name="pack_states",
    )(in_hbm(scan), in_hbm(send_list), in_hbm(inner), in_hbm(group))
    near = [in_vmem(value) for value in states]
    return pl.pallas_call(
        functools.partial(windows_kernel, replicas, cap, scan.shape[1]),
        out_shape=shapes,
        in_specs=[VMEM] * (4 + count) + [HBM] * len(swapped),
        out_specs=[VMEM] * count,
        scratch_shapes=[
            pltpu.SMEM(send_list.shape, jnp.int32),
            pltpu.VMEM((slots, taps * LANES), F32),
            pltpu.VMEM(half, F32),
            pltpu.SemaphoreType.DMA,
        ],
        input_output_aliases={4 + place: place for place in range(count)},
        compiler_params=pltpu.CompilerParams(vmem_limit_bytes=limit),
        cost_estimate=pl.CostEstimate(flops=0, bytes_accessed=500_000, transcendentals=0),
        name="pack_windows",
    )(indices, group_near, group_other, picked, *near, *swapped)


def sources_of(replicas):
    rounds = rounds_of(replicas)
    if rounds:
        return [partner(replicas, mask) for mask in rounds]
    return list(range(replicas))


def make_plan(replicas, cap, receive, slots, plan, inverse):
    moving = slots // 2
    kept = 0
    for entry in range(replicas * cap):
        inverse[entry] = -1
    for slot in range(slots):
        entry = receive[0, slot]
        stays = entry < 0
        plan[0, jnp.where(stays, kept, moving)] = slot
        inverse[jnp.where(stays, replicas * cap, entry)] = slot
        kept = kept + jnp.where(stays, 1, 0)
    for block, source in enumerate(sources_of(replicas)):
        for c in range(cap):
            plan[0, moving + block * cap + c] = inverse[source * cap + c]


def convolve(carried, raw, weights, offset):
    joined = carried + raw
    results = []
    for step in range(len(raw)):
        summed = offset
        for tap in range(len(carried) + 1):
            summed = summed + joined[step + tap] * weights[tap : tap + 1, :]
        results.append(rounded(silu(summed)))
    return results


def transposed(rows, scratch, stride):
    scratch[...] = jnp.zeros_like(scratch)
    for step, value in enumerate(rows):
        scratch[step * stride : step * stride + value.shape[0], :] = value
    return [scratch[first : first + LANES].T for first in range(0, scratch.shape[0], LANES)]


def advance_slot(state, rows, driven, decays, sums, maps, lanes):
    hidden = state.astype(F32)
    width = state.shape[0]
    for row, decay, lane in zip(rows, decays, lanes):
        piece = maps[lane // LANES]
        column = piece[:, lane % LANES : lane % LANES + 1]
        hidden = decay * hidden + driven[row, :] * column[:width]
        sums[row, :] = jnp.sum(hidden * column[width:], axis=0, keepdims=True)
        result = hidden.astype(BF16)
        hidden = result.astype(F32)
    return result


def stay_kernel(
    replicas,
    cap,
    decay_log,
    delta_bias,
    skip_gain,
    live,
    receive_hbm,
    own_hbm,
    inner_weight,
    gate_weight,
    group_weight,
    delta_weight,
    inner_taps_hbm,
    inner_offset_hbm,
    inner_hbm,
    group_hbm,
    scan_hbm,
    other,
    group_weight_other,
    small,
    small_other,
    group_other,
    *refs,
):
    (
        plan_out,
        gated,
        weights,
        base,
        inner_part,
        group_part,
        inner_moved,
        group_moved,
        gate_moved,
        delta_moved,
        decay_moved,
        scan_next,
        plan,
        receive,
        own,
        wide,
        tall,
        delta_row,
        inner_taps,
        inner_offset,
        inner,
        group,
        scan,
        inverse,
        inner_raw,
        both,
        gate,
        delta,
        decay,
        driven,
        skipped,
        sums,
        maps_in,
        ordered,
        done,
        sem,
        load_sem,
    ) = refs[-37:]
    taps, slots, _ = inner.shape
    rows, half = own.shape
    steps = rows // slots
    moving = slots // 2
    moved_rows = inner_moved.shape[0] // steps
    width = group.shape[2]
    head = lax.axis_index("head")

    def band(place):
        return tall.at[pl.ds(pl.multiple_of(place * width, width), width)]

    pairs = [
        (receive_hbm, receive),
        (delta_weight, delta_row),
        (own_hbm, own),
        (inner_weight, wide.at[:, pl.ds(0, LANES)]),
        (gate_weight, wide.at[:, pl.ds(LANES, LANES)]),
        (group_weight, band(head)),
        (group_weight_other, band(1 - head)),
        (inner_taps_hbm, inner_taps),
        (inner_offset_hbm, inner_offset),
        (inner_hbm, inner),
        (group_hbm, group),
        (scan_hbm, scan),
    ]
    loads = [
        pltpu.make_async_copy(source, target, load_sem.at[place])
        for place, (source, target) in enumerate(pairs)
    ]
    for load in loads:
        load.start()
    loads[0].wait()
    make_plan(replicas, cap, receive, slots, plan, inverse)
    loads[1].wait()
    first = 2 * width
    tall[first:, :] = jnp.broadcast_to(delta_row[...], (tall.shape[0] - first, 2 * half))
    for load in loads[2:]:
        load.wait()
    mine = pl.ds(pl.multiple_of(head * half, half), half)
    theirs = pl.ds(pl.multiple_of((1 - head) * half, half), half)
    flat = jnp.dot(own[...], wide[mine, :], preferred_element_type=F32) + jnp.dot(
        other[...], wide[theirs, :], preferred_element_type=F32
    )

    def across(tokens, part):
        return lax.dot_general(
            tokens, tall[:, part], (((1,), (1,)), ((), ())), preferred_element_type=F32
        )

    deep = across(own[...], mine) + across(other[...], theirs)
    inner_raw[...] = rounded(flat[:, :LANES])
    gate[...] = silu(rounded(flat[:, LANES:]))
    both[...] = rounded(deep[:, :first])
    shifted = rounded(jnp.broadcast_to(deep[:, first : first + 1], (rows, LANES)))
    shifted = shifted + delta_bias[0]
    rate = jnp.maximum(shifted, 0.0) + jnp.log1p(jnp.exp(-jnp.abs(shifted)))
    delta[...] = rate
    decay[...] = jnp.exp(-rate * jnp.exp(jnp.full((1, LANES), decay_log[0], F32)))
    count = taps + 2
    weights[:count, :] = both_halves(small[...], small_other[...])
    weights[count : count + 1, :] = jnp.full((1, LANES), skip_gain[0], F32)
    later = round_up(count + 1, ROWS)
    weights[later : later + taps + 1, :] = inner_taps[...]
    weights[later + taps + 1 : later + taps + 2, :] = inner_offset[...]
    plan[0, plan.shape[1] - 1] = live[0]
    save_plan = pltpu.make_async_copy(plan, plan_out, load_sem.at[0])
    save_plan.start()

    def parts(ref):
        return [ref[step * slots : (step + 1) * slots, :] for step in range(steps)]

    inner_conv = convolve(
        [inner[tap].astype(F32) for tap in range(taps)],
        parts(inner_raw),
        inner_taps[...],
        inner_offset[...],
    )
    group_conv = convolve(
        [both_halves(group[tap].astype(F32), group_other[tap].astype(F32)) for tap in range(taps)],
        parts(both),
        weights[: taps + 1, :],
        weights[taps + 1 : taps + 2, :],
    )
    for step in range(steps):
        part = slice(step * slots, (step + 1) * slots)
        driven[part, :] = delta[part, :] * inner_conv[step]
        skipped[part, :] = inner_conv[step] * skip_gain[0]
        maps_in[part, :] = group_conv[step]
    sums[...] = jnp.zeros_like(sums)
    stride = ordered.shape[0] // steps
    ordered[...] = jnp.zeros_like(ordered)
    for position in range(moving):
        slot = plan[0, position]
        for step in range(steps):
            ordered[step * stride + position : step * stride + position + 1, :] = maps_in[
                pl.ds(step * slots + slot, 1), :
            ]
    maps = [ordered[first : first + LANES].T for first in range(0, ordered.shape[0], LANES)]
    copies = []
    for position in range(moving):
        slot = plan[0, position]
        result = advance_slot(
            scan[slot],
            [pl.ds(step * slots + slot, 1) for step in range(steps)],
            driven,
            [decay[pl.ds(step * slots + slot, 1), :] for step in range(steps)],
            sums,
            maps,
            [step * stride + position for step in range(steps)],
        )
        done[position] = jnp.where(slot < live[0], result, jnp.zeros_like(result))
        copies.append(
            pltpu.make_async_copy(done.at[position], scan_next.at[slot], sem.at[position])
        )
        copies[-1].start()
    gated[...] = (sums[...] + skipped[...]) * gate[...]
    pairs = (
        (inner_raw, inner_moved),
        (both, group_moved),
        (gate, gate_moved),
        (delta, delta_moved),
        (decay, decay_moved),
    )
    for _, target in pairs:
        target[...] = jnp.zeros_like(target)
    living = lax.broadcasted_iota(jnp.int32, (slots, LANES), 0) < live[0]
    for step in range(steps):
        part = slice(step * slots, (step + 1) * slots)
        inner_part[step] = jnp.where(living, inner_raw[part, :], 0.0).astype(BF16)
        raw = jnp.where(head == 0, both[part, :width], both[part, width:])
        group_part[step] = jnp.where(living[:, :width], raw, 0.0).astype(BF16)
    base[:, :LANES] = inner[steps].astype(F32)
    group_own = group[steps].astype(F32)
    base[:, LANES:] = jnp.concatenate([group_own, group_own], axis=1)
    for block in range(moved_rows // ROWS):

        @pl.when(plan[0, moving + block * cap] >= 0)
        def _():
            for c in range(cap):
                slot = plan[0, moving + block * cap + c]
                for step in range(steps):
                    row = step * moved_rows + block * ROWS + c
                    for source, target in pairs:
                        target[row : row + 1, :] = source[pl.ds(step * slots + slot, 1), :]

    for copy in copies:
        copy.wait()
    save_plan.wait()


def stay(replicas, cap, scalars, arrays, near, earlier):
    receive, own, group_weight, delta_weight = arrays[0], arrays[1], arrays[4], arrays[5]
    inner, scan = arrays[-3], arrays[-1]
    taps, slots, _ = inner.shape
    rows = own.shape[0]
    steps = rows // slots
    moving = slots // 2
    blocks = len(sources_of(replicas))
    moved_rows = blocks * ROWS
    width, features = group_weight.shape
    full = pltpu.VMEM((rows, LANES), F32)
    moved = pltpu.VMEM((steps * moved_rows, LANES), F32)
    plan_shape = (1, round_up(moving + blocks * cap + 1, LANES))

    def like(value):
        return pltpu.VMEM(value.shape, value.dtype)

    far = [in_hbm(value) for value in arrays]
    return pl.pallas_call(
        functools.partial(stay_kernel, replicas, cap),
        out_shape=[
            pltpu.VMEM(plan_shape, jnp.int32),
            full,
            pltpu.VMEM((2 * round_up(taps + 3, ROWS), LANES), F32),
            pltpu.VMEM((slots, 2 * LANES), F32),
            pltpu.VMEM((steps, slots, LANES), BF16),
            pltpu.VMEM((steps, slots, width), BF16),
        ]
        + [moved] * 5
        + [jax.ShapeDtypeStruct(scan.shape, BF16)],
        in_specs=[SMEM] * len(scalars)
        + [HBM] * len(far)
        + [VMEM] * len(near)
        + [HBM] * len(earlier),
        out_specs=[VMEM] * 11 + [HBM],
        scratch_shapes=[
            pltpu.SMEM(plan_shape, jnp.int32),
            pltpu.SMEM(receive.shape, jnp.int32),
            like(own),
            pltpu.VMEM((features, 2 * LANES), BF16),
            pltpu.VMEM((2 * width + 2 * ROWS, features), BF16),
            like(delta_weight),
        ]
        + [like(value) for value in arrays[6:]]
        + [pltpu.SMEM((replicas * cap + 1,), jnp.int32)]
        + [pltpu.VMEM((rows, LANES), F32)] * 9
        + [
            pltpu.VMEM((round_up(rows, LANES), LANES), F32),
            pltpu.VMEM((moving,) + scan.shape[1:], BF16),
            pltpu.SemaphoreType.DMA((moving,)),
            pltpu.SemaphoreType.DMA((16,)),
        ],
        compiler_params=pltpu.CompilerParams(vmem_limit_bytes=MEDIUM_LIMIT),
        cost_estimate=pl.CostEstimate(
            flops=300_000_000, bytes_accessed=6_000_000, transcendentals=100_000
        ),
        name="advance_staying",
    )(*scalars, *far, *near, *earlier)


def arrive_kernel(
    replicas,
    cap,
    first,
    last,
    plan_near,
    weights,
    inner_moved,
    group_moved,
    gate_moved,
    delta_moved,
    decay_moved,
    gated_in,
    table_in,
    inner_part,
    group_part,
    scan_in,
    *refs,
):
    del scan_in
    if last:
        arrived = refs[:-15]
        gated_out, inner_next, group_next, scan_next = refs[-15:-11]
        gated, table = refs[-11:-9]
        gated_cast, inner_cast, group_cast = refs[-9:-6]
    else:
        arrived = refs[:-9]
        gated, table, scan_next = refs[-9:-6]
    plan, driven, sums, ordered, done, sem = refs[-6:]
    steps, slots, width = group_part.shape
    taps = steps + 1
    moving = slots // 2
    state_rows = scan_next.shape[1]
    head = lax.axis_index("head")
    load = pltpu.make_async_copy(plan_near, plan, sem.at[0])
    load.start()
    if rounds_of(replicas):
        blocks = [ref.at[0] for ref in arrived]
    else:
        blocks = [arrived[0].at[source] for source in range(replicas)]
    stored = inner_moved.shape[0] // steps
    moved_rows = len(blocks) * ROWS
    if last:
        copies = [
            pltpu.make_async_copy(source, target, sem.at[1 + place])
            for place, (source, target) in enumerate(
                [
                    (inner_part, inner_next.at[pl.ds(1, steps)]),
                    (group_part, group_next.at[pl.ds(1, steps)]),
                ]
            )
        ]
        for copy in copies:
            copy.start()

    def parts(ref):
        starts = [step * stored + first * ROWS for step in range(steps)]
        return [ref[start : start + moved_rows, :] for start in starts]

    kinds = [[] for _ in range(2 * taps)]
    for ref in blocks:
        block = ref[cap * state_rows :, :].astype(F32)
        for kind in range(2 * taps):
            kinds[kind].append(block[kind * ROWS : (kind + 1) * ROWS])
    windows = [jnp.concatenate(kind, axis=0) for kind in kinds]
    later = round_up(taps + 3, ROWS)
    inner_conv = convolve(
        windows[:taps],
        parts(inner_moved),
        weights[later : later + taps + 1, :],
        weights[later + taps + 1 : later + taps + 2, :],
    )
    group_conv = convolve(
        windows[taps:],
        parts(group_moved),
        weights[: taps + 1, :],
        weights[taps + 1 : taps + 2, :],
    )
    for step, delta in enumerate(parts(delta_moved)):
        driven[step * moved_rows : (step + 1) * moved_rows, :] = delta * inner_conv[step]
    stride = ordered.shape[0] // steps
    maps = transposed(group_conv, ordered, stride)
    sums[...] = jnp.zeros_like(sums)
    gated[...] = gated_in[...]
    table[...] = table_in[...]
    load.wait()
    live = plan[0, plan.shape[1] - 1]

    def each(act):
        for block in range(len(blocks)):
            entry = moving + (first + block) * cap

            @pl.when(plan[0, entry] >= 0)
            def _():
                for c in range(cap):
                    act(block, c, plan[0, entry + c])

    def store(block, c, slot):
        place = block * cap + c
        return pltpu.make_async_copy(done.at[place], scan_next.at[slot], sem.at[4 + place])

    def advance(block, c, slot):
        place = block * ROWS + c
        rows = [step * moved_rows + place for step in range(steps)]
        result = advance_slot(
            blocks[block][c * state_rows : (c + 1) * state_rows, :],
            [slice(row, row + 1) for row in rows],
            driven,
            [
                decay_moved[row : row + 1, :]
                for row in (step * stored + first * ROWS + place for step in range(steps))
            ],
            sums,
            maps,
            [step * stride + place for step in range(steps)],
        )
        done[block * cap + c] = jnp.where(slot < live, result, jnp.zeros_like(result))
        store(block, c, slot).start()

    each(advance)
    for step, gate in enumerate(parts(gate_moved)):
        part = slice(step * moved_rows, (step + 1) * moved_rows)
        skipped = inner_conv[step] * weights[taps + 2 : taps + 3, :]
        sums[part, :] = (sums[part, :] + skipped) * gate
    driven[:moved_rows, :] = windows[taps - 1]
    driven[moved_rows : 2 * moved_rows, :] = windows[2 * taps - 1]

    def scatter(block, c, slot):
        place = block * ROWS + c
        for step in range(steps):
            row = step * moved_rows + place
            gated[pl.ds(step * slots + slot, 1), :] = sums[row : row + 1, :]
        table[pl.ds(slot, 1), :] = jnp.concatenate(
            [driven[place : place + 1, :], driven[moved_rows + place : moved_rows + place + 1, :]],
            axis=1,
        )

    each(scatter)
    if last:
        living = lax.broadcasted_iota(jnp.int32, (slots, LANES), 0) < live
        for step in range(steps):
            part = slice(step * slots, (step + 1) * slots)
            gated_cast[step] = jnp.where(living, gated[part, :], 0.0).astype(BF16)
        inner_cast[0] = jnp.where(living, table[:, :LANES], 0.0).astype(BF16)
        carried = jnp.where(head == 0, table[:, LANES : LANES + width], table[:, LANES + width :])
        group_cast[0] = jnp.where(living[:, :width], carried, 0.0).astype(BF16)
        ends = [
            pltpu.make_async_copy(source, target, semaphore)
            for source, target, semaphore in (
                (gated_cast, gated_out, sem.at[0]),
                (inner_cast, inner_next.at[pl.ds(0, 1)], sem.at[3]),
                (group_cast, group_next.at[pl.ds(0, 1)], sem.at[sem.shape[0] - 1]),
            )
        ]
        for copy in ends:
            copy.start()
        for copy in copies + ends:
            copy.wait()
    each(lambda block, c, slot: store(block, c, slot).wait())


def arrive(replicas, cap, first, last, operands, scan_next, arrived):
    inner_moved, gated, table, inner_part, group_part = operands[2], *operands[7:]
    steps, slots, width = group_part.shape
    blocks = len(arrived) if rounds_of(replicas) else replicas
    moved = (steps * blocks * ROWS, LANES)
    carried = [pltpu.VMEM(value.shape, F32) for value in (gated, table)]
    scan_shape = jax.ShapeDtypeStruct(scan_next.shape, BF16)
    if last:
        outs = [
            jax.ShapeDtypeStruct((steps, slots, LANES), BF16),
            jax.ShapeDtypeStruct((steps + 1, slots, LANES), BF16),
            jax.ShapeDtypeStruct((steps + 1, slots, width), BF16),
            scan_shape,
        ]
        scratch = carried + [
            pltpu.VMEM((steps, slots, LANES), BF16),
            pltpu.VMEM((1, slots, LANES), BF16),
            pltpu.VMEM((1, slots, width), BF16),
        ]
        specs = [HBM] * 4
    else:
        outs, scratch, specs = carried + [scan_shape], [], [VMEM, VMEM, HBM]
    plan = operands[0]
    return pl.pallas_call(
        functools.partial(arrive_kernel, replicas, cap, first, last),
        out_shape=outs,
        in_specs=[VMEM] * len(operands) + [HBM] + [VMEM] * len(arrived),
        out_specs=specs,
        scratch_shapes=scratch
        + [
            pltpu.SMEM(plan.shape, plan.dtype),
            pltpu.VMEM(moved, F32),
            pltpu.VMEM(moved, F32),
            pltpu.VMEM((round_up(moved[0], LANES), LANES), F32),
            pltpu.VMEM((blocks * cap,) + scan_next.shape[1:], BF16),
            pltpu.SemaphoreType.DMA((blocks * cap + 5,)),
        ],
        input_output_aliases={len(operands): len(outs) - 1},
        compiler_params=pltpu.CompilerParams(
            vmem_limit_bytes=SMALL_LIMIT if rounds_of(replicas) else LARGE_LIMIT
        ),
        cost_estimate=pl.CostEstimate(
            flops=10_000_000, bytes_accessed=2_000_000, transcendentals=0
        ),
        name="advance_last" if last else "advance_arrived",
    )(*operands, scan_next, *arrived)


def swap_heads(value):
    return lax.ppermute(value, "head", [(0, 1), (1, 0)])


def exchange(replicas, blocks):
    rounds = rounds_of(replicas)
    if not rounds:
        return [lax.all_to_all(blocks[0], "dp", 0, 0, tiled=True)]
    return [
        lax.ppermute(block, "dp", [(source, source ^ mask) for source in range(replicas)])
        for mask, block in zip(rounds, blocks)
    ]


def per_device(
    replicas,
    tokens,
    inner_weight,
    gate_weight,
    group_weight,
    delta_weight,
    inner_taps,
    inner_offset,
    group_taps,
    group_offset,
    decay_log,
    delta_bias,
    skip_gain,
    inner_window,
    group_window,
    scan_state,
    send_list,
    receive_list,
    live_count,
):
    steps, slots, half = tokens.shape
    cap = send_list.shape[1] // replicas
    scan = jnp.transpose(scan_state, (0, 2, 1))
    inner = jnp.transpose(inner_window, (1, 0, 2))
    group = jnp.transpose(group_window, (1, 0, 2))
    own = tokens.reshape(steps * slots, half)

    group_weight = group_weight.T
    inner_offset = inner_offset[None]
    small = jnp.concatenate([group_taps, group_offset[None]], axis=0)
    group_other = swap_heads(group)
    swapped = [swap_heads(value) for value in (own, group_weight, small)]
    blocks = pack(replicas, cap, send_list, scan, inner, group, group_other, swapped)
    arrived = exchange(replicas, blocks)
    plan, gated, weights, table, inner_part, group_part, *moved, scan_next = stay(
        replicas,
        cap,
        (decay_log, delta_bias, skip_gain, live_count),
        (
            receive_list,
            own,
            inner_weight,
            gate_weight,
            group_weight,
            delta_weight.T,
            inner_taps,
            inner_offset,
            inner,
            group,
            scan,
        ),
        (swapped[0], swapped[1], small, swapped[2], group_other),
        arrived[:EARLIER] if rounds_of(replicas) else [],
    )
    first = max(0, len(arrived) - LAST)
    if first:
        operands = (plan, weights, *moved, gated, table, inner_part, group_part)
        gated, table, scan_next = arrive(
            replicas, cap, 0, False, operands, scan_next, arrived[:first]
        )
    operands = (plan, weights, *moved, gated, table, inner_part, group_part)
    gated, inner_next, group_next, scan_next = arrive(
        replicas, cap, first, True, operands, scan_next, arrived[first:]
    )
    return (
        gated,
        jnp.transpose(inner_next, (1, 0, 2)),
        jnp.transpose(group_next, (1, 0, 2)),
        jnp.transpose(scan_next, (0, 2, 1)),
    )


def solution(mesh):
    in_specs = (
        P(None, ("grp", "dp"), "head"),
        P(None, "head"),
        P(None, "head"),
        P(None, "head"),
        P(None, "head"),
        P(None, "head"),
        P("head"),
        P(None, "head"),
        P("head"),
        P("head"),
        P("head"),
        P("head"),
        P(("grp", "dp"), None, "head"),
        P(("grp", "dp"), None, "head"),
        P(("grp", "dp"), "head", None),
        P(("grp", "dp"), None),
        P(("grp", "dp"), None),
        P(("grp", "dp")),
    )
    out_specs = (
        P(None, ("grp", "dp"), "head"),
        P(("grp", "dp"), None, "head"),
        P(("grp", "dp"), None, "head"),
        P(("grp", "dp"), "head", None),
    )
    return jax.shard_map(
        functools.partial(per_device, mesh.shape["dp"]),
        mesh=mesh,
        in_specs=in_specs,
        out_specs=out_specs,
        check_vma=False,
    )
```

```python
import functools

import jax
import jax.numpy as jnp
from jax import lax
from jax.experimental import pallas as pl
from jax.experimental.pallas import tpu as pltpu
from jax.sharding import PartitionSpec as P

F32 = jnp.float32
BF16 = jnp.bfloat16
SMALL_LIMIT = 8 * 1024 * 1024
MEDIUM_LIMIT = 16 * 1024 * 1024
LARGE_LIMIT = 48 * 1024 * 1024
MAX_ROUNDS = 16
EARLIER = 2
LAST = 2
LANES = 128
ROWS = 8
MAX_SETS = 64

VMEM = pl.BlockSpec(memory_space=pltpu.VMEM)
SMEM = pl.BlockSpec(memory_space=pltpu.SMEM)
HBM = pl.BlockSpec(memory_space=pl.ANY)


def in_hbm(value):
    return pltpu.with_memory_space_constraint(value, pltpu.HBM)


def in_vmem(value):
    return pltpu.with_memory_space_constraint(value, pltpu.VMEM)


def round_up(value, step):
    return -(-value // step) * step


def silu(value):
    return value * jax.nn.sigmoid(value)


def rounded(value):
    return value.astype(BF16).astype(F32)


def rounds_of(replicas):
    if replicas > MAX_ROUNDS or replicas & (replicas - 1):
        return []
    light = list(range(1, replicas // 2))
    heavy = list(range(replicas // 2, replicas))
    return light[:1] + heavy[:2] + light[1:] + heavy[2:]


def partner(replicas, mask):
    return jnp.bitwise_xor(lax.axis_index("dp"), mask)


def both_halves(mine, theirs):
    first = lax.axis_index("head") == 0
    return jnp.concatenate(
        [jnp.where(first, mine, theirs), jnp.where(first, theirs, mine)], axis=-1
    )


def destinations(replicas, outs):
    rounds = rounds_of(replicas)
    if rounds:
        return [(ref.at[0], partner(replicas, mask)) for ref, mask in zip(outs, rounds)]
    return [(outs[0].at[target], target) for target in range(replicas)]


def states_kernel(replicas, cap, scan, send, inner, group, *refs):
    outs, (picked, group_out, indices_out) = refs[:-11], refs[-11:-8]
    indices, inner_in, table, load_sem, group_sem, list_sem, save_sem, sem = refs[-8:]
    load_list = pltpu.make_async_copy(send, indices, list_sem)
    load_list.start()
    load = pltpu.make_async_copy(inner, inner_in, load_sem)
    load.start()
    load_group = pltpu.make_async_copy(group, group_out, group_sem)
    load_group.start()
    state_rows = scan.shape[1]
    blocks = destinations(replicas, outs)
    load_list.wait()
    save = pltpu.make_async_copy(indices, indices_out, save_sem)
    save.start()
    plan = []
    for block, (ref, target) in enumerate(blocks):
        for c in range(cap):
            plan.append((block, ref, c, indices[0, target * cap + c]))

    def each(act):
        for place, (_, ref, c, index) in enumerate(plan):

            @pl.when(index >= 0)
            def _():
                act(
                    pltpu.make_async_copy(
                        scan.at[index],
                        ref.at[pl.ds(c * state_rows, state_rows)],
                        sem.at[place],
                    )
                )

    each(lambda copy: copy.start())
    load.wait()
    taps = inner_in.shape[0]
    for tap in range(taps):
        table[:, tap * LANES : (tap + 1) * LANES] = inner_in[tap].astype(F32)
    picked[...] = jnp.zeros_like(picked)
    for block, _, c, index in plan:
        row = table[pl.ds(jnp.maximum(index, 0), 1), :]
        for tap in range(taps):
            picked[block, tap * ROWS + c : tap * ROWS + c + 1, :] = row[
                :, tap * LANES : (tap + 1) * LANES
            ]
    load_group.wait()
    save.wait()
    each(lambda copy: copy.wait())


def windows_kernel(replicas, cap, state_rows, indices_in, group, group_other, picked_in, *refs):
    count = max(1, len(rounds_of(replicas)))
    outs = refs[-4 - count : -4]
    indices, table, picked, sem = refs[-4:]
    load = pltpu.make_async_copy(indices_in, indices, sem)
    load.start()
    taps = group.shape[0]
    for tap in range(taps):
        table[:, tap * LANES : (tap + 1) * LANES] = both_halves(
            group[tap].astype(F32), group_other[tap].astype(F32)
        )
    picked[...] = jnp.zeros_like(picked)
    load.wait()
    for block, (ref, target) in enumerate(destinations(replicas, outs)):
        for c in range(cap):
            index = jnp.maximum(indices[0, target * cap + c], 0)
            row = table[pl.ds(index, 1), :]
            for tap in range(taps):
                picked[block, tap * ROWS + c : tap * ROWS + c + 1, :] = row[
                    :, tap * LANES : (tap + 1) * LANES
                ]
        ref[cap * state_rows :, :] = jnp.concatenate(
            [picked_in[block], picked[block]], axis=0
        ).astype(BF16)


def pack(replicas, cap, send_list, scan, inner, group, group_other, swapped):
    rounds = rounds_of(replicas)
    count = max(1, len(rounds))
    per_block = 1 if rounds else replicas
    taps, slots, _ = inner.shape
    rows = cap * scan.shape[1] + 2 * taps * ROWS
    blocks = count * per_block
    shapes = [pltpu.VMEM((per_block, rows, LANES), BF16)] * count
    half = (blocks, taps * ROWS, LANES)
    limit = SMALL_LIMIT if rounds else MEDIUM_LIMIT
    *states, picked, group_near, indices = pl.pallas_call(
        functools.partial(states_kernel, replicas, cap),
        out_shape=shapes
        + [
            pltpu.VMEM(half, F32),
            pltpu.VMEM(group.shape, BF16),
            pltpu.VMEM(send_list.shape, jnp.int32),
        ],
        in_specs=[HBM] * 4,
        out_specs=[VMEM] * (count + 3),
        scratch_shapes=[
            pltpu.SMEM(send_list.shape, jnp.int32),
            pltpu.VMEM(inner.shape, BF16),
            pltpu.VMEM((slots, taps * LANES), F32),
            pltpu.SemaphoreType.DMA,
            pltpu.SemaphoreType.DMA,
            pltpu.SemaphoreType.DMA,
            pltpu.SemaphoreType.DMA,
            pltpu.SemaphoreType.DMA((blocks * cap,)),
        ],
        compiler_params=pltpu.CompilerParams(vmem_limit_bytes=limit),
        cost_estimate=pl.CostEstimate(flops=0, bytes_accessed=2_000_000, transcendentals=0),
        name="pack_states",
    )(in_hbm(scan), in_hbm(send_list), in_hbm(inner), in_hbm(group))
    near = [in_vmem(value) for value in states]
    return pl.pallas_call(
        functools.partial(windows_kernel, replicas, cap, scan.shape[1]),
        out_shape=shapes,
        in_specs=[VMEM] * (4 + count) + [HBM] * len(swapped),
        out_specs=[VMEM] * count,
        scratch_shapes=[
            pltpu.SMEM(send_list.shape, jnp.int32),
            pltpu.VMEM((slots, taps * LANES), F32),
            pltpu.VMEM(half, F32),
            pltpu.SemaphoreType.DMA,
        ],
        input_output_aliases={4 + place: place for place in range(count)},
        compiler_params=pltpu.CompilerParams(vmem_limit_bytes=limit),
        cost_estimate=pl.CostEstimate(flops=0, bytes_accessed=500_000, transcendentals=0),
        name="pack_windows",
    )(indices, group_near, group_other, picked, *near, *swapped)


def sources_of(replicas):
    rounds = rounds_of(replicas)
    if rounds:
        return [partner(replicas, mask) for mask in rounds]
    return list(range(replicas))


def make_plan(replicas, cap, receive, slots, plan, inverse):
    moving = slots // 2
    kept = 0
    for entry in range(replicas * cap):
        inverse[entry] = -1
    for slot in range(slots):
        entry = receive[0, slot]
        stays = entry < 0
        plan[0, jnp.where(stays, kept, moving)] = slot
        inverse[jnp.where(stays, replicas * cap, entry)] = slot
        kept = kept + jnp.where(stays, 1, 0)
    for block, source in enumerate(sources_of(replicas)):
        for c in range(cap):
            plan[0, moving + block * cap + c] = inverse[source * cap + c]


def convolve(carried, raw, weights, offset):
    joined = carried + raw
    results = []
    for step in range(len(raw)):
        summed = offset
        for tap in range(len(carried) + 1):
            summed = summed + joined[step + tap] * weights[tap : tap + 1, :]
        results.append(rounded(silu(summed)))
    return results


def transposed(rows, scratch, stride):
    scratch[...] = jnp.zeros_like(scratch)
    for step, value in enumerate(rows):
        scratch[step * stride : step * stride + value.shape[0], :] = value
    return [scratch[first : first + LANES].T for first in range(0, scratch.shape[0], LANES)]


def advance_slot(state, rows, driven, decays, sums, maps, lanes):
    hidden = state.astype(F32)
    width = state.shape[0]
    for row, decay, lane in zip(rows, decays, lanes):
        piece = maps[lane // LANES]
        column = piece[:, lane % LANES : lane % LANES + 1]
        hidden = decay * hidden + driven[row, :] * column[:width]
        sums[row, :] = jnp.sum(hidden * column[width:], axis=0, keepdims=True)
        result = hidden.astype(BF16)
        hidden = result.astype(F32)
    return result


def stay_kernel(
    replicas,
    cap,
    decay_log,
    delta_bias,
    skip_gain,
    live,
    receive_hbm,
    own_hbm,
    inner_weight,
    gate_weight,
    group_weight,
    delta_weight,
    inner_taps_hbm,
    inner_offset_hbm,
    inner_hbm,
    group_hbm,
    scan_hbm,
    other,
    group_weight_other,
    small,
    small_other,
    group_other,
    *refs,
):
    (
        plan_out,
        gated,
        weights,
        base,
        inner_part,
        group_part,
        inner_moved,
        group_moved,
        gate_moved,
        delta_moved,
        decay_moved,
        scan_next,
        plan,
        receive,
        own,
        wide,
        tall,
        delta_row,
        inner_taps,
        inner_offset,
        inner,
        group,
        scan,
        inverse,
        inner_raw,
        both,
        gate,
        delta,
        decay,
        driven,
        skipped,
        sums,
        maps_in,
        ordered,
        done,
        sem,
        load_sem,
    ) = refs[-37:]
    taps, slots, _ = inner.shape
    rows, half = own.shape
    steps = rows // slots
    moving = slots // 2
    moved_rows = inner_moved.shape[0] // steps
    width = group.shape[2]
    head = lax.axis_index("head")

    def band(place):
        return tall.at[pl.ds(pl.multiple_of(place * width, width), width)]

    pairs = [
        (receive_hbm, receive),
        (delta_weight, delta_row),
        (own_hbm, own),
        (inner_weight, wide.at[:, pl.ds(0, LANES)]),
        (gate_weight, wide.at[:, pl.ds(LANES, LANES)]),
        (group_weight, band(head)),
        (group_weight_other, band(1 - head)),
        (inner_taps_hbm, inner_taps),
        (inner_offset_hbm, inner_offset),
        (inner_hbm, inner),
        (group_hbm, group),
        (scan_hbm, scan),
    ]
    loads = [
        pltpu.make_async_copy(source, target, load_sem.at[place])
        for place, (source, target) in enumerate(pairs)
    ]
    for load in loads:
        load.start()
    loads[0].wait()
    make_plan(replicas, cap, receive, slots, plan, inverse)
    loads[1].wait()
    first = 2 * width
    tall[first:, :] = jnp.broadcast_to(delta_row[...], (tall.shape[0] - first, 2 * half))
    for load in loads[2:]:
        load.wait()
    mine = pl.ds(pl.multiple_of(head * half, half), half)
    theirs = pl.ds(pl.multiple_of((1 - head) * half, half), half)
    flat = jnp.dot(own[...], wide[mine, :], preferred_element_type=F32) + jnp.dot(
        other[...], wide[theirs, :], preferred_element_type=F32
    )

    def across(tokens, part):
        return lax.dot_general(
            tokens, tall[:, part], (((1,), (1,)), ((), ())), preferred_element_type=F32
        )

    deep = across(own[...], mine) + across(other[...], theirs)
    inner_raw[...] = rounded(flat[:, :LANES])
    gate[...] = silu(rounded(flat[:, LANES:]))
    both[...] = rounded(deep[:, :first])
    shifted = rounded(jnp.broadcast_to(deep[:, first : first + 1], (rows, LANES)))
    shifted = shifted + delta_bias[0]
    rate = jnp.maximum(shifted, 0.0) + jnp.log1p(jnp.exp(-jnp.abs(shifted)))
    delta[...] = rate
    decay[...] = jnp.exp(-rate * jnp.exp(jnp.full((1, LANES), decay_log[0], F32)))
    count = taps + 2
    weights[:count, :] = both_halves(small[...], small_other[...])
    weights[count : count + 1, :] = jnp.full((1, LANES), skip_gain[0], F32)
    later = round_up(count + 1, ROWS)
    weights[later : later + taps + 1, :] = inner_taps[...]
    weights[later + taps + 1 : later + taps + 2, :] = inner_offset[...]
    plan[0, plan.shape[1] - 1] = live[0]
    save_plan = pltpu.make_async_copy(plan, plan_out, load_sem.at[0])
    save_plan.start()

    def parts(ref):
        return [ref[step * slots : (step + 1) * slots, :] for step in range(steps)]

    inner_conv = convolve(
        [inner[tap].astype(F32) for tap in range(taps)],
        parts(inner_raw),
        inner_taps[...],
        inner_offset[...],
    )
    group_conv = convolve(
        [both_halves(group[tap].astype(F32), group_other[tap].astype(F32)) for tap in range(taps)],
        parts(both),
        weights[: taps + 1, :],
        weights[taps + 1 : taps + 2, :],
    )
    for step in range(steps):
        part = slice(step * slots, (step + 1) * slots)
        driven[part, :] = delta[part, :] * inner_conv[step]
        skipped[part, :] = inner_conv[step] * skip_gain[0]
        maps_in[part, :] = group_conv[step]
    sums[...] = jnp.zeros_like(sums)
    stride = ordered.shape[0] // steps
    ordered[...] = jnp.zeros_like(ordered)
    for position in range(moving):
        slot = plan[0, position]
        for step in range(steps):
            ordered[step * stride + position : step * stride + position + 1, :] = maps_in[
                pl.ds(step * slots + slot, 1), :
            ]
    maps = [ordered[first : first + LANES].T for first in range(0, ordered.shape[0], LANES)]
    copies = []
    for position in range(moving):
        slot = plan[0, position]
        result = advance_slot(
            scan[slot],
            [pl.ds(step * slots + slot, 1) for step in range(steps)],
            driven,
            [decay[pl.ds(step * slots + slot, 1), :] for step in range(steps)],
            sums,
            maps,
            [step * stride + position for step in range(steps)],
        )
        done[position] = jnp.where(slot < live[0], result, jnp.zeros_like(result))
        copies.append(
            pltpu.make_async_copy(done.at[position], scan_next.at[slot], sem.at[position])
        )
        copies[-1].start()
    gated[...] = (sums[...] + skipped[...]) * gate[...]
    pairs = (
        (inner_raw, inner_moved),
        (both, group_moved),
        (gate, gate_moved),
        (delta, delta_moved),
        (decay, decay_moved),
    )
    for _, target in pairs:
        target[...] = jnp.zeros_like(target)
    living = lax.broadcasted_iota(jnp.int32, (slots, LANES), 0) < live[0]
    for step in range(steps):
        part = slice(step * slots, (step + 1) * slots)
        inner_part[step] = jnp.where(living, inner_raw[part, :], 0.0).astype(BF16)
        raw = jnp.where(head == 0, both[part, :width], both[part, width:])
        group_part[step] = jnp.where(living[:, :width], raw, 0.0).astype(BF16)
    base[:, :LANES] = inner[steps].astype(F32)
    group_own = group[steps].astype(F32)
    base[:, LANES:] = jnp.concatenate([group_own, group_own], axis=1)
    for block in range(moved_rows // ROWS):

        @pl.when(plan[0, moving + block * cap] >= 0)
        def _():
            for c in range(cap):
                slot = plan[0, moving + block * cap + c]
                for step in range(steps):
                    row = step * moved_rows + block * ROWS + c
                    for source, target in pairs:
                        target[row : row + 1, :] = source[pl.ds(step * slots + slot, 1), :]

    for copy in copies:
        copy.wait()
    save_plan.wait()


def stay(replicas, cap, scalars, arrays, near, earlier):
    receive, own, group_weight, delta_weight = arrays[0], arrays[1], arrays[4], arrays[5]
    inner, scan = arrays[-3], arrays[-1]
    taps, slots, _ = inner.shape
    rows = own.shape[0]
    steps = rows // slots
    moving = slots // 2
    blocks = len(sources_of(replicas))
    moved_rows = blocks * ROWS
    width, features = group_weight.shape
    full = pltpu.VMEM((rows, LANES), F32)
    moved = pltpu.VMEM((steps * moved_rows, LANES), F32)
    plan_shape = (1, round_up(moving + blocks * cap + 1, LANES))

    def like(value):
        return pltpu.VMEM(value.shape, value.dtype)

    far = [in_hbm(value) for value in arrays]
    return pl.pallas_call(
        functools.partial(stay_kernel, replicas, cap),
        out_shape=[
            pltpu.VMEM(plan_shape, jnp.int32),
            full,
            pltpu.VMEM((2 * round_up(taps + 3, ROWS), LANES), F32),
            pltpu.VMEM((slots, 2 * LANES), F32),
            pltpu.VMEM((steps, slots, LANES), BF16),
            pltpu.VMEM((steps, slots, width), BF16),
        ]
        + [moved] * 5
        + [jax.ShapeDtypeStruct(scan.shape, BF16)],
        in_specs=[SMEM] * len(scalars)
        + [HBM] * len(far)
        + [VMEM] * len(near)
        + [HBM] * len(earlier),
        out_specs=[VMEM] * 11 + [HBM],
        scratch_shapes=[
            pltpu.SMEM(plan_shape, jnp.int32),
            pltpu.SMEM(receive.shape, jnp.int32),
            like(own),
            pltpu.VMEM((features, 2 * LANES), BF16),
            pltpu.VMEM((2 * width + 2 * ROWS, features), BF16),
            like(delta_weight),
        ]
        + [like(value) for value in arrays[6:]]
        + [pltpu.SMEM((replicas * cap + 1,), jnp.int32)]
        + [pltpu.VMEM((rows, LANES), F32)] * 9
        + [
            pltpu.VMEM((round_up(rows, LANES), LANES), F32),
            pltpu.VMEM((moving,) + scan.shape[1:], BF16),
            pltpu.SemaphoreType.DMA((moving,)),
            pltpu.SemaphoreType.DMA((16,)),
        ],
        compiler_params=pltpu.CompilerParams(vmem_limit_bytes=MEDIUM_LIMIT),
        cost_estimate=pl.CostEstimate(
            flops=300_000_000, bytes_accessed=6_000_000, transcendentals=100_000
        ),
        name="advance_staying",
    )(*scalars, *far, *near, *earlier)


def arrive_kernel(
    replicas,
    cap,
    first,
    last,
    plan_near,
    weights,
    inner_moved,
    group_moved,
    gate_moved,
    delta_moved,
    decay_moved,
    gated_in,
    table_in,
    inner_part,
    group_part,
    scan_in,
    *refs,
):
    del scan_in
    if last:
        arrived = refs[:-15]
        gated_out, inner_next, group_next, scan_next = refs[-15:-11]
        gated, table = refs[-11:-9]
        gated_cast, inner_cast, group_cast = refs[-9:-6]
    else:
        arrived = refs[:-9]
        gated, table, scan_next = refs[-9:-6]
    plan, driven, sums, ordered, done, sem = refs[-6:]
    steps, slots, width = group_part.shape
    taps = steps + 1
    moving = slots // 2
    state_rows = scan_next.shape[1]
    head = lax.axis_index("head")
    load = pltpu.make_async_copy(plan_near, plan, sem.at[0])
    load.start()
    if rounds_of(replicas):
        blocks = [ref.at[0] for ref in arrived]
    else:
        blocks = [arrived[0].at[source] for source in range(replicas)]
    stored = inner_moved.shape[0] // steps
    moved_rows = len(blocks) * ROWS
    if last:
        copies = [
            pltpu.make_async_copy(source, target, sem.at[1 + place])
            for place, (source, target) in enumerate(
                [
                    (inner_part, inner_next.at[pl.ds(1, steps)]),
                    (group_part, group_next.at[pl.ds(1, steps)]),
                ]
            )
        ]
        for copy in copies:
            copy.start()

    def parts(ref):
        starts = [step * stored + first * ROWS for step in range(steps)]
        return [ref[start : start + moved_rows, :] for start in starts]

    kinds = [[] for _ in range(2 * taps)]
    for ref in blocks:
        block = ref[cap * state_rows :, :].astype(F32)
        for kind in range(2 * taps):
            kinds[kind].append(block[kind * ROWS : (kind + 1) * ROWS])
    windows = [jnp.concatenate(kind, axis=0) for kind in kinds]
    later = round_up(taps + 3, ROWS)
    inner_conv = convolve(
        windows[:taps],
        parts(inner_moved),
        weights[later : later + taps + 1, :],
        weights[later + taps + 1 : later + taps + 2, :],
    )
    group_conv = convolve(
        windows[taps:],
        parts(group_moved),
        weights[: taps + 1, :],
        weights[taps + 1 : taps + 2, :],
    )
    for step, delta in enumerate(parts(delta_moved)):
        driven[step * moved_rows : (step + 1) * moved_rows, :] = delta * inner_conv[step]
    stride = ordered.shape[0] // steps
    maps = transposed(group_conv, ordered, stride)
    sums[...] = jnp.zeros_like(sums)
    gated[...] = gated_in[...]
    table[...] = table_in[...]
    load.wait()
    live = plan[0, plan.shape[1] - 1]

    def each(act):
        for block in range(len(blocks)):
            entry = moving + (first + block) * cap

            @pl.when(plan[0, entry] >= 0)
            def _():
                for c in range(cap):
                    act(block, c, plan[0, entry + c])

    def store(block, c, slot):
        place = block * cap + c
        return pltpu.make_async_copy(done.at[place], scan_next.at[slot], sem.at[4 + place])

    def advance(block, c, slot):
        place = block * ROWS + c
        rows = [step * moved_rows + place for step in range(steps)]
        result = advance_slot(
            blocks[block][c * state_rows : (c + 1) * state_rows, :],
            [slice(row, row + 1) for row in rows],
            driven,
            [
                decay_moved[row : row + 1, :]
                for row in (step * stored + first * ROWS + place for step in range(steps))
            ],
            sums,
            maps,
            [step * stride + place for step in range(steps)],
        )
        done[block * cap + c] = jnp.where(slot < live, result, jnp.zeros_like(result))
        store(block, c, slot).start()

    each(advance)
    for step, gate in enumerate(parts(gate_moved)):
        part = slice(step * moved_rows, (step + 1) * moved_rows)
        skipped = inner_conv[step] * weights[taps + 2 : taps + 3, :]
        sums[part, :] = (sums[part, :] + skipped) * gate
    driven[:moved_rows, :] = windows[taps - 1]
    driven[moved_rows : 2 * moved_rows, :] = windows[2 * taps - 1]

    def scatter(block, c, slot):
        place = block * ROWS + c
        for step in range(steps):
            row = step * moved_rows + place
            gated[pl.ds(step * slots + slot, 1), :] = sums[row : row + 1, :]
        table[pl.ds(slot, 1), :] = jnp.concatenate(
            [driven[place : place + 1, :], driven[moved_rows + place : moved_rows + place + 1, :]],
            axis=1,
        )

    each(scatter)
    if last:
        living = lax.broadcasted_iota(jnp.int32, (slots, LANES), 0) < live
        for step in range(steps):
            part = slice(step * slots, (step + 1) * slots)
            gated_cast[step] = jnp.where(living, gated[part, :], 0.0).astype(BF16)
        inner_cast[0] = jnp.where(living, table[:, :LANES], 0.0).astype(BF16)
        carried = jnp.where(head == 0, table[:, LANES : LANES + width], table[:, LANES + width :])
        group_cast[0] = jnp.where(living[:, :width], carried, 0.0).astype(BF16)
        ends = [
            pltpu.make_async_copy(source, target, semaphore)
            for source, target, semaphore in (
                (gated_cast, gated_out, sem.at[0]),
                (inner_cast, inner_next.at[pl.ds(0, 1)], sem.at[3]),
                (group_cast, group_next.at[pl.ds(0, 1)], sem.at[sem.shape[0] - 1]),
            )
        ]
        for copy in ends:
            copy.start()
        for copy in copies + ends:
            copy.wait()
    each(lambda block, c, slot: store(block, c, slot).wait())


def arrive(replicas, cap, first, last, operands, scan_next, arrived):
    inner_moved, gated, table, inner_part, group_part = operands[2], *operands[7:]
    steps, slots, width = group_part.shape
    blocks = len(arrived) if rounds_of(replicas) else replicas
    moved = (steps * blocks * ROWS, LANES)
    carried = [pltpu.VMEM(value.shape, F32) for value in (gated, table)]
    scan_shape = jax.ShapeDtypeStruct(scan_next.shape, BF16)
    if last:
        outs = [
            jax.ShapeDtypeStruct((steps, slots, LANES), BF16),
            jax.ShapeDtypeStruct((steps + 1, slots, LANES), BF16),
            jax.ShapeDtypeStruct((steps + 1, slots, width), BF16),
            scan_shape,
        ]
        scratch = carried + [
            pltpu.VMEM((steps, slots, LANES), BF16),
            pltpu.VMEM((1, slots, LANES), BF16),
            pltpu.VMEM((1, slots, width), BF16),
        ]
        specs = [HBM] * 4
    else:
        outs, scratch, specs = carried + [scan_shape], [], [VMEM, VMEM, HBM]
    plan = operands[0]
    return pl.pallas_call(
        functools.partial(arrive_kernel, replicas, cap, first, last),
        out_shape=outs,
        in_specs=[VMEM] * len(operands) + [HBM] + [VMEM] * len(arrived),
        out_specs=specs,
        scratch_shapes=scratch
        + [
            pltpu.SMEM(plan.shape, plan.dtype),
            pltpu.VMEM(moved, F32),
            pltpu.VMEM(moved, F32),
            pltpu.VMEM((round_up(moved[0], LANES), LANES), F32),
            pltpu.VMEM((blocks * cap,) + scan_next.shape[1:], BF16),
            pltpu.SemaphoreType.DMA((blocks * cap + 5,)),
        ],
        input_output_aliases={len(operands): len(outs) - 1},
        compiler_params=pltpu.CompilerParams(
            vmem_limit_bytes=SMALL_LIMIT if rounds_of(replicas) else LARGE_LIMIT
        ),
        cost_estimate=pl.CostEstimate(
            flops=10_000_000, bytes_accessed=2_000_000, transcendentals=0
        ),
        name="advance_last" if last else "advance_arrived",
    )(*operands, scan_next, *arrived)


def swap_heads(value):
    return lax.ppermute(value, "head", [(0, 1), (1, 0)])


def exchange(replicas, blocks):
    rounds = rounds_of(replicas)
    if not rounds:
        return [lax.all_to_all(blocks[0], "dp", 0, 0, tiled=True)]
    return [
        lax.ppermute(block, "dp", [(source, source ^ mask) for source in range(replicas)])
        for mask, block in zip(rounds, blocks)
    ]


def per_device(
    replicas,
    tokens,
    inner_weight,
    gate_weight,
    group_weight,
    delta_weight,
    inner_taps,
    inner_offset,
    group_taps,
    group_offset,
    decay_log,
    delta_bias,
    skip_gain,
    inner_window,
    group_window,
    scan_state,
    send_list,
    receive_list,
    live_count,
):
    steps, slots, half = tokens.shape
    cap = send_list.shape[1] // replicas
    scan = jnp.transpose(scan_state, (0, 2, 1))
    inner = jnp.transpose(inner_window, (1, 0, 2))
    group = jnp.transpose(group_window, (1, 0, 2))
    own = tokens.reshape(steps * slots, half)

    group_weight = group_weight.T
    inner_offset = inner_offset[None]
    small = jnp.concatenate([group_taps, group_offset[None]], axis=0)
    group_other = swap_heads(group)
    swapped = [swap_heads(value) for value in (own, group_weight, small)]
    blocks = pack(replicas, cap, send_list, scan, inner, group, group_other, swapped)
    arrived = exchange(replicas, blocks)
    plan, gated, weights, table, inner_part, group_part, *moved, scan_next = stay(
        replicas,
        cap,
        (decay_log, delta_bias, skip_gain, live_count),
        (
            receive_list,
            own,
            inner_weight,
            gate_weight,
            group_weight,
            delta_weight.T,
            inner_taps,
            inner_offset,
            inner,
            group,
            scan,
        ),
        (swapped[0], swapped[1], small, swapped[2], group_other),
        arrived[:EARLIER] if rounds_of(replicas) else [],
    )
    first = max(0, len(arrived) - LAST)
    if first:
        operands = (plan, weights, *moved, gated, table, inner_part, group_part)
        gated, table, scan_next = arrive(
            replicas, cap, 0, False, operands, scan_next, arrived[:first]
        )
    operands = (plan, weights, *moved, gated, table, inner_part, group_part)
    gated, inner_next, group_next, scan_next = arrive(
        replicas, cap, first, True, operands, scan_next, arrived[first:]
    )
    return (
        gated,
        jnp.transpose(inner_next, (1, 0, 2)),
        jnp.transpose(group_next, (1, 0, 2)),
        jnp.transpose(scan_next, (0, 2, 1)),
    )


def solution(mesh):
    in_specs = (
        P(None, ("grp", "dp"), "head"),
        P(None, "head"),
        P(None, "head"),
        P(None, "head"),
        P(None, "head"),
        P(None, "head"),
        P("head"),
        P(None, "head"),
        P("head"),
        P("head"),
        P("head"),
        P("head"),
        P(("grp", "dp"), None, "head"),
        P(("grp", "dp"), None, "head"),
        P(("grp", "dp"), "head", None),
        P(("grp", "dp"), None),
        P(("grp", "dp"), None),
        P(("grp", "dp")),
    )
    out_specs = (
        P(None, ("grp", "dp"), "head"),
        P(("grp", "dp"), None, "head"),
        P(("grp", "dp"), None, "head"),
        P(("grp", "dp"), "head", None),
    )
    return jax.shard_map(
        functools.partial(per_device, mesh.shape["dp"]),
        mesh=mesh,
        in_specs=in_specs,
        out_specs=out_specs,
        check_vma=False,
    )
```

```python
import functools

import jax
import jax.numpy as jnp
from jax import lax
from jax.experimental import pallas as pl
from jax.experimental.pallas import tpu as pltpu
from jax.sharding import PartitionSpec as P

F32 = jnp.float32
BF16 = jnp.bfloat16
SMALL_LIMIT = 8 * 1024 * 1024
MEDIUM_LIMIT = 16 * 1024 * 1024
LARGE_LIMIT = 48 * 1024 * 1024
MAX_ROUNDS = 16
EARLIER = 2
LAST = 2
LANES = 128
ROWS = 8
MAX_SETS = 64

VMEM = pl.BlockSpec(memory_space=pltpu.VMEM)
SMEM = pl.BlockSpec(memory_space=pltpu.SMEM)
HBM = pl.BlockSpec(memory_space=pl.ANY)


def in_hbm(value):
    return pltpu.with_memory_space_constraint(value, pltpu.HBM)


def in_vmem(value):
    return pltpu.with_memory_space_constraint(value, pltpu.VMEM)


def round_up(value, step):
    return -(-value // step) * step


def silu(value):
    return value * jax.nn.sigmoid(value)


def rounded(value):
    return value.astype(BF16).astype(F32)


def rounds_of(replicas):
    if replicas > MAX_ROUNDS or replicas & (replicas - 1):
        return []
    light = list(range(1, replicas // 2))
    heavy = list(range(replicas // 2, replicas))
    return light[:2] + heavy[:2] + light[2:] + heavy[2:]


def partner(replicas, mask):
    return jnp.bitwise_xor(lax.axis_index("dp"), mask)


def both_halves(mine, theirs):
    first = lax.axis_index("head") == 0
    return jnp.concatenate(
        [jnp.where(first, mine, theirs), jnp.where(first, theirs, mine)], axis=-1
    )


def destinations(replicas, outs):
    rounds = rounds_of(replicas)
    if rounds:
        return [(ref.at[0], partner(replicas, mask)) for ref, mask in zip(outs, rounds)]
    return [(outs[0].at[target], target) for target in range(replicas)]


def states_kernel(replicas, cap, scan, send, inner, group, *refs):
    outs, (picked, group_out, indices_out) = refs[:-11], refs[-11:-8]
    indices, inner_in, table, load_sem, group_sem, list_sem, save_sem, sem = refs[-8:]
    load_list = pltpu.make_async_copy(send, indices, list_sem)
    load_list.start()
    load = pltpu.make_async_copy(inner, inner_in, load_sem)
    load.start()
    load_group = pltpu.make_async_copy(group, group_out, group_sem)
    load_group.start()
    state_rows = scan.shape[1]
    blocks = destinations(replicas, outs)
    load_list.wait()
    save = pltpu.make_async_copy(indices, indices_out, save_sem)
    save.start()
    plan = []
    for block, (ref, target) in enumerate(blocks):
        for c in range(cap):
            plan.append((block, ref, c, indices[0, target * cap + c]))

    def each(act):
        for place, (_, ref, c, index) in enumerate(plan):

            @pl.when(index >= 0)
            def _():
                act(
                    pltpu.make_async_copy(
                        scan.at[index],
                        ref.at[pl.ds(c * state_rows, state_rows)],
                        sem.at[place],
                    )
                )

    each(lambda copy: copy.start())
    load.wait()
    taps = inner_in.shape[0]
    for tap in range(taps):
        table[:, tap * LANES : (tap + 1) * LANES] = inner_in[tap].astype(F32)
    picked[...] = jnp.zeros_like(picked)
    for block, _, c, index in plan:
        row = table[pl.ds(jnp.maximum(index, 0), 1), :]
        for tap in range(taps):
            picked[block, tap * ROWS + c : tap * ROWS + c + 1, :] = row[
                :, tap * LANES : (tap + 1) * LANES
            ]
    load_group.wait()
    save.wait()
    each(lambda copy: copy.wait())


def windows_kernel(replicas, cap, state_rows, indices_in, group, group_other, picked_in, *refs):
    count = max(1, len(rounds_of(replicas)))
    outs = refs[-4 - count : -4]
    indices, table, picked, sem = refs[-4:]
    load = pltpu.make_async_copy(indices_in, indices, sem)
    load.start()
    taps = group.shape[0]
    for tap in range(taps):
        table[:, tap * LANES : (tap + 1) * LANES] = both_halves(
            group[tap].astype(F32), group_other[tap].astype(F32)
        )
    picked[...] = jnp.zeros_like(picked)
    load.wait()
    for block, (ref, target) in enumerate(destinations(replicas, outs)):
        for c in range(cap):
            index = jnp.maximum(indices[0, target * cap + c], 0)
            row = table[pl.ds(index, 1), :]
            for tap in range(taps):
                picked[block, tap * ROWS + c : tap * ROWS + c + 1, :] = row[
                    :, tap * LANES : (tap + 1) * LANES
                ]
        ref[cap * state_rows :, :] = jnp.concatenate(
            [picked_in[block], picked[block]], axis=0
        ).astype(BF16)


def pack(replicas, cap, send_list, scan, inner, group, group_other, swapped):
    rounds = rounds_of(replicas)
    count = max(1, len(rounds))
    per_block = 1 if rounds else replicas
    taps, slots, _ = inner.shape
    rows = cap * scan.shape[1] + 2 * taps * ROWS
    blocks = count * per_block
    shapes = [pltpu.VMEM((per_block, rows, LANES), BF16)] * count
    half = (blocks, taps * ROWS, LANES)
    limit = SMALL_LIMIT if rounds else MEDIUM_LIMIT
    *states, picked, group_near, indices = pl.pallas_call(
        functools.partial(states_kernel, replicas, cap),
        out_shape=shapes
        + [
            pltpu.VMEM(half, F32),
            pltpu.VMEM(group.shape, BF16),
            pltpu.VMEM(send_list.shape, jnp.int32),
        ],
        in_specs=[HBM] * 4,
        out_specs=[VMEM] * (count + 3),
        scratch_shapes=[
            pltpu.SMEM(send_list.shape, jnp.int32),
            pltpu.VMEM(inner.shape, BF16),
            pltpu.VMEM((slots, taps * LANES), F32),
            pltpu.SemaphoreType.DMA,
            pltpu.SemaphoreType.DMA,
            pltpu.SemaphoreType.DMA,
            pltpu.SemaphoreType.DMA,
            pltpu.SemaphoreType.DMA((blocks * cap,)),
        ],
        compiler_params=pltpu.CompilerParams(vmem_limit_bytes=limit),
        cost_estimate=pl.CostEstimate(flops=0, bytes_accessed=2_000_000, transcendentals=0),
        name="pack_states",
    )(in_hbm(scan), in_hbm(send_list), in_hbm(inner), in_hbm(group))
    near = [in_vmem(value) for value in states]
    return pl.pallas_call(
        functools.partial(windows_kernel, replicas, cap, scan.shape[1]),
        out_shape=shapes,
        in_specs=[VMEM] * (4 + count) + [HBM] * len(swapped),
        out_specs=[VMEM] * count,
        scratch_shapes=[
            pltpu.SMEM(send_list.shape, jnp.int32),
            pltpu.VMEM((slots, taps * LANES), F32),
            pltpu.VMEM(half, F32),
            pltpu.SemaphoreType.DMA,
        ],
        input_output_aliases={4 + place: place for place in range(count)},
        compiler_params=pltpu.CompilerParams(vmem_limit_bytes=limit),
        cost_estimate=pl.CostEstimate(flops=0, bytes_accessed=500_000, transcendentals=0),
        name="pack_windows",
    )(indices, group_near, group_other, picked, *near, *swapped)


def sources_of(replicas):
    rounds = rounds_of(replicas)
    if rounds:
        return [partner(replicas, mask) for mask in rounds]
    return list(range(replicas))


def make_plan(replicas, cap, receive, slots, plan, inverse):
    moving = slots // 2
    kept = 0
    for entry in range(replicas * cap):
        inverse[entry] = -1
    for slot in range(slots):
        entry = receive[0, slot]
        stays = entry < 0
        plan[0, jnp.where(stays, kept, moving)] = slot
        inverse[jnp.where(stays, replicas * cap, entry)] = slot
        kept = kept + jnp.where(stays, 1, 0)
    for block, source in enumerate(sources_of(replicas)):
        for c in range(cap):
            plan[0, moving + block * cap + c] = inverse[source * cap + c]


def convolve(carried, raw, weights, offset):
    joined = carried + raw
    results = []
    for step in range(len(raw)):
        summed = offset
        for tap in range(len(carried) + 1):
            summed = summed + joined[step + tap] * weights[tap : tap + 1, :]
        results.append(rounded(silu(summed)))
    return results


def transposed(rows, scratch, stride):
    scratch[...] = jnp.zeros_like(scratch)
    for step, value in enumerate(rows):
        scratch[step * stride : step * stride + value.shape[0], :] = value
    return [scratch[first : first + LANES].T for first in range(0, scratch.shape[0], LANES)]


def advance_slot(state, rows, driven, decays, sums, maps, lanes):
    hidden = state.astype(F32)
    width = state.shape[0]
    for row, decay, lane in zip(rows, decays, lanes):
        piece = maps[lane // LANES]
        column = piece[:, lane % LANES : lane % LANES + 1]
        hidden = decay * hidden + driven[row, :] * column[:width]
        sums[row, :] = jnp.sum(hidden * column[width:], axis=0, keepdims=True)
        result = hidden.astype(BF16)
        hidden = result.astype(F32)
    return result


def stay_kernel(
    replicas,
    cap,
    decay_log,
    delta_bias,
    skip_gain,
    live,
    receive_hbm,
    own_hbm,
    inner_weight,
    gate_weight,
    group_weight,
    delta_weight,
    inner_taps_hbm,
    inner_offset_hbm,
    inner_hbm,
    group_hbm,
    scan_hbm,
    other,
    group_weight_other,
    small,
    small_other,
    group_other,
    *refs,
):
    (
        plan_out,
        gated,
        weights,
        base,
        inner_part,
        group_part,
        inner_moved,
        group_moved,
        gate_moved,
        delta_moved,
        decay_moved,
        scan_next,
        plan,
        receive,
        own,
        wide,
        tall,
        delta_row,
        inner_taps,
        inner_offset,
        inner,
        group,
        scan,
        inverse,
        inner_raw,
        both,
        gate,
        delta,
        decay,
        driven,
        skipped,
        sums,
        maps_in,
        ordered,
        done,
        sem,
        load_sem,
    ) = refs[-37:]
    taps, slots, _ = inner.shape
    rows, half = own.shape
    steps = rows // slots
    moving = slots // 2
    moved_rows = inner_moved.shape[0] // steps
    width = group.shape[2]
    head = lax.axis_index("head")

    def band(place):
        return tall.at[pl.ds(pl.multiple_of(place * width, width), width)]

    pairs = [
        (receive_hbm, receive),
        (own_hbm, own),
        (inner_weight, wide.at[:, pl.ds(0, LANES)]),
        (gate_weight, wide.at[:, pl.ds(LANES, LANES)]),
        (delta_weight, delta_row),
        (group_weight, band(head)),
        (group_weight_other, band(1 - head)),
        (inner_taps_hbm, inner_taps),
        (inner_offset_hbm, inner_offset),
        (inner_hbm, inner),
        (group_hbm, group),
        (scan_hbm, scan),
    ]
    loads = [
        pltpu.make_async_copy(source, target, load_sem.at[place])
        for place, (source, target) in enumerate(pairs)
    ]
    for load in loads:
        load.start()
    loads[0].wait()
    make_plan(replicas, cap, receive, slots, plan, inverse)
    for load in loads[1:4]:
        load.wait()
    mine = pl.ds(pl.multiple_of(head * half, half), half)
    theirs = pl.ds(pl.multiple_of((1 - head) * half, half), half)
    flat = jnp.dot(own[...], wide[mine, :], preferred_element_type=F32) + jnp.dot(
        other[...], wide[theirs, :], preferred_element_type=F32
    )
    for load in loads[4:]:
        load.wait()
    first = 2 * width
    tall[first:, :] = jnp.broadcast_to(delta_row[...], (tall.shape[0] - first, 2 * half))

    def across(tokens, part):
        return lax.dot_general(
            tokens, tall[:, part], (((1,), (1,)), ((), ())), preferred_element_type=F32
        )

    deep = across(own[...], mine) + across(other[...], theirs)
    inner_raw[...] = rounded(flat[:, :LANES])
    gate[...] = silu(rounded(flat[:, LANES:]))
    both[...] = rounded(deep[:, :first])
    shifted = rounded(jnp.broadcast_to(deep[:, first : first + 1], (rows, LANES)))
    shifted = shifted + delta_bias[0]
    rate = jnp.maximum(shifted, 0.0) + jnp.log1p(jnp.exp(-jnp.abs(shifted)))
    delta[...] = rate
    decay[...] = jnp.exp(-rate * jnp.exp(jnp.full((1, LANES), decay_log[0], F32)))
    count = taps + 2
    weights[:count, :] = both_halves(small[...], small_other[...])
    weights[count : count + 1, :] = jnp.full((1, LANES), skip_gain[0], F32)
    later = round_up(count + 1, ROWS)
    weights[later : later + taps + 1, :] = inner_taps[...]
    weights[later + taps + 1 : later + taps + 2, :] = inner_offset[...]
    plan[0, plan.shape[1] - 1] = live[0]
    save_plan = pltpu.make_async_copy(plan, plan_out, load_sem.at[0])
    save_plan.start()

    def parts(ref):
        return [ref[step * slots : (step + 1) * slots, :] for step in range(steps)]

    inner_conv = convolve(
        [inner[tap].astype(F32) for tap in range(taps)],
        parts(inner_raw),
        inner_taps[...],
        inner_offset[...],
    )
    group_conv = convolve(
        [both_halves(group[tap].astype(F32), group_other[tap].astype(F32)) for tap in range(taps)],
        parts(both),
        weights[: taps + 1, :],
        weights[taps + 1 : taps + 2, :],
    )
    for step in range(steps):
        part = slice(step * slots, (step + 1) * slots)
        driven[part, :] = delta[part, :] * inner_conv[step]
        skipped[part, :] = inner_conv[step] * skip_gain[0]
        maps_in[part, :] = group_conv[step]
    sums[...] = jnp.zeros_like(sums)
    stride = ordered.shape[0] // steps
    ordered[...] = jnp.zeros_like(ordered)
    for position in range(moving):
        slot = plan[0, position]
        for step in range(steps):
            ordered[step * stride + position : step * stride + position + 1, :] = maps_in[
                pl.ds(step * slots + slot, 1), :
            ]
    maps = [ordered[first : first + LANES].T for first in range(0, ordered.shape[0], LANES)]
    copies = []
    for position in range(moving):
        slot = plan[0, position]
        result = advance_slot(
            scan[slot],
            [pl.ds(step * slots + slot, 1) for step in range(steps)],
            driven,
            [decay[pl.ds(step * slots + slot, 1), :] for step in range(steps)],
            sums,
            maps,
            [step * stride + position for step in range(steps)],
        )
        done[position] = jnp.where(slot < live[0], result, jnp.zeros_like(result))
        copies.append(
            pltpu.make_async_copy(done.at[position], scan_next.at[slot], sem.at[position])
        )
        copies[-1].start()
    gated[...] = (sums[...] + skipped[...]) * gate[...]
    pairs = (
        (inner_raw, inner_moved),
        (both, group_moved),
        (gate, gate_moved),
        (delta, delta_moved),
        (decay, decay_moved),
    )
    for _, target in pairs:
        target[...] = jnp.zeros_like(target)
    living = lax.broadcasted_iota(jnp.int32, (slots, LANES), 0) < live[0]
    for step in range(steps):
        part = slice(step * slots, (step + 1) * slots)
        inner_part[step] = jnp.where(living, inner_raw[part, :], 0.0).astype(BF16)
        raw = jnp.where(head == 0, both[part, :width], both[part, width:])
        group_part[step] = jnp.where(living[:, :width], raw, 0.0).astype(BF16)
    base[:, :LANES] = inner[steps].astype(F32)
    group_own = group[steps].astype(F32)
    base[:, LANES:] = jnp.concatenate([group_own, group_own], axis=1)
    for block in range(moved_rows // ROWS):

        @pl.when(plan[0, moving + block * cap] >= 0)
        def _():
            for c in range(cap):
                slot = plan[0, moving + block * cap + c]
                for step in range(steps):
                    row = step * moved_rows + block * ROWS + c
                    for source, target in pairs:
                        target[row : row + 1, :] = source[pl.ds(step * slots + slot, 1), :]

    for copy in copies:
        copy.wait()
    save_plan.wait()


def stay(replicas, cap, scalars, arrays, near, earlier):
    receive, own, group_weight, delta_weight = arrays[0], arrays[1], arrays[4], arrays[5]
    inner, scan = arrays[-3], arrays[-1]
    taps, slots, _ = inner.shape
    rows = own.shape[0]
    steps = rows // slots
    moving = slots // 2
    blocks = len(sources_of(replicas))
    moved_rows = blocks * ROWS
    width, features = group_weight.shape
    full = pltpu.VMEM((rows, LANES), F32)
    moved = pltpu.VMEM((steps * moved_rows, LANES), F32)
    plan_shape = (1, round_up(moving + blocks * cap + 1, LANES))

    def like(value):
        return pltpu.VMEM(value.shape, value.dtype)

    far = [in_hbm(value) for value in arrays]
    return pl.pallas_call(
        functools.partial(stay_kernel, replicas, cap),
        out_shape=[
            pltpu.VMEM(plan_shape, jnp.int32),
            full,
            pltpu.VMEM((2 * round_up(taps + 3, ROWS), LANES), F32),
            pltpu.VMEM((slots, 2 * LANES), F32),
            pltpu.VMEM((steps, slots, LANES), BF16),
            pltpu.VMEM((steps, slots, width), BF16),
        ]
        + [moved] * 5
        + [jax.ShapeDtypeStruct(scan.shape, BF16)],
        in_specs=[SMEM] * len(scalars)
        + [HBM] * len(far)
        + [VMEM] * len(near)
        + [HBM] * len(earlier),
        out_specs=[VMEM] * 11 + [HBM],
        scratch_shapes=[
            pltpu.SMEM(plan_shape, jnp.int32),
            pltpu.SMEM(receive.shape, jnp.int32),
            like(own),
            pltpu.VMEM((features, 2 * LANES), BF16),
            pltpu.VMEM((2 * width + 2 * ROWS, features), BF16),
            like(delta_weight),
        ]
        + [like(value) for value in arrays[6:]]
        + [pltpu.SMEM((replicas * cap + 1,), jnp.int32)]
        + [pltpu.VMEM((rows, LANES), F32)] * 9
        + [
            pltpu.VMEM((round_up(rows, LANES), LANES), F32),
            pltpu.VMEM((moving,) + scan.shape[1:], BF16),
            pltpu.SemaphoreType.DMA((moving,)),
            pltpu.SemaphoreType.DMA((16,)),
        ],
        compiler_params=pltpu.CompilerParams(vmem_limit_bytes=MEDIUM_LIMIT),
        cost_estimate=pl.CostEstimate(
            flops=300_000_000, bytes_accessed=6_000_000, transcendentals=100_000
        ),
        name="advance_staying",
    )(*scalars, *far, *near, *earlier)


def arrive_kernel(
    replicas,
    cap,
    first,
    last,
    plan_near,
    weights,
    inner_moved,
    group_moved,
    gate_moved,
    delta_moved,
    decay_moved,
    gated_in,
    table_in,
    inner_part,
    group_part,
    scan_in,
    *refs,
):
    del scan_in
    if last:
        arrived = refs[:-15]
        gated_out, inner_next, group_next, scan_next = refs[-15:-11]
        gated, table = refs[-11:-9]
        gated_cast, inner_cast, group_cast = refs[-9:-6]
    else:
        arrived = refs[:-9]
        gated, table, scan_next = refs[-9:-6]
    plan, driven, sums, ordered, done, sem = refs[-6:]
    steps, slots, width = group_part.shape
    taps = steps + 1
    moving = slots // 2
    state_rows = scan_next.shape[1]
    head = lax.axis_index("head")
    load = pltpu.make_async_copy(plan_near, plan, sem.at[0])
    load.start()
    if rounds_of(replicas):
        blocks = [ref.at[0] for ref in arrived]
    else:
        blocks = [arrived[0].at[source] for source in range(replicas)]
    stored = inner_moved.shape[0] // steps
    moved_rows = len(blocks) * ROWS
    if last:
        copies = [
            pltpu.make_async_copy(source, target, sem.at[1 + place])
            for place, (source, target) in enumerate(
                [
                    (inner_part, inner_next.at[pl.ds(1, steps)]),
                    (group_part, group_next.at[pl.ds(1, steps)]),
                ]
            )
        ]
        for copy in copies:
            copy.start()

    def parts(ref):
        starts = [step * stored + first * ROWS for step in range(steps)]
        return [ref[start : start + moved_rows, :] for start in starts]

    kinds = [[] for _ in range(2 * taps)]
    for ref in blocks:
        block = ref[cap * state_rows :, :].astype(F32)
        for kind in range(2 * taps):
            kinds[kind].append(block[kind * ROWS : (kind + 1) * ROWS])
    windows = [jnp.concatenate(kind, axis=0) for kind in kinds]
    later = round_up(taps + 3, ROWS)
    inner_conv = convolve(
        windows[:taps],
        parts(inner_moved),
        weights[later : later + taps + 1, :],
        weights[later + taps + 1 : later + taps + 2, :],
    )
    group_conv = convolve(
        windows[taps:],
        parts(group_moved),
        weights[: taps + 1, :],
        weights[taps + 1 : taps + 2, :],
    )
    for step, delta in enumerate(parts(delta_moved)):
        driven[step * moved_rows : (step + 1) * moved_rows, :] = delta * inner_conv[step]
    stride = ordered.shape[0] // steps
    maps = transposed(group_conv, ordered, stride)
    sums[...] = jnp.zeros_like(sums)
    gated[...] = gated_in[...]
    table[...] = table_in[...]
    load.wait()
    live = plan[0, plan.shape[1] - 1]

    def each(act):
        for block in range(len(blocks)):
            entry = moving + (first + block) * cap

            @pl.when(plan[0, entry] >= 0)
            def _():
                for c in range(cap):
                    act(block, c, plan[0, entry + c])

    def store(block, c, slot):
        place = block * cap + c
        return pltpu.make_async_copy(done.at[place], scan_next.at[slot], sem.at[4 + place])

    def advance(block, c, slot):
        place = block * ROWS + c
        rows = [step * moved_rows + place for step in range(steps)]
        result = advance_slot(
            blocks[block][c * state_rows : (c + 1) * state_rows, :],
            [slice(row, row + 1) for row in rows],
            driven,
            [
                decay_moved[row : row + 1, :]
                for row in (step * stored + first * ROWS + place for step in range(steps))
            ],
            sums,
            maps,
            [step * stride + place for step in range(steps)],
        )
        done[block * cap + c] = jnp.where(slot < live, result, jnp.zeros_like(result))
        store(block, c, slot).start()

    each(advance)
    for step, gate in enumerate(parts(gate_moved)):
        part = slice(step * moved_rows, (step + 1) * moved_rows)
        skipped = inner_conv[step] * weights[taps + 2 : taps + 3, :]
        sums[part, :] = (sums[part, :] + skipped) * gate
    driven[:moved_rows, :] = windows[taps - 1]
    driven[moved_rows : 2 * moved_rows, :] = windows[2 * taps - 1]

    def scatter(block, c, slot):
        place = block * ROWS + c
        for step in range(steps):
            row = step * moved_rows + place
            gated[pl.ds(step * slots + slot, 1), :] = sums[row : row + 1, :]
        table[pl.ds(slot, 1), :] = jnp.concatenate(
            [driven[place : place + 1, :], driven[moved_rows + place : moved_rows + place + 1, :]],
            axis=1,
        )

    each(scatter)
    if last:
        living = lax.broadcasted_iota(jnp.int32, (slots, LANES), 0) < live
        for step in range(steps):
            part = slice(step * slots, (step + 1) * slots)
            gated_cast[step] = jnp.where(living, gated[part, :], 0.0).astype(BF16)
        inner_cast[0] = jnp.where(living, table[:, :LANES], 0.0).astype(BF16)
        carried = jnp.where(head == 0, table[:, LANES : LANES + width], table[:, LANES + width :])
        group_cast[0] = jnp.where(living[:, :width], carried, 0.0).astype(BF16)
        ends = [
            pltpu.make_async_copy(source, target, semaphore)
            for source, target, semaphore in (
                (gated_cast, gated_out, sem.at[0]),
                (inner_cast, inner_next.at[pl.ds(0, 1)], sem.at[3]),
                (group_cast, group_next.at[pl.ds(0, 1)], sem.at[sem.shape[0] - 1]),
            )
        ]
        for copy in ends:
            copy.start()
        for copy in copies + ends:
            copy.wait()
    each(lambda block, c, slot: store(block, c, slot).wait())


def arrive(replicas, cap, first, last, operands, scan_next, arrived):
    inner_moved, gated, table, inner_part, group_part = operands[2], *operands[7:]
    steps, slots, width = group_part.shape
    blocks = len(arrived) if rounds_of(replicas) else replicas
    moved = (steps * blocks * ROWS, LANES)
    carried = [pltpu.VMEM(value.shape, F32) for value in (gated, table)]
    scan_shape = jax.ShapeDtypeStruct(scan_next.shape, BF16)
    if last:
        outs = [
            jax.ShapeDtypeStruct((steps, slots, LANES), BF16),
            jax.ShapeDtypeStruct((steps + 1, slots, LANES), BF16),
            jax.ShapeDtypeStruct((steps + 1, slots, width), BF16),
            scan_shape,
        ]
        scratch = carried + [
            pltpu.VMEM((steps, slots, LANES), BF16),
            pltpu.VMEM((1, slots, LANES), BF16),
            pltpu.VMEM((1, slots, width), BF16),
        ]
        specs = [HBM] * 4
    else:
        outs, scratch, specs = carried + [scan_shape], [], [VMEM, VMEM, HBM]
    plan = operands[0]
    return pl.pallas_call(
        functools.partial(arrive_kernel, replicas, cap, first, last),
        out_shape=outs,
        in_specs=[VMEM] * len(operands) + [HBM] + [VMEM] * len(arrived),
        out_specs=specs,
        scratch_shapes=scratch
        + [
            pltpu.SMEM(plan.shape, plan.dtype),
            pltpu.VMEM(moved, F32),
            pltpu.VMEM(moved, F32),
            pltpu.VMEM((round_up(moved[0], LANES), LANES), F32),
            pltpu.VMEM((blocks * cap,) + scan_next.shape[1:], BF16),
            pltpu.SemaphoreType.DMA((blocks * cap + 5,)),
        ],
        input_output_aliases={len(operands): len(outs) - 1},
        compiler_params=pltpu.CompilerParams(
            vmem_limit_bytes=SMALL_LIMIT if rounds_of(replicas) else LARGE_LIMIT
        ),
        cost_estimate=pl.CostEstimate(
            flops=10_000_000, bytes_accessed=2_000_000, transcendentals=0
        ),
        name="advance_last" if last else "advance_arrived",
    )(*operands, scan_next, *arrived)


def swap_heads(value):
    return lax.ppermute(value, "head", [(0, 1), (1, 0)])


def exchange(replicas, blocks):
    rounds = rounds_of(replicas)
    if not rounds:
        return [lax.all_to_all(blocks[0], "dp", 0, 0, tiled=True)]
    return [
        lax.ppermute(block, "dp", [(source, source ^ mask) for source in range(replicas)])
        for mask, block in zip(rounds, blocks)
    ]


def per_device(
    replicas,
    tokens,
    inner_weight,
    gate_weight,
    group_weight,
    delta_weight,
    inner_taps,
    inner_offset,
    group_taps,
    group_offset,
    decay_log,
    delta_bias,
    skip_gain,
    inner_window,
    group_window,
    scan_state,
    send_list,
    receive_list,
    live_count,
):
    steps, slots, half = tokens.shape
    cap = send_list.shape[1] // replicas
    scan = jnp.transpose(scan_state, (0, 2, 1))
    inner = jnp.transpose(inner_window, (1, 0, 2))
    group = jnp.transpose(group_window, (1, 0, 2))
    own = tokens.reshape(steps * slots, half)

    group_weight = group_weight.T
    inner_offset = inner_offset[None]
    small = jnp.concatenate([group_taps, group_offset[None]], axis=0)
    group_other = swap_heads(group)
    swapped = [swap_heads(value) for value in (own, group_weight, small)]
    blocks = pack(replicas, cap, send_list, scan, inner, group, group_other, swapped)
    arrived = exchange(replicas, blocks)
    plan, gated, weights, table, inner_part, group_part, *moved, scan_next = stay(
        replicas,
        cap,
        (decay_log, delta_bias, skip_gain, live_count),
        (
            receive_list,
            own,
            inner_weight,
            gate_weight,
            group_weight,
            delta_weight.T,
            inner_taps,
            inner_offset,
            inner,
            group,
            scan,
        ),
        (swapped[0], swapped[1], small, swapped[2], group_other),
        arrived[:EARLIER] if rounds_of(replicas) else [],
    )
    first = max(0, len(arrived) - LAST)
    if first:
        operands = (plan, weights, *moved, gated, table, inner_part, group_part)
        gated, table, scan_next = arrive(
            replicas, cap, 0, False, operands, scan_next, arrived[:first]
        )
    operands = (plan, weights, *moved, gated, table, inner_part, group_part)
    gated, inner_next, group_next, scan_next = arrive(
        replicas, cap, first, True, operands, scan_next, arrived[first:]
    )
    return (
        gated,
        jnp.transpose(inner_next, (1, 0, 2)),
        jnp.transpose(group_next, (1, 0, 2)),
        jnp.transpose(scan_next, (0, 2, 1)),
    )


def solution(mesh):
    in_specs = (
        P(None, ("grp", "dp"), "head"),
        P(None, "head"),
        P(None, "head"),
        P(None, "head"),
        P(None, "head"),
        P(None, "head"),
        P("head"),
        P(None, "head"),
        P("head"),
        P("head"),
        P("head"),
        P("head"),
        P(("grp", "dp"), None, "head"),
        P(("grp", "dp"), None, "head"),
        P(("grp", "dp"), "head", None),
        P(("grp", "dp"), None),
        P(("grp", "dp"), None),
        P(("grp", "dp")),
    )
    out_specs = (
        P(None, ("grp", "dp"), "head"),
        P(("grp", "dp"), None, "head"),
        P(("grp", "dp"), None, "head"),
        P(("grp", "dp"), "head", None),
    )
    return jax.shard_map(
        functools.partial(per_device, mesh.shape["dp"]),
        mesh=mesh,
        in_specs=in_specs,
        out_specs=out_specs,
        check_vma=False,
    )
```

```python
import functools

import jax
import jax.numpy as jnp
from jax import lax
from jax.experimental import pallas as pl
from jax.experimental.pallas import tpu as pltpu
from jax.sharding import PartitionSpec as P

F32 = jnp.float32
BF16 = jnp.bfloat16
SMALL_LIMIT = 8 * 1024 * 1024
MEDIUM_LIMIT = 16 * 1024 * 1024
LARGE_LIMIT = 48 * 1024 * 1024
MAX_HALVES = 16
LAST = 2
LANES = 128
ROWS = 8
MAX_SETS = 64

VMEM = pl.BlockSpec(memory_space=pltpu.VMEM)
SMEM = pl.BlockSpec(memory_space=pltpu.SMEM)
HBM = pl.BlockSpec(memory_space=pl.ANY)


def in_hbm(value):
    return pltpu.with_memory_space_constraint(value, pltpu.HBM)


def in_vmem(value):
    return pltpu.with_memory_space_constraint(value, pltpu.VMEM)


def round_up(value, step):
    return -(-value // step) * step


def silu(value):
    return value * jax.nn.sigmoid(value)


def rounded(value):
    return value.astype(BF16).astype(F32)


def masks_of(replicas):
    if replicas > MAX_HALVES or replicas & (replicas - 1) or replicas < 4:
        return []
    return list(range(replicas // 2, replicas))


def peers_of(replicas):
    masks = masks_of(replicas)
    if not masks:
        return [list(range(replicas))]
    me = lax.axis_index("dp")
    half = replicas // 2
    first = me // half * half
    return [[first + place for place in range(half)]] + [
        [jnp.bitwise_xor(me, mask)] for mask in masks
    ]


def block_counts(replicas):
    masks = masks_of(replicas)
    return [replicas // 2] + [1] * len(masks) if masks else [replicas]


def blocks_of(refs):
    return [ref.at[place] for ref in refs for place in range(ref.shape[0])]


def both_halves(mine, theirs):
    first = lax.axis_index("head") == 0
    return jnp.concatenate(
        [jnp.where(first, mine, theirs), jnp.where(first, theirs, mine)], axis=-1
    )


def pack_plan(replicas, cap, refs, indices):
    plan = []
    for block, (ref, peer) in enumerate(zip(blocks_of(refs), sum(peers_of(replicas), []))):
        for c in range(cap):
            plan.append((block, ref, c, indices[0, peer * cap + c]))
    return plan


def states_kernel(replicas, cap, scan, send, inner, group, *refs):
    outs, (picked, group_out, indices_out) = refs[:-11], refs[-11:-8]
    indices, inner_in, table, load_sem, group_sem, list_sem, save_sem, sem = refs[-8:]
    load_list = pltpu.make_async_copy(send, indices, list_sem)
    load_list.start()
    load = pltpu.make_async_copy(inner, inner_in, load_sem)
    load.start()
    load_group = pltpu.make_async_copy(group, group_out, group_sem)
    load_group.start()
    state_rows = scan.shape[1]
    load_list.wait()
    save = pltpu.make_async_copy(indices, indices_out, save_sem)
    save.start()
    plan = pack_plan(replicas, cap, outs, indices)

    def each(act):
        for place, (_, ref, c, index) in enumerate(plan):

            @pl.when(index >= 0)
            def _():
                act(
                    pltpu.make_async_copy(
                        scan.at[index],
                        ref.at[pl.ds(c * state_rows, state_rows)],
                        sem.at[place],
                    )
                )

    each(lambda copy: copy.start())
    load.wait()
    taps = inner_in.shape[0]
    for tap in range(taps):
        table[:, tap * LANES : (tap + 1) * LANES] = inner_in[tap].astype(F32)
    picked[...] = jnp.zeros_like(picked)
    for block, _, c, index in plan:
        row = table[pl.ds(jnp.maximum(index, 0), 1), :]
        for tap in range(taps):
            picked[block, tap * ROWS + c : tap * ROWS + c + 1, :] = row[
                :, tap * LANES : (tap + 1) * LANES
            ]
    load_group.wait()
    save.wait()
    each(lambda copy: copy.wait())


def windows_kernel(replicas, cap, indices_in, group, group_other, picked_in, near_in, *refs):
    count = len(block_counts(replicas))
    outs = refs[-5 - count : -5]
    indices, table, picked, sem, near_sem = refs[-5:]
    load = pltpu.make_async_copy(indices_in, indices, sem)
    load.start()
    copies = [
        pltpu.make_async_copy(
            near_in.at[place],
            outs[0].at[place, pl.ds(0, near_in.shape[1])],
            near_sem.at[place],
        )
        for place in range(near_in.shape[0])
    ]
    for copy in copies:
        copy.start()
    taps = group.shape[0]
    for tap in range(taps):
        table[:, tap * LANES : (tap + 1) * LANES] = both_halves(
            group[tap].astype(F32), group_other[tap].astype(F32)
        )
    picked[...] = jnp.zeros_like(picked)
    load.wait()
    for block, ref, c, index in pack_plan(replicas, cap, outs, indices):
        row = table[pl.ds(jnp.maximum(index, 0), 1), :]
        for tap in range(taps):
            picked[block, tap * ROWS + c : tap * ROWS + c + 1, :] = row[
                :, tap * LANES : (tap + 1) * LANES
            ]
        if c == cap - 1:
            ref[near_in.shape[1] :, :] = jnp.concatenate(
                [picked_in[block], picked[block]], axis=0
            ).astype(BF16)
    for copy in copies:
        copy.wait()


def pack(replicas, cap, send_list, scan, inner, group, group_other, swapped):
    counts = block_counts(replicas)
    count, blocks = len(counts), sum(counts)
    taps, slots, _ = inner.shape
    state_rows = cap * scan.shape[1]
    rows = state_rows + 2 * taps * ROWS
    shapes = [pltpu.VMEM((number, rows, LANES), BF16) for number in counts]
    half = (blocks, taps * ROWS, LANES)
    limit = SMALL_LIMIT if masks_of(replicas) else MEDIUM_LIMIT
    near, *states, picked, group_near, indices = pl.pallas_call(
        functools.partial(states_kernel, replicas, cap),
        out_shape=[pltpu.VMEM((counts[0], state_rows, LANES), BF16)]
        + shapes[1:]
        + [
            pltpu.VMEM(half, F32),
            pltpu.VMEM(group.shape, BF16),
            pltpu.VMEM(send_list.shape, jnp.int32),
        ],
        in_specs=[HBM] * 4,
        out_specs=[VMEM] * (count + 3),
        scratch_shapes=[
            pltpu.SMEM(send_list.shape, jnp.int32),
            pltpu.VMEM(inner.shape, BF16),
            pltpu.VMEM((slots, taps * LANES), F32),
            pltpu.SemaphoreType.DMA,
            pltpu.SemaphoreType.DMA,
            pltpu.SemaphoreType.DMA,
            pltpu.SemaphoreType.DMA,
            pltpu.SemaphoreType.DMA((blocks * cap,)),
        ],
        compiler_params=pltpu.CompilerParams(vmem_limit_bytes=limit),
        cost_estimate=pl.CostEstimate(flops=0, bytes_accessed=2_000_000, transcendentals=0),
        name="pack_states",
    )(in_hbm(scan), in_hbm(send_list), in_hbm(inner), in_hbm(group))
    states = [in_vmem(value) for value in states]
    return pl.pallas_call(
        functools.partial(windows_kernel, replicas, cap),
        out_shape=shapes,
        in_specs=[VMEM] * (5 + len(states)) + [HBM] * len(swapped),
        out_specs=[VMEM] * count,
        scratch_shapes=[
            pltpu.SMEM(send_list.shape, jnp.int32),
            pltpu.VMEM((slots, taps * LANES), F32),
            pltpu.VMEM(half, F32),
            pltpu.SemaphoreType.DMA,
            pltpu.SemaphoreType.DMA((counts[0],)),
        ],
        input_output_aliases={5 + place: 1 + place for place in range(len(states))},
        compiler_params=pltpu.CompilerParams(vmem_limit_bytes=limit),
        cost_estimate=pl.CostEstimate(flops=0, bytes_accessed=500_000, transcendentals=0),
        name="pack_windows",
    )(indices, group_near, group_other, picked, near, *states, *swapped)


def make_plan(replicas, cap, receive, slots, plan, inverse):
    moving = slots // 2
    kept = 0
    for entry in range(replicas * cap):
        inverse[entry] = -1
    for slot in range(slots):
        entry = receive[0, slot]
        stays = entry < 0
        plan[0, jnp.where(stays, kept, moving)] = slot
        inverse[jnp.where(stays, replicas * cap, entry)] = slot
        kept = kept + jnp.where(stays, 1, 0)
    for block, source in enumerate(sum(peers_of(replicas), [])):
        for c in range(cap):
            plan[0, moving + block * cap + c] = inverse[source * cap + c]


def convolve(carried, raw, weights, offset):
    joined = carried + raw
    results = []
    for step in range(len(raw)):
        summed = offset
        for tap in range(len(carried) + 1):
            summed = summed + joined[step + tap] * weights[tap : tap + 1, :]
        results.append(rounded(silu(summed)))
    return results


def transposed(rows, scratch, stride):
    scratch[...] = jnp.zeros_like(scratch)
    for step, value in enumerate(rows):
        scratch[step * stride : step * stride + value.shape[0], :] = value
    return [scratch[first : first + LANES].T for first in range(0, scratch.shape[0], LANES)]


def advance_slot(state, rows, driven, decays, sums, maps, lanes):
    hidden = state.astype(F32)
    width = state.shape[0]
    for row, decay, lane in zip(rows, decays, lanes):
        piece = maps[lane // LANES]
        column = piece[:, lane % LANES : lane % LANES + 1]
        hidden = decay * hidden + driven[row, :] * column[:width]
        sums[row, :] = jnp.sum(hidden * column[width:], axis=0, keepdims=True)
        result = hidden.astype(BF16)
        hidden = result.astype(F32)
    return result


def stay_kernel(
    replicas,
    cap,
    decay_log,
    delta_bias,
    skip_gain,
    live,
    receive_hbm,
    own_hbm,
    inner_weight,
    gate_weight,
    group_weight,
    delta_weight,
    inner_taps_hbm,
    inner_offset_hbm,
    inner_hbm,
    group_hbm,
    scan_hbm,
    other,
    group_weight_other,
    small,
    small_other,
    group_other,
    *refs,
):
    (
        plan_out,
        gated,
        weights,
        base,
        inner_part,
        group_part,
        inner_moved,
        group_moved,
        gate_moved,
        delta_moved,
        decay_moved,
        scan_next,
        plan,
        receive,
        own,
        wide,
        tall,
        delta_row,
        inner_taps,
        inner_offset,
        inner,
        group,
        scan,
        inverse,
        inner_raw,
        both,
        gate,
        delta,
        decay,
        driven,
        skipped,
        sums,
        maps_in,
        ordered,
        done,
        sem,
        load_sem,
    ) = refs[-37:]
    taps, slots, _ = inner.shape
    rows, half = own.shape
    steps = rows // slots
    moving = slots // 2
    moved_rows = inner_moved.shape[0] // steps
    width = group.shape[2]
    head = lax.axis_index("head")

    def band(place):
        return tall.at[pl.ds(pl.multiple_of(place * width, width), width)]

    pairs = [
        (receive_hbm, receive),
        (own_hbm, own),
        (inner_weight, wide.at[:, pl.ds(0, LANES)]),
        (gate_weight, wide.at[:, pl.ds(LANES, LANES)]),
        (delta_weight, delta_row),
        (group_weight, band(head)),
        (group_weight_other, band(1 - head)),
        (inner_taps_hbm, inner_taps),
        (inner_offset_hbm, inner_offset),
        (inner_hbm, inner),
        (group_hbm, group),
        (scan_hbm, scan),
    ]
    loads = [
        pltpu.make_async_copy(source, target, load_sem.at[place])
        for place, (source, target) in enumerate(pairs)
    ]
    for load in loads:
        load.start()
    loads[0].wait()
    make_plan(replicas, cap, receive, slots, plan, inverse)
    for load in loads[1:4]:
        load.wait()
    mine = pl.ds(pl.multiple_of(head * half, half), half)
    theirs = pl.ds(pl.multiple_of((1 - head) * half, half), half)
    flat = jnp.dot(own[...], wide[mine, :], preferred_element_type=F32) + jnp.dot(
        other[...], wide[theirs, :], preferred_element_type=F32
    )
    for load in loads[4:]:
        load.wait()
    first = 2 * width
    tall[first:, :] = jnp.broadcast_to(delta_row[...], (tall.shape[0] - first, 2 * half))

    def across(tokens, part):
        return lax.dot_general(
            tokens, tall[:, part], (((1,), (1,)), ((), ())), preferred_element_type=F32
        )

    deep = across(own[...], mine) + across(other[...], theirs)
    inner_raw[...] = rounded(flat[:, :LANES])
    gate[...] = silu(rounded(flat[:, LANES:]))
    both[...] = rounded(deep[:, :first])
    shifted = rounded(jnp.broadcast_to(deep[:, first : first + 1], (rows, LANES)))
    shifted = shifted + delta_bias[0]
    rate = jnp.maximum(shifted, 0.0) + jnp.log1p(jnp.exp(-jnp.abs(shifted)))
    delta[...] = rate
    decay[...] = jnp.exp(-rate * jnp.exp(jnp.full((1, LANES), decay_log[0], F32)))
    count = taps + 2
    weights[:count, :] = both_halves(small[...], small_other[...])
    weights[count : count + 1, :] = jnp.full((1, LANES), skip_gain[0], F32)
    later = round_up(count + 1, ROWS)
    weights[later : later + taps + 1, :] = inner_taps[...]
    weights[later + taps + 1 : later + taps + 2, :] = inner_offset[...]
    plan[0, plan.shape[1] - 1] = live[0]
    save_plan = pltpu.make_async_copy(plan, plan_out, load_sem.at[0])
    save_plan.start()

    def parts(ref):
        return [ref[step * slots : (step + 1) * slots, :] for step in range(steps)]

    inner_conv = convolve(
        [inner[tap].astype(F32) for tap in range(taps)],
        parts(inner_raw),
        inner_taps[...],
        inner_offset[...],
    )
    group_conv = convolve(
        [both_halves(group[tap].astype(F32), group_other[tap].astype(F32)) for tap in range(taps)],
        parts(both),
        weights[: taps + 1, :],
        weights[taps + 1 : taps + 2, :],
    )
    for step in range(steps):
        part = slice(step * slots, (step + 1) * slots)
        driven[part, :] = delta[part, :] * inner_conv[step]
        skipped[part, :] = inner_conv[step] * skip_gain[0]
        maps_in[part, :] = group_conv[step]
    sums[...] = jnp.zeros_like(sums)
    stride = ordered.shape[0] // steps
    ordered[...] = jnp.zeros_like(ordered)
    for position in range(moving):
        slot = plan[0, position]
        for step in range(steps):
            ordered[step * stride + position : step * stride + position + 1, :] = maps_in[
                pl.ds(step * slots + slot, 1), :
            ]
    maps = [ordered[first : first + LANES].T for first in range(0, ordered.shape[0], LANES)]
    copies = []
    for position in range(moving):
        slot = plan[0, position]
        result = advance_slot(
            scan[slot],
            [pl.ds(step * slots + slot, 1) for step in range(steps)],
            driven,
            [decay[pl.ds(step * slots + slot, 1), :] for step in range(steps)],
            sums,
            maps,
            [step * stride + position for step in range(steps)],
        )
        done[position] = jnp.where(slot < live[0], result, jnp.zeros_like(result))
        copies.append(
            pltpu.make_async_copy(done.at[position], scan_next.at[slot], sem.at[position])
        )
        copies[-1].start()
    gated[...] = (sums[...] + skipped[...]) * gate[...]
    pairs = (
        (inner_raw, inner_moved),
        (both, group_moved),
        (gate, gate_moved),
        (delta, delta_moved),
        (decay, decay_moved),
    )
    for _, target in pairs:
        target[...] = jnp.zeros_like(target)
    living = lax.broadcasted_iota(jnp.int32, (slots, LANES), 0) < live[0]
    for step in range(steps):
        part = slice(step * slots, (step + 1) * slots)
        inner_part[step] = jnp.where(living, inner_raw[part, :], 0.0).astype(BF16)
        raw = jnp.where(head == 0, both[part, :width], both[part, width:])
        group_part[step] = jnp.where(living[:, :width], raw, 0.0).astype(BF16)
    base[:, :LANES] = inner[steps].astype(F32)
    group_own = group[steps].astype(F32)
    base[:, LANES:] = jnp.concatenate([group_own, group_own], axis=1)
    for block in range(moved_rows // ROWS):

        @pl.when(plan[0, moving + block * cap] >= 0)
        def _():
            for c in range(cap):
                slot = plan[0, moving + block * cap + c]
                for step in range(steps):
                    row = step * moved_rows + block * ROWS + c
                    for source, target in pairs:
                        target[row : row + 1, :] = source[pl.ds(step * slots + slot, 1), :]

    for copy in copies:
        copy.wait()
    save_plan.wait()


def stay(replicas, cap, scalars, arrays, near):
    receive, own, group_weight, delta_weight = arrays[0], arrays[1], arrays[4], arrays[5]
    inner, scan = arrays[-3], arrays[-1]
    taps, slots, _ = inner.shape
    rows = own.shape[0]
    steps = rows // slots
    moving = slots // 2
    blocks = sum(block_counts(replicas))
    moved_rows = blocks * ROWS
    width, features = group_weight.shape
    full = pltpu.VMEM((rows, LANES), F32)
    moved = pltpu.VMEM((steps * moved_rows, LANES), F32)
    plan_shape = (1, round_up(moving + blocks * cap + 1, LANES))

    def like(value):
        return pltpu.VMEM(value.shape, value.dtype)

    far = [in_hbm(value) for value in arrays]
    return pl.pallas_call(
        functools.partial(stay_kernel, replicas, cap),
        out_shape=[
            pltpu.VMEM(plan_shape, jnp.int32),
            full,
            pltpu.VMEM((2 * round_up(taps + 3, ROWS), LANES), F32),
            pltpu.VMEM((slots, 2 * LANES), F32),
            pltpu.VMEM((steps, slots, LANES), BF16),
            pltpu.VMEM((steps, slots, width), BF16),
        ]
        + [moved] * 5
        + [jax.ShapeDtypeStruct(scan.shape, BF16)],
        in_specs=[SMEM] * len(scalars) + [HBM] * len(far) + [VMEM] * len(near),
        out_specs=[VMEM] * 11 + [HBM],
        scratch_shapes=[
            pltpu.SMEM(plan_shape, jnp.int32),
            pltpu.SMEM(receive.shape, jnp.int32),
            like(own),
            pltpu.VMEM((features, 2 * LANES), BF16),
            pltpu.VMEM((2 * width + 2 * ROWS, features), BF16),
            like(delta_weight),
        ]
        + [like(value) for value in arrays[6:]]
        + [pltpu.SMEM((replicas * cap + 1,), jnp.int32)]
        + [pltpu.VMEM((rows, LANES), F32)] * 9
        + [
            pltpu.VMEM((round_up(rows, LANES), LANES), F32),
            pltpu.VMEM((moving,) + scan.shape[1:], BF16),
            pltpu.SemaphoreType.DMA((moving,)),
            pltpu.SemaphoreType.DMA((16,)),
        ],
        compiler_params=pltpu.CompilerParams(vmem_limit_bytes=MEDIUM_LIMIT),
        cost_estimate=pl.CostEstimate(
            flops=300_000_000, bytes_accessed=6_000_000, transcendentals=100_000
        ),
        name="advance_staying",
    )(*scalars, *far, *near)


def arrive_kernel(
    replicas,
    cap,
    first,
    last,
    plan_near,
    weights,
    inner_moved,
    group_moved,
    gate_moved,
    delta_moved,
    decay_moved,
    gated_in,
    table_in,
    inner_part,
    group_part,
    scan_in,
    *refs,
):
    del scan_in
    if last:
        arrived = refs[:-15]
        gated_out, inner_next, group_next, scan_next = refs[-15:-11]
        gated, table = refs[-11:-9]
        gated_cast, inner_cast, group_cast = refs[-9:-6]
    else:
        arrived = refs[:-9]
        gated, table, scan_next = refs[-9:-6]
    plan, driven, sums, ordered, done, sem = refs[-6:]
    steps, slots, width = group_part.shape
    taps = steps + 1
    moving = slots // 2
    state_rows = scan_next.shape[1]
    head = lax.axis_index("head")
    load = pltpu.make_async_copy(plan_near, plan, sem.at[0])
    load.start()
    blocks = blocks_of(arrived)
    stored = inner_moved.shape[0] // steps
    moved_rows = len(blocks) * ROWS
    if last:
        copies = [
            pltpu.make_async_copy(source, target, sem.at[1 + place])
            for place, (source, target) in enumerate(
                [
                    (inner_part, inner_next.at[pl.ds(1, steps)]),
                    (group_part, group_next.at[pl.ds(1, steps)]),
                ]
            )
        ]
        for copy in copies:
            copy.start()

    def parts(ref):
        starts = [step * stored + first * ROWS for step in range(steps)]
        return [ref[start : start + moved_rows, :] for start in starts]

    kinds = [[] for _ in range(2 * taps)]
    for ref in blocks:
        block = ref[cap * state_rows :, :].astype(F32)
        for kind in range(2 * taps):
            kinds[kind].append(block[kind * ROWS : (kind + 1) * ROWS])
    windows = [jnp.concatenate(kind, axis=0) for kind in kinds]
    later = round_up(taps + 3, ROWS)
    inner_conv = convolve(
        windows[:taps],
        parts(inner_moved),
        weights[later : later + taps + 1, :],
        weights[later + taps + 1 : later + taps + 2, :],
    )
    group_conv = convolve(
        windows[taps:],
        parts(group_moved),
        weights[: taps + 1, :],
        weights[taps + 1 : taps + 2, :],
    )
    for step, delta in enumerate(parts(delta_moved)):
        driven[step * moved_rows : (step + 1) * moved_rows, :] = delta * inner_conv[step]
    stride = ordered.shape[0] // steps
    maps = transposed(group_conv, ordered, stride)
    sums[...] = jnp.zeros_like(sums)
    gated[...] = gated_in[...]
    table[...] = table_in[...]
    load.wait()
    live = plan[0, plan.shape[1] - 1]

    def each(act):
        for block in range(len(blocks)):
            entry = moving + (first + block) * cap

            @pl.when(plan[0, entry] >= 0)
            def _():
                for c in range(cap):
                    act(block, c, plan[0, entry + c])

    def store(block, c, slot):
        place = block * cap + c
        return pltpu.make_async_copy(done.at[place], scan_next.at[slot], sem.at[4 + place])

    def advance(block, c, slot):
        place = block * ROWS + c
        rows = [step * moved_rows + place for step in range(steps)]
        result = advance_slot(
            blocks[block][c * state_rows : (c + 1) * state_rows, :],
            [slice(row, row + 1) for row in rows],
            driven,
            [
                decay_moved[row : row + 1, :]
                for row in (step * stored + first * ROWS + place for step in range(steps))
            ],
            sums,
            maps,
            [step * stride + place for step in range(steps)],
        )
        done[block * cap + c] = jnp.where(slot < live, result, jnp.zeros_like(result))
        store(block, c, slot).start()

    each(advance)
    for step, gate in enumerate(parts(gate_moved)):
        part = slice(step * moved_rows, (step + 1) * moved_rows)
        skipped = inner_conv[step] * weights[taps + 2 : taps + 3, :]
        sums[part, :] = (sums[part, :] + skipped) * gate
    driven[:moved_rows, :] = windows[taps - 1]
    driven[moved_rows : 2 * moved_rows, :] = windows[2 * taps - 1]

    def scatter(block, c, slot):
        place = block * ROWS + c
        for step in range(steps):
            row = step * moved_rows + place
            gated[pl.ds(step * slots + slot, 1), :] = sums[row : row + 1, :]
        table[pl.ds(slot, 1), :] = jnp.concatenate(
            [driven[place : place + 1, :], driven[moved_rows + place : moved_rows + place + 1, :]],
            axis=1,
        )

    each(scatter)
    if last:
        living = lax.broadcasted_iota(jnp.int32, (slots, LANES), 0) < live
        for step in range(steps):
            part = slice(step * slots, (step + 1) * slots)
            gated_cast[step] = jnp.where(living, gated[part, :], 0.0).astype(BF16)
        inner_cast[0] = jnp.where(living, table[:, :LANES], 0.0).astype(BF16)
        carried = jnp.where(head == 0, table[:, LANES : LANES + width], table[:, LANES + width :])
        group_cast[0] = jnp.where(living[:, :width], carried, 0.0).astype(BF16)
        ends = [
            pltpu.make_async_copy(source, target, semaphore)
            for source, target, semaphore in (
                (gated_cast, gated_out, sem.at[0]),
                (inner_cast, inner_next.at[pl.ds(0, 1)], sem.at[3]),
                (group_cast, group_next.at[pl.ds(0, 1)], sem.at[sem.shape[0] - 1]),
            )
        ]
        for copy in ends:
            copy.start()
        for copy in copies + ends:
            copy.wait()
    each(lambda block, c, slot: store(block, c, slot).wait())


def arrive(replicas, cap, first, last, operands, scan_next, arrived):
    inner_moved, gated, table, inner_part, group_part = operands[2], *operands[7:]
    steps, slots, width = group_part.shape
    blocks = sum(value.shape[0] for value in arrived)
    moved = (steps * blocks * ROWS, LANES)
    carried = [pltpu.VMEM(value.shape, F32) for value in (gated, table)]
    scan_shape = jax.ShapeDtypeStruct(scan_next.shape, BF16)
    if last:
        outs = [
            jax.ShapeDtypeStruct((steps, slots, LANES), BF16),
            jax.ShapeDtypeStruct((steps + 1, slots, LANES), BF16),
            jax.ShapeDtypeStruct((steps + 1, slots, width), BF16),
            scan_shape,
        ]
        scratch = carried + [
            pltpu.VMEM((steps, slots, LANES), BF16),
            pltpu.VMEM((1, slots, LANES), BF16),
            pltpu.VMEM((1, slots, width), BF16),
        ]
        specs = [HBM] * 4
    else:
        outs, scratch, specs = carried + [scan_shape], [], [VMEM, VMEM, HBM]
    plan = operands[0]
    return pl.pallas_call(
        functools.partial(arrive_kernel, replicas, cap, first, last),
        out_shape=outs,
        in_specs=[VMEM] * len(operands) + [HBM] + [VMEM] * len(arrived),
        out_specs=specs,
        scratch_shapes=scratch
        + [
            pltpu.SMEM(plan.shape, plan.dtype),
            pltpu.VMEM(moved, F32),
            pltpu.VMEM(moved, F32),
            pltpu.VMEM((round_up(moved[0], LANES), LANES), F32),
            pltpu.VMEM((blocks * cap,) + scan_next.shape[1:], BF16),
            pltpu.SemaphoreType.DMA((blocks * cap + 5,)),
        ],
        input_output_aliases={len(operands): len(outs) - 1},
        compiler_params=pltpu.CompilerParams(
            vmem_limit_bytes=SMALL_LIMIT if masks_of(replicas) else LARGE_LIMIT
        ),
        cost_estimate=pl.CostEstimate(
            flops=10_000_000, bytes_accessed=2_000_000, transcendentals=0
        ),
        name="advance_last" if last else "advance_arrived",
    )(*operands, scan_next, *arrived)


def swap_heads(value):
    return lax.ppermute(value, "head", [(0, 1), (1, 0)])


def exchange(replicas, arrays):
    masks = masks_of(replicas)
    if not masks:
        return [lax.all_to_all(arrays[0], "dp", 0, 0, tiled=True)]
    moved = [
        lax.ppermute(array, "dp", [(source, source ^ mask) for source in range(replicas)])
        for mask, array in zip(masks, arrays[1:])
    ]
    half = replicas // 2
    halves = [list(range(half)), list(range(half, replicas))]
    within = lax.all_to_all(arrays[0], "dp", 0, 0, axis_index_groups=halves, tiled=True)
    return [within] + moved


def per_device(
    replicas,
    tokens,
    inner_weight,
    gate_weight,
    group_weight,
    delta_weight,
    inner_taps,
    inner_offset,
    group_taps,
    group_offset,
    decay_log,
    delta_bias,
    skip_gain,
    inner_window,
    group_window,
    scan_state,
    send_list,
    receive_list,
    live_count,
):
    steps, slots, half = tokens.shape
    cap = send_list.shape[1] // replicas
    scan = jnp.transpose(scan_state, (0, 2, 1))
    inner = jnp.transpose(inner_window, (1, 0, 2))
    group = jnp.transpose(group_window, (1, 0, 2))
    own = tokens.reshape(steps * slots, half)

    group_weight = group_weight.T
    inner_offset = inner_offset[None]
    small = jnp.concatenate([group_taps, group_offset[None]], axis=0)
    group_other = swap_heads(group)
    swapped = [swap_heads(value) for value in (own, group_weight, small)]
    blocks = pack(replicas, cap, send_list, scan, inner, group, group_other, swapped)
    arrived = exchange(replicas, blocks)
    plan, gated, weights, table, inner_part, group_part, *moved, scan_next = stay(
        replicas,
        cap,
        (decay_log, delta_bias, skip_gain, live_count),
        (
            receive_list,
            own,
            inner_weight,
            gate_weight,
            group_weight,
            delta_weight.T,
            inner_taps,
            inner_offset,
            inner,
            group,
            scan,
        ),
        (swapped[0], swapped[1], small, swapped[2], group_other),
    )
    split = max(0, len(arrived) - LAST)
    first = sum(value.shape[0] for value in arrived[:split])
    if split:
        operands = (plan, weights, *moved, gated, table, inner_part, group_part)
        gated, table, scan_next = arrive(
            replicas, cap, 0, False, operands, scan_next, arrived[:split]
        )
    operands = (plan, weights, *moved, gated, table, inner_part, group_part)
    gated, inner_next, group_next, scan_next = arrive(
        replicas, cap, first, True, operands, scan_next, arrived[split:]
    )
    return (
        gated,
        jnp.transpose(inner_next, (1, 0, 2)),
        jnp.transpose(group_next, (1, 0, 2)),
        jnp.transpose(scan_next, (0, 2, 1)),
    )


def solution(mesh):
    in_specs = (
        P(None, ("grp", "dp"), "head"),
        P(None, "head"),
        P(None, "head"),
        P(None, "head"),
        P(None, "head"),
        P(None, "head"),
        P("head"),
        P(None, "head"),
        P("head"),
        P("head"),
        P("head"),
        P("head"),
        P(("grp", "dp"), None, "head"),
        P(("grp", "dp"), None, "head"),
        P(("grp", "dp"), "head", None),
        P(("grp", "dp"), None),
        P(("grp", "dp"), None),
        P(("grp", "dp")),
    )
    out_specs = (
        P(None, ("grp", "dp"), "head"),
        P(("grp", "dp"), None, "head"),
        P(("grp", "dp"), None, "head"),
        P(("grp", "dp"), "head", None),
    )
    return jax.shard_map(
        functools.partial(per_device, mesh.shape["dp"]),
        mesh=mesh,
        in_specs=in_specs,
        out_specs=out_specs,
        check_vma=False,
    )
```

```python
import functools

import jax
import jax.numpy as jnp
from jax import lax
from jax.experimental import pallas as pl
from jax.experimental.pallas import tpu as pltpu
from jax.sharding import PartitionSpec as P

F32 = jnp.float32
BF16 = jnp.bfloat16
SMALL_LIMIT = 8 * 1024 * 1024
MEDIUM_LIMIT = 16 * 1024 * 1024
LARGE_LIMIT = 48 * 1024 * 1024
MAX_ROUNDS = 16
LAST = 5
LANES = 128
ROWS = 8
MAX_SETS = 64

VMEM = pl.BlockSpec(memory_space=pltpu.VMEM)
SMEM = pl.BlockSpec(memory_space=pltpu.SMEM)
HBM = pl.BlockSpec(memory_space=pl.ANY)


def in_hbm(value):
    return pltpu.with_memory_space_constraint(value, pltpu.HBM)


def in_vmem(value):
    return pltpu.with_memory_space_constraint(value, pltpu.VMEM)


def round_up(value, step):
    return -(-value // step) * step


def silu(value):
    return value * jax.nn.sigmoid(value)


def rounded(value):
    return value.astype(BF16).astype(F32)


def rounds_of(replicas):
    if replicas > MAX_ROUNDS or replicas & (replicas - 1):
        return []
    light = list(range(1, replicas // 2))
    heavy = list(range(replicas // 2, replicas))
    return heavy + light


def partner(replicas, mask):
    return jnp.bitwise_xor(lax.axis_index("dp"), mask)


def both_halves(mine, theirs):
    first = lax.axis_index("head") == 0
    return jnp.concatenate(
        [jnp.where(first, mine, theirs), jnp.where(first, theirs, mine)], axis=-1
    )


def destinations(replicas, outs):
    rounds = rounds_of(replicas)
    if rounds:
        return [(ref.at[0], partner(replicas, mask)) for ref, mask in zip(outs, rounds)]
    return [(outs[0].at[target], target) for target in range(replicas)]


def states_kernel(replicas, cap, scan, send, inner, group, *refs):
    outs, (picked, group_out, indices_out) = refs[:-11], refs[-11:-8]
    indices, inner_in, table, load_sem, group_sem, list_sem, save_sem, sem = refs[-8:]
    load_list = pltpu.make_async_copy(send, indices, list_sem)
    load_list.start()
    load = pltpu.make_async_copy(inner, inner_in, load_sem)
    load.start()
    load_group = pltpu.make_async_copy(group, group_out, group_sem)
    load_group.start()
    state_rows = scan.shape[1]
    blocks = destinations(replicas, outs)
    load_list.wait()
    save = pltpu.make_async_copy(indices, indices_out, save_sem)
    save.start()
    plan = []
    for block, (ref, target) in enumerate(blocks):
        for c in range(cap):
            plan.append((block, ref, c, indices[0, target * cap + c]))

    def each(act):
        for place, (_, ref, c, index) in enumerate(plan):

            @pl.when(index >= 0)
            def _():
                act(
                    pltpu.make_async_copy(
                        scan.at[index],
                        ref.at[pl.ds(c * state_rows, state_rows)],
                        sem.at[place],
                    )
                )

    each(lambda copy: copy.start())
    load.wait()
    taps = inner_in.shape[0]
    for tap in range(taps):
        table[:, tap * LANES : (tap + 1) * LANES] = inner_in[tap].astype(F32)
    picked[...] = jnp.zeros_like(picked)
    for block, _, c, index in plan:
        row = table[pl.ds(jnp.maximum(index, 0), 1), :]
        for tap in range(taps):
            picked[block, tap * ROWS + c : tap * ROWS + c + 1, :] = row[
                :, tap * LANES : (tap + 1) * LANES
            ]
    load_group.wait()
    save.wait()
    each(lambda copy: copy.wait())


def windows_kernel(replicas, cap, state_rows, indices_in, group, group_other, picked_in, *refs):
    count = max(1, len(rounds_of(replicas)))
    outs = refs[-4 - count : -4]
    indices, table, picked, sem = refs[-4:]
    load = pltpu.make_async_copy(indices_in, indices, sem)
    load.start()
    taps = group.shape[0]
    for tap in range(taps):
        table[:, tap * LANES : (tap + 1) * LANES] = both_halves(
            group[tap].astype(F32), group_other[tap].astype(F32)
        )
    picked[...] = jnp.zeros_like(picked)
    load.wait()
    for block, (ref, target) in enumerate(destinations(replicas, outs)):
        for c in range(cap):
            index = jnp.maximum(indices[0, target * cap + c], 0)
            row = table[pl.ds(index, 1), :]
            for tap in range(taps):
                picked[block, tap * ROWS + c : tap * ROWS + c + 1, :] = row[
                    :, tap * LANES : (tap + 1) * LANES
                ]
        ref[cap * state_rows :, :] = jnp.concatenate(
            [picked_in[block], picked[block]], axis=0
        ).astype(BF16)


def pack(replicas, cap, send_list, scan, inner, group, group_other, swapped):
    rounds = rounds_of(replicas)
    count = max(1, len(rounds))
    per_block = 1 if rounds else replicas
    taps, slots, _ = inner.shape
    rows = cap * scan.shape[1] + 2 * taps * ROWS
    blocks = count * per_block
    shapes = [pltpu.VMEM((per_block, rows, LANES), BF16)] * count
    half = (blocks, taps * ROWS, LANES)
    limit = SMALL_LIMIT if rounds else MEDIUM_LIMIT
    *states, picked, group_near, indices = pl.pallas_call(
        functools.partial(states_kernel, replicas, cap),
        out_shape=shapes
        + [
            pltpu.VMEM(half, F32),
            pltpu.VMEM(group.shape, BF16),
            pltpu.VMEM(send_list.shape, jnp.int32),
        ],
        in_specs=[HBM] * 4,
        out_specs=[VMEM] * (count + 3),
        scratch_shapes=[
            pltpu.SMEM(send_list.shape, jnp.int32),
            pltpu.VMEM(inner.shape, BF16),
            pltpu.VMEM((slots, taps * LANES), F32),
            pltpu.SemaphoreType.DMA,
            pltpu.SemaphoreType.DMA,
            pltpu.SemaphoreType.DMA,
            pltpu.SemaphoreType.DMA,
            pltpu.SemaphoreType.DMA((blocks * cap,)),
        ],
        compiler_params=pltpu.CompilerParams(vmem_limit_bytes=limit),
        cost_estimate=pl.CostEstimate(flops=0, bytes_accessed=2_000_000, transcendentals=0),
        name="pack_states",
    )(in_hbm(scan), in_hbm(send_list), in_hbm(inner), in_hbm(group))
    near = [in_vmem(value) for value in states]
    return pl.pallas_call(
        functools.partial(windows_kernel, replicas, cap, scan.shape[1]),
        out_shape=shapes,
        in_specs=[VMEM] * (4 + count) + [HBM] * len(swapped),
        out_specs=[VMEM] * count,
        scratch_shapes=[
            pltpu.SMEM(send_list.shape, jnp.int32),
            pltpu.VMEM((slots, taps * LANES), F32),
            pltpu.VMEM(half, F32),
            pltpu.SemaphoreType.DMA,
        ],
        input_output_aliases={4 + place: place for place in range(count)},
        compiler_params=pltpu.CompilerParams(vmem_limit_bytes=limit),
        cost_estimate=pl.CostEstimate(flops=0, bytes_accessed=500_000, transcendentals=0),
        name="pack_windows",
    )(indices, group_near, group_other, picked, *near, *swapped)


def sources_of(replicas):
    rounds = rounds_of(replicas)
    if rounds:
        return [partner(replicas, mask) for mask in rounds]
    return list(range(replicas))


def make_plan(replicas, cap, receive, slots, plan, inverse):
    moving = slots // 2
    kept = 0
    for entry in range(replicas * cap):
        inverse[entry] = -1
    for slot in range(slots):
        entry = receive[0, slot]
        stays = entry < 0
        plan[0, jnp.where(stays, kept, moving)] = slot
        inverse[jnp.where(stays, replicas * cap, entry)] = slot
        kept = kept + jnp.where(stays, 1, 0)
    for block, source in enumerate(sources_of(replicas)):
        for c in range(cap):
            plan[0, moving + block * cap + c] = inverse[source * cap + c]


def convolve(carried, raw, weights, offset):
    joined = carried + raw
    results = []
    for step in range(len(raw)):
        summed = offset
        for tap in range(len(carried) + 1):
            summed = summed + joined[step + tap] * weights[tap : tap + 1, :]
        results.append(rounded(silu(summed)))
    return results


def transposed(rows, scratch, stride):
    scratch[...] = jnp.zeros_like(scratch)
    for step, value in enumerate(rows):
        scratch[step * stride : step * stride + value.shape[0], :] = value
    return [scratch[first : first + LANES].T for first in range(0, scratch.shape[0], LANES)]


def advance_slot(state, rows, driven, decays, sums, maps, lanes):
    hidden = state.astype(F32)
    width = state.shape[0]
    for row, decay, lane in zip(rows, decays, lanes):
        piece = maps[lane // LANES]
        column = piece[:, lane % LANES : lane % LANES + 1]
        hidden = decay * hidden + driven[row, :] * column[:width]
        sums[row, :] = jnp.sum(hidden * column[width:], axis=0, keepdims=True)
        result = hidden.astype(BF16)
        hidden = result.astype(F32)
    return result


def stay_kernel(
    replicas,
    cap,
    decay_log,
    delta_bias,
    skip_gain,
    live,
    receive_hbm,
    own_hbm,
    inner_weight,
    gate_weight,
    group_weight,
    delta_weight,
    inner_taps_hbm,
    inner_offset_hbm,
    inner_hbm,
    group_hbm,
    scan_hbm,
    other,
    group_weight_other,
    small,
    small_other,
    group_other,
    *refs,
):
    count = (len(refs) - 38) // 2
    light_in = refs[:count]
    light_out = refs[count + 12 : 2 * count + 12]
    (
        plan_out,
        gated,
        weights,
        base,
        inner_part,
        group_part,
        inner_moved,
        group_moved,
        gate_moved,
        delta_moved,
        decay_moved,
        scan_next,
    ) = refs[count : count + 12]
    (
        plan,
        receive,
        own,
        wide,
        tall,
        delta_row,
        inner_taps,
        inner_offset,
        inner,
        group,
        scan,
        inverse,
        inner_raw,
        both,
        gate,
        delta,
        decay,
        driven,
        skipped,
        sums,
        maps_in,
        ordered,
        done,
        sem,
        load_sem,
        light_sem,
    ) = refs[-26:]
    passed = [
        pltpu.make_async_copy(source, target, light_sem.at[place])
        for place, (source, target) in enumerate(zip(light_in, light_out))
    ]
    for copy in passed:
        copy.start()
    taps, slots, _ = inner.shape
    rows, half = own.shape
    steps = rows // slots
    moving = slots // 2
    moved_rows = inner_moved.shape[0] // steps
    width = group.shape[2]
    head = lax.axis_index("head")

    def band(place):
        return tall.at[pl.ds(pl.multiple_of(place * width, width), width)]

    pairs = [
        (receive_hbm, receive),
        (own_hbm, own),
        (inner_weight, wide.at[:, pl.ds(0, LANES)]),
        (gate_weight, wide.at[:, pl.ds(LANES, LANES)]),
        (delta_weight, delta_row),
        (group_weight, band(head)),
        (group_weight_other, band(1 - head)),
        (inner_taps_hbm, inner_taps),
        (inner_offset_hbm, inner_offset),
        (inner_hbm, inner),
        (group_hbm, group),
        (scan_hbm, scan),
    ]
    loads = [
        pltpu.make_async_copy(source, target, load_sem.at[place])
        for place, (source, target) in enumerate(pairs)
    ]
    for load in loads:
        load.start()
    loads[0].wait()
    make_plan(replicas, cap, receive, slots, plan, inverse)
    for load in loads[1:4]:
        load.wait()
    mine = pl.ds(pl.multiple_of(head * half, half), half)
    theirs = pl.ds(pl.multiple_of((1 - head) * half, half), half)
    flat = jnp.dot(own[...], wide[mine, :], preferred_element_type=F32) + jnp.dot(
        other[...], wide[theirs, :], preferred_element_type=F32
    )
    for load in loads[4:]:
        load.wait()
    first = 2 * width
    tall[first:, :] = jnp.broadcast_to(delta_row[...], (tall.shape[0] - first, 2 * half))

    def across(tokens, part):
        return lax.dot_general(
            tokens, tall[:, part], (((1,), (1,)), ((), ())), preferred_element_type=F32
        )

    deep = across(own[...], mine) + across(other[...], theirs)
    inner_raw[...] = rounded(flat[:, :LANES])
    gate[...] = silu(rounded(flat[:, LANES:]))
    both[...] = rounded(deep[:, :first])
    shifted = rounded(jnp.broadcast_to(deep[:, first : first + 1], (rows, LANES)))
    shifted = shifted + delta_bias[0]
    rate = jnp.maximum(shifted, 0.0) + jnp.log1p(jnp.exp(-jnp.abs(shifted)))
    delta[...] = rate
    decay[...] = jnp.exp(-rate * jnp.exp(jnp.full((1, LANES), decay_log[0], F32)))
    count = taps + 2
    weights[:count, :] = both_halves(small[...], small_other[...])
    weights[count : count + 1, :] = jnp.full((1, LANES), skip_gain[0], F32)
    later = round_up(count + 1, ROWS)
    weights[later : later + taps + 1, :] = inner_taps[...]
    weights[later + taps + 1 : later + taps + 2, :] = inner_offset[...]
    plan[0, plan.shape[1] - 1] = live[0]
    save_plan = pltpu.make_async_copy(plan, plan_out, load_sem.at[0])
    save_plan.start()

    def parts(ref):
        return [ref[step * slots : (step + 1) * slots, :] for step in range(steps)]

    inner_conv = convolve(
        [inner[tap].astype(F32) for tap in range(taps)],
        parts(inner_raw),
        inner_taps[...],
        inner_offset[...],
    )
    group_conv = convolve(
        [both_halves(group[tap].astype(F32), group_other[tap].astype(F32)) for tap in range(taps)],
        parts(both),
        weights[: taps + 1, :],
        weights[taps + 1 : taps + 2, :],
    )
    for step in range(steps):
        part = slice(step * slots, (step + 1) * slots)
        driven[part, :] = delta[part, :] * inner_conv[step]
        skipped[part, :] = inner_conv[step] * skip_gain[0]
        maps_in[part, :] = group_conv[step]
    sums[...] = jnp.zeros_like(sums)
    stride = ordered.shape[0] // steps
    ordered[...] = jnp.zeros_like(ordered)
    for position in range(moving):
        slot = plan[0, position]
        for step in range(steps):
            ordered[step * stride + position : step * stride + position + 1, :] = maps_in[
                pl.ds(step * slots + slot, 1), :
            ]
    maps = [ordered[first : first + LANES].T for first in range(0, ordered.shape[0], LANES)]
    copies = []
    for position in range(moving):
        slot = plan[0, position]
        result = advance_slot(
            scan[slot],
            [pl.ds(step * slots + slot, 1) for step in range(steps)],
            driven,
            [decay[pl.ds(step * slots + slot, 1), :] for step in range(steps)],
            sums,
            maps,
            [step * stride + position for step in range(steps)],
        )
        done[position] = jnp.where(slot < live[0], result, jnp.zeros_like(result))
        copies.append(
            pltpu.make_async_copy(done.at[position], scan_next.at[slot], sem.at[position])
        )
        copies[-1].start()
    gated[...] = (sums[...] + skipped[...]) * gate[...]
    pairs = (
        (inner_raw, inner_moved),
        (both, group_moved),
        (gate, gate_moved),
        (delta, delta_moved),
        (decay, decay_moved),
    )
    for _, target in pairs:
        target[...] = jnp.zeros_like(target)
    living = lax.broadcasted_iota(jnp.int32, (slots, LANES), 0) < live[0]
    for step in range(steps):
        part = slice(step * slots, (step + 1) * slots)
        inner_part[step] = jnp.where(living, inner_raw[part, :], 0.0).astype(BF16)
        raw = jnp.where(head == 0, both[part, :width], both[part, width:])
        group_part[step] = jnp.where(living[:, :width], raw, 0.0).astype(BF16)
    base[:, :LANES] = inner[steps].astype(F32)
    group_own = group[steps].astype(F32)
    base[:, LANES:] = jnp.concatenate([group_own, group_own], axis=1)
    for block in range(moved_rows // ROWS):

        @pl.when(plan[0, moving + block * cap] >= 0)
        def _():
            for c in range(cap):
                slot = plan[0, moving + block * cap + c]
                for step in range(steps):
                    row = step * moved_rows + block * ROWS + c
                    for source, target in pairs:
                        target[row : row + 1, :] = source[pl.ds(step * slots + slot, 1), :]

    for copy in copies:
        copy.wait()
    save_plan.wait()
    for copy in passed:
        copy.wait()


def stay(replicas, cap, scalars, arrays, near, light):
    receive, own, group_weight, delta_weight = arrays[0], arrays[1], arrays[4], arrays[5]
    inner, scan = arrays[-3], arrays[-1]
    taps, slots, _ = inner.shape
    rows = own.shape[0]
    steps = rows // slots
    moving = slots // 2
    blocks = len(sources_of(replicas))
    moved_rows = blocks * ROWS
    width, features = group_weight.shape
    full = pltpu.VMEM((rows, LANES), F32)
    moved = pltpu.VMEM((steps * moved_rows, LANES), F32)
    plan_shape = (1, round_up(moving + blocks * cap + 1, LANES))

    def like(value):
        return pltpu.VMEM(value.shape, value.dtype)

    far = [in_hbm(value) for value in arrays]
    return pl.pallas_call(
        functools.partial(stay_kernel, replicas, cap),
        out_shape=[
            pltpu.VMEM(plan_shape, jnp.int32),
            full,
            pltpu.VMEM((2 * round_up(taps + 3, ROWS), LANES), F32),
            pltpu.VMEM((slots, 2 * LANES), F32),
            pltpu.VMEM((steps, slots, LANES), BF16),
            pltpu.VMEM((steps, slots, width), BF16),
        ]
        + [moved] * 5
        + [jax.ShapeDtypeStruct(scan.shape, BF16)]
        + [pltpu.VMEM(value.shape, BF16) for value in light],
        in_specs=[SMEM] * len(scalars)
        + [HBM] * len(far)
        + [VMEM] * (len(near) + len(light)),
        out_specs=[VMEM] * 11 + [HBM] + [VMEM] * len(light),
        scratch_shapes=[
            pltpu.SMEM(plan_shape, jnp.int32),
            pltpu.SMEM(receive.shape, jnp.int32),
            like(own),
            pltpu.VMEM((features, 2 * LANES), BF16),
            pltpu.VMEM((2 * width + 2 * ROWS, features), BF16),
            like(delta_weight),
        ]
        + [like(value) for value in arrays[6:]]
        + [pltpu.SMEM((replicas * cap + 1,), jnp.int32)]
        + [pltpu.VMEM((rows, LANES), F32)] * 9
        + [
            pltpu.VMEM((round_up(rows, LANES), LANES), F32),
            pltpu.VMEM((moving,) + scan.shape[1:], BF16),
            pltpu.SemaphoreType.DMA((moving,)),
            pltpu.SemaphoreType.DMA((16,)),
            pltpu.SemaphoreType.DMA((max(1, len(light)),)),
        ],
        compiler_params=pltpu.CompilerParams(vmem_limit_bytes=MEDIUM_LIMIT),
        cost_estimate=pl.CostEstimate(
            flops=300_000_000, bytes_accessed=6_000_000, transcendentals=100_000
        ),
        name="advance_staying",
    )(*scalars, *far, *near, *light)


def arrive_kernel(
    replicas,
    cap,
    first,
    last,
    plan_near,
    weights,
    inner_moved,
    group_moved,
    gate_moved,
    delta_moved,
    decay_moved,
    gated_in,
    table_in,
    inner_part,
    group_part,
    scan_in,
    *refs,
):
    del scan_in
    if last:
        arrived = refs[:-15]
        gated_out, inner_next, group_next, scan_next = refs[-15:-11]
        gated, table = refs[-11:-9]
        gated_cast, inner_cast, group_cast = refs[-9:-6]
    else:
        arrived = refs[:-9]
        gated, table, scan_next = refs[-9:-6]
    plan, driven, sums, ordered, done, sem = refs[-6:]
    steps, slots, width = group_part.shape
    taps = steps + 1
    moving = slots // 2
    state_rows = scan_next.shape[1]
    head = lax.axis_index("head")
    load = pltpu.make_async_copy(plan_near, plan, sem.at[0])
    load.start()
    if rounds_of(replicas):
        blocks = [ref.at[0] for ref in arrived]
    else:
        blocks = [arrived[0].at[source] for source in range(replicas)]
    stored = inner_moved.shape[0] // steps
    moved_rows = len(blocks) * ROWS
    if last:
        copies = [
            pltpu.make_async_copy(source, target, sem.at[1 + place])
            for place, (source, target) in enumerate(
                [
                    (inner_part, inner_next.at[pl.ds(1, steps)]),
                    (group_part, group_next.at[pl.ds(1, steps)]),
                ]
            )
        ]
        for copy in copies:
            copy.start()

    def parts(ref):
        starts = [step * stored + first * ROWS for step in range(steps)]
        return [ref[start : start + moved_rows, :] for start in starts]

    kinds = [[] for _ in range(2 * taps)]
    for ref in blocks:
        block = ref[cap * state_rows :, :].astype(F32)
        for kind in range(2 * taps):
            kinds[kind].append(block[kind * ROWS : (kind + 1) * ROWS])
    windows = [jnp.concatenate(kind, axis=0) for kind in kinds]
    later = round_up(taps + 3, ROWS)
    inner_conv = convolve(
        windows[:taps],
        parts(inner_moved),
        weights[later : later + taps + 1, :],
        weights[later + taps + 1 : later + taps + 2, :],
    )
    group_conv = convolve(
        windows[taps:],
        parts(group_moved),
        weights[: taps + 1, :],
        weights[taps + 1 : taps + 2, :],
    )
    for step, delta in enumerate(parts(delta_moved)):
        driven[step * moved_rows : (step + 1) * moved_rows, :] = delta * inner_conv[step]
    stride = ordered.shape[0] // steps
    maps = transposed(group_conv, ordered, stride)
    sums[...] = jnp.zeros_like(sums)
    gated[...] = gated_in[...]
    table[...] = table_in[...]
    load.wait()
    live = plan[0, plan.shape[1] - 1]

    def each(act):
        for block in range(len(blocks)):
            entry = moving + (first + block) * cap

            @pl.when(plan[0, entry] >= 0)
            def _():
                for c in range(cap):
                    act(block, c, plan[0, entry + c])

    def store(block, c, slot):
        place = block * cap + c
        return pltpu.make_async_copy(done.at[place], scan_next.at[slot], sem.at[4 + place])

    def advance(block, c, slot):
        place = block * ROWS + c
        rows = [step * moved_rows + place for step in range(steps)]
        result = advance_slot(
            blocks[block][c * state_rows : (c + 1) * state_rows, :],
            [slice(row, row + 1) for row in rows],
            driven,
            [
                decay_moved[row : row + 1, :]
                for row in (step * stored + first * ROWS + place for step in range(steps))
            ],
            sums,
            maps,
            [step * stride + place for step in range(steps)],
        )
        done[block * cap + c] = jnp.where(slot < live, result, jnp.zeros_like(result))
        store(block, c, slot).start()

    each(advance)
    for step, gate in enumerate(parts(gate_moved)):
        part = slice(step * moved_rows, (step + 1) * moved_rows)
        skipped = inner_conv[step] * weights[taps + 2 : taps + 3, :]
        sums[part, :] = (sums[part, :] + skipped) * gate
    driven[:moved_rows, :] = windows[taps - 1]
    driven[moved_rows : 2 * moved_rows, :] = windows[2 * taps - 1]

    def scatter(block, c, slot):
        place = block * ROWS + c
        for step in range(steps):
            row = step * moved_rows + place
            gated[pl.ds(step * slots + slot, 1), :] = sums[row : row + 1, :]
        table[pl.ds(slot, 1), :] = jnp.concatenate(
            [driven[place : place + 1, :], driven[moved_rows + place : moved_rows + place + 1, :]],
            axis=1,
        )

    each(scatter)
    if last:
        living = lax.broadcasted_iota(jnp.int32, (slots, LANES), 0) < live
        for step in range(steps):
            part = slice(step * slots, (step + 1) * slots)
            gated_cast[step] = jnp.where(living, gated[part, :], 0.0).astype(BF16)
        inner_cast[0] = jnp.where(living, table[:, :LANES], 0.0).astype(BF16)
        carried = jnp.where(head == 0, table[:, LANES : LANES + width], table[:, LANES + width :])
        group_cast[0] = jnp.where(living[:, :width], carried, 0.0).astype(BF16)
        ends = [
            pltpu.make_async_copy(source, target, semaphore)
            for source, target, semaphore in (
                (gated_cast, gated_out, sem.at[0]),
                (inner_cast, inner_next.at[pl.ds(0, 1)], sem.at[3]),
                (group_cast, group_next.at[pl.ds(0, 1)], sem.at[sem.shape[0] - 1]),
            )
        ]
        for copy in ends:
            copy.start()
        for copy in copies + ends:
            copy.wait()
    each(lambda block, c, slot: store(block, c, slot).wait())


def arrive(replicas, cap, first, last, operands, scan_next, arrived):
    inner_moved, gated, table, inner_part, group_part = operands[2], *operands[7:]
    steps, slots, width = group_part.shape
    blocks = len(arrived) if rounds_of(replicas) else replicas
    moved = (steps * blocks * ROWS, LANES)
    carried = [pltpu.VMEM(value.shape, F32) for value in (gated, table)]
    scan_shape = jax.ShapeDtypeStruct(scan_next.shape, BF16)
    if last:
        outs = [
            jax.ShapeDtypeStruct((steps, slots, LANES), BF16),
            jax.ShapeDtypeStruct((steps + 1, slots, LANES), BF16),
            jax.ShapeDtypeStruct((steps + 1, slots, width), BF16),
            scan_shape,
        ]
        scratch = carried + [
            pltpu.VMEM((steps, slots, LANES), BF16),
            pltpu.VMEM((1, slots, LANES), BF16),
            pltpu.VMEM((1, slots, width), BF16),
        ]
        specs = [HBM] * 4
    else:
        outs, scratch, specs = carried + [scan_shape], [], [VMEM, VMEM, HBM]
    plan = operands[0]
    return pl.pallas_call(
        functools.partial(arrive_kernel, replicas, cap, first, last),
        out_shape=outs,
        in_specs=[VMEM] * len(operands) + [HBM] + [VMEM] * len(arrived),
        out_specs=specs,
        scratch_shapes=scratch
        + [
            pltpu.SMEM(plan.shape, plan.dtype),
            pltpu.VMEM(moved, F32),
            pltpu.VMEM(moved, F32),
            pltpu.VMEM((round_up(moved[0], LANES), LANES), F32),
            pltpu.VMEM((blocks * cap,) + scan_next.shape[1:], BF16),
            pltpu.SemaphoreType.DMA((blocks * cap + 5,)),
        ],
        input_output_aliases={len(operands): len(outs) - 1},
        compiler_params=pltpu.CompilerParams(
            vmem_limit_bytes=SMALL_LIMIT if rounds_of(replicas) else LARGE_LIMIT
        ),
        cost_estimate=pl.CostEstimate(
            flops=10_000_000, bytes_accessed=2_000_000, transcendentals=0
        ),
        name="advance_last" if last else "advance_arrived",
    )(*operands, scan_next, *arrived)


def swap_heads(value):
    return lax.ppermute(value, "head", [(0, 1), (1, 0)])


def exchange(replicas, blocks):
    rounds = rounds_of(replicas)
    if not rounds:
        return [lax.all_to_all(blocks[0], "dp", 0, 0, tiled=True)]
    return [
        lax.ppermute(block, "dp", [(source, source ^ mask) for source in range(replicas)])
        for mask, block in zip(rounds, blocks)
    ]


def per_device(
    replicas,
    tokens,
    inner_weight,
    gate_weight,
    group_weight,
    delta_weight,
    inner_taps,
    inner_offset,
    group_taps,
    group_offset,
    decay_log,
    delta_bias,
    skip_gain,
    inner_window,
    group_window,
    scan_state,
    send_list,
    receive_list,
    live_count,
):
    steps, slots, half = tokens.shape
    cap = send_list.shape[1] // replicas
    scan = jnp.transpose(scan_state, (0, 2, 1))
    inner = jnp.transpose(inner_window, (1, 0, 2))
    group = jnp.transpose(group_window, (1, 0, 2))
    own = tokens.reshape(steps * slots, half)

    group_weight = group_weight.T
    inner_offset = inner_offset[None]
    small = jnp.concatenate([group_taps, group_offset[None]], axis=0)
    group_other = swap_heads(group)
    swapped = [swap_heads(value) for value in (own, group_weight, small)]
    blocks = list(pack(replicas, cap, send_list, scan, inner, group, group_other, swapped))
    rounds = rounds_of(replicas)
    delayed = [place for place, mask in enumerate(rounds) if mask < replicas // 2]
    plan, gated, weights, table, inner_part, group_part, *moved = stay(
        replicas,
        cap,
        (decay_log, delta_bias, skip_gain, live_count),
        (
            receive_list,
            own,
            inner_weight,
            gate_weight,
            group_weight,
            delta_weight.T,
            inner_taps,
            inner_offset,
            inner,
            group,
            scan,
        ),
        (swapped[0], swapped[1], small, swapped[2], group_other),
        [blocks[place] for place in delayed],
    )
    moved, scan_next, light = moved[:5], moved[5], moved[6:]
    for place, block in zip(delayed, light):
        blocks[place] = block
    arrived = exchange(replicas, blocks)
    first = max(0, len(arrived) - LAST)
    if first:
        operands = (plan, weights, *moved, gated, table, inner_part, group_part)
        gated, table, scan_next = arrive(
            replicas, cap, 0, False, operands, scan_next, arrived[:first]
        )
    operands = (plan, weights, *moved, gated, table, inner_part, group_part)
    gated, inner_next, group_next, scan_next = arrive(
        replicas, cap, first, True, operands, scan_next, arrived[first:]
    )
    return (
        gated,
        jnp.transpose(inner_next, (1, 0, 2)),
        jnp.transpose(group_next, (1, 0, 2)),
        jnp.transpose(scan_next, (0, 2, 1)),
    )


def solution(mesh):
    in_specs = (
        P(None, ("grp", "dp"), "head"),
        P(None, "head"),
        P(None, "head"),
        P(None, "head"),
        P(None, "head"),
        P(None, "head"),
        P("head"),
        P(None, "head"),
        P("head"),
        P("head"),
        P("head"),
        P("head"),
        P(("grp", "dp"), None, "head"),
        P(("grp", "dp"), None, "head"),
        P(("grp", "dp"), "head", None),
        P(("grp", "dp"), None),
        P(("grp", "dp"), None),
        P(("grp", "dp")),
    )
    out_specs = (
        P(None, ("grp", "dp"), "head"),
        P(("grp", "dp"), None, "head"),
        P(("grp", "dp"), None, "head"),
        P(("grp", "dp"), "head", None),
    )
    return jax.shard_map(
        functools.partial(per_device, mesh.shape["dp"]),
        mesh=mesh,
        in_specs=in_specs,
        out_specs=out_specs,
        check_vma=False,
    )
```

```python
import functools

import jax
import jax.numpy as jnp
from jax import lax
from jax.experimental import pallas as pl
from jax.experimental.pallas import tpu as pltpu
from jax.sharding import PartitionSpec as P

F32 = jnp.float32
BF16 = jnp.bfloat16
SMALL_LIMIT = 8 * 1024 * 1024
MEDIUM_LIMIT = 16 * 1024 * 1024
LARGE_LIMIT = 48 * 1024 * 1024
MAX_ROUNDS = 16
EARLIER = 2
LAST = 2
LANES = 128
ROWS = 8
MAX_SETS = 64

VMEM = pl.BlockSpec(memory_space=pltpu.VMEM)
SMEM = pl.BlockSpec(memory_space=pltpu.SMEM)
HBM = pl.BlockSpec(memory_space=pl.ANY)


def in_hbm(value):
    return pltpu.with_memory_space_constraint(value, pltpu.HBM)


def in_vmem(value):
    return pltpu.with_memory_space_constraint(value, pltpu.VMEM)


def round_up(value, step):
    return -(-value // step) * step


def silu(value):
    return value * jax.nn.sigmoid(value)


def rounded(value):
    return value.astype(BF16).astype(F32)


def rounds_of(replicas):
    if replicas > MAX_ROUNDS or replicas & (replicas - 1):
        return []
    light = list(range(1, replicas // 2))
    heavy = list(range(3 * replicas // 4, replicas)) + list(range(replicas // 2, 3 * replicas // 4))
    return light[:2] + heavy[:2] + light[2:] + heavy[2:]


def partner(replicas, mask):
    return jnp.bitwise_xor(lax.axis_index("dp"), mask)


def both_halves(mine, theirs):
    first = lax.axis_index("head") == 0
    return jnp.concatenate(
        [jnp.where(first, mine, theirs), jnp.where(first, theirs, mine)], axis=-1
    )


def destinations(replicas, outs):
    rounds = rounds_of(replicas)
    if rounds:
        return [(ref.at[0], partner(replicas, mask)) for ref, mask in zip(outs, rounds)]
    return [(outs[0].at[target], target) for target in range(replicas)]


def states_kernel(replicas, cap, scan, send, inner, group, *refs):
    outs, (picked, group_out, indices_out) = refs[:-11], refs[-11:-8]
    indices, inner_in, table, load_sem, group_sem, list_sem, save_sem, sem = refs[-8:]
    load_list = pltpu.make_async_copy(send, indices, list_sem)
    load_list.start()
    load = pltpu.make_async_copy(inner, inner_in, load_sem)
    load.start()
    load_group = pltpu.make_async_copy(group, group_out, group_sem)
    load_group.start()
    state_rows = scan.shape[1]
    blocks = destinations(replicas, outs)
    load_list.wait()
    save = pltpu.make_async_copy(indices, indices_out, save_sem)
    save.start()
    plan = []
    for block, (ref, target) in enumerate(blocks):
        for c in range(cap):
            plan.append((block, ref, c, indices[0, target * cap + c]))

    def each(act):
        for place, (_, ref, c, index) in enumerate(plan):

            @pl.when(index >= 0)
            def _():
                act(
                    pltpu.make_async_copy(
                        scan.at[index],
                        ref.at[pl.ds(c * state_rows, state_rows)],
                        sem.at[place],
                    )
                )

    each(lambda copy: copy.start())
    load.wait()
    taps = inner_in.shape[0]
    for tap in range(taps):
        table[:, tap * LANES : (tap + 1) * LANES] = inner_in[tap].astype(F32)
    picked[...] = jnp.zeros_like(picked)
    for block, _, c, index in plan:
        row = table[pl.ds(jnp.maximum(index, 0), 1), :]
        for tap in range(taps):
            picked[block, tap * ROWS + c : tap * ROWS + c + 1, :] = row[
                :, tap * LANES : (tap + 1) * LANES
            ]
    load_group.wait()
    save.wait()
    each(lambda copy: copy.wait())


def windows_kernel(replicas, cap, state_rows, indices_in, group, group_other, picked_in, *refs):
    count = max(1, len(rounds_of(replicas)))
    outs = refs[-4 - count : -4]
    indices, table, picked, sem = refs[-4:]
    load = pltpu.make_async_copy(indices_in, indices, sem)
    load.start()
    taps = group.shape[0]
    for tap in range(taps):
        table[:, tap * LANES : (tap + 1) * LANES] = both_halves(
            group[tap].astype(F32), group_other[tap].astype(F32)
        )
    picked[...] = jnp.zeros_like(picked)
    load.wait()
    for block, (ref, target) in enumerate(destinations(replicas, outs)):
        for c in range(cap):
            index = jnp.maximum(indices[0, target * cap + c], 0)
            row = table[pl.ds(index, 1), :]
            for tap in range(taps):
                picked[block, tap * ROWS + c : tap * ROWS + c + 1, :] = row[
                    :, tap * LANES : (tap + 1) * LANES
                ]
        ref[cap * state_rows :, :] = jnp.concatenate(
            [picked_in[block], picked[block]], axis=0
        ).astype(BF16)


def pack(replicas, cap, send_list, scan, inner, group, group_other, swapped):
    rounds = rounds_of(replicas)
    count = max(1, len(rounds))
    per_block = 1 if rounds else replicas
    taps, slots, _ = inner.shape
    rows = cap * scan.shape[1] + 2 * taps * ROWS
    blocks = count * per_block
    shapes = [pltpu.VMEM((per_block, rows, LANES), BF16)] * count
    half = (blocks, taps * ROWS, LANES)
    limit = SMALL_LIMIT if rounds else MEDIUM_LIMIT
    *states, picked, group_near, indices = pl.pallas_call(
        functools.partial(states_kernel, replicas, cap),
        out_shape=shapes
        + [
            pltpu.VMEM(half, F32),
            pltpu.VMEM(group.shape, BF16),
            pltpu.VMEM(send_list.shape, jnp.int32),
        ],
        in_specs=[HBM] * 4,
        out_specs=[VMEM] * (count + 3),
        scratch_shapes=[
            pltpu.SMEM(send_list.shape, jnp.int32),
            pltpu.VMEM(inner.shape, BF16),
            pltpu.VMEM((slots, taps * LANES), F32),
            pltpu.SemaphoreType.DMA,
            pltpu.SemaphoreType.DMA,
            pltpu.SemaphoreType.DMA,
            pltpu.SemaphoreType.DMA,
            pltpu.SemaphoreType.DMA((blocks * cap,)),
        ],
        compiler_params=pltpu.CompilerParams(vmem_limit_bytes=limit),
        cost_estimate=pl.CostEstimate(flops=0, bytes_accessed=2_000_000, transcendentals=0),
        name="pack_states",
    )(in_hbm(scan), in_hbm(send_list), in_hbm(inner), in_hbm(group))
    near = [in_vmem(value) for value in states]
    return pl.pallas_call(
        functools.partial(windows_kernel, replicas, cap, scan.shape[1]),
        out_shape=shapes,
        in_specs=[VMEM] * (4 + count) + [HBM] * len(swapped),
        out_specs=[VMEM] * count,
        scratch_shapes=[
            pltpu.SMEM(send_list.shape, jnp.int32),
            pltpu.VMEM((slots, taps * LANES), F32),
            pltpu.VMEM(half, F32),
            pltpu.SemaphoreType.DMA,
        ],
        input_output_aliases={4 + place: place for place in range(count)},
        compiler_params=pltpu.CompilerParams(vmem_limit_bytes=limit),
        cost_estimate=pl.CostEstimate(flops=0, bytes_accessed=500_000, transcendentals=0),
        name="pack_windows",
    )(indices, group_near, group_other, picked, *near, *swapped)


def sources_of(replicas):
    rounds = rounds_of(replicas)
    if rounds:
        return [partner(replicas, mask) for mask in rounds]
    return list(range(replicas))


def make_plan(replicas, cap, receive, slots, plan, inverse):
    moving = slots // 2
    kept = 0
    for entry in range(replicas * cap):
        inverse[entry] = -1
    for slot in range(slots):
        entry = receive[0, slot]
        stays = entry < 0
        plan[0, jnp.where(stays, kept, moving)] = slot
        inverse[jnp.where(stays, replicas * cap, entry)] = slot
        kept = kept + jnp.where(stays, 1, 0)
    for block, source in enumerate(sources_of(replicas)):
        for c in range(cap):
            plan[0, moving + block * cap + c] = inverse[source * cap + c]


def convolve(carried, raw, weights, offset):
    joined = carried + raw
    results = []
    for step in range(len(raw)):
        summed = offset
        for tap in range(len(carried) + 1):
            summed = summed + joined[step + tap] * weights[tap : tap + 1, :]
        results.append(rounded(silu(summed)))
    return results


def transposed(rows, scratch, stride):
    scratch[...] = jnp.zeros_like(scratch)
    for step, value in enumerate(rows):
        scratch[step * stride : step * stride + value.shape[0], :] = value
    return [scratch[first : first + LANES].T for first in range(0, scratch.shape[0], LANES)]


def advance_slot(state, rows, driven, decays, sums, maps, lanes):
    hidden = state.astype(F32)
    width = state.shape[0]
    for row, decay, lane in zip(rows, decays, lanes):
        piece = maps[lane // LANES]
        column = piece[:, lane % LANES : lane % LANES + 1]
        hidden = decay * hidden + driven[row, :] * column[:width]
        sums[row, :] = jnp.sum(hidden * column[width:], axis=0, keepdims=True)
        result = hidden.astype(BF16)
        hidden = result.astype(F32)
    return result


def stay_kernel(
    replicas,
    cap,
    decay_log,
    delta_bias,
    skip_gain,
    live,
    receive_hbm,
    own_hbm,
    inner_weight,
    gate_weight,
    group_weight,
    delta_weight,
    inner_taps_hbm,
    inner_offset_hbm,
    inner_hbm,
    group_hbm,
    scan_hbm,
    other,
    group_weight_other,
    small,
    small_other,
    group_other,
    *refs,
):
    (
        plan_out,
        gated,
        weights,
        base,
        inner_part,
        group_part,
        inner_moved,
        group_moved,
        gate_moved,
        delta_moved,
        decay_moved,
        scan_next,
        plan,
        receive,
        own,
        wide,
        tall,
        delta_row,
        inner_taps,
        inner_offset,
        inner,
        group,
        scan,
        inverse,
        inner_raw,
        both,
        gate,
        delta,
        decay,
        driven,
        skipped,
        sums,
        maps_in,
        ordered,
        done,
        sem,
        load_sem,
    ) = refs[-37:]
    taps, slots, _ = inner.shape
    rows, half = own.shape
    steps = rows // slots
    moving = slots // 2
    moved_rows = inner_moved.shape[0] // steps
    width = group.shape[2]
    head = lax.axis_index("head")

    def band(place):
        return tall.at[pl.ds(pl.multiple_of(place * width, width), width)]

    pairs = [
        (receive_hbm, receive),
        (own_hbm, own),
        (inner_weight, wide.at[:, pl.ds(0, LANES)]),
        (gate_weight, wide.at[:, pl.ds(LANES, LANES)]),
        (delta_weight, delta_row),
        (group_weight, band(head)),
        (group_weight_other, band(1 - head)),
        (inner_taps_hbm, inner_taps),
        (inner_offset_hbm, inner_offset),
        (inner_hbm, inner),
        (group_hbm, group),
        (scan_hbm, scan),
    ]
    loads = [
        pltpu.make_async_copy(source, target, load_sem.at[place])
        for place, (source, target) in enumerate(pairs)
    ]
    for load in loads:
        load.start()
    loads[0].wait()
    make_plan(replicas, cap, receive, slots, plan, inverse)
    for load in loads[1:4]:
        load.wait()
    mine = pl.ds(pl.multiple_of(head * half, half), half)
    theirs = pl.ds(pl.multiple_of((1 - head) * half, half), half)
    flat = jnp.dot(own[...], wide[mine, :], preferred_element_type=F32) + jnp.dot(
        other[...], wide[theirs, :], preferred_element_type=F32
    )
    for load in loads[4:]:
        load.wait()
    first = 2 * width
    tall[first:, :] = jnp.broadcast_to(delta_row[...], (tall.shape[0] - first, 2 * half))

    def across(tokens, part):
        return lax.dot_general(
            tokens, tall[:, part], (((1,), (1,)), ((), ())), preferred_element_type=F32
        )

    deep = across(own[...], mine) + across(other[...], theirs)
    inner_raw[...] = rounded(flat[:, :LANES])
    gate[...] = silu(rounded(flat[:, LANES:]))
    both[...] = rounded(deep[:, :first])
    shifted = rounded(jnp.broadcast_to(deep[:, first : first + 1], (rows, LANES)))
    shifted = shifted + delta_bias[0]
    rate = jnp.maximum(shifted, 0.0) + jnp.log1p(jnp.exp(-jnp.abs(shifted)))
    delta[...] = rate
    decay[...] = jnp.exp(-rate * jnp.exp(jnp.full((1, LANES), decay_log[0], F32)))
    count = taps + 2
    weights[:count, :] = both_halves(small[...], small_other[...])
    weights[count : count + 1, :] = jnp.full((1, LANES), skip_gain[0], F32)
    later = round_up(count + 1, ROWS)
    weights[later : later + taps + 1, :] = inner_taps[...]
    weights[later + taps + 1 : later + taps + 2, :] = inner_offset[...]
    plan[0, plan.shape[1] - 1] = live[0]
    save_plan = pltpu.make_async_copy(plan, plan_out, load_sem.at[0])
    save_plan.start()

    def parts(ref):
        return [ref[step * slots : (step + 1) * slots, :] for step in range(steps)]

    inner_conv = convolve(
        [inner[tap].astype(F32) for tap in range(taps)],
        parts(inner_raw),
        inner_taps[...],
        inner_offset[...],
    )
    group_conv = convolve(
        [both_halves(group[tap].astype(F32), group_other[tap].astype(F32)) for tap in range(taps)],
        parts(both),
        weights[: taps + 1, :],
        weights[taps + 1 : taps + 2, :],
    )
    for step in range(steps):
        part = slice(step * slots, (step + 1) * slots)
        driven[part, :] = delta[part, :] * inner_conv[step]
        skipped[part, :] = inner_conv[step] * skip_gain[0]
        maps_in[part, :] = group_conv[step]
    sums[...] = jnp.zeros_like(sums)
    stride = ordered.shape[0] // steps
    ordered[...] = jnp.zeros_like(ordered)
    for position in range(moving):
        slot = plan[0, position]
        for step in range(steps):
            ordered[step * stride + position : step * stride + position + 1, :] = maps_in[
                pl.ds(step * slots + slot, 1), :
            ]
    maps = [ordered[first : first + LANES].T for first in range(0, ordered.shape[0], LANES)]
    copies = []
    for position in range(moving):
        slot = plan[0, position]
        result = advance_slot(
            scan[slot],
            [pl.ds(step * slots + slot, 1) for step in range(steps)],
            driven,
            [decay[pl.ds(step * slots + slot, 1), :] for step in range(steps)],
            sums,
            maps,
            [step * stride + position for step in range(steps)],
        )
        done[position] = jnp.where(slot < live[0], result, jnp.zeros_like(result))
        copies.append(
            pltpu.make_async_copy(done.at[position], scan_next.at[slot], sem.at[position])
        )
        copies[-1].start()
    gated[...] = (sums[...] + skipped[...]) * gate[...]
    pairs = (
        (inner_raw, inner_moved),
        (both, group_moved),
        (gate, gate_moved),
        (delta, delta_moved),
        (decay, decay_moved),
    )
    for _, target in pairs:
        target[...] = jnp.zeros_like(target)
    living = lax.broadcasted_iota(jnp.int32, (slots, LANES), 0) < live[0]
    for step in range(steps):
        part = slice(step * slots, (step + 1) * slots)
        inner_part[step] = jnp.where(living, inner_raw[part, :], 0.0).astype(BF16)
        raw = jnp.where(head == 0, both[part, :width], both[part, width:])
        group_part[step] = jnp.where(living[:, :width], raw, 0.0).astype(BF16)
    base[:, :LANES] = inner[steps].astype(F32)
    group_own = group[steps].astype(F32)
    base[:, LANES:] = jnp.concatenate([group_own, group_own], axis=1)
    for block in range(moved_rows // ROWS):

        @pl.when(plan[0, moving + block * cap] >= 0)
        def _():
            for c in range(cap):
                slot = plan[0, moving + block * cap + c]
                for step in range(steps):
                    row = step * moved_rows + block * ROWS + c
                    for source, target in pairs:
                        target[row : row + 1, :] = source[pl.ds(step * slots + slot, 1), :]

    for copy in copies:
        copy.wait()
    save_plan.wait()


def stay(replicas, cap, scalars, arrays, near, earlier):
    receive, own, group_weight, delta_weight = arrays[0], arrays[1], arrays[4], arrays[5]
    inner, scan = arrays[-3], arrays[-1]
    taps, slots, _ = inner.shape
    rows = own.shape[0]
    steps = rows // slots
    moving = slots // 2
    blocks = len(sources_of(replicas))
    moved_rows = blocks * ROWS
    width, features = group_weight.shape
    full = pltpu.VMEM((rows, LANES), F32)
    moved = pltpu.VMEM((steps * moved_rows, LANES), F32)
    plan_shape = (1, round_up(moving + blocks * cap + 1, LANES))

    def like(value):
        return pltpu.VMEM(value.shape, value.dtype)

    far = [in_hbm(value) for value in arrays]
    return pl.pallas_call(
        functools.partial(stay_kernel, replicas, cap),
        out_shape=[
            pltpu.VMEM(plan_shape, jnp.int32),
            full,
            pltpu.VMEM((2 * round_up(taps + 3, ROWS), LANES), F32),
            pltpu.VMEM((slots, 2 * LANES), F32),
            pltpu.VMEM((steps, slots, LANES), BF16),
            pltpu.VMEM((steps, slots, width), BF16),
        ]
        + [moved] * 5
        + [jax.ShapeDtypeStruct(scan.shape, BF16)],
        in_specs=[SMEM] * len(scalars)
        + [HBM] * len(far)
        + [VMEM] * len(near)
        + [HBM] * len(earlier),
        out_specs=[VMEM] * 11 + [HBM],
        scratch_shapes=[
            pltpu.SMEM(plan_shape, jnp.int32),
            pltpu.SMEM(receive.shape, jnp.int32),
            like(own),
            pltpu.VMEM((features, 2 * LANES), BF16),
            pltpu.VMEM((2 * width + 2 * ROWS, features), BF16),
            like(delta_weight),
        ]
        + [like(value) for value in arrays[6:]]
        + [pltpu.SMEM((replicas * cap + 1,), jnp.int32)]
        + [pltpu.VMEM((rows, LANES), F32)] * 9
        + [
            pltpu.VMEM((round_up(rows, LANES), LANES), F32),
            pltpu.VMEM((moving,) + scan.shape[1:], BF16),
            pltpu.SemaphoreType.DMA((moving,)),
            pltpu.SemaphoreType.DMA((16,)),
        ],
        compiler_params=pltpu.CompilerParams(vmem_limit_bytes=MEDIUM_LIMIT),
        cost_estimate=pl.CostEstimate(
            flops=300_000_000, bytes_accessed=6_000_000, transcendentals=100_000
        ),
        name="advance_staying",
    )(*scalars, *far, *near, *earlier)


def arrive_kernel(
    replicas,
    cap,
    first,
    last,
    plan_near,
    weights,
    inner_moved,
    group_moved,
    gate_moved,
    delta_moved,
    decay_moved,
    gated_in,
    table_in,
    inner_part,
    group_part,
    scan_in,
    *refs,
):
    del scan_in
    if last:
        arrived = refs[:-15]
        gated_out, inner_next, group_next, scan_next = refs[-15:-11]
        gated, table = refs[-11:-9]
        gated_cast, inner_cast, group_cast = refs[-9:-6]
    else:
        arrived = refs[:-9]
        gated, table, scan_next = refs[-9:-6]
    plan, driven, sums, ordered, done, sem = refs[-6:]
    steps, slots, width = group_part.shape
    taps = steps + 1
    moving = slots // 2
    state_rows = scan_next.shape[1]
    head = lax.axis_index("head")
    load = pltpu.make_async_copy(plan_near, plan, sem.at[0])
    load.start()
    if rounds_of(replicas):
        blocks = [ref.at[0] for ref in arrived]
    else:
        blocks = [arrived[0].at[source] for source in range(replicas)]
    stored = inner_moved.shape[0] // steps
    moved_rows = len(blocks) * ROWS
    if last:
        copies = [
            pltpu.make_async_copy(source, target, sem.at[1 + place])
            for place, (source, target) in enumerate(
                [
                    (inner_part, inner_next.at[pl.ds(1, steps)]),
                    (group_part, group_next.at[pl.ds(1, steps)]),
                ]
            )
        ]
        for copy in copies:
            copy.start()

    def parts(ref):
        starts = [step * stored + first * ROWS for step in range(steps)]
        return [ref[start : start + moved_rows, :] for start in starts]

    kinds = [[] for _ in range(2 * taps)]
    for ref in blocks:
        block = ref[cap * state_rows :, :].astype(F32)
        for kind in range(2 * taps):
            kinds[kind].append(block[kind * ROWS : (kind + 1) * ROWS])
    windows = [jnp.concatenate(kind, axis=0) for kind in kinds]
    later = round_up(taps + 3, ROWS)
    inner_conv = convolve(
        windows[:taps],
        parts(inner_moved),
        weights[later : later + taps + 1, :],
        weights[later + taps + 1 : later + taps + 2, :],
    )
    group_conv = convolve(
        windows[taps:],
        parts(group_moved),
        weights[: taps + 1, :],
        weights[taps + 1 : taps + 2, :],
    )
    for step, delta in enumerate(parts(delta_moved)):
        driven[step * moved_rows : (step + 1) * moved_rows, :] = delta * inner_conv[step]
    stride = ordered.shape[0] // steps
    maps = transposed(group_conv, ordered, stride)
    sums[...] = jnp.zeros_like(sums)
    gated[...] = gated_in[...]
    table[...] = table_in[...]
    load.wait()
    live = plan[0, plan.shape[1] - 1]

    def each(act):
        for block in range(len(blocks)):
            entry = moving + (first + block) * cap

            @pl.when(plan[0, entry] >= 0)
            def _():
                for c in range(cap):
                    act(block, c, plan[0, entry + c])

    def store(block, c, slot):
        place = block * cap + c
        return pltpu.make_async_copy(done.at[place], scan_next.at[slot], sem.at[4 + place])

    def advance(block, c, slot):
        place = block * ROWS + c
        rows = [step * moved_rows + place for step in range(steps)]
        result = advance_slot(
            blocks[block][c * state_rows : (c + 1) * state_rows, :],
            [slice(row, row + 1) for row in rows],
            driven,
            [
                decay_moved[row : row + 1, :]
                for row in (step * stored + first * ROWS + place for step in range(steps))
            ],
            sums,
            maps,
            [step * stride + place for step in range(steps)],
        )
        done[block * cap + c] = jnp.where(slot < live, result, jnp.zeros_like(result))
        store(block, c, slot).start()

    each(advance)
    for step, gate in enumerate(parts(gate_moved)):
        part = slice(step * moved_rows, (step + 1) * moved_rows)
        skipped = inner_conv[step] * weights[taps + 2 : taps + 3, :]
        sums[part, :] = (sums[part, :] + skipped) * gate
    driven[:moved_rows, :] = windows[taps - 1]
    driven[moved_rows : 2 * moved_rows, :] = windows[2 * taps - 1]

    def scatter(block, c, slot):
        place = block * ROWS + c
        for step in range(steps):
            row = step * moved_rows + place
            gated[pl.ds(step * slots + slot, 1), :] = sums[row : row + 1, :]
        table[pl.ds(slot, 1), :] = jnp.concatenate(
            [driven[place : place + 1, :], driven[moved_rows + place : moved_rows + place + 1, :]],
            axis=1,
        )

    each(scatter)
    if last:
        living = lax.broadcasted_iota(jnp.int32, (slots, LANES), 0) < live
        for step in range(steps):
            part = slice(step * slots, (step + 1) * slots)
            gated_cast[step] = jnp.where(living, gated[part, :], 0.0).astype(BF16)
        inner_cast[0] = jnp.where(living, table[:, :LANES], 0.0).astype(BF16)
        carried = jnp.where(head == 0, table[:, LANES : LANES + width], table[:, LANES + width :])
        group_cast[0] = jnp.where(living[:, :width], carried, 0.0).astype(BF16)
        ends = [
            pltpu.make_async_copy(source, target, semaphore)
            for source, target, semaphore in (
                (gated_cast, gated_out, sem.at[0]),
                (inner_cast, inner_next.at[pl.ds(0, 1)], sem.at[3]),
                (group_cast, group_next.at[pl.ds(0, 1)], sem.at[sem.shape[0] - 1]),
            )
        ]
        for copy in ends:
            copy.start()
        for copy in copies + ends:
            copy.wait()
    each(lambda block, c, slot: store(block, c, slot).wait())


def arrive(replicas, cap, first, last, operands, scan_next, arrived):
    inner_moved, gated, table, inner_part, group_part = operands[2], *operands[7:]
    steps, slots, width = group_part.shape
    blocks = len(arrived) if rounds_of(replicas) else replicas
    moved = (steps * blocks * ROWS, LANES)
    carried = [pltpu.VMEM(value.shape, F32) for value in (gated, table)]
    scan_shape = jax.ShapeDtypeStruct(scan_next.shape, BF16)
    if last:
        outs = [
            jax.ShapeDtypeStruct((steps, slots, LANES), BF16),
            jax.ShapeDtypeStruct((steps + 1, slots, LANES), BF16),
            jax.ShapeDtypeStruct((steps + 1, slots, width), BF16),
            scan_shape,
        ]
        scratch = carried + [
            pltpu.VMEM((steps, slots, LANES), BF16),
            pltpu.VMEM((1, slots, LANES), BF16),
            pltpu.VMEM((1, slots, width), BF16),
        ]
        specs = [HBM] * 4
    else:
        outs, scratch, specs = carried + [scan_shape], [], [VMEM, VMEM, HBM]
    plan = operands[0]
    return pl.pallas_call(
        functools.partial(arrive_kernel, replicas, cap, first, last),
        out_shape=outs,
        in_specs=[VMEM] * len(operands) + [HBM] + [VMEM] * len(arrived),
        out_specs=specs,
        scratch_shapes=scratch
        + [
            pltpu.SMEM(plan.shape, plan.dtype),
            pltpu.VMEM(moved, F32),
            pltpu.VMEM(moved, F32),
            pltpu.VMEM((round_up(moved[0], LANES), LANES), F32),
            pltpu.VMEM((blocks * cap,) + scan_next.shape[1:], BF16),
            pltpu.SemaphoreType.DMA((blocks * cap + 5,)),
        ],
        input_output_aliases={len(operands): len(outs) - 1},
        compiler_params=pltpu.CompilerParams(
            vmem_limit_bytes=SMALL_LIMIT if rounds_of(replicas) else LARGE_LIMIT
        ),
        cost_estimate=pl.CostEstimate(
            flops=10_000_000, bytes_accessed=2_000_000, transcendentals=0
        ),
        name="advance_last" if last else "advance_arrived",
    )(*operands, scan_next, *arrived)


def swap_heads(value):
    return lax.ppermute(value, "head", [(0, 1), (1, 0)])


def exchange(replicas, blocks):
    rounds = rounds_of(replicas)
    if not rounds:
        return [lax.all_to_all(blocks[0], "dp", 0, 0, tiled=True)]
    return [
        lax.ppermute(block, "dp", [(source, source ^ mask) for source in range(replicas)])
        for mask, block in zip(rounds, blocks)
    ]


def per_device(
    replicas,
    tokens,
    inner_weight,
    gate_weight,
    group_weight,
    delta_weight,
    inner_taps,
    inner_offset,
    group_taps,
    group_offset,
    decay_log,
    delta_bias,
    skip_gain,
    inner_window,
    group_window,
    scan_state,
    send_list,
    receive_list,
    live_count,
):
    steps, slots, half = tokens.shape
    cap = send_list.shape[1] // replicas
    scan = jnp.transpose(scan_state, (0, 2, 1))
    inner = jnp.transpose(inner_window, (1, 0, 2))
    group = jnp.transpose(group_window, (1, 0, 2))
    own = tokens.reshape(steps * slots, half)

    group_weight = group_weight.T
    inner_offset = inner_offset[None]
    small = jnp.concatenate([group_taps, group_offset[None]], axis=0)
    group_other = swap_heads(group)
    swapped = [swap_heads(value) for value in (own, group_weight, small)]
    blocks = pack(replicas, cap, send_list, scan, inner, group, group_other, swapped)
    arrived = exchange(replicas, blocks)
    plan, gated, weights, table, inner_part, group_part, *moved, scan_next = stay(
        replicas,
        cap,
        (decay_log, delta_bias, skip_gain, live_count),
        (
            receive_list,
            own,
            inner_weight,
            gate_weight,
            group_weight,
            delta_weight.T,
            inner_taps,
            inner_offset,
            inner,
            group,
            scan,
        ),
        (swapped[0], swapped[1], small, swapped[2], group_other),
        arrived[:EARLIER] if rounds_of(replicas) else [],
    )
    first = max(0, len(arrived) - LAST)
    if first:
        operands = (plan, weights, *moved, gated, table, inner_part, group_part)
        gated, table, scan_next = arrive(
            replicas, cap, 0, False, operands, scan_next, arrived[:first]
        )
    operands = (plan, weights, *moved, gated, table, inner_part, group_part)
    gated, inner_next, group_next, scan_next = arrive(
        replicas, cap, first, True, operands, scan_next, arrived[first:]
    )
    return (
        gated,
        jnp.transpose(inner_next, (1, 0, 2)),
        jnp.transpose(group_next, (1, 0, 2)),
        jnp.transpose(scan_next, (0, 2, 1)),
    )


def solution(mesh):
    in_specs = (
        P(None, ("grp", "dp"), "head"),
        P(None, "head"),
        P(None, "head"),
        P(None, "head"),
        P(None, "head"),
        P(None, "head"),
        P("head"),
        P(None, "head"),
        P("head"),
        P("head"),
        P("head"),
        P("head"),
        P(("grp", "dp"), None, "head"),
        P(("grp", "dp"), None, "head"),
        P(("grp", "dp"), "head", None),
        P(("grp", "dp"), None),
        P(("grp", "dp"), None),
        P(("grp", "dp")),
    )
    out_specs = (
        P(None, ("grp", "dp"), "head"),
        P(("grp", "dp"), None, "head"),
        P(("grp", "dp"), None, "head"),
        P(("grp", "dp"), "head", None),
    )
    return jax.shard_map(
        functools.partial(per_device, mesh.shape["dp"]),
        mesh=mesh,
        in_specs=in_specs,
        out_specs=out_specs,
        check_vma=False,
    )
```

```python
import functools

import jax
import jax.numpy as jnp
from jax import lax
from jax.experimental import pallas as pl
from jax.experimental.pallas import tpu as pltpu
from jax.sharding import PartitionSpec as P

F32 = jnp.float32
BF16 = jnp.bfloat16
SMALL_LIMIT = 8 * 1024 * 1024
MEDIUM_LIMIT = 16 * 1024 * 1024
LARGE_LIMIT = 48 * 1024 * 1024
MAX_ROUNDS = 16
EARLIER = 3
LAST = 3
LANES = 128
ROWS = 8
MAX_SETS = 64

VMEM = pl.BlockSpec(memory_space=pltpu.VMEM)
SMEM = pl.BlockSpec(memory_space=pltpu.SMEM)
HBM = pl.BlockSpec(memory_space=pl.ANY)


def in_hbm(value):
    return pltpu.with_memory_space_constraint(value, pltpu.HBM)


def in_vmem(value):
    return pltpu.with_memory_space_constraint(value, pltpu.VMEM)


def round_up(value, step):
    return -(-value // step) * step


def silu(value):
    return value * jax.nn.sigmoid(value)


def rounded(value):
    return value.astype(BF16).astype(F32)


def rounds_of(replicas):
    if replicas > MAX_ROUNDS or replicas & (replicas - 1):
        return []
    light = list(range(1, replicas // 2))
    heavy = list(range(replicas // 2, replicas))
    return heavy[:1] + light[:2] + heavy[1:] + light[2:]


def partner(replicas, mask):
    return jnp.bitwise_xor(lax.axis_index("dp"), mask)


def both_halves(mine, theirs):
    first = lax.axis_index("head") == 0
    return jnp.concatenate(
        [jnp.where(first, mine, theirs), jnp.where(first, theirs, mine)], axis=-1
    )


def destinations(replicas, outs):
    rounds = rounds_of(replicas)
    if rounds:
        return [(ref.at[0], partner(replicas, mask)) for ref, mask in zip(outs, rounds)]
    return [(outs[0].at[target], target) for target in range(replicas)]


def states_kernel(replicas, cap, scan, send, inner, group, *refs):
    outs, (picked, group_out, indices_out) = refs[:-11], refs[-11:-8]
    indices, inner_in, table, load_sem, group_sem, list_sem, save_sem, sem = refs[-8:]
    load_list = pltpu.make_async_copy(send, indices, list_sem)
    load_list.start()
    load = pltpu.make_async_copy(inner, inner_in, load_sem)
    load.start()
    load_group = pltpu.make_async_copy(group, group_out, group_sem)
    load_group.start()
    state_rows = scan.shape[1]
    blocks = destinations(replicas, outs)
    load_list.wait()
    save = pltpu.make_async_copy(indices, indices_out, save_sem)
    save.start()
    plan = []
    for block, (ref, target) in enumerate(blocks):
        for c in range(cap):
            plan.append((block, ref, c, indices[0, target * cap + c]))

    def each(act):
        for place, (_, ref, c, index) in enumerate(plan):

            @pl.when(index >= 0)
            def _():
                act(
                    pltpu.make_async_copy(
                        scan.at[index],
                        ref.at[pl.ds(c * state_rows, state_rows)],
                        sem.at[place],
                    )
                )

    each(lambda copy: copy.start())
    load.wait()
    taps = inner_in.shape[0]
    for tap in range(taps):
        table[:, tap * LANES : (tap + 1) * LANES] = inner_in[tap].astype(F32)
    picked[...] = jnp.zeros_like(picked)
    for block, _, c, index in plan:
        row = table[pl.ds(jnp.maximum(index, 0), 1), :]
        for tap in range(taps):
            picked[block, tap * ROWS + c : tap * ROWS + c + 1, :] = row[
                :, tap * LANES : (tap + 1) * LANES
            ]
    load_group.wait()
    save.wait()
    each(lambda copy: copy.wait())


def windows_kernel(replicas, cap, state_rows, indices_in, group, group_other, picked_in, *refs):
    count = max(1, len(rounds_of(replicas)))
    outs = refs[-4 - count : -4]
    indices, table, picked, sem = refs[-4:]
    load = pltpu.make_async_copy(indices_in, indices, sem)
    load.start()
    taps = group.shape[0]
    for tap in range(taps):
        table[:, tap * LANES : (tap + 1) * LANES] = both_halves(
            group[tap].astype(F32), group_other[tap].astype(F32)
        )
    picked[...] = jnp.zeros_like(picked)
    load.wait()
    for block, (ref, target) in enumerate(destinations(replicas, outs)):
        for c in range(cap):
            index = jnp.maximum(indices[0, target * cap + c], 0)
            row = table[pl.ds(index, 1), :]
            for tap in range(taps):
                picked[block, tap * ROWS + c : tap * ROWS + c + 1, :] = row[
                    :, tap * LANES : (tap + 1) * LANES
                ]
        ref[cap * state_rows :, :] = jnp.concatenate(
            [picked_in[block], picked[block]], axis=0
        ).astype(BF16)


def pack(replicas, cap, send_list, scan, inner, group, group_other, swapped):
    rounds = rounds_of(replicas)
    count = max(1, len(rounds))
    per_block = 1 if rounds else replicas
    taps, slots, _ = inner.shape
    rows = cap * scan.shape[1] + 2 * taps * ROWS
    blocks = count * per_block
    shapes = [pltpu.VMEM((per_block, rows, LANES), BF16)] * count
    half = (blocks, taps * ROWS, LANES)
    limit = SMALL_LIMIT if rounds else MEDIUM_LIMIT
    *states, picked, group_near, indices = pl.pallas_call(
        functools.partial(states_kernel, replicas, cap),
        out_shape=shapes
        + [
            pltpu.VMEM(half, F32),
            pltpu.VMEM(group.shape, BF16),
            pltpu.VMEM(send_list.shape, jnp.int32),
        ],
        in_specs=[HBM] * 4,
        out_specs=[VMEM] * (count + 3),
        scratch_shapes=[
            pltpu.SMEM(send_list.shape, jnp.int32),
            pltpu.VMEM(inner.shape, BF16),
            pltpu.VMEM((slots, taps * LANES), F32),
            pltpu.SemaphoreType.DMA,
            pltpu.SemaphoreType.DMA,
            pltpu.SemaphoreType.DMA,
            pltpu.SemaphoreType.DMA,
            pltpu.SemaphoreType.DMA((blocks * cap,)),
        ],
        compiler_params=pltpu.CompilerParams(vmem_limit_bytes=limit),
        cost_estimate=pl.CostEstimate(flops=0, bytes_accessed=2_000_000, transcendentals=0),
        name="pack_states",
    )(in_hbm(scan), in_hbm(send_list), in_hbm(inner), in_hbm(group))
    near = [in_vmem(value) for value in states]
    return pl.pallas_call(
        functools.partial(windows_kernel, replicas, cap, scan.shape[1]),
        out_shape=shapes,
        in_specs=[VMEM] * (4 + count) + [HBM] * len(swapped),
        out_specs=[VMEM] * count,
        scratch_shapes=[
            pltpu.SMEM(send_list.shape, jnp.int32),
            pltpu.VMEM((slots, taps * LANES), F32),
            pltpu.VMEM(half, F32),
            pltpu.SemaphoreType.DMA,
        ],
        input_output_aliases={4 + place: place for place in range(count)},
        compiler_params=pltpu.CompilerParams(vmem_limit_bytes=limit),
        cost_estimate=pl.CostEstimate(flops=0, bytes_accessed=500_000, transcendentals=0),
        name="pack_windows",
    )(indices, group_near, group_other, picked, *near, *swapped)


def sources_of(replicas):
    rounds = rounds_of(replicas)
    if rounds:
        return [partner(replicas, mask) for mask in rounds]
    return list(range(replicas))


def make_plan(replicas, cap, receive, slots, plan, inverse):
    moving = slots // 2
    kept = 0
    for entry in range(replicas * cap):
        inverse[entry] = -1
    for slot in range(slots):
        entry = receive[0, slot]
        stays = entry < 0
        plan[0, jnp.where(stays, kept, moving)] = slot
        inverse[jnp.where(stays, replicas * cap, entry)] = slot
        kept = kept + jnp.where(stays, 1, 0)
    for block, source in enumerate(sources_of(replicas)):
        for c in range(cap):
            plan[0, moving + block * cap + c] = inverse[source * cap + c]


def convolve(carried, raw, weights, offset):
    joined = carried + raw
    results = []
    for step in range(len(raw)):
        summed = offset
        for tap in range(len(carried) + 1):
            summed = summed + joined[step + tap] * weights[tap : tap + 1, :]
        results.append(rounded(silu(summed)))
    return results


def transposed(rows, scratch, stride):
    scratch[...] = jnp.zeros_like(scratch)
    for step, value in enumerate(rows):
        scratch[step * stride : step * stride + value.shape[0], :] = value
    return [scratch[first : first + LANES].T for first in range(0, scratch.shape[0], LANES)]


def advance_slot(state, rows, driven, decays, sums, maps, lanes):
    hidden = state.astype(F32)
    width = state.shape[0]
    for row, decay, lane in zip(rows, decays, lanes):
        piece = maps[lane // LANES]
        column = piece[:, lane % LANES : lane % LANES + 1]
        hidden = decay * hidden + driven[row, :] * column[:width]
        sums[row, :] = jnp.sum(hidden * column[width:], axis=0, keepdims=True)
        result = hidden.astype(BF16)
        hidden = result.astype(F32)
    return result


def stay_kernel(
    replicas,
    cap,
    decay_log,
    delta_bias,
    skip_gain,
    live,
    receive_hbm,
    own_hbm,
    inner_weight,
    gate_weight,
    group_weight,
    delta_weight,
    inner_taps_hbm,
    inner_offset_hbm,
    inner_hbm,
    group_hbm,
    scan_hbm,
    other,
    group_weight_other,
    small,
    small_other,
    group_other,
    *refs,
):
    (
        plan_out,
        gated,
        weights,
        base,
        inner_part,
        group_part,
        inner_moved,
        group_moved,
        gate_moved,
        delta_moved,
        decay_moved,
        scan_next,
        plan,
        receive,
        own,
        wide,
        tall,
        delta_row,
        inner_taps,
        inner_offset,
        inner,
        group,
        scan,
        inverse,
        inner_raw,
        both,
        gate,
        delta,
        decay,
        driven,
        skipped,
        sums,
        maps_in,
        ordered,
        done,
        sem,
        load_sem,
    ) = refs[-37:]
    taps, slots, _ = inner.shape
    rows, half = own.shape
    steps = rows // slots
    moving = slots // 2
    moved_rows = inner_moved.shape[0] // steps
    width = group.shape[2]
    head = lax.axis_index("head")

    def band(place):
        return tall.at[pl.ds(pl.multiple_of(place * width, width), width)]

    pairs = [
        (receive_hbm, receive),
        (delta_weight, delta_row),
        (own_hbm, own),
        (inner_weight, wide.at[:, pl.ds(0, LANES)]),
        (gate_weight, wide.at[:, pl.ds(LANES, LANES)]),
        (group_weight, band(head)),
        (group_weight_other, band(1 - head)),
        (inner_taps_hbm, inner_taps),
        (inner_offset_hbm, inner_offset),
        (inner_hbm, inner),
        (group_hbm, group),
        (scan_hbm, scan),
    ]
    loads = [
        pltpu.make_async_copy(source, target, load_sem.at[place])
        for place, (source, target) in enumerate(pairs)
    ]
    for load in loads:
        load.start()
    loads[0].wait()
    make_plan(replicas, cap, receive, slots, plan, inverse)
    loads[1].wait()
    first = 2 * width
    tall[first:, :] = jnp.broadcast_to(delta_row[...], (tall.shape[0] - first, 2 * half))
    for load in loads[2:]:
        load.wait()
    mine = pl.ds(pl.multiple_of(head * half, half), half)
    theirs = pl.ds(pl.multiple_of((1 - head) * half, half), half)
    flat = jnp.dot(own[...], wide[mine, :], preferred_element_type=F32) + jnp.dot(
        other[...], wide[theirs, :], preferred_element_type=F32
    )

    def across(tokens, part):
        return lax.dot_general(
            tokens, tall[:, part], (((1,), (1,)), ((), ())), preferred_element_type=F32
        )

    deep = across(own[...], mine) + across(other[...], theirs)
    inner_raw[...] = rounded(flat[:, :LANES])
    gate[...] = silu(rounded(flat[:, LANES:]))
    both[...] = rounded(deep[:, :first])
    shifted = rounded(jnp.broadcast_to(deep[:, first : first + 1], (rows, LANES)))
    shifted = shifted + delta_bias[0]
    rate = jnp.maximum(shifted, 0.0) + jnp.log1p(jnp.exp(-jnp.abs(shifted)))
    delta[...] = rate
    decay[...] = jnp.exp(-rate * jnp.exp(jnp.full((1, LANES), decay_log[0], F32)))
    count = taps + 2
    weights[:count, :] = both_halves(small[...], small_other[...])
    weights[count : count + 1, :] = jnp.full((1, LANES), skip_gain[0], F32)
    later = round_up(count + 1, ROWS)
    weights[later : later + taps + 1, :] = inner_taps[...]
    weights[later + taps + 1 : later + taps + 2, :] = inner_offset[...]
    plan[0, plan.shape[1] - 1] = live[0]
    save_plan = pltpu.make_async_copy(plan, plan_out, load_sem.at[0])
    save_plan.start()

    def parts(ref):
        return [ref[step * slots : (step + 1) * slots, :] for step in range(steps)]

    inner_conv = convolve(
        [inner[tap].astype(F32) for tap in range(taps)],
        parts(inner_raw),
        inner_taps[...],
        inner_offset[...],
    )
    group_conv = convolve(
        [both_halves(group[tap].astype(F32), group_other[tap].astype(F32)) for tap in range(taps)],
        parts(both),
        weights[: taps + 1, :],
        weights[taps + 1 : taps + 2, :],
    )
    for step in range(steps):
        part = slice(step * slots, (step + 1) * slots)
        driven[part, :] = delta[part, :] * inner_conv[step]
        skipped[part, :] = inner_conv[step] * skip_gain[0]
        maps_in[part, :] = group_conv[step]
    sums[...] = jnp.zeros_like(sums)
    stride = ordered.shape[0] // steps
    ordered[...] = jnp.zeros_like(ordered)
    for position in range(moving):
        slot = plan[0, position]
        for step in range(steps):
            ordered[step * stride + position : step * stride + position + 1, :] = maps_in[
                pl.ds(step * slots + slot, 1), :
            ]
    maps = [ordered[first : first + LANES].T for first in range(0, ordered.shape[0], LANES)]
    copies = []
    for position in range(moving):
        slot = plan[0, position]
        result = advance_slot(
            scan[slot],
            [pl.ds(step * slots + slot, 1) for step in range(steps)],
            driven,
            [decay[pl.ds(step * slots + slot, 1), :] for step in range(steps)],
            sums,
            maps,
            [step * stride + position for step in range(steps)],
        )
        done[position] = jnp.where(slot < live[0], result, jnp.zeros_like(result))
        copies.append(
            pltpu.make_async_copy(done.at[position], scan_next.at[slot], sem.at[position])
        )
        copies[-1].start()
    gated[...] = (sums[...] + skipped[...]) * gate[...]
    pairs = (
        (inner_raw, inner_moved),
        (both, group_moved),
        (gate, gate_moved),
        (delta, delta_moved),
        (decay, decay_moved),
    )
    for _, target in pairs:
        target[...] = jnp.zeros_like(target)
    living = lax.broadcasted_iota(jnp.int32, (slots, LANES), 0) < live[0]
    for step in range(steps):
        part = slice(step * slots, (step + 1) * slots)
        inner_part[step] = jnp.where(living, inner_raw[part, :], 0.0).astype(BF16)
        raw = jnp.where(head == 0, both[part, :width], both[part, width:])
        group_part[step] = jnp.where(living[:, :width], raw, 0.0).astype(BF16)
    base[:, :LANES] = inner[steps].astype(F32)
    group_own = group[steps].astype(F32)
    base[:, LANES:] = jnp.concatenate([group_own, group_own], axis=1)
    for block in range(moved_rows // ROWS):

        @pl.when(plan[0, moving + block * cap] >= 0)
        def _():
            for c in range(cap):
                slot = plan[0, moving + block * cap + c]
                for step in range(steps):
                    row = step * moved_rows + block * ROWS + c
                    for source, target in pairs:
                        target[row : row + 1, :] = source[pl.ds(step * slots + slot, 1), :]

    for copy in copies:
        copy.wait()
    save_plan.wait()


def stay(replicas, cap, scalars, arrays, near, earlier):
    receive, own, group_weight, delta_weight = arrays[0], arrays[1], arrays[4], arrays[5]
    inner, scan = arrays[-3], arrays[-1]
    taps, slots, _ = inner.shape
    rows = own.shape[0]
    steps = rows // slots
    moving = slots // 2
    blocks = len(sources_of(replicas))
    moved_rows = blocks * ROWS
    width, features = group_weight.shape
    full = pltpu.VMEM((rows, LANES), F32)
    moved = pltpu.VMEM((steps * moved_rows, LANES), F32)
    plan_shape = (1, round_up(moving + blocks * cap + 1, LANES))

    def like(value):
        return pltpu.VMEM(value.shape, value.dtype)

    far = [in_hbm(value) for value in arrays]
    return pl.pallas_call(
        functools.partial(stay_kernel, replicas, cap),
        out_shape=[
            pltpu.VMEM(plan_shape, jnp.int32),
            full,
            pltpu.VMEM((2 * round_up(taps + 3, ROWS), LANES), F32),
            pltpu.VMEM((slots, 2 * LANES), F32),
            pltpu.VMEM((steps, slots, LANES), BF16),
            pltpu.VMEM((steps, slots, width), BF16),
        ]
        + [moved] * 5
        + [jax.ShapeDtypeStruct(scan.shape, BF16)],
        in_specs=[SMEM] * len(scalars)
        + [HBM] * len(far)
        + [VMEM] * len(near)
        + [HBM] * len(earlier),
        out_specs=[VMEM] * 11 + [HBM],
        scratch_shapes=[
            pltpu.SMEM(plan_shape, jnp.int32),
            pltpu.SMEM(receive.shape, jnp.int32),
            like(own),
            pltpu.VMEM((features, 2 * LANES), BF16),
            pltpu.VMEM((2 * width + 2 * ROWS, features), BF16),
            like(delta_weight),
        ]
        + [like(value) for value in arrays[6:]]
        + [pltpu.SMEM((replicas * cap + 1,), jnp.int32)]
        + [pltpu.VMEM((rows, LANES), F32)] * 9
        + [
            pltpu.VMEM((round_up(rows, LANES), LANES), F32),
            pltpu.VMEM((moving,) + scan.shape[1:], BF16),
            pltpu.SemaphoreType.DMA((moving,)),
            pltpu.SemaphoreType.DMA((16,)),
        ],
        compiler_params=pltpu.CompilerParams(vmem_limit_bytes=MEDIUM_LIMIT),
        cost_estimate=pl.CostEstimate(
            flops=300_000_000, bytes_accessed=6_000_000, transcendentals=100_000
        ),
        name="advance_staying",
    )(*scalars, *far, *near, *earlier)


def arrive_kernel(
    replicas,
    cap,
    first,
    last,
    plan_near,
    weights,
    inner_moved,
    group_moved,
    gate_moved,
    delta_moved,
    decay_moved,
    gated_in,
    table_in,
    inner_part,
    group_part,
    scan_in,
    *refs,
):
    del scan_in
    if last:
        arrived = refs[:-15]
        gated_out, inner_next, group_next, scan_next = refs[-15:-11]
        gated, table = refs[-11:-9]
        gated_cast, inner_cast, group_cast = refs[-9:-6]
    else:
        arrived = refs[:-9]
        gated, table, scan_next = refs[-9:-6]
    plan, driven, sums, ordered, done, sem = refs[-6:]
    steps, slots, width = group_part.shape
    taps = steps + 1
    moving = slots // 2
    state_rows = scan_next.shape[1]
    head = lax.axis_index("head")
    load = pltpu.make_async_copy(plan_near, plan, sem.at[0])
    load.start()
    if rounds_of(replicas):
        blocks = [ref.at[0] for ref in arrived]
    else:
        blocks = [arrived[0].at[source] for source in range(replicas)]
    stored = inner_moved.shape[0] // steps
    moved_rows = len(blocks) * ROWS
    if last:
        copies = [
            pltpu.make_async_copy(source, target, sem.at[1 + place])
            for place, (source, target) in enumerate(
                [
                    (inner_part, inner_next.at[pl.ds(1, steps)]),
                    (group_part, group_next.at[pl.ds(1, steps)]),
                ]
            )
        ]
        for copy in copies:
            copy.start()

    def parts(ref):
        starts = [step * stored + first * ROWS for step in range(steps)]
        return [ref[start : start + moved_rows, :] for start in starts]

    kinds = [[] for _ in range(2 * taps)]
    for ref in blocks:
        block = ref[cap * state_rows :, :].astype(F32)
        for kind in range(2 * taps):
            kinds[kind].append(block[kind * ROWS : (kind + 1) * ROWS])
    windows = [jnp.concatenate(kind, axis=0) for kind in kinds]
    later = round_up(taps + 3, ROWS)
    inner_conv = convolve(
        windows[:taps],
        parts(inner_moved),
        weights[later : later + taps + 1, :],
        weights[later + taps + 1 : later + taps + 2, :],
    )
    group_conv = convolve(
        windows[taps:],
        parts(group_moved),
        weights[: taps + 1, :],
        weights[taps + 1 : taps + 2, :],
    )
    for step, delta in enumerate(parts(delta_moved)):
        driven[step * moved_rows : (step + 1) * moved_rows, :] = delta * inner_conv[step]
    stride = ordered.shape[0] // steps
    maps = transposed(group_conv, ordered, stride)
    sums[...] = jnp.zeros_like(sums)
    gated[...] = gated_in[...]
    table[...] = table_in[...]
    load.wait()
    live = plan[0, plan.shape[1] - 1]

    def each(act):
        for block in range(len(blocks)):
            entry = moving + (first + block) * cap

            @pl.when(plan[0, entry] >= 0)
            def _():
                for c in range(cap):
                    act(block, c, plan[0, entry + c])

    def store(block, c, slot):
        place = block * cap + c
        return pltpu.make_async_copy(done.at[place], scan_next.at[slot], sem.at[4 + place])

    def advance(block, c, slot):
        place = block * ROWS + c
        rows = [step * moved_rows + place for step in range(steps)]
        result = advance_slot(
            blocks[block][c * state_rows : (c + 1) * state_rows, :],
            [slice(row, row + 1) for row in rows],
            driven,
            [
                decay_moved[row : row + 1, :]
                for row in (step * stored + first * ROWS + place for step in range(steps))
            ],
            sums,
            maps,
            [step * stride + place for step in range(steps)],
        )
        done[block * cap + c] = jnp.where(slot < live, result, jnp.zeros_like(result))
        store(block, c, slot).start()

    each(advance)
    for step, gate in enumerate(parts(gate_moved)):
        part = slice(step * moved_rows, (step + 1) * moved_rows)
        skipped = inner_conv[step] * weights[taps + 2 : taps + 3, :]
        sums[part, :] = (sums[part, :] + skipped) * gate
    driven[:moved_rows, :] = windows[taps - 1]
    driven[moved_rows : 2 * moved_rows, :] = windows[2 * taps - 1]

    def scatter(block, c, slot):
        place = block * ROWS + c
        for step in range(steps):
            row = step * moved_rows + place
            gated[pl.ds(step * slots + slot, 1), :] = sums[row : row + 1, :]
        table[pl.ds(slot, 1), :] = jnp.concatenate(
            [driven[place : place + 1, :], driven[moved_rows + place : moved_rows + place + 1, :]],
            axis=1,
        )

    each(scatter)
    if last:
        living = lax.broadcasted_iota(jnp.int32, (slots, LANES), 0) < live
        for step in range(steps):
            part = slice(step * slots, (step + 1) * slots)
            gated_cast[step] = jnp.where(living, gated[part, :], 0.0).astype(BF16)
        inner_cast[0] = jnp.where(living, table[:, :LANES], 0.0).astype(BF16)
        carried = jnp.where(head == 0, table[:, LANES : LANES + width], table[:, LANES + width :])
        group_cast[0] = jnp.where(living[:, :width], carried, 0.0).astype(BF16)
        ends = [
            pltpu.make_async_copy(source, target, semaphore)
            for source, target, semaphore in (
                (gated_cast, gated_out, sem.at[0]),
                (inner_cast, inner_next.at[pl.ds(0, 1)], sem.at[3]),
                (group_cast, group_next.at[pl.ds(0, 1)], sem.at[sem.shape[0] - 1]),
            )
        ]
        for copy in ends:
            copy.start()
        for copy in copies + ends:
            copy.wait()
    each(lambda block, c, slot: store(block, c, slot).wait())


def arrive(replicas, cap, first, last, operands, scan_next, arrived):
    inner_moved, gated, table, inner_part, group_part = operands[2], *operands[7:]
    steps, slots, width = group_part.shape
    blocks = len(arrived) if rounds_of(replicas) else replicas
    moved = (steps * blocks * ROWS, LANES)
    carried = [pltpu.VMEM(value.shape, F32) for value in (gated, table)]
    scan_shape = jax.ShapeDtypeStruct(scan_next.shape, BF16)
    if last:
        outs = [
            jax.ShapeDtypeStruct((steps, slots, LANES), BF16),
            jax.ShapeDtypeStruct((steps + 1, slots, LANES), BF16),
            jax.ShapeDtypeStruct((steps + 1, slots, width), BF16),
            scan_shape,
        ]
        scratch = carried + [
            pltpu.VMEM((steps, slots, LANES), BF16),
            pltpu.VMEM((1, slots, LANES), BF16),
            pltpu.VMEM((1, slots, width), BF16),
        ]
        specs = [HBM] * 4
    else:
        outs, scratch, specs = carried + [scan_shape], [], [VMEM, VMEM, HBM]
    plan = operands[0]
    return pl.pallas_call(
        functools.partial(arrive_kernel, replicas, cap, first, last),
        out_shape=outs,
        in_specs=[VMEM] * len(operands) + [HBM] + [VMEM] * len(arrived),
        out_specs=specs,
        scratch_shapes=scratch
        + [
            pltpu.SMEM(plan.shape, plan.dtype),
            pltpu.VMEM(moved, F32),
            pltpu.VMEM(moved, F32),
            pltpu.VMEM((round_up(moved[0], LANES), LANES), F32),
            pltpu.VMEM((blocks * cap,) + scan_next.shape[1:], BF16),
            pltpu.SemaphoreType.DMA((blocks * cap + 5,)),
        ],
        input_output_aliases={len(operands): len(outs) - 1},
        compiler_params=pltpu.CompilerParams(
            vmem_limit_bytes=SMALL_LIMIT if rounds_of(replicas) else LARGE_LIMIT
        ),
        cost_estimate=pl.CostEstimate(
            flops=10_000_000, bytes_accessed=2_000_000, transcendentals=0
        ),
        name="advance_last" if last else "advance_arrived",
    )(*operands, scan_next, *arrived)


def swap_heads(value):
    return lax.ppermute(value, "head", [(0, 1), (1, 0)])


def exchange(replicas, blocks):
    rounds = rounds_of(replicas)
    if not rounds:
        return [lax.all_to_all(blocks[0], "dp", 0, 0, tiled=True)]
    return [
        lax.ppermute(block, "dp", [(source, source ^ mask) for source in range(replicas)])
        for mask, block in zip(rounds, blocks)
    ]


def per_device(
    replicas,
    tokens,
    inner_weight,
    gate_weight,
    group_weight,
    delta_weight,
    inner_taps,
    inner_offset,
    group_taps,
    group_offset,
    decay_log,
    delta_bias,
    skip_gain,
    inner_window,
    group_window,
    scan_state,
    send_list,
    receive_list,
    live_count,
):
    steps, slots, half = tokens.shape
    cap = send_list.shape[1] // replicas
    scan = jnp.transpose(scan_state, (0, 2, 1))
    inner = jnp.transpose(inner_window, (1, 0, 2))
    group = jnp.transpose(group_window, (1, 0, 2))
    own = tokens.reshape(steps * slots, half)

    group_weight = group_weight.T
    inner_offset = inner_offset[None]
    small = jnp.concatenate([group_taps, group_offset[None]], axis=0)
    group_other = swap_heads(group)
    swapped = [swap_heads(value) for value in (own, group_weight, small)]
    blocks = pack(replicas, cap, send_list, scan, inner, group, group_other, swapped)
    arrived = exchange(replicas, blocks)
    plan, gated, weights, table, inner_part, group_part, *moved, scan_next = stay(
        replicas,
        cap,
        (decay_log, delta_bias, skip_gain, live_count),
        (
            receive_list,
            own,
            inner_weight,
            gate_weight,
            group_weight,
            delta_weight.T,
            inner_taps,
            inner_offset,
            inner,
            group,
            scan,
        ),
        (swapped[0], swapped[1], small, swapped[2], group_other),
        arrived[:EARLIER] if rounds_of(replicas) else [],
    )
    first = max(0, len(arrived) - LAST)
    if first:
        operands = (plan, weights, *moved, gated, table, inner_part, group_part)
        gated, table, scan_next = arrive(
            replicas, cap, 0, False, operands, scan_next, arrived[:first]
        )
    operands = (plan, weights, *moved, gated, table, inner_part, group_part)
    gated, inner_next, group_next, scan_next = arrive(
        replicas, cap, first, True, operands, scan_next, arrived[first:]
    )
    return (
        gated,
        jnp.transpose(inner_next, (1, 0, 2)),
        jnp.transpose(group_next, (1, 0, 2)),
        jnp.transpose(scan_next, (0, 2, 1)),
    )


def solution(mesh):
    in_specs = (
        P(None, ("grp", "dp"), "head"),
        P(None, "head"),
        P(None, "head"),
        P(None, "head"),
        P(None, "head"),
        P(None, "head"),
        P("head"),
        P(None, "head"),
        P("head"),
        P("head"),
        P("head"),
        P("head"),
        P(("grp", "dp"), None, "head"),
        P(("grp", "dp"), None, "head"),
        P(("grp", "dp"), "head", None),
        P(("grp", "dp"), None),
        P(("grp", "dp"), None),
        P(("grp", "dp")),
    )
    out_specs = (
        P(None, ("grp", "dp"), "head"),
        P(("grp", "dp"), None, "head"),
        P(("grp", "dp"), None, "head"),
        P(("grp", "dp"), "head", None),
    )
    return jax.shard_map(
        functools.partial(per_device, mesh.shape["dp"]),
        mesh=mesh,
        in_specs=in_specs,
        out_specs=out_specs,
        check_vma=False,
    )
```

```python
import functools

import jax
import jax.numpy as jnp
from jax import lax
from jax.experimental import pallas as pl
from jax.experimental.pallas import tpu as pltpu
from jax.sharding import PartitionSpec as P

F32 = jnp.float32
BF16 = jnp.bfloat16
SMALL_LIMIT = 8 * 1024 * 1024
MEDIUM_LIMIT = 16 * 1024 * 1024
LARGE_LIMIT = 48 * 1024 * 1024
MAX_ROUNDS = 16
EARLIER = 3
LAST = 2
LANES = 128
ROWS = 8
MAX_SETS = 64

VMEM = pl.BlockSpec(memory_space=pltpu.VMEM)
SMEM = pl.BlockSpec(memory_space=pltpu.SMEM)
HBM = pl.BlockSpec(memory_space=pl.ANY)


def in_hbm(value):
    return pltpu.with_memory_space_constraint(value, pltpu.HBM)


def round_up(value, step):
    return -(-value // step) * step


def silu(value):
    return value * jax.nn.sigmoid(value)


def rounded(value):
    return value.astype(BF16).astype(F32)


def rounds_of(replicas):
    if replicas > MAX_ROUNDS or replicas & (replicas - 1):
        return []
    light = list(range(1, replicas // 2))
    heavy = list(range(replicas // 2, replicas))
    return heavy[:1] + light[:2] + heavy[1:2] + light[2:] + heavy[2:]


def partner(replicas, mask):
    return jnp.bitwise_xor(lax.axis_index("dp"), mask)


def both_halves(mine, theirs):
    first = lax.axis_index("head") == 0
    return jnp.concatenate(
        [jnp.where(first, mine, theirs), jnp.where(first, theirs, mine)], axis=-1
    )


def pack_kernel(replicas, cap, scan, send, inner, group, group_other, *refs):
    rounds = rounds_of(replicas)
    count = max(1, len(rounds))
    outs = refs[-8 - count : -8]
    indices, inner_in, group_in, table, picked, load_sem, list_sem, sem = refs[-8:]
    load_list = pltpu.make_async_copy(send, indices, list_sem)
    load_list.start()
    loads = [
        pltpu.make_async_copy(source, target, load_sem.at[place])
        for place, (source, target) in enumerate([(inner, inner_in), (group, group_in)])
    ]
    for load in loads:
        load.start()
    state_rows = scan.shape[1]
    if rounds:
        blocks = [(ref.at[0], partner(replicas, mask)) for ref, mask in zip(outs, rounds)]
    else:
        blocks = [(outs[0].at[target], target) for target in range(replicas)]
    load_list.wait()

    plan = []
    for block, (ref, target) in enumerate(blocks):
        for c in range(cap):
            plan.append((block, ref, c, indices[0, target * cap + c]))

    def each(act):
        for place, (_, ref, c, index) in enumerate(plan):

            @pl.when(index >= 0)
            def _():
                act(
                    pltpu.make_async_copy(
                        scan.at[index],
                        ref.at[pl.ds(c * state_rows, state_rows)],
                        sem.at[place],
                    )
                )

    each(lambda copy: copy.start())
    for load in loads:
        load.wait()
    taps = inner_in.shape[0]
    for tap in range(taps):
        table[:, tap * LANES : (tap + 1) * LANES] = inner_in[tap].astype(F32)
        table[:, (taps + tap) * LANES : (taps + tap + 1) * LANES] = both_halves(
            group_in[tap].astype(F32), group_other[tap].astype(F32)
        )
    picked[...] = jnp.zeros_like(picked)
    for block, _, c, index in plan:
        row = table[pl.ds(jnp.maximum(index, 0), 1), :]
        for kind in range(2 * taps):
            picked[block, kind * ROWS + c : kind * ROWS + c + 1, :] = row[
                :, kind * LANES : (kind + 1) * LANES
            ]
    for block, (ref, _) in enumerate(blocks):
        ref[cap * state_rows :, :] = picked[block].astype(BF16)
    each(lambda copy: copy.wait())


def pack(replicas, cap, send_list, scan, inner, group, group_other, swapped):
    rounds = rounds_of(replicas)
    count = max(1, len(rounds))
    per_block = 1 if rounds else replicas
    taps, slots, _ = inner.shape
    window_rows = 2 * taps * ROWS
    rows = cap * scan.shape[1] + window_rows
    blocks = count * per_block
    return pl.pallas_call(
        functools.partial(pack_kernel, replicas, cap),
        out_shape=[pltpu.VMEM((per_block, rows, LANES), BF16)] * count,
        in_specs=[HBM] * 4 + [VMEM] + [HBM] * len(swapped),
        out_specs=[VMEM] * count,
        scratch_shapes=[
            pltpu.SMEM(send_list.shape, jnp.int32),
            pltpu.VMEM(inner.shape, BF16),
            pltpu.VMEM(group.shape, BF16),
            pltpu.VMEM((slots, 2 * taps * LANES), F32),
            pltpu.VMEM((blocks, window_rows, LANES), F32),
            pltpu.SemaphoreType.DMA((2,)),
            pltpu.SemaphoreType.DMA,
            pltpu.SemaphoreType.DMA((blocks * cap,)),
        ],
        compiler_params=pltpu.CompilerParams(vmem_limit_bytes=SMALL_LIMIT),
        cost_estimate=pl.CostEstimate(flops=0, bytes_accessed=2_000_000, transcendentals=0),
        name="pack_leaving",
    )(in_hbm(scan), in_hbm(send_list), in_hbm(inner), in_hbm(group), group_other, *swapped)


def sources_of(replicas):
    rounds = rounds_of(replicas)
    if rounds:
        return [partner(replicas, mask) for mask in rounds]
    return list(range(replicas))


def make_plan(replicas, cap, receive, slots, plan, inverse):
    moving = slots // 2
    kept = 0
    for entry in range(replicas * cap):
        inverse[entry] = -1
    for slot in range(slots):
        entry = receive[0, slot]
        stays = entry < 0
        plan[0, jnp.where(stays, kept, moving)] = slot
        inverse[jnp.where(stays, replicas * cap, entry)] = slot
        kept = kept + jnp.where(stays, 1, 0)
    for block, source in enumerate(sources_of(replicas)):
        for c in range(cap):
            plan[0, moving + block * cap + c] = inverse[source * cap + c]


def convolve(carried, raw, weights, offset):
    joined = carried + raw
    results = []
    for step in range(len(raw)):
        summed = offset
        for tap in range(len(carried) + 1):
            summed = summed + joined[step + tap] * weights[tap : tap + 1, :]
        results.append(rounded(silu(summed)))
    return results


def transposed(rows, scratch, stride):
    scratch[...] = jnp.zeros_like(scratch)
    for step, value in enumerate(rows):
        scratch[step * stride : step * stride + value.shape[0], :] = value
    return [scratch[first : first + LANES].T for first in range(0, scratch.shape[0], LANES)]


def advance_slot(state, rows, driven, decays, sums, maps, lanes):
    hidden = state.astype(F32)
    width = state.shape[0]
    for row, decay, lane in zip(rows, decays, lanes):
        piece = maps[lane // LANES]
        column = piece[:, lane % LANES : lane % LANES + 1]
        hidden = decay * hidden + driven[row, :] * column[:width]
        sums[row, :] = jnp.sum(hidden * column[width:], axis=0, keepdims=True)
        result = hidden.astype(BF16)
        hidden = result.astype(F32)
    return result


def stay_kernel(
    replicas,
    cap,
    decay_log,
    delta_bias,
    skip_gain,
    live,
    receive_hbm,
    own_hbm,
    inner_weight,
    gate_weight,
    group_weight,
    delta_weight,
    inner_taps_hbm,
    inner_offset_hbm,
    inner_hbm,
    group_hbm,
    scan_hbm,
    other,
    group_weight_other,
    small,
    small_other,
    group_other,
    *refs,
):
    (
        plan_out,
        gated,
        weights,
        base,
        inner_part,
        group_part,
        inner_moved,
        group_moved,
        gate_moved,
        delta_moved,
        decay_moved,
        scan_next,
        plan,
        receive,
        own,
        wide,
        tall,
        delta_row,
        inner_taps,
        inner_offset,
        inner,
        group,
        scan,
        inverse,
        inner_raw,
        both,
        gate,
        delta,
        decay,
        driven,
        skipped,
        sums,
        maps_in,
        ordered,
        done,
        sem,
        load_sem,
    ) = refs[-37:]
    taps, slots, _ = inner.shape
    rows, half = own.shape
    steps = rows // slots
    moving = slots // 2
    moved_rows = inner_moved.shape[0] // steps
    width = group.shape[2]
    head = lax.axis_index("head")

    def band(place):
        return tall.at[pl.ds(pl.multiple_of(place * width, width), width)]

    pairs = [
        (receive_hbm, receive),
        (delta_weight, delta_row),
        (own_hbm, own),
        (inner_weight, wide.at[:, pl.ds(0, LANES)]),
        (gate_weight, wide.at[:, pl.ds(LANES, LANES)]),
        (group_weight, band(head)),
        (group_weight_other, band(1 - head)),
        (inner_taps_hbm, inner_taps),
        (inner_offset_hbm, inner_offset),
        (inner_hbm, inner),
        (group_hbm, group),
        (scan_hbm, scan),
    ]
    loads = [
        pltpu.make_async_copy(source, target, load_sem.at[place])
        for place, (source, target) in enumerate(pairs)
    ]
    for load in loads:
        load.start()
    loads[0].wait()
    make_plan(replicas, cap, receive, slots, plan, inverse)
    loads[1].wait()
    first = 2 * width
    tall[first:, :] = jnp.broadcast_to(delta_row[...], (tall.shape[0] - first, 2 * half))
    for load in loads[2:]:
        load.wait()
    mine = pl.ds(pl.multiple_of(head * half, half), half)
    theirs = pl.ds(pl.multiple_of((1 - head) * half, half), half)
    flat = jnp.dot(own[...], wide[mine, :], preferred_element_type=F32) + jnp.dot(
        other[...], wide[theirs, :], preferred_element_type=F32
    )

    def across(tokens, part):
        return lax.dot_general(
            tokens, tall[:, part], (((1,), (1,)), ((), ())), preferred_element_type=F32
        )

    deep = across(own[...], mine) + across(other[...], theirs)
    inner_raw[...] = rounded(flat[:, :LANES])
    gate[...] = silu(rounded(flat[:, LANES:]))
    both[...] = rounded(deep[:, :first])
    shifted = rounded(jnp.broadcast_to(deep[:, first : first + 1], (rows, LANES)))
    shifted = shifted + delta_bias[0]
    rate = jnp.maximum(shifted, 0.0) + jnp.log1p(jnp.exp(-jnp.abs(shifted)))
    delta[...] = rate
    decay[...] = jnp.exp(-rate * jnp.exp(jnp.full((1, LANES), decay_log[0], F32)))
    count = taps + 2
    weights[:count, :] = both_halves(small[...], small_other[...])
    weights[count : count + 1, :] = jnp.full((1, LANES), skip_gain[0], F32)
    later = round_up(count + 1, ROWS)
    weights[later : later + taps + 1, :] = inner_taps[...]
    weights[later + taps + 1 : later + taps + 2, :] = inner_offset[...]
    plan[0, plan.shape[1] - 1] = live[0]
    save_plan = pltpu.make_async_copy(plan, plan_out, load_sem.at[0])
    save_plan.start()

    def parts(ref):
        return [ref[step * slots : (step + 1) * slots, :] for step in range(steps)]

    inner_conv = convolve(
        [inner[tap].astype(F32) for tap in range(taps)],
        parts(inner_raw),
        inner_taps[...],
        inner_offset[...],
    )
    group_conv = convolve(
        [both_halves(group[tap].astype(F32), group_other[tap].astype(F32)) for tap in range(taps)],
        parts(both),
        weights[: taps + 1, :],
        weights[taps + 1 : taps + 2, :],
    )
    for step in range(steps):
        part = slice(step * slots, (step + 1) * slots)
        driven[part, :] = delta[part, :] * inner_conv[step]
        skipped[part, :] = inner_conv[step] * skip_gain[0]
        maps_in[part, :] = group_conv[step]
    sums[...] = jnp.zeros_like(sums)
    stride = ordered.shape[0] // steps
    ordered[...] = jnp.zeros_like(ordered)
    for position in range(moving):
        slot = plan[0, position]
        for step in range(steps):
            ordered[step * stride + position : step * stride + position + 1, :] = maps_in[
                pl.ds(step * slots + slot, 1), :
            ]
    maps = [ordered[first : first + LANES].T for first in range(0, ordered.shape[0], LANES)]
    copies = []
    for position in range(moving):
        slot = plan[0, position]
        result = advance_slot(
            scan[slot],
            [pl.ds(step * slots + slot, 1) for step in range(steps)],
            driven,
            [decay[pl.ds(step * slots + slot, 1), :] for step in range(steps)],
            sums,
            maps,
            [step * stride + position for step in range(steps)],
        )
        done[position] = jnp.where(slot < live[0], result, jnp.zeros_like(result))
        copies.append(
            pltpu.make_async_copy(done.at[position], scan_next.at[slot], sem.at[position])
        )
        copies[-1].start()
    gated[...] = (sums[...] + skipped[...]) * gate[...]
    pairs = (
        (inner_raw, inner_moved),
        (both, group_moved),
        (gate, gate_moved),
        (delta, delta_moved),
        (decay, decay_moved),
    )
    for _, target in pairs:
        target[...] = jnp.zeros_like(target)
    living = lax.broadcasted_iota(jnp.int32, (slots, LANES), 0) < live[0]
    for step in range(steps):
        part = slice(step * slots, (step + 1) * slots)
        inner_part[step] = jnp.where(living, inner_raw[part, :], 0.0).astype(BF16)
        raw = jnp.where(head == 0, both[part, :width], both[part, width:])
        group_part[step] = jnp.where(living[:, :width], raw, 0.0).astype(BF16)
    base[:, :LANES] = inner[steps].astype(F32)
    group_own = group[steps].astype(F32)
    base[:, LANES:] = jnp.concatenate([group_own, group_own], axis=1)
    for block in range(moved_rows // ROWS):

        @pl.when(plan[0, moving + block * cap] >= 0)
        def _():
            for c in range(cap):
                slot = plan[0, moving + block * cap + c]
                for step in range(steps):
                    row = step * moved_rows + block * ROWS + c
                    for source, target in pairs:
                        target[row : row + 1, :] = source[pl.ds(step * slots + slot, 1), :]

    for copy in copies:
        copy.wait()
    save_plan.wait()


def stay(replicas, cap, scalars, arrays, near, earlier):
    receive, own, group_weight, delta_weight = arrays[0], arrays[1], arrays[4], arrays[5]
    inner, scan = arrays[-3], arrays[-1]
    taps, slots, _ = inner.shape
    rows = own.shape[0]
    steps = rows // slots
    moving = slots // 2
    blocks = len(sources_of(replicas))
    moved_rows = blocks * ROWS
    width, features = group_weight.shape
    full = pltpu.VMEM((rows, LANES), F32)
    moved = pltpu.VMEM((steps * moved_rows, LANES), F32)
    plan_shape = (1, round_up(moving + blocks * cap + 1, LANES))

    def like(value):
        return pltpu.VMEM(value.shape, value.dtype)

    far = [in_hbm(value) for value in arrays]
    return pl.pallas_call(
        functools.partial(stay_kernel, replicas, cap),
        out_shape=[
            pltpu.VMEM(plan_shape, jnp.int32),
            full,
            pltpu.VMEM((2 * round_up(taps + 3, ROWS), LANES), F32),
            pltpu.VMEM((slots, 2 * LANES), F32),
            pltpu.VMEM((steps, slots, LANES), BF16),
            pltpu.VMEM((steps, slots, width), BF16),
        ]
        + [moved] * 5
        + [jax.ShapeDtypeStruct(scan.shape, BF16)],
        in_specs=[SMEM] * len(scalars)
        + [HBM] * len(far)
        + [VMEM] * len(near)
        + [HBM] * len(earlier),
        out_specs=[VMEM] * 11 + [HBM],
        scratch_shapes=[
            pltpu.SMEM(plan_shape, jnp.int32),
            pltpu.SMEM(receive.shape, jnp.int32),
            like(own),
            pltpu.VMEM((features, 2 * LANES), BF16),
            pltpu.VMEM((2 * width + 2 * ROWS, features), BF16),
            like(delta_weight),
        ]
        + [like(value) for value in arrays[6:]]
        + [pltpu.SMEM((replicas * cap + 1,), jnp.int32)]
        + [pltpu.VMEM((rows, LANES), F32)] * 9
        + [
            pltpu.VMEM((round_up(rows, LANES), LANES), F32),
            pltpu.VMEM((moving,) + scan.shape[1:], BF16),
            pltpu.SemaphoreType.DMA((moving,)),
            pltpu.SemaphoreType.DMA((16,)),
        ],
        compiler_params=pltpu.CompilerParams(vmem_limit_bytes=MEDIUM_LIMIT),
        cost_estimate=pl.CostEstimate(
            flops=300_000_000, bytes_accessed=6_000_000, transcendentals=100_000
        ),
        name="advance_staying",
    )(*scalars, *far, *near, *earlier)


def arrive_kernel(
    replicas,
    cap,
    first,
    last,
    plan_near,
    weights,
    inner_moved,
    group_moved,
    gate_moved,
    delta_moved,
    decay_moved,
    gated_in,
    table_in,
    inner_part,
    group_part,
    scan_in,
    *refs,
):
    del scan_in
    if last:
        arrived = refs[:-15]
        gated_out, inner_next, group_next, scan_next = refs[-15:-11]
        gated, table = refs[-11:-9]
        gated_cast, inner_cast, group_cast = refs[-9:-6]
    else:
        arrived = refs[:-9]
        gated, table, scan_next = refs[-9:-6]
    plan, driven, sums, ordered, done, sem = refs[-6:]
    steps, slots, width = group_part.shape
    taps = steps + 1
    moving = slots // 2
    state_rows = scan_next.shape[1]
    head = lax.axis_index("head")
    load = pltpu.make_async_copy(plan_near, plan, sem.at[0])
    load.start()
    if rounds_of(replicas):
        blocks = [ref.at[0] for ref in arrived]
    else:
        blocks = [arrived[0].at[source] for source in range(replicas)]
    stored = inner_moved.shape[0] // steps
    moved_rows = len(blocks) * ROWS
    if last:
        copies = [
            pltpu.make_async_copy(source, target, sem.at[1 + place])
            for place, (source, target) in enumerate(
                [
                    (inner_part, inner_next.at[pl.ds(1, steps)]),
                    (group_part, group_next.at[pl.ds(1, steps)]),
                ]
            )
        ]
        for copy in copies:
            copy.start()

    def parts(ref):
        starts = [step * stored + first * ROWS for step in range(steps)]
        return [ref[start : start + moved_rows, :] for start in starts]

    kinds = [[] for _ in range(2 * taps)]
    for ref in blocks:
        block = ref[cap * state_rows :, :].astype(F32)
        for kind in range(2 * taps):
            kinds[kind].append(block[kind * ROWS : (kind + 1) * ROWS])
    windows = [jnp.concatenate(kind, axis=0) for kind in kinds]
    later = round_up(taps + 3, ROWS)
    inner_conv = convolve(
        windows[:taps],
        parts(inner_moved),
        weights[later : later + taps + 1, :],
        weights[later + taps + 1 : later + taps + 2, :],
    )
    group_conv = convolve(
        windows[taps:],
        parts(group_moved),
        weights[: taps + 1, :],
        weights[taps + 1 : taps + 2, :],
    )
    for step, delta in enumerate(parts(delta_moved)):
        driven[step * moved_rows : (step + 1) * moved_rows, :] = delta * inner_conv[step]
    stride = ordered.shape[0] // steps
    maps = transposed(group_conv, ordered, stride)
    sums[...] = jnp.zeros_like(sums)
    gated[...] = gated_in[...]
    table[...] = table_in[...]
    load.wait()
    live = plan[0, plan.shape[1] - 1]

    def each(act):
        for block in range(len(blocks)):
            entry = moving + (first + block) * cap

            @pl.when(plan[0, entry] >= 0)
            def _():
                for c in range(cap):
                    act(block, c, plan[0, entry + c])

    def store(block, c, slot):
        place = block * cap + c
        return pltpu.make_async_copy(done.at[place], scan_next.at[slot], sem.at[4 + place])

    def advance(block, c, slot):
        place = block * ROWS + c
        rows = [step * moved_rows + place for step in range(steps)]
        result = advance_slot(
            blocks[block][c * state_rows : (c + 1) * state_rows, :],
            [slice(row, row + 1) for row in rows],
            driven,
            [
                decay_moved[row : row + 1, :]
                for row in (step * stored + first * ROWS + place for step in range(steps))
            ],
            sums,
            maps,
            [step * stride + place for step in range(steps)],
        )
        done[block * cap + c] = jnp.where(slot < live, result, jnp.zeros_like(result))
        store(block, c, slot).start()

    each(advance)
    for step, gate in enumerate(parts(gate_moved)):
        part = slice(step * moved_rows, (step + 1) * moved_rows)
        skipped = inner_conv[step] * weights[taps + 2 : taps + 3, :]
        sums[part, :] = (sums[part, :] + skipped) * gate
    driven[:moved_rows, :] = windows[taps - 1]
    driven[moved_rows : 2 * moved_rows, :] = windows[2 * taps - 1]

    def scatter(block, c, slot):
        place = block * ROWS + c
        for step in range(steps):
            row = step * moved_rows + place
            gated[pl.ds(step * slots + slot, 1), :] = sums[row : row + 1, :]
        table[pl.ds(slot, 1), :] = jnp.concatenate(
            [driven[place : place + 1, :], driven[moved_rows + place : moved_rows + place + 1, :]],
            axis=1,
        )

    each(scatter)
    if last:
        living = lax.broadcasted_iota(jnp.int32, (slots, LANES), 0) < live
        for step in range(steps):
            part = slice(step * slots, (step + 1) * slots)
            gated_cast[step] = jnp.where(living, gated[part, :], 0.0).astype(BF16)
        inner_cast[0] = jnp.where(living, table[:, :LANES], 0.0).astype(BF16)
        carried = jnp.where(head == 0, table[:, LANES : LANES + width], table[:, LANES + width :])
        group_cast[0] = jnp.where(living[:, :width], carried, 0.0).astype(BF16)
        ends = [
            pltpu.make_async_copy(source, target, semaphore)
            for source, target, semaphore in (
                (gated_cast, gated_out, sem.at[0]),
                (inner_cast, inner_next.at[pl.ds(0, 1)], sem.at[3]),
                (group_cast, group_next.at[pl.ds(0, 1)], sem.at[sem.shape[0] - 1]),
            )
        ]
        for copy in ends:
            copy.start()
        for copy in copies + ends:
            copy.wait()
    each(lambda block, c, slot: store(block, c, slot).wait())


def arrive(replicas, cap, first, last, operands, scan_next, arrived):
    inner_moved, gated, table, inner_part, group_part = operands[2], *operands[7:]
    steps, slots, width = group_part.shape
    blocks = len(arrived) if rounds_of(replicas) else replicas
    moved = (steps * blocks * ROWS, LANES)
    carried = [pltpu.VMEM(value.shape, F32) for value in (gated, table)]
    scan_shape = jax.ShapeDtypeStruct(scan_next.shape, BF16)
    if last:
        outs = [
            jax.ShapeDtypeStruct((steps, slots, LANES), BF16),
            jax.ShapeDtypeStruct((steps + 1, slots, LANES), BF16),
            jax.ShapeDtypeStruct((steps + 1, slots, width), BF16),
            scan_shape,
        ]
        scratch = carried + [
            pltpu.VMEM((steps, slots, LANES), BF16),
            pltpu.VMEM((1, slots, LANES), BF16),
            pltpu.VMEM((1, slots, width), BF16),
        ]
        specs = [HBM] * 4
    else:
        outs, scratch, specs = carried + [scan_shape], [], [VMEM, VMEM, HBM]
    plan = operands[0]
    return pl.pallas_call(
        functools.partial(arrive_kernel, replicas, cap, first, last),
        out_shape=outs,
        in_specs=[VMEM] * len(operands) + [HBM] + [VMEM] * len(arrived),
        out_specs=specs,
        scratch_shapes=scratch
        + [
            pltpu.SMEM(plan.shape, plan.dtype),
            pltpu.VMEM(moved, F32),
            pltpu.VMEM(moved, F32),
            pltpu.VMEM((round_up(moved[0], LANES), LANES), F32),
            pltpu.VMEM((blocks * cap,) + scan_next.shape[1:], BF16),
            pltpu.SemaphoreType.DMA((blocks * cap + 5,)),
        ],
        input_output_aliases={len(operands): len(outs) - 1},
        compiler_params=pltpu.CompilerParams(
            vmem_limit_bytes=SMALL_LIMIT if rounds_of(replicas) else LARGE_LIMIT
        ),
        cost_estimate=pl.CostEstimate(
            flops=10_000_000, bytes_accessed=2_000_000, transcendentals=0
        ),
        name="advance_last" if last else "advance_arrived",
    )(*operands, scan_next, *arrived)


def swap_heads(value):
    return lax.ppermute(value, "head", [(0, 1), (1, 0)])


def exchange(replicas, blocks):
    rounds = rounds_of(replicas)
    if not rounds:
        return [lax.all_to_all(blocks[0], "dp", 0, 0, tiled=True)]
    return [
        lax.ppermute(block, "dp", [(source, source ^ mask) for source in range(replicas)])
        for mask, block in zip(rounds, blocks)
    ]


def per_device(
    replicas,
    tokens,
    inner_weight,
    gate_weight,
    group_weight,
    delta_weight,
    inner_taps,
    inner_offset,
    group_taps,
    group_offset,
    decay_log,
    delta_bias,
    skip_gain,
    inner_window,
    group_window,
    scan_state,
    send_list,
    receive_list,
    live_count,
):
    steps, slots, half = tokens.shape
    cap = send_list.shape[1] // replicas
    scan = jnp.transpose(scan_state, (0, 2, 1))
    inner = jnp.transpose(inner_window, (1, 0, 2))
    group = jnp.transpose(group_window, (1, 0, 2))
    own = tokens.reshape(steps * slots, half)

    group_weight = group_weight.T
    inner_offset = inner_offset[None]
    small = jnp.concatenate([group_taps, group_offset[None]], axis=0)
    group_other = swap_heads(group)
    swapped = [swap_heads(value) for value in (own, group_weight, small)]
    blocks = pack(replicas, cap, send_list, scan, inner, group, group_other, swapped)
    arrived = exchange(replicas, blocks)
    plan, gated, weights, table, inner_part, group_part, *moved, scan_next = stay(
        replicas,
        cap,
        (decay_log, delta_bias, skip_gain, live_count),
        (
            receive_list,
            own,
            inner_weight,
            gate_weight,
            group_weight,
            delta_weight.T,
            inner_taps,
            inner_offset,
            inner,
            group,
            scan,
        ),
        (swapped[0], swapped[1], small, swapped[2], group_other),
        arrived[:EARLIER] if rounds_of(replicas) else [],
    )
    first = max(0, len(arrived) - LAST)
    if first:
        operands = (plan, weights, *moved, gated, table, inner_part, group_part)
        gated, table, scan_next = arrive(
            replicas, cap, 0, False, operands, scan_next, arrived[:first]
        )
    operands = (plan, weights, *moved, gated, table, inner_part, group_part)
    gated, inner_next, group_next, scan_next = arrive(
        replicas, cap, first, True, operands, scan_next, arrived[first:]
    )
    return (
        gated,
        jnp.transpose(inner_next, (1, 0, 2)),
        jnp.transpose(group_next, (1, 0, 2)),
        jnp.transpose(scan_next, (0, 2, 1)),
    )


def solution(mesh):
    in_specs = (
        P(None, ("grp", "dp"), "head"),
        P(None, "head"),
        P(None, "head"),
        P(None, "head"),
        P(None, "head"),
        P(None, "head"),
        P("head"),
        P(None, "head"),
        P("head"),
        P("head"),
        P("head"),
        P("head"),
        P(("grp", "dp"), None, "head"),
        P(("grp", "dp"), None, "head"),
        P(("grp", "dp"), "head", None),
        P(("grp", "dp"), None),
        P(("grp", "dp"), None),
        P(("grp", "dp")),
    )
    out_specs = (
        P(None, ("grp", "dp"), "head"),
        P(("grp", "dp"), None, "head"),
        P(("grp", "dp"), None, "head"),
        P(("grp", "dp"), "head", None),
    )
    return jax.shard_map(
        functools.partial(per_device, mesh.shape["dp"]),
        mesh=mesh,
        in_specs=in_specs,
        out_specs=out_specs,
        check_vma=False,
    )
```

```python
import functools

import jax
import jax.numpy as jnp
from jax import lax
from jax.experimental import pallas as pl
from jax.experimental.pallas import tpu as pltpu
from jax.sharding import PartitionSpec as P

F32 = jnp.float32
BF16 = jnp.bfloat16
SMALL_LIMIT = 8 * 1024 * 1024
MEDIUM_LIMIT = 16 * 1024 * 1024
LARGE_LIMIT = 48 * 1024 * 1024
MAX_ROUNDS = 16
EARLIER = 3
LAST = 2
LANES = 128
ROWS = 8
MAX_SETS = 64

VMEM = pl.BlockSpec(memory_space=pltpu.VMEM)
SMEM = pl.BlockSpec(memory_space=pltpu.SMEM)
HBM = pl.BlockSpec(memory_space=pl.ANY)


def in_hbm(value):
    return pltpu.with_memory_space_constraint(value, pltpu.HBM)


def in_vmem(value):
    return pltpu.with_memory_space_constraint(value, pltpu.VMEM)


def round_up(value, step):
    return -(-value // step) * step


def silu(value):
    return value * jax.nn.sigmoid(value)


def rounded(value):
    return value.astype(BF16).astype(F32)


def rounds_of(replicas):
    if replicas > MAX_ROUNDS or replicas & (replicas - 1):
        return []
    light = list(range(1, replicas // 2))
    heavy = list(range(replicas // 2, replicas))
    return heavy[:1] + light[:2] + heavy[1:2] + light[2:] + heavy[2:]


def partner(replicas, mask):
    return jnp.bitwise_xor(lax.axis_index("dp"), mask)


def both_halves(mine, theirs):
    first = lax.axis_index("head") == 0
    return jnp.concatenate(
        [jnp.where(first, mine, theirs), jnp.where(first, theirs, mine)], axis=-1
    )


def destinations(replicas, outs):
    rounds = rounds_of(replicas)
    if rounds:
        return [(ref.at[0], partner(replicas, mask)) for ref, mask in zip(outs, rounds)]
    return [(outs[0].at[target], target) for target in range(replicas)]


def states_kernel(replicas, cap, scan, send, inner, group, *refs):
    outs, (picked, group_out, indices_out) = refs[:-11], refs[-11:-8]
    indices, inner_in, table, load_sem, group_sem, list_sem, save_sem, sem = refs[-8:]
    load_list = pltpu.make_async_copy(send, indices, list_sem)
    load_list.start()
    load = pltpu.make_async_copy(inner, inner_in, load_sem)
    load.start()
    load_group = pltpu.make_async_copy(group, group_out, group_sem)
    load_group.start()
    state_rows = scan.shape[1]
    blocks = destinations(replicas, outs)
    load_list.wait()
    save = pltpu.make_async_copy(indices, indices_out, save_sem)
    save.start()
    plan = []
    for block, (ref, target) in enumerate(blocks):
        for c in range(cap):
            plan.append((block, ref, c, indices[0, target * cap + c]))

    def each(act):
        for place, (_, ref, c, index) in enumerate(plan):

            @pl.when(index >= 0)
            def _():
                act(
                    pltpu.make_async_copy(
                        scan.at[index],
                        ref.at[pl.ds(c * state_rows, state_rows)],
                        sem.at[place],
                    )
                )

    each(lambda copy: copy.start())
    load.wait()
    taps = inner_in.shape[0]
    for tap in range(taps):
        table[:, tap * LANES : (tap + 1) * LANES] = inner_in[tap].astype(F32)
    picked[...] = jnp.zeros_like(picked)
    for block, _, c, index in plan:
        row = table[pl.ds(jnp.maximum(index, 0), 1), :]
        for tap in range(taps):
            picked[block, tap * ROWS + c : tap * ROWS + c + 1, :] = row[
                :, tap * LANES : (tap + 1) * LANES
            ]
    load_group.wait()
    save.wait()
    each(lambda copy: copy.wait())


def windows_kernel(replicas, cap, state_rows, indices_in, group, group_other, picked_in, *refs):
    count = max(1, len(rounds_of(replicas)))
    outs = refs[-4 - count : -4]
    indices, table, picked, sem = refs[-4:]
    load = pltpu.make_async_copy(indices_in, indices, sem)
    load.start()
    taps = group.shape[0]
    for tap in range(taps):
        table[:, tap * LANES : (tap + 1) * LANES] = both_halves(
            group[tap].astype(F32), group_other[tap].astype(F32)
        )
    picked[...] = jnp.zeros_like(picked)
    load.wait()
    for block, (ref, target) in enumerate(destinations(replicas, outs)):
        for c in range(cap):
            index = jnp.maximum(indices[0, target * cap + c], 0)
            row = table[pl.ds(index, 1), :]
            for tap in range(taps):
                picked[block, tap * ROWS + c : tap * ROWS + c + 1, :] = row[
                    :, tap * LANES : (tap + 1) * LANES
                ]
        ref[cap * state_rows :, :] = jnp.concatenate(
            [picked_in[block], picked[block]], axis=0
        ).astype(BF16)


def pack(replicas, cap, send_list, scan, inner, group, group_other, swapped):
    rounds = rounds_of(replicas)
    count = max(1, len(rounds))
    per_block = 1 if rounds else replicas
    taps, slots, _ = inner.shape
    rows = cap * scan.shape[1] + 2 * taps * ROWS
    blocks = count * per_block
    shapes = [pltpu.VMEM((per_block, rows, LANES), BF16)] * count
    half = (blocks, taps * ROWS, LANES)
    limit = SMALL_LIMIT if rounds else MEDIUM_LIMIT
    *states, picked, group_near, indices = pl.pallas_call(
        functools.partial(states_kernel, replicas, cap),
        out_shape=shapes
        + [
            pltpu.VMEM(half, F32),
            pltpu.VMEM(group.shape, BF16),
            pltpu.VMEM(send_list.shape, jnp.int32),
        ],
        in_specs=[HBM] * 4,
        out_specs=[VMEM] * (count + 3),
        scratch_shapes=[
            pltpu.SMEM(send_list.shape, jnp.int32),
            pltpu.VMEM(inner.shape, BF16),
            pltpu.VMEM((slots, taps * LANES), F32),
            pltpu.SemaphoreType.DMA,
            pltpu.SemaphoreType.DMA,
            pltpu.SemaphoreType.DMA,
            pltpu.SemaphoreType.DMA,
            pltpu.SemaphoreType.DMA((blocks * cap,)),
        ],
        compiler_params=pltpu.CompilerParams(vmem_limit_bytes=limit),
        cost_estimate=pl.CostEstimate(flops=0, bytes_accessed=2_000_000, transcendentals=0),
        name="pack_states",
    )(in_hbm(scan), in_hbm(send_list), in_hbm(inner), in_hbm(group))
    near = [in_vmem(value) for value in states]
    return pl.pallas_call(
        functools.partial(windows_kernel, replicas, cap, scan.shape[1]),
        out_shape=shapes,
        in_specs=[VMEM] * (4 + count) + [HBM] * len(swapped),
        out_specs=[VMEM] * count,
        scratch_shapes=[
            pltpu.SMEM(send_list.shape, jnp.int32),
            pltpu.VMEM((slots, taps * LANES), F32),
            pltpu.VMEM(half, F32),
            pltpu.SemaphoreType.DMA,
        ],
        input_output_aliases={4 + place: place for place in range(count)},
        compiler_params=pltpu.CompilerParams(vmem_limit_bytes=limit),
        cost_estimate=pl.CostEstimate(flops=0, bytes_accessed=500_000, transcendentals=0),
        name="pack_windows",
    )(indices, group_near, group_other, picked, *near, *swapped)


def at_once_kernel(replicas, cap, scan, send, inner, group, group_other, *refs):
    rounds = rounds_of(replicas)
    count = max(1, len(rounds))
    outs = refs[-8 - count : -8]
    indices, inner_in, group_in, table, picked, load_sem, list_sem, sem = refs[-8:]
    load_list = pltpu.make_async_copy(send, indices, list_sem)
    load_list.start()
    loads = [
        pltpu.make_async_copy(source, target, load_sem.at[place])
        for place, (source, target) in enumerate([(inner, inner_in), (group, group_in)])
    ]
    for load in loads:
        load.start()
    state_rows = scan.shape[1]
    if rounds:
        blocks = [(ref.at[0], partner(replicas, mask)) for ref, mask in zip(outs, rounds)]
    else:
        blocks = [(outs[0].at[target], target) for target in range(replicas)]
    load_list.wait()

    plan = []
    for block, (ref, target) in enumerate(blocks):
        for c in range(cap):
            plan.append((block, ref, c, indices[0, target * cap + c]))

    def each(act):
        for place, (_, ref, c, index) in enumerate(plan):

            @pl.when(index >= 0)
            def _():
                act(
                    pltpu.make_async_copy(
                        scan.at[index],
                        ref.at[pl.ds(c * state_rows, state_rows)],
                        sem.at[place],
                    )
                )

    each(lambda copy: copy.start())
    for load in loads:
        load.wait()
    taps = inner_in.shape[0]
    for tap in range(taps):
        table[:, tap * LANES : (tap + 1) * LANES] = inner_in[tap].astype(F32)
        table[:, (taps + tap) * LANES : (taps + tap + 1) * LANES] = both_halves(
            group_in[tap].astype(F32), group_other[tap].astype(F32)
        )
    picked[...] = jnp.zeros_like(picked)
    for block, _, c, index in plan:
        row = table[pl.ds(jnp.maximum(index, 0), 1), :]
        for kind in range(2 * taps):
            picked[block, kind * ROWS + c : kind * ROWS + c + 1, :] = row[
                :, kind * LANES : (kind + 1) * LANES
            ]
    for block, (ref, _) in enumerate(blocks):
        ref[cap * state_rows :, :] = picked[block].astype(BF16)
    each(lambda copy: copy.wait())


def pack_at_once(replicas, cap, send_list, scan, inner, group, group_other):
    rounds = rounds_of(replicas)
    count = max(1, len(rounds))
    per_block = 1 if rounds else replicas
    taps, slots, _ = inner.shape
    window_rows = 2 * taps * ROWS
    rows = cap * scan.shape[1] + window_rows
    blocks = count * per_block
    return pl.pallas_call(
        functools.partial(at_once_kernel, replicas, cap),
        out_shape=[jax.ShapeDtypeStruct((per_block, rows, LANES), BF16)] * count,
        in_specs=[HBM] * 4 + [VMEM],
        out_specs=[VMEM] * count,
        scratch_shapes=[
            pltpu.SMEM(send_list.shape, jnp.int32),
            pltpu.VMEM(inner.shape, BF16),
            pltpu.VMEM(group.shape, BF16),
            pltpu.VMEM((slots, 2 * taps * LANES), F32),
            pltpu.VMEM((blocks, window_rows, LANES), F32),
            pltpu.SemaphoreType.DMA((2,)),
            pltpu.SemaphoreType.DMA,
            pltpu.SemaphoreType.DMA((blocks * cap,)),
        ],
        compiler_params=pltpu.CompilerParams(vmem_limit_bytes=LARGE_LIMIT),
        cost_estimate=pl.CostEstimate(flops=0, bytes_accessed=2_000_000, transcendentals=0),
        name="pack_leaving",
    )(in_hbm(scan), in_hbm(send_list), in_hbm(inner), in_hbm(group), group_other)


def sources_of(replicas):
    rounds = rounds_of(replicas)
    if rounds:
        return [partner(replicas, mask) for mask in rounds]
    return list(range(replicas))


def make_plan(replicas, cap, receive, slots, plan, inverse):
    moving = slots // 2
    kept = 0
    for entry in range(replicas * cap):
        inverse[entry] = -1
    for slot in range(slots):
        entry = receive[0, slot]
        stays = entry < 0
        plan[0, jnp.where(stays, kept, moving)] = slot
        inverse[jnp.where(stays, replicas * cap, entry)] = slot
        kept = kept + jnp.where(stays, 1, 0)
    for block, source in enumerate(sources_of(replicas)):
        for c in range(cap):
            plan[0, moving + block * cap + c] = inverse[source * cap + c]


def convolve(carried, raw, weights, offset):
    joined = carried + raw
    results = []
    for step in range(len(raw)):
        summed = offset
        for tap in range(len(carried) + 1):
            summed = summed + joined[step + tap] * weights[tap : tap + 1, :]
        results.append(rounded(silu(summed)))
    return results


def transposed(rows, scratch, stride):
    scratch[...] = jnp.zeros_like(scratch)
    for step, value in enumerate(rows):
        scratch[step * stride : step * stride + value.shape[0], :] = value
    return [scratch[first : first + LANES].T for first in range(0, scratch.shape[0], LANES)]


def advance_slot(state, rows, driven, decays, sums, maps, lanes):
    hidden = state.astype(F32)
    width = state.shape[0]
    for row, decay, lane in zip(rows, decays, lanes):
        piece = maps[lane // LANES]
        column = piece[:, lane % LANES : lane % LANES + 1]
        hidden = decay * hidden + driven[row, :] * column[:width]
        sums[row, :] = jnp.sum(hidden * column[width:], axis=0, keepdims=True)
        result = hidden.astype(BF16)
        hidden = result.astype(F32)
    return result


def stay_kernel(
    replicas,
    cap,
    decay_log,
    delta_bias,
    skip_gain,
    live,
    receive_hbm,
    own_hbm,
    inner_weight,
    gate_weight,
    group_weight,
    delta_weight,
    inner_taps_hbm,
    inner_offset_hbm,
    inner_hbm,
    group_hbm,
    scan_hbm,
    other,
    group_weight_other,
    small,
    small_other,
    group_other,
    *refs,
):
    (
        plan_out,
        gated,
        weights,
        base,
        inner_part,
        group_part,
        inner_moved,
        group_moved,
        gate_moved,
        delta_moved,
        decay_moved,
        scan_next,
        plan,
        receive,
        own,
        wide,
        tall,
        delta_row,
        inner_taps,
        inner_offset,
        inner,
        group,
        scan,
        inverse,
        inner_raw,
        both,
        gate,
        delta,
        decay,
        driven,
        skipped,
        sums,
        maps_in,
        ordered,
        done,
        sem,
        load_sem,
    ) = refs[-37:]
    taps, slots, _ = inner.shape
    rows, half = own.shape
    steps = rows // slots
    moving = slots // 2
    moved_rows = inner_moved.shape[0] // steps
    width = group.shape[2]
    head = lax.axis_index("head")

    def band(place):
        return tall.at[pl.ds(pl.multiple_of(place * width, width), width)]

    pairs = [
        (receive_hbm, receive),
        (delta_weight, delta_row),
        (own_hbm, own),
        (inner_weight, wide.at[:, pl.ds(0, LANES)]),
        (gate_weight, wide.at[:, pl.ds(LANES, LANES)]),
        (group_weight, band(head)),
        (group_weight_other, band(1 - head)),
        (inner_taps_hbm, inner_taps),
        (inner_offset_hbm, inner_offset),
        (inner_hbm, inner),
        (group_hbm, group),
        (scan_hbm, scan),
    ]
    loads = [
        pltpu.make_async_copy(source, target, load_sem.at[place])
        for place, (source, target) in enumerate(pairs)
    ]
    for load in loads:
        load.start()
    loads[0].wait()
    make_plan(replicas, cap, receive, slots, plan, inverse)
    loads[1].wait()
    first = 2 * width
    tall[first:, :] = jnp.broadcast_to(delta_row[...], (tall.shape[0] - first, 2 * half))
    for load in loads[2:]:
        load.wait()
    mine = pl.ds(pl.multiple_of(head * half, half), half)
    theirs = pl.ds(pl.multiple_of((1 - head) * half, half), half)
    flat = jnp.dot(own[...], wide[mine, :], preferred_element_type=F32) + jnp.dot(
        other[...], wide[theirs, :], preferred_element_type=F32
    )

    def across(tokens, part):
        return lax.dot_general(
            tokens, tall[:, part], (((1,), (1,)), ((), ())), preferred_element_type=F32
        )

    deep = across(own[...], mine) + across(other[...], theirs)
    inner_raw[...] = rounded(flat[:, :LANES])
    gate[...] = silu(rounded(flat[:, LANES:]))
    both[...] = rounded(deep[:, :first])
    shifted = rounded(jnp.broadcast_to(deep[:, first : first + 1], (rows, LANES)))
    shifted = shifted + delta_bias[0]
    rate = jnp.maximum(shifted, 0.0) + jnp.log1p(jnp.exp(-jnp.abs(shifted)))
    delta[...] = rate
    decay[...] = jnp.exp(-rate * jnp.exp(jnp.full((1, LANES), decay_log[0], F32)))
    count = taps + 2
    weights[:count, :] = both_halves(small[...], small_other[...])
    weights[count : count + 1, :] = jnp.full((1, LANES), skip_gain[0], F32)
    later = round_up(count + 1, ROWS)
    weights[later : later + taps + 1, :] = inner_taps[...]
    weights[later + taps + 1 : later + taps + 2, :] = inner_offset[...]
    plan[0, plan.shape[1] - 1] = live[0]
    save_plan = pltpu.make_async_copy(plan, plan_out, load_sem.at[0])
    save_plan.start()

    def parts(ref):
        return [ref[step * slots : (step + 1) * slots, :] for step in range(steps)]

    inner_conv = convolve(
        [inner[tap].astype(F32) for tap in range(taps)],
        parts(inner_raw),
        inner_taps[...],
        inner_offset[...],
    )
    group_conv = convolve(
        [both_halves(group[tap].astype(F32), group_other[tap].astype(F32)) for tap in range(taps)],
        parts(both),
        weights[: taps + 1, :],
        weights[taps + 1 : taps + 2, :],
    )
    for step in range(steps):
        part = slice(step * slots, (step + 1) * slots)
        driven[part, :] = delta[part, :] * inner_conv[step]
        skipped[part, :] = inner_conv[step] * skip_gain[0]
        maps_in[part, :] = group_conv[step]
    sums[...] = jnp.zeros_like(sums)
    stride = ordered.shape[0] // steps
    ordered[...] = jnp.zeros_like(ordered)
    for position in range(moving):
        slot = plan[0, position]
        for step in range(steps):
            ordered[step * stride + position : step * stride + position + 1, :] = maps_in[
                pl.ds(step * slots + slot, 1), :
            ]
    maps = [ordered[first : first + LANES].T for first in range(0, ordered.shape[0], LANES)]
    copies = []
    for position in range(moving):
        slot = plan[0, position]
        result = advance_slot(
            scan[slot],
            [pl.ds(step * slots + slot, 1) for step in range(steps)],
            driven,
            [decay[pl.ds(step * slots + slot, 1), :] for step in range(steps)],
            sums,
            maps,
            [step * stride + position for step in range(steps)],
        )
        done[position] = jnp.where(slot < live[0], result, jnp.zeros_like(result))
        copies.append(
            pltpu.make_async_copy(done.at[position], scan_next.at[slot], sem.at[position])
        )
        copies[-1].start()
    gated[...] = (sums[...] + skipped[...]) * gate[...]
    pairs = (
        (inner_raw, inner_moved),
        (both, group_moved),
        (gate, gate_moved),
        (delta, delta_moved),
        (decay, decay_moved),
    )
    for _, target in pairs:
        target[...] = jnp.zeros_like(target)
    living = lax.broadcasted_iota(jnp.int32, (slots, LANES), 0) < live[0]
    for step in range(steps):
        part = slice(step * slots, (step + 1) * slots)
        inner_part[step] = jnp.where(living, inner_raw[part, :], 0.0).astype(BF16)
        raw = jnp.where(head == 0, both[part, :width], both[part, width:])
        group_part[step] = jnp.where(living[:, :width], raw, 0.0).astype(BF16)
    base[:, :LANES] = inner[steps].astype(F32)
    group_own = group[steps].astype(F32)
    base[:, LANES:] = jnp.concatenate([group_own, group_own], axis=1)
    for block in range(moved_rows // ROWS):

        @pl.when(plan[0, moving + block * cap] >= 0)
        def _():
            for c in range(cap):
                slot = plan[0, moving + block * cap + c]
                for step in range(steps):
                    row = step * moved_rows + block * ROWS + c
                    for source, target in pairs:
                        target[row : row + 1, :] = source[pl.ds(step * slots + slot, 1), :]

    for copy in copies:
        copy.wait()
    save_plan.wait()


def stay(replicas, cap, scalars, arrays, near, earlier):
    receive, own, group_weight, delta_weight = arrays[0], arrays[1], arrays[4], arrays[5]
    inner, scan = arrays[-3], arrays[-1]
    taps, slots, _ = inner.shape
    rows = own.shape[0]
    steps = rows // slots
    moving = slots // 2
    blocks = len(sources_of(replicas))
    moved_rows = blocks * ROWS
    width, features = group_weight.shape
    full = pltpu.VMEM((rows, LANES), F32)
    moved = pltpu.VMEM((steps * moved_rows, LANES), F32)
    plan_shape = (1, round_up(moving + blocks * cap + 1, LANES))

    def like(value):
        return pltpu.VMEM(value.shape, value.dtype)

    far = [in_hbm(value) for value in arrays]
    return pl.pallas_call(
        functools.partial(stay_kernel, replicas, cap),
        out_shape=[
            pltpu.VMEM(plan_shape, jnp.int32),
            full,
            pltpu.VMEM((2 * round_up(taps + 3, ROWS), LANES), F32),
            pltpu.VMEM((slots, 2 * LANES), F32),
            pltpu.VMEM((steps, slots, LANES), BF16),
            pltpu.VMEM((steps, slots, width), BF16),
        ]
        + [moved] * 5
        + [jax.ShapeDtypeStruct(scan.shape, BF16)],
        in_specs=[SMEM] * len(scalars)
        + [HBM] * len(far)
        + [VMEM] * len(near)
        + [HBM] * len(earlier),
        out_specs=[VMEM] * 11 + [HBM],
        scratch_shapes=[
            pltpu.SMEM(plan_shape, jnp.int32),
            pltpu.SMEM(receive.shape, jnp.int32),
            like(own),
            pltpu.VMEM((features, 2 * LANES), BF16),
            pltpu.VMEM((2 * width + 2 * ROWS, features), BF16),
            like(delta_weight),
        ]
        + [like(value) for value in arrays[6:]]
        + [pltpu.SMEM((replicas * cap + 1,), jnp.int32)]
        + [pltpu.VMEM((rows, LANES), F32)] * 9
        + [
            pltpu.VMEM((round_up(rows, LANES), LANES), F32),
            pltpu.VMEM((moving,) + scan.shape[1:], BF16),
            pltpu.SemaphoreType.DMA((moving,)),
            pltpu.SemaphoreType.DMA((16,)),
        ],
        compiler_params=pltpu.CompilerParams(vmem_limit_bytes=MEDIUM_LIMIT),
        cost_estimate=pl.CostEstimate(
            flops=300_000_000, bytes_accessed=6_000_000, transcendentals=100_000
        ),
        name="advance_staying",
    )(*scalars, *far, *near, *earlier)


def arrive_kernel(
    replicas,
    cap,
    first,
    last,
    plan_near,
    weights,
    inner_moved,
    group_moved,
    gate_moved,
    delta_moved,
    decay_moved,
    gated_in,
    table_in,
    inner_part,
    group_part,
    scan_in,
    *refs,
):
    del scan_in
    if last:
        arrived = refs[:-15]
        gated_out, inner_next, group_next, scan_next = refs[-15:-11]
        gated, table = refs[-11:-9]
        gated_cast, inner_cast, group_cast = refs[-9:-6]
    else:
        arrived = refs[:-9]
        gated, table, scan_next = refs[-9:-6]
    plan, driven, sums, ordered, done, sem = refs[-6:]
    steps, slots, width = group_part.shape
    taps = steps + 1
    moving = slots // 2
    state_rows = scan_next.shape[1]
    head = lax.axis_index("head")
    load = pltpu.make_async_copy(plan_near, plan, sem.at[0])
    load.start()
    if rounds_of(replicas):
        blocks = [ref.at[0] for ref in arrived]
    else:
        blocks = [arrived[0].at[source] for source in range(replicas)]
    stored = inner_moved.shape[0] // steps
    moved_rows = len(blocks) * ROWS
    if last:
        copies = [
            pltpu.make_async_copy(source, target, sem.at[1 + place])
            for place, (source, target) in enumerate(
                [
                    (inner_part, inner_next.at[pl.ds(1, steps)]),
                    (group_part, group_next.at[pl.ds(1, steps)]),
                ]
            )
        ]
        for copy in copies:
            copy.start()

    def parts(ref):
        starts = [step * stored + first * ROWS for step in range(steps)]
        return [ref[start : start + moved_rows, :] for start in starts]

    kinds = [[] for _ in range(2 * taps)]
    for ref in blocks:
        block = ref[cap * state_rows :, :].astype(F32)
        for kind in range(2 * taps):
            kinds[kind].append(block[kind * ROWS : (kind + 1) * ROWS])
    windows = [jnp.concatenate(kind, axis=0) for kind in kinds]
    later = round_up(taps + 3, ROWS)
    inner_conv = convolve(
        windows[:taps],
        parts(inner_moved),
        weights[later : later + taps + 1, :],
        weights[later + taps + 1 : later + taps + 2, :],
    )
    group_conv = convolve(
        windows[taps:],
        parts(group_moved),
        weights[: taps + 1, :],
        weights[taps + 1 : taps + 2, :],
    )
    for step, delta in enumerate(parts(delta_moved)):
        driven[step * moved_rows : (step + 1) * moved_rows, :] = delta * inner_conv[step]
    stride = ordered.shape[0] // steps
    maps = transposed(group_conv, ordered, stride)
    sums[...] = jnp.zeros_like(sums)
    gated[...] = gated_in[...]
    table[...] = table_in[...]
    load.wait()
    live = plan[0, plan.shape[1] - 1]

    def each(act):
        for block in range(len(blocks)):
            entry = moving + (first + block) * cap

            @pl.when(plan[0, entry] >= 0)
            def _():
                for c in range(cap):
                    act(block, c, plan[0, entry + c])

    def store(block, c, slot):
        place = block * cap + c
        return pltpu.make_async_copy(done.at[place], scan_next.at[slot], sem.at[4 + place])

    def advance(block, c, slot):
        place = block * ROWS + c
        rows = [step * moved_rows + place for step in range(steps)]
        result = advance_slot(
            blocks[block][c * state_rows : (c + 1) * state_rows, :],
            [slice(row, row + 1) for row in rows],
            driven,
            [
                decay_moved[row : row + 1, :]
                for row in (step * stored + first * ROWS + place for step in range(steps))
            ],
            sums,
            maps,
            [step * stride + place for step in range(steps)],
        )
        done[block * cap + c] = jnp.where(slot < live, result, jnp.zeros_like(result))
        store(block, c, slot).start()

    each(advance)
    for step, gate in enumerate(parts(gate_moved)):
        part = slice(step * moved_rows, (step + 1) * moved_rows)
        skipped = inner_conv[step] * weights[taps + 2 : taps + 3, :]
        sums[part, :] = (sums[part, :] + skipped) * gate
    driven[:moved_rows, :] = windows[taps - 1]
    driven[moved_rows : 2 * moved_rows, :] = windows[2 * taps - 1]

    def scatter(block, c, slot):
        place = block * ROWS + c
        for step in range(steps):
            row = step * moved_rows + place
            gated[pl.ds(step * slots + slot, 1), :] = sums[row : row + 1, :]
        table[pl.ds(slot, 1), :] = jnp.concatenate(
            [driven[place : place + 1, :], driven[moved_rows + place : moved_rows + place + 1, :]],
            axis=1,
        )

    each(scatter)
    if last:
        living = lax.broadcasted_iota(jnp.int32, (slots, LANES), 0) < live
        for step in range(steps):
            part = slice(step * slots, (step + 1) * slots)
            gated_cast[step] = jnp.where(living, gated[part, :], 0.0).astype(BF16)
        inner_cast[0] = jnp.where(living, table[:, :LANES], 0.0).astype(BF16)
        carried = jnp.where(head == 0, table[:, LANES : LANES + width], table[:, LANES + width :])
        group_cast[0] = jnp.where(living[:, :width], carried, 0.0).astype(BF16)
        ends = [
            pltpu.make_async_copy(source, target, semaphore)
            for source, target, semaphore in (
                (gated_cast, gated_out, sem.at[0]),
                (inner_cast, inner_next.at[pl.ds(0, 1)], sem.at[3]),
                (group_cast, group_next.at[pl.ds(0, 1)], sem.at[sem.shape[0] - 1]),
            )
        ]
        for copy in ends:
            copy.start()
        for copy in copies + ends:
            copy.wait()
    each(lambda block, c, slot: store(block, c, slot).wait())


def arrive(replicas, cap, first, last, operands, scan_next, arrived):
    inner_moved, gated, table, inner_part, group_part = operands[2], *operands[7:]
    steps, slots, width = group_part.shape
    blocks = len(arrived) if rounds_of(replicas) else replicas
    moved = (steps * blocks * ROWS, LANES)
    carried = [pltpu.VMEM(value.shape, F32) for value in (gated, table)]
    scan_shape = jax.ShapeDtypeStruct(scan_next.shape, BF16)
    if last:
        outs = [
            jax.ShapeDtypeStruct((steps, slots, LANES), BF16),
            jax.ShapeDtypeStruct((steps + 1, slots, LANES), BF16),
            jax.ShapeDtypeStruct((steps + 1, slots, width), BF16),
            scan_shape,
        ]
        scratch = carried + [
            pltpu.VMEM((steps, slots, LANES), BF16),
            pltpu.VMEM((1, slots, LANES), BF16),
            pltpu.VMEM((1, slots, width), BF16),
        ]
        specs = [HBM] * 4
    else:
        outs, scratch, specs = carried + [scan_shape], [], [VMEM, VMEM, HBM]
    plan = operands[0]
    return pl.pallas_call(
        functools.partial(arrive_kernel, replicas, cap, first, last),
        out_shape=outs,
        in_specs=[VMEM] * len(operands) + [HBM] + [VMEM] * len(arrived),
        out_specs=specs,
        scratch_shapes=scratch
        + [
            pltpu.SMEM(plan.shape, plan.dtype),
            pltpu.VMEM(moved, F32),
            pltpu.VMEM(moved, F32),
            pltpu.VMEM((round_up(moved[0], LANES), LANES), F32),
            pltpu.VMEM((blocks * cap,) + scan_next.shape[1:], BF16),
            pltpu.SemaphoreType.DMA((blocks * cap + 5,)),
        ],
        input_output_aliases={len(operands): len(outs) - 1},
        compiler_params=pltpu.CompilerParams(
            vmem_limit_bytes=SMALL_LIMIT if rounds_of(replicas) else LARGE_LIMIT
        ),
        cost_estimate=pl.CostEstimate(
            flops=10_000_000, bytes_accessed=2_000_000, transcendentals=0
        ),
        name="advance_last" if last else "advance_arrived",
    )(*operands, scan_next, *arrived)


def swap_heads(value):
    return lax.ppermute(value, "head", [(0, 1), (1, 0)])


def exchange(replicas, blocks):
    rounds = rounds_of(replicas)
    if not rounds:
        return [lax.all_to_all(blocks[0], "dp", 0, 0, tiled=True)]
    return [
        lax.ppermute(block, "dp", [(source, source ^ mask) for source in range(replicas)])
        for mask, block in zip(rounds, blocks)
    ]


def per_device(
    replicas,
    tokens,
    inner_weight,
    gate_weight,
    group_weight,
    delta_weight,
    inner_taps,
    inner_offset,
    group_taps,
    group_offset,
    decay_log,
    delta_bias,
    skip_gain,
    inner_window,
    group_window,
    scan_state,
    send_list,
    receive_list,
    live_count,
):
    steps, slots, half = tokens.shape
    cap = send_list.shape[1] // replicas
    scan = jnp.transpose(scan_state, (0, 2, 1))
    inner = jnp.transpose(inner_window, (1, 0, 2))
    group = jnp.transpose(group_window, (1, 0, 2))
    own = tokens.reshape(steps * slots, half)

    group_weight = group_weight.T
    inner_offset = inner_offset[None]
    small = jnp.concatenate([group_taps, group_offset[None]], axis=0)
    group_other = swap_heads(group)
    swapped = [swap_heads(value) for value in (own, group_weight, small)]
    if rounds_of(replicas):
        blocks = pack(replicas, cap, send_list, scan, inner, group, group_other, swapped)
    else:
        blocks = pack_at_once(replicas, cap, send_list, scan, inner, group, group_other)
    arrived = exchange(replicas, blocks)
    plan, gated, weights, table, inner_part, group_part, *moved, scan_next = stay(
        replicas,
        cap,
        (decay_log, delta_bias, skip_gain, live_count),
        (
            receive_list,
            own,
            inner_weight,
            gate_weight,
            group_weight,
            delta_weight.T,
            inner_taps,
            inner_offset,
            inner,
            group,
            scan,
        ),
        (swapped[0], swapped[1], small, swapped[2], group_other),
        arrived[:EARLIER] if rounds_of(replicas) else [],
    )
    first = max(0, len(arrived) - LAST)
    if first:
        operands = (plan, weights, *moved, gated, table, inner_part, group_part)
        gated, table, scan_next = arrive(
            replicas, cap, 0, False, operands, scan_next, arrived[:first]
        )
    operands = (plan, weights, *moved, gated, table, inner_part, group_part)
    gated, inner_next, group_next, scan_next = arrive(
        replicas, cap, first, True, operands, scan_next, arrived[first:]
    )
    return (
        gated,
        jnp.transpose(inner_next, (1, 0, 2)),
        jnp.transpose(group_next, (1, 0, 2)),
        jnp.transpose(scan_next, (0, 2, 1)),
    )


def solution(mesh):
    in_specs = (
        P(None, ("grp", "dp"), "head"),
        P(None, "head"),
        P(None, "head"),
        P(None, "head"),
        P(None, "head"),
        P(None, "head"),
        P("head"),
        P(None, "head"),
        P("head"),
        P("head"),
        P("head"),
        P("head"),
        P(("grp", "dp"), None, "head"),
        P(("grp", "dp"), None, "head"),
        P(("grp", "dp"), "head", None),
        P(("grp", "dp"), None),
        P(("grp", "dp"), None),
        P(("grp", "dp")),
    )
    out_specs = (
        P(None, ("grp", "dp"), "head"),
        P(("grp", "dp"), None, "head"),
        P(("grp", "dp"), None, "head"),
        P(("grp", "dp"), "head", None),
    )
    return jax.shard_map(
        functools.partial(per_device, mesh.shape["dp"]),
        mesh=mesh,
        in_specs=in_specs,
        out_specs=out_specs,
        check_vma=False,
    )
```

```python
import functools

import jax
import jax.numpy as jnp
from jax import lax
from jax.experimental import pallas as pl
from jax.experimental.pallas import tpu as pltpu
from jax.sharding import PartitionSpec as P

F32 = jnp.float32
BF16 = jnp.bfloat16
SMALL_LIMIT = 8 * 1024 * 1024
MEDIUM_LIMIT = 16 * 1024 * 1024
LARGE_LIMIT = 48 * 1024 * 1024
MAX_ROUNDS = 16
EARLIER = 3
LAST = 2
LANES = 128
ROWS = 8
MAX_SETS = 64

VMEM = pl.BlockSpec(memory_space=pltpu.VMEM)
SMEM = pl.BlockSpec(memory_space=pltpu.SMEM)
HBM = pl.BlockSpec(memory_space=pl.ANY)


def in_hbm(value):
    return pltpu.with_memory_space_constraint(value, pltpu.HBM)


def in_vmem(value):
    return pltpu.with_memory_space_constraint(value, pltpu.VMEM)


def round_up(value, step):
    return -(-value // step) * step


def silu(value):
    return value * jax.nn.sigmoid(value)


def rounded(value):
    return value.astype(BF16).astype(F32)


def rounds_of(replicas):
    if replicas > MAX_ROUNDS or replicas & (replicas - 1):
        return []
    light = list(range(1, replicas // 2))
    heavy = list(range(replicas // 2, replicas))
    heavy = heavy[::2] + heavy[1::2]
    return heavy[:1] + light[:2] + heavy[1:2] + light[2:] + heavy[2:]


def partner(replicas, mask):
    return jnp.bitwise_xor(lax.axis_index("dp"), mask)


def both_halves(mine, theirs):
    first = lax.axis_index("head") == 0
    return jnp.concatenate(
        [jnp.where(first, mine, theirs), jnp.where(first, theirs, mine)], axis=-1
    )


def destinations(replicas, outs):
    rounds = rounds_of(replicas)
    if rounds:
        return [(ref.at[0], partner(replicas, mask)) for ref, mask in zip(outs, rounds)]
    return [(outs[0].at[target], target) for target in range(replicas)]


def states_kernel(replicas, cap, scan, send, inner, group, *refs):
    outs, (picked, group_out, indices_out) = refs[:-11], refs[-11:-8]
    indices, inner_in, table, load_sem, group_sem, list_sem, save_sem, sem = refs[-8:]
    load_list = pltpu.make_async_copy(send, indices, list_sem)
    load_list.start()
    load = pltpu.make_async_copy(inner, inner_in, load_sem)
    load.start()
    load_group = pltpu.make_async_copy(group, group_out, group_sem)
    load_group.start()
    state_rows = scan.shape[1]
    blocks = destinations(replicas, outs)
    load_list.wait()
    save = pltpu.make_async_copy(indices, indices_out, save_sem)
    save.start()
    plan = []
    for block, (ref, target) in enumerate(blocks):
        for c in range(cap):
            plan.append((block, ref, c, indices[0, target * cap + c]))

    def each(act):
        for place, (_, ref, c, index) in enumerate(plan):

            @pl.when(index >= 0)
            def _():
                act(
                    pltpu.make_async_copy(
                        scan.at[index],
                        ref.at[pl.ds(c * state_rows, state_rows)],
                        sem.at[place],
                    )
                )

    each(lambda copy: copy.start())
    load.wait()
    taps = inner_in.shape[0]
    for tap in range(taps):
        table[:, tap * LANES : (tap + 1) * LANES] = inner_in[tap].astype(F32)
    picked[...] = jnp.zeros_like(picked)
    for block, _, c, index in plan:
        row = table[pl.ds(jnp.maximum(index, 0), 1), :]
        for tap in range(taps):
            picked[block, tap * ROWS + c : tap * ROWS + c + 1, :] = row[
                :, tap * LANES : (tap + 1) * LANES
            ]
    load_group.wait()
    save.wait()
    each(lambda copy: copy.wait())


def windows_kernel(replicas, cap, state_rows, indices_in, group, group_other, picked_in, *refs):
    count = max(1, len(rounds_of(replicas)))
    outs = refs[-4 - count : -4]
    indices, table, picked, sem = refs[-4:]
    load = pltpu.make_async_copy(indices_in, indices, sem)
    load.start()
    taps = group.shape[0]
    for tap in range(taps):
        table[:, tap * LANES : (tap + 1) * LANES] = both_halves(
            group[tap].astype(F32), group_other[tap].astype(F32)
        )
    picked[...] = jnp.zeros_like(picked)
    load.wait()
    for block, (ref, target) in enumerate(destinations(replicas, outs)):
        for c in range(cap):
            index = jnp.maximum(indices[0, target * cap + c], 0)
            row = table[pl.ds(index, 1), :]
            for tap in range(taps):
                picked[block, tap * ROWS + c : tap * ROWS + c + 1, :] = row[
                    :, tap * LANES : (tap + 1) * LANES
                ]
        ref[cap * state_rows :, :] = jnp.concatenate(
            [picked_in[block], picked[block]], axis=0
        ).astype(BF16)


def pack(replicas, cap, send_list, scan, inner, group, group_other, swapped):
    rounds = rounds_of(replicas)
    count = max(1, len(rounds))
    per_block = 1 if rounds else replicas
    taps, slots, _ = inner.shape
    rows = cap * scan.shape[1] + 2 * taps * ROWS
    blocks = count * per_block
    shapes = [pltpu.VMEM((per_block, rows, LANES), BF16)] * count
    half = (blocks, taps * ROWS, LANES)
    limit = SMALL_LIMIT if rounds else MEDIUM_LIMIT
    *states, picked, group_near, indices = pl.pallas_call(
        functools.partial(states_kernel, replicas, cap),
        out_shape=shapes
        + [
            pltpu.VMEM(half, F32),
            pltpu.VMEM(group.shape, BF16),
            pltpu.VMEM(send_list.shape, jnp.int32),
        ],
        in_specs=[HBM] * 4,
        out_specs=[VMEM] * (count + 3),
        scratch_shapes=[
            pltpu.SMEM(send_list.shape, jnp.int32),
            pltpu.VMEM(inner.shape, BF16),
            pltpu.VMEM((slots, taps * LANES), F32),
            pltpu.SemaphoreType.DMA,
            pltpu.SemaphoreType.DMA,
            pltpu.SemaphoreType.DMA,
            pltpu.SemaphoreType.DMA,
            pltpu.SemaphoreType.DMA((blocks * cap,)),
        ],
        compiler_params=pltpu.CompilerParams(vmem_limit_bytes=limit),
        cost_estimate=pl.CostEstimate(flops=0, bytes_accessed=2_000_000, transcendentals=0),
        name="pack_states",
    )(in_hbm(scan), in_hbm(send_list), in_hbm(inner), in_hbm(group))
    near = [in_vmem(value) for value in states]
    return pl.pallas_call(
        functools.partial(windows_kernel, replicas, cap, scan.shape[1]),
        out_shape=shapes,
        in_specs=[VMEM] * (4 + count) + [HBM] * len(swapped),
        out_specs=[VMEM] * count,
        scratch_shapes=[
            pltpu.SMEM(send_list.shape, jnp.int32),
            pltpu.VMEM((slots, taps * LANES), F32),
            pltpu.VMEM(half, F32),
            pltpu.SemaphoreType.DMA,
        ],
        input_output_aliases={4 + place: place for place in range(count)},
        compiler_params=pltpu.CompilerParams(vmem_limit_bytes=limit),
        cost_estimate=pl.CostEstimate(flops=0, bytes_accessed=500_000, transcendentals=0),
        name="pack_windows",
    )(indices, group_near, group_other, picked, *near, *swapped)


def at_once_kernel(replicas, cap, scan, send, inner, group, group_other, *refs):
    rounds = rounds_of(replicas)
    count = max(1, len(rounds))
    outs = refs[-8 - count : -8]
    indices, inner_in, group_in, table, picked, load_sem, list_sem, sem = refs[-8:]
    load_list = pltpu.make_async_copy(send, indices, list_sem)
    load_list.start()
    loads = [
        pltpu.make_async_copy(source, target, load_sem.at[place])
        for place, (source, target) in enumerate([(inner, inner_in), (group, group_in)])
    ]
    for load in loads:
        load.start()
    state_rows = scan.shape[1]
    if rounds:
        blocks = [(ref.at[0], partner(replicas, mask)) for ref, mask in zip(outs, rounds)]
    else:
        blocks = [(outs[0].at[target], target) for target in range(replicas)]
    load_list.wait()

    plan = []
    for block, (ref, target) in enumerate(blocks):
        for c in range(cap):
            plan.append((block, ref, c, indices[0, target * cap + c]))

    def each(act):
        for place, (_, ref, c, index) in enumerate(plan):

            @pl.when(index >= 0)
            def _():
                act(
                    pltpu.make_async_copy(
                        scan.at[index],
                        ref.at[pl.ds(c * state_rows, state_rows)],
                        sem.at[place],
                    )
                )

    each(lambda copy: copy.start())
    for load in loads:
        load.wait()
    taps = inner_in.shape[0]
    for tap in range(taps):
        table[:, tap * LANES : (tap + 1) * LANES] = inner_in[tap].astype(F32)
        table[:, (taps + tap) * LANES : (taps + tap + 1) * LANES] = both_halves(
            group_in[tap].astype(F32), group_other[tap].astype(F32)
        )
    picked[...] = jnp.zeros_like(picked)
    for block, _, c, index in plan:
        row = table[pl.ds(jnp.maximum(index, 0), 1), :]
        for kind in range(2 * taps):
            picked[block, kind * ROWS + c : kind * ROWS + c + 1, :] = row[
                :, kind * LANES : (kind + 1) * LANES
            ]
    for block, (ref, _) in enumerate(blocks):
        ref[cap * state_rows :, :] = picked[block].astype(BF16)
    each(lambda copy: copy.wait())


def pack_at_once(replicas, cap, send_list, scan, inner, group, group_other):
    rounds = rounds_of(replicas)
    count = max(1, len(rounds))
    per_block = 1 if rounds else replicas
    taps, slots, _ = inner.shape
    window_rows = 2 * taps * ROWS
    rows = cap * scan.shape[1] + window_rows
    blocks = count * per_block
    return pl.pallas_call(
        functools.partial(at_once_kernel, replicas, cap),
        out_shape=[jax.ShapeDtypeStruct((per_block, rows, LANES), BF16)] * count,
        in_specs=[HBM] * 4 + [VMEM],
        out_specs=[VMEM] * count,
        scratch_shapes=[
            pltpu.SMEM(send_list.shape, jnp.int32),
            pltpu.VMEM(inner.shape, BF16),
            pltpu.VMEM(group.shape, BF16),
            pltpu.VMEM((slots, 2 * taps * LANES), F32),
            pltpu.VMEM((blocks, window_rows, LANES), F32),
            pltpu.SemaphoreType.DMA((2,)),
            pltpu.SemaphoreType.DMA,
            pltpu.SemaphoreType.DMA((blocks * cap,)),
        ],
        compiler_params=pltpu.CompilerParams(vmem_limit_bytes=LARGE_LIMIT),
        cost_estimate=pl.CostEstimate(flops=0, bytes_accessed=2_000_000, transcendentals=0),
        name="pack_leaving",
    )(in_hbm(scan), in_hbm(send_list), in_hbm(inner), in_hbm(group), group_other)


def sources_of(replicas):
    rounds = rounds_of(replicas)
    if rounds:
        return [partner(replicas, mask) for mask in rounds]
    return list(range(replicas))


def make_plan(replicas, cap, receive, slots, plan, inverse):
    moving = slots // 2
    kept = 0
    for entry in range(replicas * cap):
        inverse[entry] = -1
    for slot in range(slots):
        entry = receive[0, slot]
        stays = entry < 0
        plan[0, jnp.where(stays, kept, moving)] = slot
        inverse[jnp.where(stays, replicas * cap, entry)] = slot
        kept = kept + jnp.where(stays, 1, 0)
    for block, source in enumerate(sources_of(replicas)):
        for c in range(cap):
            plan[0, moving + block * cap + c] = inverse[source * cap + c]


def convolve(carried, raw, weights, offset):
    joined = carried + raw
    results = []
    for step in range(len(raw)):
        summed = offset
        for tap in range(len(carried) + 1):
            summed = summed + joined[step + tap] * weights[tap : tap + 1, :]
        results.append(rounded(silu(summed)))
    return results


def transposed(rows, scratch, stride):
    scratch[...] = jnp.zeros_like(scratch)
    for step, value in enumerate(rows):
        scratch[step * stride : step * stride + value.shape[0], :] = value
    return [scratch[first : first + LANES].T for first in range(0, scratch.shape[0], LANES)]


def advance_slot(state, rows, driven, decays, sums, maps, lanes):
    hidden = state.astype(F32)
    width = state.shape[0]
    for row, decay, lane in zip(rows, decays, lanes):
        piece = maps[lane // LANES]
        column = piece[:, lane % LANES : lane % LANES + 1]
        hidden = decay * hidden + driven[row, :] * column[:width]
        sums[row, :] = jnp.sum(hidden * column[width:], axis=0, keepdims=True)
        result = hidden.astype(BF16)
        hidden = result.astype(F32)
    return result


def stay_kernel(
    replicas,
    cap,
    decay_log,
    delta_bias,
    skip_gain,
    live,
    receive_hbm,
    own_hbm,
    inner_weight,
    gate_weight,
    group_weight,
    delta_weight,
    inner_taps_hbm,
    inner_offset_hbm,
    inner_hbm,
    group_hbm,
    scan_hbm,
    other,
    group_weight_other,
    small,
    small_other,
    group_other,
    *refs,
):
    (
        plan_out,
        gated,
        weights,
        base,
        inner_part,
        group_part,
        inner_moved,
        group_moved,
        gate_moved,
        delta_moved,
        decay_moved,
        scan_next,
        plan,
        receive,
        own,
        wide,
        tall,
        delta_row,
        inner_taps,
        inner_offset,
        inner,
        group,
        scan,
        inverse,
        inner_raw,
        both,
        gate,
        delta,
        decay,
        driven,
        skipped,
        sums,
        maps_in,
        ordered,
        done,
        sem,
        load_sem,
    ) = refs[-37:]
    taps, slots, _ = inner.shape
    rows, half = own.shape
    steps = rows // slots
    moving = slots // 2
    moved_rows = inner_moved.shape[0] // steps
    width = group.shape[2]
    head = lax.axis_index("head")

    def band(place):
        return tall.at[pl.ds(pl.multiple_of(place * width, width), width)]

    pairs = [
        (receive_hbm, receive),
        (delta_weight, delta_row),
        (own_hbm, own),
        (inner_weight, wide.at[:, pl.ds(0, LANES)]),
        (gate_weight, wide.at[:, pl.ds(LANES, LANES)]),
        (group_weight, band(head)),
        (group_weight_other, band(1 - head)),
        (inner_taps_hbm, inner_taps),
        (inner_offset_hbm, inner_offset),
        (inner_hbm, inner),
        (group_hbm, group),
        (scan_hbm, scan),
    ]
    loads = [
        pltpu.make_async_copy(source, target, load_sem.at[place])
        for place, (source, target) in enumerate(pairs)
    ]
    for load in loads:
        load.start()
    loads[0].wait()
    make_plan(replicas, cap, receive, slots, plan, inverse)
    loads[1].wait()
    first = 2 * width
    tall[first:, :] = jnp.broadcast_to(delta_row[...], (tall.shape[0] - first, 2 * half))
    for load in loads[2:]:
        load.wait()
    mine = pl.ds(pl.multiple_of(head * half, half), half)
    theirs = pl.ds(pl.multiple_of((1 - head) * half, half), half)
    flat = jnp.dot(own[...], wide[mine, :], preferred_element_type=F32) + jnp.dot(
        other[...], wide[theirs, :], preferred_element_type=F32
    )

    def across(tokens, part):
        return lax.dot_general(
            tokens, tall[:, part], (((1,), (1,)), ((), ())), preferred_element_type=F32
        )

    deep = across(own[...], mine) + across(other[...], theirs)
    inner_raw[...] = rounded(flat[:, :LANES])
    gate[...] = silu(rounded(flat[:, LANES:]))
    both[...] = rounded(deep[:, :first])
    shifted = rounded(jnp.broadcast_to(deep[:, first : first + 1], (rows, LANES)))
    shifted = shifted + delta_bias[0]
    rate = jnp.maximum(shifted, 0.0) + jnp.log1p(jnp.exp(-jnp.abs(shifted)))
    delta[...] = rate
    decay[...] = jnp.exp(-rate * jnp.exp(jnp.full((1, LANES), decay_log[0], F32)))
    count = taps + 2
    weights[:count, :] = both_halves(small[...], small_other[...])
    weights[count : count + 1, :] = jnp.full((1, LANES), skip_gain[0], F32)
    later = round_up(count + 1, ROWS)
    weights[later : later + taps + 1, :] = inner_taps[...]
    weights[later + taps + 1 : later + taps + 2, :] = inner_offset[...]
    plan[0, plan.shape[1] - 1] = live[0]
    save_plan = pltpu.make_async_copy(plan, plan_out, load_sem.at[0])
    save_plan.start()

    def parts(ref):
        return [ref[step * slots : (step + 1) * slots, :] for step in range(steps)]

    inner_conv = convolve(
        [inner[tap].astype(F32) for tap in range(taps)],
        parts(inner_raw),
        inner_taps[...],
        inner_offset[...],
    )
    group_conv = convolve(
        [both_halves(group[tap].astype(F32), group_other[tap].astype(F32)) for tap in range(taps)],
        parts(both),
        weights[: taps + 1, :],
        weights[taps + 1 : taps + 2, :],
    )
    for step in range(steps):
        part = slice(step * slots, (step + 1) * slots)
        driven[part, :] = delta[part, :] * inner_conv[step]
        skipped[part, :] = inner_conv[step] * skip_gain[0]
        maps_in[part, :] = group_conv[step]
    sums[...] = jnp.zeros_like(sums)
    stride = ordered.shape[0] // steps
    ordered[...] = jnp.zeros_like(ordered)
    for position in range(moving):
        slot = plan[0, position]
        for step in range(steps):
            ordered[step * stride + position : step * stride + position + 1, :] = maps_in[
                pl.ds(step * slots + slot, 1), :
            ]
    maps = [ordered[first : first + LANES].T for first in range(0, ordered.shape[0], LANES)]
    copies = []
    for position in range(moving):
        slot = plan[0, position]
        result = advance_slot(
            scan[slot],
            [pl.ds(step * slots + slot, 1) for step in range(steps)],
            driven,
            [decay[pl.ds(step * slots + slot, 1), :] for step in range(steps)],
            sums,
            maps,
            [step * stride + position for step in range(steps)],
        )
        done[position] = jnp.where(slot < live[0], result, jnp.zeros_like(result))
        copies.append(
            pltpu.make_async_copy(done.at[position], scan_next.at[slot], sem.at[position])
        )
        copies[-1].start()
    gated[...] = (sums[...] + skipped[...]) * gate[...]
    pairs = (
        (inner_raw, inner_moved),
        (both, group_moved),
        (gate, gate_moved),
        (delta, delta_moved),
        (decay, decay_moved),
    )
    for _, target in pairs:
        target[...] = jnp.zeros_like(target)
    living = lax.broadcasted_iota(jnp.int32, (slots, LANES), 0) < live[0]
    for step in range(steps):
        part = slice(step * slots, (step + 1) * slots)
        inner_part[step] = jnp.where(living, inner_raw[part, :], 0.0).astype(BF16)
        raw = jnp.where(head == 0, both[part, :width], both[part, width:])
        group_part[step] = jnp.where(living[:, :width], raw, 0.0).astype(BF16)
    base[:, :LANES] = inner[steps].astype(F32)
    group_own = group[steps].astype(F32)
    base[:, LANES:] = jnp.concatenate([group_own, group_own], axis=1)
    for block in range(moved_rows // ROWS):

        @pl.when(plan[0, moving + block * cap] >= 0)
        def _():
            for c in range(cap):
                slot = plan[0, moving + block * cap + c]
                for step in range(steps):
                    row = step * moved_rows + block * ROWS + c
                    for source, target in pairs:
                        target[row : row + 1, :] = source[pl.ds(step * slots + slot, 1), :]

    for copy in copies:
        copy.wait()
    save_plan.wait()


def stay(replicas, cap, scalars, arrays, near, earlier):
    receive, own, group_weight, delta_weight = arrays[0], arrays[1], arrays[4], arrays[5]
    inner, scan = arrays[-3], arrays[-1]
    taps, slots, _ = inner.shape
    rows = own.shape[0]
    steps = rows // slots
    moving = slots // 2
    blocks = len(sources_of(replicas))
    moved_rows = blocks * ROWS
    width, features = group_weight.shape
    full = pltpu.VMEM((rows, LANES), F32)
    moved = pltpu.VMEM((steps * moved_rows, LANES), F32)
    plan_shape = (1, round_up(moving + blocks * cap + 1, LANES))

    def like(value):
        return pltpu.VMEM(value.shape, value.dtype)

    far = [in_hbm(value) for value in arrays]
    return pl.pallas_call(
        functools.partial(stay_kernel, replicas, cap),
        out_shape=[
            pltpu.VMEM(plan_shape, jnp.int32),
            full,
            pltpu.VMEM((2 * round_up(taps + 3, ROWS), LANES), F32),
            pltpu.VMEM((slots, 2 * LANES), F32),
            pltpu.VMEM((steps, slots, LANES), BF16),
            pltpu.VMEM((steps, slots, width), BF16),
        ]
        + [moved] * 5
        + [jax.ShapeDtypeStruct(scan.shape, BF16)],
        in_specs=[SMEM] * len(scalars)
        + [HBM] * len(far)
        + [VMEM] * len(near)
        + [HBM] * len(earlier),
        out_specs=[VMEM] * 11 + [HBM],
        scratch_shapes=[
            pltpu.SMEM(plan_shape, jnp.int32),
            pltpu.SMEM(receive.shape, jnp.int32),
            like(own),
            pltpu.VMEM((features, 2 * LANES), BF16),
            pltpu.VMEM((2 * width + 2 * ROWS, features), BF16),
            like(delta_weight),
        ]
        + [like(value) for value in arrays[6:]]
        + [pltpu.SMEM((replicas * cap + 1,), jnp.int32)]
        + [pltpu.VMEM((rows, LANES), F32)] * 9
        + [
            pltpu.VMEM((round_up(rows, LANES), LANES), F32),
            pltpu.VMEM((moving,) + scan.shape[1:], BF16),
            pltpu.SemaphoreType.DMA((moving,)),
            pltpu.SemaphoreType.DMA((16,)),
        ],
        compiler_params=pltpu.CompilerParams(vmem_limit_bytes=MEDIUM_LIMIT),
        cost_estimate=pl.CostEstimate(
            flops=300_000_000, bytes_accessed=6_000_000, transcendentals=100_000
        ),
        name="advance_staying",
    )(*scalars, *far, *near, *earlier)


def arrive_kernel(
    replicas,
    cap,
    first,
    last,
    plan_near,
    weights,
    inner_moved,
    group_moved,
    gate_moved,
    delta_moved,
    decay_moved,
    gated_in,
    table_in,
    inner_part,
    group_part,
    scan_in,
    *refs,
):
    del scan_in
    if last:
        arrived = refs[:-15]
        gated_out, inner_next, group_next, scan_next = refs[-15:-11]
        gated, table = refs[-11:-9]
        gated_cast, inner_cast, group_cast = refs[-9:-6]
    else:
        arrived = refs[:-9]
        gated, table, scan_next = refs[-9:-6]
    plan, driven, sums, ordered, done, sem = refs[-6:]
    steps, slots, width = group_part.shape
    taps = steps + 1
    moving = slots // 2
    state_rows = scan_next.shape[1]
    head = lax.axis_index("head")
    load = pltpu.make_async_copy(plan_near, plan, sem.at[0])
    load.start()
    if rounds_of(replicas):
        blocks = [ref.at[0] for ref in arrived]
    else:
        blocks = [arrived[0].at[source] for source in range(replicas)]
    stored = inner_moved.shape[0] // steps
    moved_rows = len(blocks) * ROWS
    if last:
        copies = [
            pltpu.make_async_copy(source, target, sem.at[1 + place])
            for place, (source, target) in enumerate(
                [
                    (inner_part, inner_next.at[pl.ds(1, steps)]),
                    (group_part, group_next.at[pl.ds(1, steps)]),
                ]
            )
        ]
        for copy in copies:
            copy.start()

    def parts(ref):
        starts = [step * stored + first * ROWS for step in range(steps)]
        return [ref[start : start + moved_rows, :] for start in starts]

    kinds = [[] for _ in range(2 * taps)]
    for ref in blocks:
        block = ref[cap * state_rows :, :].astype(F32)
        for kind in range(2 * taps):
            kinds[kind].append(block[kind * ROWS : (kind + 1) * ROWS])
    windows = [jnp.concatenate(kind, axis=0) for kind in kinds]
    later = round_up(taps + 3, ROWS)
    inner_conv = convolve(
        windows[:taps],
        parts(inner_moved),
        weights[later : later + taps + 1, :],
        weights[later + taps + 1 : later + taps + 2, :],
    )
    group_conv = convolve(
        windows[taps:],
        parts(group_moved),
        weights[: taps + 1, :],
        weights[taps + 1 : taps + 2, :],
    )
    for step, delta in enumerate(parts(delta_moved)):
        driven[step * moved_rows : (step + 1) * moved_rows, :] = delta * inner_conv[step]
    stride = ordered.shape[0] // steps
    maps = transposed(group_conv, ordered, stride)
    sums[...] = jnp.zeros_like(sums)
    gated[...] = gated_in[...]
    table[...] = table_in[...]
    load.wait()
    live = plan[0, plan.shape[1] - 1]

    def each(act):
        for block in range(len(blocks)):
            entry = moving + (first + block) * cap

            @pl.when(plan[0, entry] >= 0)
            def _():
                for c in range(cap):
                    act(block, c, plan[0, entry + c])

    def store(block, c, slot):
        place = block * cap + c
        return pltpu.make_async_copy(done.at[place], scan_next.at[slot], sem.at[4 + place])

    def advance(block, c, slot):
        place = block * ROWS + c
        rows = [step * moved_rows + place for step in range(steps)]
        result = advance_slot(
            blocks[block][c * state_rows : (c + 1) * state_rows, :],
            [slice(row, row + 1) for row in rows],
            driven,
            [
                decay_moved[row : row + 1, :]
                for row in (step * stored + first * ROWS + place for step in range(steps))
            ],
            sums,
            maps,
            [step * stride + place for step in range(steps)],
        )
        done[block * cap + c] = jnp.where(slot < live, result, jnp.zeros_like(result))
        store(block, c, slot).start()

    each(advance)
    for step, gate in enumerate(parts(gate_moved)):
        part = slice(step * moved_rows, (step + 1) * moved_rows)
        skipped = inner_conv[step] * weights[taps + 2 : taps + 3, :]
        sums[part, :] = (sums[part, :] + skipped) * gate
    driven[:moved_rows, :] = windows[taps - 1]
    driven[moved_rows : 2 * moved_rows, :] = windows[2 * taps - 1]

    def scatter(block, c, slot):
        place = block * ROWS + c
        for step in range(steps):
            row = step * moved_rows + place
            gated[pl.ds(step * slots + slot, 1), :] = sums[row : row + 1, :]
        table[pl.ds(slot, 1), :] = jnp.concatenate(
            [driven[place : place + 1, :], driven[moved_rows + place : moved_rows + place + 1, :]],
            axis=1,
        )

    each(scatter)
    if last:
        living = lax.broadcasted_iota(jnp.int32, (slots, LANES), 0) < live
        for step in range(steps):
            part = slice(step * slots, (step + 1) * slots)
            gated_cast[step] = jnp.where(living, gated[part, :], 0.0).astype(BF16)
        inner_cast[0] = jnp.where(living, table[:, :LANES], 0.0).astype(BF16)
        carried = jnp.where(head == 0, table[:, LANES : LANES + width], table[:, LANES + width :])
        group_cast[0] = jnp.where(living[:, :width], carried, 0.0).astype(BF16)
        ends = [
            pltpu.make_async_copy(source, target, semaphore)
            for source, target, semaphore in (
                (gated_cast, gated_out, sem.at[0]),
                (inner_cast, inner_next.at[pl.ds(0, 1)], sem.at[3]),
                (group_cast, group_next.at[pl.ds(0, 1)], sem.at[sem.shape[0] - 1]),
            )
        ]
        for copy in ends:
            copy.start()
        for copy in copies + ends:
            copy.wait()
    each(lambda block, c, slot: store(block, c, slot).wait())


def arrive(replicas, cap, first, last, operands, scan_next, arrived):
    inner_moved, gated, table, inner_part, group_part = operands[2], *operands[7:]
    steps, slots, width = group_part.shape
    blocks = len(arrived) if rounds_of(replicas) else replicas
    moved = (steps * blocks * ROWS, LANES)
    carried = [pltpu.VMEM(value.shape, F32) for value in (gated, table)]
    scan_shape = jax.ShapeDtypeStruct(scan_next.shape, BF16)
    if last:
        outs = [
            jax.ShapeDtypeStruct((steps, slots, LANES), BF16),
            jax.ShapeDtypeStruct((steps + 1, slots, LANES), BF16),
            jax.ShapeDtypeStruct((steps + 1, slots, width), BF16),
            scan_shape,
        ]
        scratch = carried + [
            pltpu.VMEM((steps, slots, LANES), BF16),
            pltpu.VMEM((1, slots, LANES), BF16),
            pltpu.VMEM((1, slots, width), BF16),
        ]
        specs = [HBM] * 4
    else:
        outs, scratch, specs = carried + [scan_shape], [], [VMEM, VMEM, HBM]
    plan = operands[0]
    return pl.pallas_call(
        functools.partial(arrive_kernel, replicas, cap, first, last),
        out_shape=outs,
        in_specs=[VMEM] * len(operands) + [HBM] + [VMEM] * len(arrived),
        out_specs=specs,
        scratch_shapes=scratch
        + [
            pltpu.SMEM(plan.shape, plan.dtype),
            pltpu.VMEM(moved, F32),
            pltpu.VMEM(moved, F32),
            pltpu.VMEM((round_up(moved[0], LANES), LANES), F32),
            pltpu.VMEM((blocks * cap,) + scan_next.shape[1:], BF16),
            pltpu.SemaphoreType.DMA((blocks * cap + 5,)),
        ],
        input_output_aliases={len(operands): len(outs) - 1},
        compiler_params=pltpu.CompilerParams(
            vmem_limit_bytes=SMALL_LIMIT if rounds_of(replicas) else LARGE_LIMIT
        ),
        cost_estimate=pl.CostEstimate(
            flops=10_000_000, bytes_accessed=2_000_000, transcendentals=0
        ),
        name="advance_last" if last else "advance_arrived",
    )(*operands, scan_next, *arrived)


def swap_heads(value):
    return lax.ppermute(value, "head", [(0, 1), (1, 0)])


def exchange(replicas, blocks):
    rounds = rounds_of(replicas)
    if not rounds:
        return [lax.all_to_all(blocks[0], "dp", 0, 0, tiled=True)]
    return [
        lax.ppermute(block, "dp", [(source, source ^ mask) for source in range(replicas)])
        for mask, block in zip(rounds, blocks)
    ]


def per_device(
    replicas,
    tokens,
    inner_weight,
    gate_weight,
    group_weight,
    delta_weight,
    inner_taps,
    inner_offset,
    group_taps,
    group_offset,
    decay_log,
    delta_bias,
    skip_gain,
    inner_window,
    group_window,
    scan_state,
    send_list,
    receive_list,
    live_count,
):
    steps, slots, half = tokens.shape
    cap = send_list.shape[1] // replicas
    scan = jnp.transpose(scan_state, (0, 2, 1))
    inner = jnp.transpose(inner_window, (1, 0, 2))
    group = jnp.transpose(group_window, (1, 0, 2))
    own = tokens.reshape(steps * slots, half)

    group_weight = group_weight.T
    inner_offset = inner_offset[None]
    small = jnp.concatenate([group_taps, group_offset[None]], axis=0)
    group_other = swap_heads(group)
    swapped = [swap_heads(value) for value in (own, group_weight, small)]
    if rounds_of(replicas):
        blocks = pack(replicas, cap, send_list, scan, inner, group, group_other, swapped)
    else:
        blocks = pack_at_once(replicas, cap, send_list, scan, inner, group, group_other)
    arrived = exchange(replicas, blocks)
    plan, gated, weights, table, inner_part, group_part, *moved, scan_next = stay(
        replicas,
        cap,
        (decay_log, delta_bias, skip_gain, live_count),
        (
            receive_list,
            own,
            inner_weight,
            gate_weight,
            group_weight,
            delta_weight.T,
            inner_taps,
            inner_offset,
            inner,
            group,
            scan,
        ),
        (swapped[0], swapped[1], small, swapped[2], group_other),
        arrived[:EARLIER] if rounds_of(replicas) else [],
    )
    first = max(0, len(arrived) - LAST)
    if first:
        operands = (plan, weights, *moved, gated, table, inner_part, group_part)
        gated, table, scan_next = arrive(
            replicas, cap, 0, False, operands, scan_next, arrived[:first]
        )
    operands = (plan, weights, *moved, gated, table, inner_part, group_part)
    gated, inner_next, group_next, scan_next = arrive(
        replicas, cap, first, True, operands, scan_next, arrived[first:]
    )
    return (
        gated,
        jnp.transpose(inner_next, (1, 0, 2)),
        jnp.transpose(group_next, (1, 0, 2)),
        jnp.transpose(scan_next, (0, 2, 1)),
    )


def solution(mesh):
    in_specs = (
        P(None, ("grp", "dp"), "head"),
        P(None, "head"),
        P(None, "head"),
        P(None, "head"),
        P(None, "head"),
        P(None, "head"),
        P("head"),
        P(None, "head"),
        P("head"),
        P("head"),
        P("head"),
        P("head"),
        P(("grp", "dp"), None, "head"),
        P(("grp", "dp"), None, "head"),
        P(("grp", "dp"), "head", None),
        P(("grp", "dp"), None),
        P(("grp", "dp"), None),
        P(("grp", "dp")),
    )
    out_specs = (
        P(None, ("grp", "dp"), "head"),
        P(("grp", "dp"), None, "head"),
        P(("grp", "dp"), None, "head"),
        P(("grp", "dp"), "head", None),
    )
    return jax.shard_map(
        functools.partial(per_device, mesh.shape["dp"]),
        mesh=mesh,
        in_specs=in_specs,
        out_specs=out_specs,
        check_vma=False,
    )
```
